32 devices in a mesh: dp: 16 (over z, y, x), tensor: 2 (over core).
Axes of the slice: x: 2, y: 2, z: 4, core: 2. Of those that a mesh axis runs over, the one named last changes fastest.
Arguments:
- page_image: bfloat16 [3, 512, 128], P(None, ('dp', 'tensor')), may hold values from -12 to 12
- embeddings: bfloat16 [16384, 768], P('dp'), may hold values from -6 to 6
- cotangent: bfloat16 [16384, 768], P('dp'), may hold values from -6 to 6
- doc_ids: int32 [16, 1024], P('dp'), may hold values from 0 to 2, never falling along the last dimension, each value on 1 to 768 neighbouring positions
- pad_mask: int32 [16, 1024], P('dp'), may hold values 0 or 1
- token_boxes: int32 [4, 16, 1024], P(None, 'dp'), may hold values from 0 to 127, as said below
- conv_first: bfloat16 [3, 128], replicated, may hold values from -3.5 to 3.5
- conv_weights: bfloat16 [8, 128, 128], replicated, may hold values from -0.5 to 0.5
- group_gain: float32 [9, 128], replicated, may hold values from 0.25 to 1.75
- group_shift: float32 [9, 128], replicated, may hold values from -3 to 3
- roi_proj: bfloat16 [128, 768], replicated, may hold values from -0.5 to 0.5
- attn_norm: float32 [768], replicated, may hold values from 0.25 to 1.75
- query_proj: bfloat16 [768, 768], P(None, 'tensor'), may hold values from -0.21875 to 0.21875
- key_proj: bfloat16 [768, 768], P(None, 'tensor'), may hold values from -0.21875 to 0.21875
- value_proj: bfloat16 [768, 768], P(None, 'tensor'), may hold values from -0.21875 to 0.21875
- output_proj: bfloat16 [768, 768], P('tensor'), may hold values from -0.625 to 0.625
- bias_tables: float32 [3, 32, 12], P(None, None, 'tensor'), may hold values from -3 to 3
- ffn_norm: float32 [768], replicated, may hold values from 0.25 to 1.75
- up_proj: bfloat16 [768, 3072], P(None, 'tensor'), may hold values from -0.21875 to 0.21875
- down_proj: bfloat16 [3072, 768], P('tensor'), may hold values from -0.109375 to 0.109375
Outputs:
- layer_out: bfloat16 [16384, 768], P('dp')
- grad_embeddings: float32 [16384, 768], P('dp')
- grad_conv_first: float32 [3, 128], replicated
- grad_conv_weights: float32 [8, 128, 128], replicated
- grad_group_gain: float32 [9, 128], replicated
- grad_group_shift: float32 [9, 128], replicated
- grad_roi_proj: float32 [128, 768], P(None, 'dp')
- grad_attn_norm: float32 [768], P('dp')
- grad_query_proj: float32 [768, 768], P('dp', 'tensor')
- grad_key_proj: float32 [768, 768], P('dp', 'tensor')
- grad_value_proj: float32 [768, 768], P('dp', 'tensor')
- grad_output_proj: float32 [768, 768], P('tensor', 'dp')
- grad_bias_tables: float32 [3, 32, 12], P(None, None, 'tensor')
- grad_ffn_norm: float32 [768], P('dp')
- grad_up_proj: float32 [768, 3072], P('dp', 'tensor')
- grad_down_proj: float32 [3072, 768], P('tensor', 'dp')
The draws below stay inside these ranges and needn't reach their ends.
Inputs may be any that keep to these rules, and one draw needn't show every extreme that they name: `doc_ids`: each row holds 3 documents in order; the longest has exactly 768 slots. `token_boxes`: x0 < x1 <= x0 + 8 and x1 <= 127; y0 < y1 <= y0 + 4 and y1 <= 31.
All inputs are finite; a program needn't handle non-finite values. No bound on the sum of `pad_mask` on one device may be relied on, other than what follows from the above.
Results may differ from the reference program's by a relative error of at most 0.013.
Values sent between devices are 32-bit elements; how exact they have to be, the bound alone decides.
A program may use at most 384 MiB of HBM per device.

```python
import math
import jax
import jax.numpy as jnp
import numpy as np
from jax import lax

D = 768
HEADS = 12
HDIM = 64
FF = 3072
NBUCKET = 32
CHAN = 128
GROUPS = 32
DOCS_DEV = 3
TOK_DEV = 1024
IW = 128
DOC_MOST = 768
TOKENS = 16384
SLOT_ROWS = 16
TILE_ROWS = 32
IMG_ROWS = 512


def draw_page_image(key, part):
    row_ramp = 1.0 + 2.0 * jnp.arange(IMG_ROWS, dtype=jnp.float32) / (IMG_ROWS - 1)
    pixels = jnp.clip(jax.random.normal(key, (3, IMG_ROWS, IW), jnp.float32), -4.0, 4.0)
    return (pixels * row_ramp[None, :, None]).astype(jnp.bfloat16)


def draw_token_boxes(key, part):
    subkeys = jax.random.split(key, 4)
    grid_shape = (SLOT_ROWS, TOK_DEV)
    slot_ids = jnp.arange(TOK_DEV, dtype=jnp.int32)[None, :]
    left_edge = jax.random.randint(subkeys[0], grid_shape, 0, IW - 8)
    width_px = jax.random.randint(subkeys[1], grid_shape, 1, 9)
    top_edge = jax.random.randint(subkeys[2], grid_shape, 0, TILE_ROWS - 4)
    height_px = jax.random.randint(subkeys[3], grid_shape, 1, 5)
    left_edge = jnp.where(slot_ids == 0, IW - 9, left_edge)
    width_px = jnp.where(slot_ids == 0, 8, width_px)
    top_edge = jnp.where(slot_ids == 1, TILE_ROWS - 5, top_edge)
    height_px = jnp.where(slot_ids == 1, 4, height_px)
    return jnp.stack([left_edge, top_edge, left_edge + width_px, top_edge + height_px]).astype(jnp.int32)


def plant(drawn, own_key, low, top_value):
    index_at = [jax.random.randint(jax.random.fold_in(own_key, axis), (), 0, length) for axis, length in enumerate(drawn.shape)]
    widest = drawn.shape.index(max(drawn.shape))
    beside = index_at[:widest] + [(index_at[widest] + 1) % drawn.shape[widest]] + index_at[widest + 1:]
    return drawn.at[tuple(index_at)].set(low).at[tuple(beside)].set(top_value)


def block_scale(own_key, shape, shards, low, largest):
    loudness, own = 1.0, jax.random.fold_in(own_key, 6)
    for axis_at, blocks in shards:
        heights = jnp.exp(jax.random.uniform(jax.random.fold_in(own, axis_at), (blocks,), jnp.float32, low / len(shards), largest / len(shards)))
        loudness = loudness * jnp.repeat(heights, shape[axis_at] // blocks).reshape([-1 if axis == axis_at else 1 for axis in range(len(shape))])
    return loudness


def length_profile(count, total, most, slope):
    portions = [(1 << 20) // math.isqrt(rank ** slope) + 1 for rank in range(2, count + 1)]
    rest, holding = total - most - (count - 1), [1] * (count - 1)
    while rest > 0:
        free = [i for i in range(count - 1) if holding[i] < most]
        mass, budget = sum([portions[i] for i in free]), rest
        for i in free:
            addition = min(most - holding[i], max(1, budget * portions[i] // mass), rest)
            holding[i] = holding[i] + addition
            rest = rest - addition
    return np.array([most] + holding)


def uneven(own_key, count, total, limit, slope):
    if count == 2:
        one = jax.random.randint(own_key, (), max(1, total - limit), min(limit, total - 1) + 1)
        return jnp.stack([one, total - one])
    sizes = jnp.asarray(length_profile(count, total, limit, slope), jnp.int32)
    pairs = (count - 1) // 2
    donor, receiver = sizes[1:1 + 2 * pairs:2], sizes[2:2 + 2 * pairs:2]
    slack = jnp.minimum(donor - 1, limit - receiver)
    moved = jax.random.randint(jax.random.fold_in(own_key, 1), (pairs,), 0, 1 << 20) % (slack + 1)
    sizes = sizes.at[1:1 + 2 * pairs:2].set(donor - moved).at[2:2 + 2 * pairs:2].set(receiver + moved)
    return sizes[jax.random.permutation(jax.random.fold_in(own_key, 2), count)]


def scatter_about(key, extent, scale, reach, cuts=(), kind=jnp.bfloat16):
    level = block_scale(key, extent, cuts, -0.22, 0.18) if cuts else 1.0
    drawn = jax.random.normal(key, extent, jnp.float32) * scale * level
    return jnp.minimum(jnp.maximum(drawn, -reach), reach).astype(kind)


def setup_inputs(seed: int = 0) -> dict:
    seeds = jax.random.split(jax.random.key(seed), 21)
    return {
        "page_image": draw_page_image(jax.random.fold_in(seeds[20], 71), 0),
        "embeddings": scatter_about(seeds[1], (TOKENS, D), 1.0, 6.0, ((0, 16),)),
        "cotangent": scatter_about(seeds[2], (TOKENS, D), 1.0, 6.0, ((0, 16),)),
        "doc_ids": jax.vmap(lambda own: jnp.searchsorted(jnp.cumsum(uneven(own, DOCS_DEV, TOK_DEV, DOC_MOST, 0)), jnp.arange(TOK_DEV), side="right"))(jax.random.split(seeds[3], SLOT_ROWS)).reshape((SLOT_ROWS, TOK_DEV)).astype(jnp.int32),
        "pad_mask": plant((jax.random.randint(seeds[4], (SLOT_ROWS, TOK_DEV), 0, 8) < 7).astype(jnp.int32), jax.random.fold_in(seeds[4], 1), 0, 1),
        "token_boxes": draw_token_boxes(jax.random.fold_in(seeds[20], 71), 0),
        "conv_first": scatter_about(seeds[6], (3, CHAN), 3 ** -0.5, 3.5),
        "conv_weights": scatter_about(seeds[7], (8, CHAN, CHAN), CHAN ** -0.5, 0.5),
        "group_gain": jnp.clip(1.0 + 0.15 * jax.random.normal(seeds[8], (9, CHAN), jnp.float32), 0.25, 1.75),
        "group_shift": scatter_about(seeds[9], (9, CHAN), 0.5, 3.0, (), jnp.float32),
        "roi_proj": scatter_about(seeds[10], (CHAN, D), CHAN ** -0.5, 0.5),
        "attn_norm": jnp.clip(1.0 + 0.15 * jax.random.normal(seeds[11], (D,), jnp.float32), 0.25, 1.75),
        "query_proj": scatter_about(seeds[12], (D, D), D ** -0.5, 0.21875, ((1, 2),)),
        "key_proj": scatter_about(seeds[13], (D, D), D ** -0.5, 0.21875, ((1, 2),)),
        "value_proj": scatter_about(seeds[14], (D, D), D ** -0.5, 0.21875, ((1, 2),)),
        "output_proj": scatter_about(seeds[15], (D, D), (D // 8) ** -0.5, 0.625, ((0, 2),)),
        "bias_tables": scatter_about(seeds[16], (3, NBUCKET, HEADS), 0.5, 3.0, ((2, 2),), jnp.float32),
        "ffn_norm": jnp.clip(1.0 + 0.15 * jax.random.normal(seeds[17], (D,), jnp.float32), 0.25, 1.75),
        "up_proj": scatter_about(seeds[18], (D, FF), D ** -0.5, 0.21875, ((1, 2),)),
        "down_proj": scatter_about(seeds[19], (FF, D), FF ** -0.5, 0.109375, ((0, 2),)),
    }


@jax.custom_vjp
def low(v):
    return lax.optimization_barrier(v.astype(jnp.bfloat16)).astype(jnp.float32)

@jax.custom_vjp
def low_back(v):
    return v

def low_keep(v):
    return (low(v), None)

def low_pass(kept, grad):
    return (grad,)

def back_keep(v):
    return (v, None)

def back_low(kept, grad):
    return (low(grad),)
low.defvjp(low_keep, low_pass)
low_back.defvjp(back_keep, back_low)
bucket_edges = (12, 16, 23, 32, 46, 64, 91)
highest = lax.Precision.HIGHEST

def rounded(values):
    return low(low_back(values))

def bucket_of(relative):
    magnitude = jnp.abs(relative)
    coarse = jnp.full(relative.shape, 8, jnp.int32)
    for edge in bucket_edges:
        coarse = coarse + (magnitude >= edge).astype(jnp.int32)
    return jnp.where(magnitude < 8, magnitude, coarse) + jnp.where(relative > 0, 16, 0).astype(jnp.int32)

def pool_down(values):
    return values.reshape(values.shape[0], values.shape[1] // 2, 2, values.shape[2] // 2, 2).mean(axis=(2, 4))

def pool_up(values):
    return jnp.repeat(jnp.repeat(values, 2, axis=1), 2, axis=2)

def conv_apply(weights, values):
    return jnp.einsum('co,crw->orw', weights, values, precision=highest)

def group_silu(values, gains, offsets):
    channels = values.shape[0]
    grouped = values.reshape(GROUPS, channels // GROUPS, values.shape[1], values.shape[2])
    centre = lax.optimization_barrier(jnp.mean(grouped, axis=(1, 2, 3), keepdims=True))
    spread = lax.optimization_barrier(jnp.mean(jnp.square(grouped - centre), axis=(1, 2, 3), keepdims=True))
    normed = ((grouped - centre) * lax.rsqrt(spread + 1e-05)).reshape(values.shape)
    return jax.nn.silu(normed * gains[:, None, None] + offsets[:, None, None])

def stem(image, conv_first, conv_weights, group_gain, group_shift):
    current = group_silu(conv_apply(conv_first, image), group_gain[0], group_shift[0])
    downs = [current]
    for level in range(1, 5):
        current = group_silu(conv_apply(conv_weights[level - 1], pool_down(current)), group_gain[level], group_shift[level])
        downs.append(current)
    for level in range(3, -1, -1):
        merged = pool_up(current) + downs[level]
        current = group_silu(conv_apply(conv_weights[7 - level], merged), group_gain[8 - level], group_shift[8 - level])
    return current

def rms_scale(values):
    return values * lax.rsqrt(lax.optimization_barrier(jnp.mean(values * values, axis=-1, keepdims=True)) + 1e-06)

def device_layer(tile, embedded, segment, padding, boxes, roi_proj, attn_norm, query_proj, key_proj, value_proj, output_proj, bias_tables, ffn_norm, up_proj, down_proj):
    row_ids = jnp.arange(TILE_ROWS, dtype=jnp.int32)
    col_ids = jnp.arange(IW, dtype=jnp.int32)
    row_mask = ((row_ids[None, :] >= boxes[1][:, None]) & (row_ids[None, :] < boxes[3][:, None])).astype(jnp.float32)
    col_mask = ((col_ids[None, :] >= boxes[0][:, None]) & (col_ids[None, :] < boxes[2][:, None])).astype(jnp.float32)
    box_area = ((boxes[3] - boxes[1]) * (boxes[2] - boxes[0])).astype(jnp.float32)
    column_sums = jnp.einsum('crw,tw->crt', tile, col_mask, precision=highest)
    box_sums = jnp.einsum('crt,tr->tc', column_sums, row_mask, precision=highest)
    pooled = low(box_sums / box_area[:, None])
    stream = embedded + low_back(jnp.dot(pooled, roi_proj, precision=highest))
    attn_in = low(rms_scale(stream) * attn_norm)
    query = rounded(jnp.dot(attn_in, query_proj, precision=highest)).reshape(TOK_DEV, HEADS, HDIM)
    keyed = rounded(jnp.dot(attn_in, key_proj, precision=highest)).reshape(TOK_DEV, HEADS, HDIM)
    valued = rounded(jnp.dot(attn_in, value_proj, precision=highest)).reshape(TOK_DEV, HEADS, HDIM)
    positions = jnp.arange(TOK_DEV, dtype=jnp.int32)
    relative = positions[None, :] - positions[:, None]
    left_edge = boxes[0]
    top_edge = boxes[1]
    bias = jnp.take(bias_tables[0].T, bucket_of(relative), axis=1)
    bias = bias + jnp.take(bias_tables[1].T, bucket_of(left_edge[None, :] - left_edge[:, None]), axis=1)
    bias = bias + jnp.take(bias_tables[2].T, bucket_of(top_edge[None, :] - top_edge[:, None]), axis=1)
    scores = low_back(jnp.einsum('qhd,khd->hqk', query, keyed, precision=highest) * HDIM ** (-0.5)) + bias
    allowed = (segment[None, :] == segment[:, None]) & ((padding[None, :] > 0) | (relative == 0))
    probs = low(jax.nn.softmax(jnp.where(allowed[None], scores, -1e+30), axis=-1))
    context = rounded(jnp.einsum('hqk,khd->qhd', probs, valued, precision=highest)).reshape(TOK_DEV, D)
    middle = stream + low_back(jnp.dot(context, output_proj, precision=highest))
    ffn_in = low(rms_scale(middle) * ffn_norm)
    hidden = low(jax.nn.gelu(low_back(jnp.dot(ffn_in, up_proj, precision=highest)), approximate=False))
    return middle + low_back(jnp.dot(hidden, down_proj, precision=highest))

def reference(page_image, embeddings, cotangent, doc_ids, pad_mask, token_boxes, conv_first, conv_weights, group_gain, group_shift, roi_proj, attn_norm, query_proj, key_proj, value_proj, output_proj, bias_tables, ffn_norm, up_proj, down_proj):
    image = page_image.astype(jnp.float32)
    params = tuple((item.astype(jnp.float32) for item in (embeddings, conv_first, conv_weights, group_gain, group_shift, roi_proj, attn_norm, query_proj, key_proj, value_proj, output_proj, bias_tables, ffn_norm, up_proj, down_proj)))

    def forward(embedded, conv_first, conv_weights, group_gain, group_shift, roi_proj, attn_norm, query_proj, key_proj, value_proj, output_proj, bias_tables, ffn_norm, up_proj, down_proj):
        canvas = stem(image, conv_first, conv_weights, group_gain, group_shift)
        tiles = canvas.reshape(CHAN, SLOT_ROWS, TILE_ROWS, IW).transpose(1, 0, 2, 3)

        def one_device(items):
            tile, embedded_rows, segment, padding, boxes = items
            return device_layer(tile, embedded_rows, segment, padding, boxes, roi_proj, attn_norm, query_proj, key_proj, value_proj, output_proj, bias_tables, ffn_norm, up_proj, down_proj)
        outputs = lax.map(jax.checkpoint(one_device), (tiles, embedded.reshape(SLOT_ROWS, TOK_DEV, D), doc_ids, pad_mask, token_boxes.transpose(1, 0, 2)))
        return outputs.reshape(TOKENS, D)
    result, pullback = jax.vjp(forward, *params)
    grads = pullback(cotangent.astype(jnp.float32))
    return (result.astype(jnp.bfloat16), grads[0], grads[1], grads[2], grads[3], grads[4], grads[5], grads[6], grads[7], grads[8], grads[9], grads[10], grads[11], grads[12], grads[13], grads[14])
```

```python
import functools

import jax
import jax.numpy as jnp
from jax import lax
from jax.experimental import pallas as pl
from jax.experimental.pallas import tpu as pltpu
from jax.sharding import PartitionSpec as P

HDIM = 64
NBUCKET = 32
GROUPS = 32
QBLK = 512


bucket_edges = (12, 16, 23, 32, 46, 64, 91)
norm_eps = 1e-06
group_eps = 1e-05
masked_score = -1e30
highest = lax.Precision.HIGHEST


def bucket_of(relative):
    magnitude = jnp.abs(relative)
    coarse = jnp.full(relative.shape, 8, jnp.int32)
    for edge in bucket_edges:
        coarse = coarse + (magnitude >= edge).astype(jnp.int32)
    return jnp.where(magnitude < 8, magnitude, coarse) + jnp.where(relative > 0, 16, 0).astype(
        jnp.int32
    )


def bucket_table(bucket_ids):
    return (bucket_ids[..., None] == jnp.arange(NBUCKET, dtype=jnp.int32)).astype(jnp.bfloat16)


MESH = pl.DeviceIdType.MESH
LAYERS = 9
PIX_CHUNK = 256


def level_of(layer):
    return layer if layer <= 4 else 8 - layer


def stem_rows(pixels):
    return [pixels >> (2 * level_of(layer)) for layer in range(LAYERS)]


def row_starts(rows):
    starts = [0]
    for count in rows:
        starts.append(starts[-1] + count)
    return starts


def split_two(values):
    high = values.astype(jnp.bfloat16)
    low = (values - high.astype(jnp.float32)).astype(jnp.bfloat16)
    return jnp.concatenate([high, low], axis=1)


def group_sum(values):
    lane = lax.broadcasted_iota(jnp.int32, values.shape, 1)
    pairs = values + jnp.where(
        lane % 2 == 0, pltpu.roll(values, 127, 1), pltpu.roll(values, 1, 1)
    )
    return pairs + jnp.where(
        (lane // 2) % 2 == 0, pltpu.roll(pairs, 126, 1), pltpu.roll(pairs, 2, 1)
    )


def wide(row):
    return jnp.broadcast_to(row, (8, row.shape[1]))


def my_index():
    return lax.axis_index("dp") * 2 + lax.axis_index("tensor")


def greet_all(count):
    barrier = pltpu.get_barrier_semaphore()
    me = my_index()

    def greet(step, carry):
        other = lax.rem(me + step, count)
        pl.semaphore_signal(
            barrier, inc=1, device_id=(other // 2, lax.rem(other, 2)), device_id_type=MESH
        )
        return carry

    lax.fori_loop(1, count, greet, 0)


def greeted(count):
    pl.semaphore_wait(pltpu.get_barrier_semaphore(), count - 1)


def send_all(count, source, target, send_sem, recv_sem):
    me = my_index()

    def send(step, carry):
        other = lax.rem(me + step, count)
        pltpu.make_async_remote_copy(
            src_ref=source,
            dst_ref=target,
            send_sem=send_sem,
            recv_sem=recv_sem,
            device_id=(other // 2, lax.rem(other, 2)),
            device_id_type=MESH,
        ).start()
        return carry

    lax.fori_loop(1, count, send, 0, unroll=count <= 32)


def wait_all(count, slots, sem):
    part = slots.at[pl.ds(0, count - 1)]
    pltpu.make_async_copy(part, part, sem).wait()


def natural_places(tile_rows, columns):
    spacing = columns // 8
    places = []
    for row in range(tile_rows):
        for col in range(spacing):
            place = 0
            for bit in range(4):
                place = place * 4 + ((row >> bit) & 1) * 2 + ((col >> bit) & 1)
            places.append((row * columns + col, place * 8))
    return places


def stem_forward_kernel(
    count,
    places,
    image_ref,
    first_ref,
    weights_ref,
    gain_ref,
    shift_ref,
    feature_ref,
    norm_ref,
    input_ref,
    scale_ref,
    natural,
    skip,
    current,
    source,
    slots,
    send_sem,
    recv_sem,
):
    me = my_index()
    greet_all(count)
    pixels = feature_ref.shape[0]
    rows = stem_rows(pixels)
    norm_at = row_starts(rows)
    input_at = row_starts(rows[1:])
    skip_at = row_starts(rows[:4])
    spacing = 16
    natural[...] = lax.dot_general(
        image_ref[...],
        first_ref[...],
        (((0,), (0,)), ((), ())),
        preferred_element_type=jnp.float32,
    )
    for start, place in places:
        norm_ref[place : place + 8, :] = natural[pl.ds(start, 8, stride=spacing), :]
    for layer in range(LAYERS):
        height = rows[layer]
        chunk = min(height, PIX_CHUNK)
        base = norm_at[layer]
        total = jnp.zeros((8, 128), jnp.float32)
        if layer > 0:
            weights = weights_ref[layer - 1]
            stacked = jnp.concatenate([weights, weights], axis=0)

            def convolve(index, total):
                at = pl.multiple_of(index * chunk, chunk)
                values = jnp.dot(
                    split_two(input_ref[pl.ds(input_at[layer - 1] + at, chunk), :]),
                    stacked,
                    preferred_element_type=jnp.float32,
                )
                norm_ref[pl.ds(base + at, chunk), :] = values
                return total + jnp.sum(values.reshape(chunk // 8, 8, 128), axis=0)

        else:

            def convolve(index, total):
                at = pl.multiple_of(index * chunk, chunk)
                values = norm_ref[pl.ds(base + at, chunk), :]
                return total + jnp.sum(values.reshape(chunk // 8, 8, 128), axis=0)

        total = lax.fori_loop(0, height // chunk, convolve, total)
        mean = jnp.sum(total, axis=0, keepdims=True) * (1.0 / height)

        def deviate(index, total):
            at = pl.multiple_of(index * chunk, chunk)
            values = norm_ref[pl.ds(base + at, chunk), :] - mean
            return total + jnp.sum((values * values).reshape(chunk // 8, 8, 128), axis=0)

        square = lax.fori_loop(0, height // chunk, deviate, jnp.zeros((8, 128), jnp.float32))
        square = jnp.sum(square, axis=0, keepdims=True)
        stats = jnp.concatenate([mean, square], axis=0)
        source[layer] = stats
        slots[layer, me] = stats
        if layer == 0:
            greeted(count)
        send_all(
            count,
            source.at[layer],
            slots.at[layer, me],
            send_sem.at[layer],
            recv_sem.at[layer],
        )
        wait_all(count, slots.at[layer], recv_sem.at[layer])
        means = slots[layer, :, 0, :]
        centre = group_sum(wide(jnp.sum(means, axis=0, keepdims=True))) * (0.25 / count)
        apart = means - centre[0:1]
        spread = jnp.sum(slots[layer, :, 1, :], axis=0, keepdims=True) + height * jnp.sum(
            apart * apart, axis=0, keepdims=True
        )
        variance = group_sum(wide(spread)) * (1.0 / (4 * height * count))
        inverse = lax.rsqrt(variance + group_eps)[0:1]
        centre = centre[0:1]
        scale_ref[layer : layer + 1, :] = inverse
        gain = gain_ref[layer : layer + 1, :]
        shift = shift_ref[layer : layer + 1, :]

        def activate(start, size):
            normed = (norm_ref[pl.ds(base + start, size), :] - centre) * inverse
            norm_ref[pl.ds(base + start, size), :] = normed
            lifted = normed * gain + shift
            return lifted / (1.0 + jnp.exp(-lifted))

        if layer < 4:
            quarter = height // 4
            part = min(quarter, 64)

            def pool(index, carry):
                at = pl.multiple_of(index * part, part)
                mean_of = jnp.zeros((part, 128), jnp.float32)
                for corner in range(4):
                    value = activate(corner * quarter + at, part)
                    skip[pl.ds(skip_at[layer] + corner * quarter + at, part), :] = value
                    mean_of = mean_of + value
                input_ref[pl.ds(input_at[layer] + at, part), :] = mean_of * 0.25
                return carry

            lax.fori_loop(0, quarter // part, pool, 0)
        elif layer < 8:
            part = min(height, 64)
            skipped = skip_at[7 - layer]

            def grow(index, carry):
                at = pl.multiple_of(index * part, part)
                value = activate(at, part)
                for corner in range(4):
                    place = corner * height + at
                    input_ref[pl.ds(input_at[layer] + place, part), :] = (
                        value + skip[pl.ds(skipped + place, part), :]
                    )
                return carry

            lax.fori_loop(0, height // part, grow, 0)
        else:

            def finish(index, carry):
                at = pl.multiple_of(index * chunk, chunk)
                current[pl.ds(at, chunk), :] = activate(at, chunk)
                return carry

            lax.fori_loop(0, height // chunk, finish, 0)
    for start, place in places:
        feature_ref[pl.ds(start, 8, stride=spacing), :] = current[place : place + 8, :]
    for layer in range(LAYERS):
        wait_all(count, slots.at[layer], send_sem.at[layer])


def stem_backward_kernel(
    count,
    places,
    grad_ref,
    image_ref,
    norm_ref,
    input_ref,
    scale_ref,
    weights_ref,
    gain_ref,
    shift_ref,
    first_out,
    weights_out,
    gain_out,
    shift_out,
    natural,
    ordered,
    active,
    grad_conv,
    skip,
    grads,
    product,
    source,
    slots,
    first_source,
    first_slots,
    parts,
    shared,
    send_sem,
    recv_sem,
    part_send,
    part_recv,
    share_send,
    share_recv,
):
    me = my_index()
    greet_all(count)
    pixels = grad_ref.shape[0]
    rows = stem_rows(pixels)
    norm_at = row_starts(rows)
    input_at = row_starts(rows[1:])
    skip_at = row_starts(rows[:4])
    spacing = 16
    owners = count // 8
    owned = parts.shape[1]
    for start, place in places:
        ordered[place : place + 8, :] = grad_ref[pl.ds(start, 8, stride=spacing), :]

    def weight_grad(layer):
        height = rows[layer]
        chunk = min(height, 512)

        def add(index, total):
            at = pl.multiple_of(index * chunk, chunk)
            return total + lax.dot_general(
                input_ref[pl.ds(input_at[layer - 1] + at, chunk), :].astype(jnp.bfloat16),
                grad_conv[pl.ds(norm_at[layer] + at, chunk), :].astype(jnp.bfloat16),
                (((0,), (0,)), ((), ())),
                preferred_element_type=jnp.float32,
            )

        product[layer - 1] = lax.fori_loop(
            0, height // chunk, add, jnp.zeros((128, 128), jnp.float32)
        ).reshape(owners, owned, 128)

        def send(index, carry):
            owner = layer - 1 + 8 * index

            @pl.when(owner != me)
            def _():
                pltpu.make_async_remote_copy(
                    src_ref=product.at[layer - 1, index],
                    dst_ref=parts.at[me],
                    send_sem=part_send,
                    recv_sem=part_recv,
                    device_id=(owner // 2, lax.rem(owner, 2)),
                    device_id_type=MESH,
                ).start()

            @pl.when(owner == me)
            def _():
                parts[me] = product[layer - 1, index]

            return carry

        lax.fori_loop(0, owners, send, 0)

    for layer in range(LAYERS - 1, -1, -1):
        height = rows[layer]
        chunk = min(height, PIX_CHUNK)
        base = norm_at[layer]
        gain = gain_ref[layer : layer + 1, :]
        shift = shift_ref[layer : layer + 1, :]
        inverse = scale_ref[layer : layer + 1, :]
        incoming = ordered if layer == 8 else grads

        def activate(index, carry):
            first, second = carry
            at = pl.multiple_of(index * chunk, chunk)
            normed = norm_ref[pl.ds(base + at, chunk), :]
            lifted = normed * gain + shift
            sigma = 1.0 / (1.0 + jnp.exp(-lifted))
            value = incoming[pl.ds(at, chunk), :] * sigma * (1.0 + lifted * (1.0 - sigma))
            active[pl.ds(at, chunk), :] = value
            first = first + jnp.sum(value.reshape(chunk // 8, 8, 128), axis=0)
            second = second + jnp.sum((value * normed).reshape(chunk // 8, 8, 128), axis=0)
            return first, second

        zero = jnp.zeros((8, 128), jnp.float32)
        first, second = lax.fori_loop(0, height // chunk, activate, (zero, zero))
        sums = jnp.concatenate(
            [jnp.sum(first, axis=0, keepdims=True), jnp.sum(second, axis=0, keepdims=True)], axis=0
        )
        source[layer] = sums
        slots[layer, me] = sums
        if layer == 8:
            greeted(count)
        send_all(
            count, source.at[layer], slots.at[layer, me], send_sem.at[layer], recv_sem.at[layer]
        )
        if layer < 8:
            weight_grad(layer + 1)
        wait_all(count, slots.at[layer], recv_sem.at[layer])
        totals = jnp.sum(slots[layer], axis=0)
        shift_out[layer : layer + 1, :] = totals[0:1]
        gain_out[layer : layer + 1, :] = totals[1:2]
        share = 1.0 / (4 * height * count)
        first_mean = group_sum(wide(totals[0:1] * gain))[0:1] * share
        second_mean = group_sum(wide(totals[1:2] * gain))[0:1] * share

        def conv_grad(start, size):
            value = inverse * (
                active[pl.ds(start, size), :] * gain
                - first_mean
                - norm_ref[pl.ds(base + start, size), :] * second_mean
            )
            grad_conv[pl.ds(base + start, size), :] = value
            return value

        if layer > 0:
            weights = weights_ref[layer - 1]
            stacked = jnp.concatenate([weights, weights], axis=1)

            def input_grad(start, size):
                return lax.dot_general(
                    split_two(conv_grad(start, size)),
                    stacked,
                    (((1,), (1,)), ((), ())),
                    preferred_element_type=jnp.float32,
                )

        if layer > 4:
            quarter = height // 4
            part = min(quarter, 64)
            skipped = skip_at[8 - layer]

            def shrink(index, carry):
                at = pl.multiple_of(index * part, part)
                total = jnp.zeros((part, 128), jnp.float32)
                for corner in range(4):
                    place = corner * quarter + at
                    value = input_grad(place, part)
                    skip[pl.ds(skipped + place, part), :] = value
                    total = total + value
                grads[pl.ds(at, part), :] = total
                return carry

            lax.fori_loop(0, quarter // part, shrink, 0)
        elif layer > 0:
            part = min(height, 128)
            skipped = skip_at[layer - 1]

            def spread_out(index, carry):
                at = pl.multiple_of(index * part, part)
                value = input_grad(at, part) * 0.25
                for corner in range(4):
                    place = corner * height + at
                    grads[pl.ds(place, part), :] = value + skip[pl.ds(skipped + place, part), :]
                return carry

            lax.fori_loop(0, height // part, spread_out, 0)
        else:

            def finish(index, carry):
                at = pl.multiple_of(index * chunk, chunk)
                conv_grad(at, chunk)
                return carry

            lax.fori_loop(0, height // chunk, finish, 0)
    for start, place in places:
        natural[pl.ds(start, 8, stride=spacing), :] = grad_conv[place : place + 8, :]
    first_part = jnp.dot(
        image_ref[...], natural[...].astype(jnp.bfloat16), preferred_element_type=jnp.float32
    )
    first_source[...] = first_part
    first_slots[me] = first_part
    send_all(count, first_source, first_slots.at[me], send_sem.at[LAYERS], recv_sem.at[LAYERS])
    wait_all(count, parts, part_recv)
    mine = jnp.sum(parts[...], axis=0)
    shared[me] = mine
    send_all(count, shared.at[me], shared.at[me], share_send, share_recv)
    wait_all(count, first_slots, recv_sem.at[LAYERS])
    first_out[...] = jnp.sum(first_slots[...], axis=0)
    wait_all(count, shared, share_recv)
    for device in range(count):
        weights_out[device % 8, (device // 8) * owned : (device // 8 + 1) * owned, :] = shared[
            device
        ]
    for layer in range(LAYERS):
        wait_all(count, slots.at[layer], send_sem.at[layer])
    wait_all(count, first_slots, send_sem.at[LAYERS])
    wait_all(count, parts, part_send)
    wait_all(count, shared, share_send)


def stem_forward(page_image, conv_first, conv_weights, group_gain, group_shift, devices):
    planes, tile_rows, columns = page_image.shape
    pixels = tile_rows * columns
    rows = stem_rows(pixels)
    image = page_image.reshape(planes, pixels)
    places = natural_places(tile_rows, columns)
    whole = pl.BlockSpec(memory_space=pltpu.VMEM)
    return pl.pallas_call(
        functools.partial(stem_forward_kernel, devices, places),
        out_shape=(
            jax.ShapeDtypeStruct((pixels, 128), jnp.float32),
            jax.ShapeDtypeStruct((sum(rows), 128), jnp.float32),
            jax.ShapeDtypeStruct((sum(rows[1:]), 128), jnp.float32),
            jax.ShapeDtypeStruct((LAYERS, 128), jnp.float32),
        ),
        in_specs=[whole] * 5,
        out_specs=(whole,) * 4,
        scratch_shapes=[
            pltpu.VMEM((pixels, 128), jnp.float32),
            pltpu.VMEM((sum(rows[:4]), 128), jnp.float32),
            pltpu.VMEM((pixels, 128), jnp.float32),
            pltpu.VMEM((LAYERS, 2, 128), jnp.float32),
            pltpu.VMEM((LAYERS, devices, 2, 128), jnp.float32),
            pltpu.SemaphoreType.DMA((LAYERS,)),
            pltpu.SemaphoreType.DMA((LAYERS,)),
        ],
        compiler_params=pltpu.CompilerParams(
            collective_id=0, has_side_effects=True, vmem_limit_bytes=40 * 2**20
        ),
        name="stem_forward",
    )(image, conv_first, conv_weights, group_gain, group_shift)


def stem_backward(
    grad_map, page_image, records, conv_weights, group_gain, group_shift, devices
):
    planes, tile_rows, columns = page_image.shape
    pixels = tile_rows * columns
    rows = stem_rows(pixels)
    norms, inputs, scales = records
    image = page_image.reshape(planes, pixels)
    places = natural_places(tile_rows, columns)
    whole = pl.BlockSpec(memory_space=pltpu.VMEM)
    owned = 1024 // devices
    return pl.pallas_call(
        functools.partial(stem_backward_kernel, devices, places),
        out_shape=(
            jax.ShapeDtypeStruct((planes, 128), jnp.float32),
            jax.ShapeDtypeStruct((8, 128, 128), jnp.float32),
            jax.ShapeDtypeStruct((LAYERS, 128), jnp.float32),
            jax.ShapeDtypeStruct((LAYERS, 128), jnp.float32),
        ),
        in_specs=[whole] * 8,
        out_specs=(whole,) * 4,
        scratch_shapes=[
            pltpu.VMEM((pixels, 128), jnp.float32),
            pltpu.VMEM((pixels, 128), jnp.float32),
            pltpu.VMEM((pixels, 128), jnp.float32),
            pltpu.VMEM((sum(rows), 128), jnp.float32),
            pltpu.VMEM((sum(rows[:4]), 128), jnp.float32),
            pltpu.VMEM((pixels, 128), jnp.float32),
            pltpu.VMEM((8, devices // 8, owned, 128), jnp.float32),
            pltpu.VMEM((LAYERS, 2, 128), jnp.float32),
            pltpu.VMEM((LAYERS, devices, 2, 128), jnp.float32),
            pltpu.VMEM((planes, 128), jnp.float32),
            pltpu.VMEM((devices, planes, 128), jnp.float32),
            pltpu.VMEM((devices, owned, 128), jnp.float32),
            pltpu.VMEM((devices, owned, 128), jnp.float32),
            pltpu.SemaphoreType.DMA((LAYERS + 1,)),
            pltpu.SemaphoreType.DMA((LAYERS + 1,)),
            pltpu.SemaphoreType.DMA,
            pltpu.SemaphoreType.DMA,
            pltpu.SemaphoreType.DMA,
            pltpu.SemaphoreType.DMA,
        ],
        compiler_params=pltpu.CompilerParams(
            collective_id=1, has_side_effects=True, vmem_limit_bytes=40 * 2**20
        ),
        name="stem_backward",
    )(grad_map, image, norms, inputs, scales, conv_weights, group_gain, group_shift)


def rms_forward(values, gains):
    inverse = lax.rsqrt(jnp.mean(values * values, axis=-1, keepdims=True) + norm_eps)
    normal = values * inverse
    return ((normal * gains).astype(jnp.bfloat16), normal, inverse)


def rms_backward(grads, normal, inverse, gains):
    scaled = grads * gains
    grad_gain = jnp.sum(grads * normal, axis=0)
    back = inverse * (scaled - normal * jnp.mean(scaled * normal, axis=-1, keepdims=True))
    return (back, grad_gain)


def exact_gelu(values):
    return jax.nn.gelu(values, approximate=False)


def block_terms(start, segment, padding, left_edge, top_edge):
    positions = jnp.arange(segment.shape[0], dtype=jnp.int32)
    query_pos = positions[start : start + QBLK]
    relative = positions[None, :] - query_pos[:, None]
    rel_bucket = bucket_of(relative)
    left_bucket = bucket_of(left_edge[None, :] - left_edge[start : start + QBLK, None])
    top_bucket = bucket_of(top_edge[None, :] - top_edge[start : start + QBLK, None])
    allowed = (segment[None, :] == segment[start : start + QBLK, None]) & (
        (padding[None, :] > 0) | (relative == 0)
    )
    return ((rel_bucket, left_bucket, top_bucket), allowed)


def block_scores(query_block, key_heads, bias_tables, buckets, allowed):
    bias = jnp.einsum(
        "qkb,bh->hqk",
        bucket_table(buckets[0]),
        bias_tables[0],
        preferred_element_type=jnp.float32,
        precision=highest,
    )
    bias = bias + jnp.einsum(
        "qkb,bh->hqk",
        bucket_table(buckets[1]),
        bias_tables[1],
        preferred_element_type=jnp.float32,
        precision=highest,
    )
    bias = bias + jnp.einsum(
        "qkb,bh->hqk",
        bucket_table(buckets[2]),
        bias_tables[2],
        preferred_element_type=jnp.float32,
        precision=highest,
    )
    scores = (
        jnp.einsum("qhd,khd->hqk", query_block, key_heads, preferred_element_type=jnp.float32)
        * HDIM ** (-0.5)
        + bias
    )
    return jnp.where(allowed[None], scores, masked_score)


def bucket_sums(grad_upper, grad_lower, bucket_ids):
    table = bucket_table(bucket_ids)
    upper = jnp.einsum("hqk,qkb->bh", grad_upper, table, preferred_element_type=jnp.float32)
    return upper + jnp.einsum("hqk,qkb->bh", grad_lower, table, preferred_element_type=jnp.float32)


def on_device(
    page_image,
    embeddings,
    cotangent,
    doc_ids,
    pad_mask,
    token_boxes,
    conv_first,
    conv_weights,
    group_gain,
    group_shift,
    roi_proj,
    attn_norm,
    query_proj,
    key_proj,
    value_proj,
    output_proj,
    bias_tables,
    ffn_norm,
    up_proj,
    down_proj,
):
    devices = lax.axis_size("dp") * lax.axis_size("tensor")
    feature_map, *records = stem_forward(
        page_image, conv_first, conv_weights, group_gain, group_shift, devices
    )
    tile_rows = page_image.shape[1]
    row_ids = lax.axis_index("tensor") * tile_rows + jnp.arange(tile_rows, dtype=jnp.int32)
    col_ids = jnp.arange(page_image.shape[2], dtype=jnp.int32)
    left_edge = token_boxes[0, 0]
    top_edge = token_boxes[1, 0]
    right_edge = token_boxes[2, 0]
    bottom_edge = token_boxes[3, 0]
    row_mask = (
        (row_ids[None, :] >= top_edge[:, None]) & (row_ids[None, :] < bottom_edge[:, None])
    ).astype(jnp.float32)
    col_mask = (
        (col_ids[None, :] >= left_edge[:, None]) & (col_ids[None, :] < right_edge[:, None])
    ).astype(jnp.float32)
    box_area = ((bottom_edge - top_edge) * (right_edge - left_edge)).astype(jnp.float32)
    box_mask = (row_mask[:, :, None] * col_mask[:, None, :]).astype(jnp.bfloat16)
    box_mask = box_mask.reshape(box_mask.shape[0], -1)
    feature_pair = split_two(feature_map)
    box_pair = jnp.dot(box_mask, feature_pair, preferred_element_type=jnp.float32)
    partial_boxes = box_pair[:, :128] + box_pair[:, 128:]
    box_sums = lax.psum(partial_boxes, "tensor")
    pooled = (box_sums / box_area[:, None]).astype(jnp.bfloat16)
    stream = embeddings.astype(jnp.float32) + jnp.dot(
        pooled, roi_proj, preferred_element_type=jnp.float32
    )
    attn_in, attn_hat, attn_inv = rms_forward(stream, attn_norm)
    tokens = stream.shape[0]
    local_heads = query_proj.shape[1] // HDIM
    query_heads = (
        jnp.dot(attn_in, query_proj, preferred_element_type=jnp.float32)
        .astype(jnp.bfloat16)
        .reshape(tokens, local_heads, HDIM)
    )
    key_heads = (
        jnp.dot(attn_in, key_proj, preferred_element_type=jnp.float32)
        .astype(jnp.bfloat16)
        .reshape(tokens, local_heads, HDIM)
    )
    value_heads = (
        jnp.dot(attn_in, value_proj, preferred_element_type=jnp.float32)
        .astype(jnp.bfloat16)
        .reshape(tokens, local_heads, HDIM)
    )
    segment = doc_ids[0]
    padding = pad_mask[0]
    scale = HDIM ** (-0.5)
    log_sums = []
    contexts = []
    for start in range(0, tokens, QBLK):
        buckets, allowed = block_terms(start, segment, padding, left_edge, top_edge)
        masked = block_scores(
            query_heads[start : start + QBLK], key_heads, bias_tables, buckets, allowed
        )
        top_score = jnp.max(masked, axis=-1, keepdims=True)
        weights = jnp.exp(masked - top_score)
        totals = jnp.sum(weights, axis=-1, keepdims=True)
        log_sums.append(top_score + jnp.log(totals))
        probs = (weights / totals).astype(jnp.bfloat16)
        contexts.append(
            jnp.einsum(
                "hqk,khd->qhd", probs, value_heads, preferred_element_type=jnp.float32
            ).astype(jnp.bfloat16)
        )
    context = jnp.concatenate(contexts, axis=0).reshape(tokens, -1)
    attn_out = lax.psum(jnp.dot(context, output_proj, preferred_element_type=jnp.float32), "tensor")
    middle = stream + attn_out
    ffn_in, ffn_hat, ffn_inv = rms_forward(middle, ffn_norm)
    pre_act = jnp.dot(ffn_in, up_proj, preferred_element_type=jnp.float32)
    activated, gelu_pullback = jax.vjp(exact_gelu, pre_act)
    hidden = activated.astype(jnp.bfloat16)
    ffn_out = lax.psum(jnp.dot(hidden, down_proj, preferred_element_type=jnp.float32), "tensor")
    layer_out = (middle + ffn_out).astype(jnp.bfloat16)
    grad_down = jnp.dot(hidden.T, cotangent, preferred_element_type=jnp.float32)
    grad_hidden = jnp.dot(cotangent, down_proj.T, preferred_element_type=jnp.float32)
    grad_pre = gelu_pullback(grad_hidden)[0].astype(jnp.bfloat16)
    grad_up = jnp.dot(ffn_in.T, grad_pre, preferred_element_type=jnp.float32)
    grad_ffn_in = lax.psum(
        jnp.dot(grad_pre, up_proj.T, preferred_element_type=jnp.float32), "tensor"
    )
    grad_mid_norm, grad_ffn_norm = rms_backward(grad_ffn_in, ffn_hat, ffn_inv, ffn_norm)
    grad_middle = cotangent.astype(jnp.float32) + grad_mid_norm
    grad_mid_low = grad_middle.astype(jnp.bfloat16)
    grad_output = jnp.dot(context.T, grad_mid_low, preferred_element_type=jnp.float32)
    grad_context = (
        jnp.dot(grad_mid_low, output_proj.T, preferred_element_type=jnp.float32)
        .astype(jnp.bfloat16)
        .reshape(tokens, local_heads, HDIM)
    )
    grad_value = jnp.zeros((tokens, local_heads, HDIM), jnp.float32)
    grad_key = jnp.zeros((tokens, local_heads, HDIM), jnp.float32)
    grad_tables = jnp.zeros((3, NBUCKET, local_heads), jnp.float32)
    grad_queries = []
    for index, start in enumerate(range(0, tokens, QBLK)):
        buckets, allowed = block_terms(start, segment, padding, left_edge, top_edge)
        masked = block_scores(
            query_heads[start : start + QBLK], key_heads, bias_tables, buckets, allowed
        )
        probs_full = jnp.exp(masked - log_sums[index])
        probs = probs_full.astype(jnp.bfloat16)
        grad_ctx_block = grad_context[start : start + QBLK]
        grad_value = grad_value + jnp.einsum(
            "hqk,qhd->khd", probs, grad_ctx_block, preferred_element_type=jnp.float32
        )
        grad_probs = jnp.einsum(
            "qhd,khd->hqk", grad_ctx_block, value_heads, preferred_element_type=jnp.float32
        )
        delta = jnp.sum(grad_probs * probs_full, axis=-1, keepdims=True)
        grad_full = probs_full * (grad_probs - delta)
        grad_scores = grad_full.astype(jnp.bfloat16)
        grad_lower = (grad_full - grad_scores.astype(jnp.float32)).astype(jnp.bfloat16)
        table_terms = jnp.stack(
            [bucket_sums(grad_scores, grad_lower, bucket_ids) for bucket_ids in buckets]
        )
        grad_tables = grad_tables + table_terms
        grad_queries.append(
            jnp.einsum("hqk,khd->qhd", grad_scores, key_heads, preferred_element_type=jnp.float32)
            * scale
        )
        grad_key = (
            grad_key
            + jnp.einsum(
                "hqk,qhd->khd",
                grad_scores,
                query_heads[start : start + QBLK],
                preferred_element_type=jnp.float32,
            )
            * scale
        )
    grad_query_low = jnp.concatenate(grad_queries, axis=0).reshape(tokens, -1).astype(jnp.bfloat16)
    grad_key_low = grad_key.reshape(tokens, -1).astype(jnp.bfloat16)
    grad_value_low = grad_value.reshape(tokens, -1).astype(jnp.bfloat16)
    grad_query_proj = jnp.dot(attn_in.T, grad_query_low, preferred_element_type=jnp.float32)
    grad_key_proj = jnp.dot(attn_in.T, grad_key_low, preferred_element_type=jnp.float32)
    grad_value_proj = jnp.dot(attn_in.T, grad_value_low, preferred_element_type=jnp.float32)
    attn_terms = jnp.dot(grad_query_low, query_proj.T, preferred_element_type=jnp.float32)
    attn_terms = attn_terms + jnp.dot(grad_key_low, key_proj.T, preferred_element_type=jnp.float32)
    attn_terms = attn_terms + jnp.dot(
        grad_value_low, value_proj.T, preferred_element_type=jnp.float32
    )
    grad_attn_in = lax.psum(attn_terms, "tensor")
    grad_stream_norm, grad_attn_norm = rms_backward(grad_attn_in, attn_hat, attn_inv, attn_norm)
    grad_stream = grad_middle + grad_stream_norm
    grad_low = grad_stream.astype(jnp.bfloat16)
    grad_roi = jnp.dot(pooled.T, grad_low, preferred_element_type=jnp.float32)
    grad_pooled = jnp.dot(grad_low, roi_proj.T, preferred_element_type=jnp.float32)
    grad_box = grad_pooled / box_area[:, None]
    map_pair = jnp.dot(box_mask.T, split_two(grad_box), preferred_element_type=jnp.float32)
    grad_map = map_pair[:, :128] + map_pair[:, 128:]
    stem_totals = stem_backward(
        grad_map, page_image, records, conv_weights, group_gain, group_shift, devices
    )
    table_totals = lax.psum(grad_tables, "dp")
    weight_parts = (
        lax.psum_scatter(grad_roi, "dp", scatter_dimension=1, tiled=True),
        lax.psum_scatter(grad_attn_norm, "dp", scatter_dimension=0, tiled=True),
        lax.psum_scatter(grad_query_proj, "dp", scatter_dimension=0, tiled=True),
        lax.psum_scatter(grad_key_proj, "dp", scatter_dimension=0, tiled=True),
        lax.psum_scatter(grad_value_proj, "dp", scatter_dimension=0, tiled=True),
        lax.psum_scatter(grad_output, "dp", scatter_dimension=1, tiled=True),
        lax.psum_scatter(grad_ffn_norm, "dp", scatter_dimension=0, tiled=True),
        lax.psum_scatter(grad_up, "dp", scatter_dimension=0, tiled=True),
        lax.psum_scatter(grad_down, "dp", scatter_dimension=1, tiled=True),
    )
    block_parts = weight_parts[:6]
    ffn_parts = weight_parts[6:]
    return (
        layer_out,
        grad_stream,
        stem_totals[0],
        stem_totals[1],
        stem_totals[2],
        stem_totals[3],
        block_parts[0],
        block_parts[1],
        block_parts[2],
        block_parts[3],
        block_parts[4],
        block_parts[5],
        table_totals,
        ffn_parts[0],
        ffn_parts[1],
        ffn_parts[2],
    )


def solution(mesh):
    placed = (
        P(None, ("dp", "tensor"), None),
        P("dp", None),
        P("dp", None),
        P("dp", None),
        P("dp", None),
        P(None, "dp", None),
        P(),
        P(),
        P(),
        P(),
        P(),
        P(),
        P(None, "tensor"),
        P(None, "tensor"),
        P(None, "tensor"),
        P("tensor", None),
        P(None, None, "tensor"),
        P(),
        P(None, "tensor"),
        P("tensor", None),
    )
    return jax.shard_map(
        on_device,
        mesh=mesh,
        in_specs=placed,
        out_specs=(
            P("dp", None),
            P("dp", None),
            P(),
            P(),
            P(),
            P(),
            P(None, "dp"),
            P("dp"),
            P("dp", "tensor"),
            P("dp", "tensor"),
            P("dp", "tensor"),
            P("tensor", "dp"),
            P(None, None, "tensor"),
            P("dp"),
            P("dp", "tensor"),
            P("tensor", "dp"),
        ),
        check_vma=False,
    )
```

```python
import functools

import jax
import jax.numpy as jnp
from jax import lax
from jax.experimental import pallas as pl
from jax.experimental.pallas import tpu as pltpu
from jax.sharding import PartitionSpec as P

HDIM = 64
NBUCKET = 32
GROUPS = 32


bucket_edges = (12, 16, 23, 32, 46, 64, 91)
norm_eps = 1e-06
group_eps = 1e-05
masked_score = -1e30
highest = lax.Precision.HIGHEST


def bucket_of(relative):
    magnitude = jnp.abs(relative)
    coarse = jnp.full(relative.shape, 8, jnp.int32)
    for edge in bucket_edges:
        coarse = coarse + (magnitude >= edge).astype(jnp.int32)
    return jnp.where(magnitude < 8, magnitude, coarse) + jnp.where(relative > 0, 16, 0).astype(
        jnp.int32
    )


MESH = pl.DeviceIdType.MESH
LAYERS = 9
PIX_CHUNK = 256


def level_of(layer):
    return layer if layer <= 4 else 8 - layer


def stem_rows(pixels):
    return [pixels >> (2 * level_of(layer)) for layer in range(LAYERS)]


def row_starts(rows):
    starts = [0]
    for count in rows:
        starts.append(starts[-1] + count)
    return starts


def split_two(values):
    high = values.astype(jnp.bfloat16)
    low = (values - high.astype(jnp.float32)).astype(jnp.bfloat16)
    return jnp.concatenate([high, low], axis=1)


def group_sum(values):
    lane = lax.broadcasted_iota(jnp.int32, values.shape, 1)
    pairs = values + jnp.where(
        lane % 2 == 0, pltpu.roll(values, 127, 1), pltpu.roll(values, 1, 1)
    )
    return pairs + jnp.where(
        (lane // 2) % 2 == 0, pltpu.roll(pairs, 126, 1), pltpu.roll(pairs, 2, 1)
    )


def wide(row):
    return jnp.broadcast_to(row, (8, row.shape[1]))


def my_index():
    return lax.axis_index("dp") * 2 + lax.axis_index("tensor")


def greet_all(count):
    barrier = pltpu.get_barrier_semaphore()
    me = my_index()

    def greet(step, carry):
        other = lax.rem(me + step, count)
        pl.semaphore_signal(
            barrier, inc=1, device_id=(other // 2, lax.rem(other, 2)), device_id_type=MESH
        )
        return carry

    lax.fori_loop(1, count, greet, 0)


def greeted(count):
    pl.semaphore_wait(pltpu.get_barrier_semaphore(), count - 1)


def send_all(count, source, target, send_sem, recv_sem):
    me = my_index()

    def send(step, carry):
        other = lax.rem(me + step, count)
        pltpu.make_async_remote_copy(
            src_ref=source,
            dst_ref=target,
            send_sem=send_sem,
            recv_sem=recv_sem,
            device_id=(other // 2, lax.rem(other, 2)),
            device_id_type=MESH,
        ).start()
        return carry

    lax.fori_loop(1, count, send, 0, unroll=count <= 32)


def wait_all(count, slots, sem):
    part = slots.at[pl.ds(0, count - 1)]
    pltpu.make_async_copy(part, part, sem).wait()


def natural_places(tile_rows, columns):
    spacing = columns // 8
    places = []
    for row in range(tile_rows):
        for col in range(spacing):
            place = 0
            for bit in range(4):
                place = place * 4 + ((row >> bit) & 1) * 2 + ((col >> bit) & 1)
            places.append((row * columns + col, place * 8))
    return places


def stem_forward_kernel(
    count,
    places,
    image_ref,
    first_ref,
    weights_ref,
    gain_ref,
    shift_ref,
    feature_ref,
    norm_ref,
    input_ref,
    scale_ref,
    natural,
    skip,
    current,
    source,
    slots,
    send_sem,
    recv_sem,
):
    me = my_index()
    greet_all(count)
    pixels = feature_ref.shape[0]
    rows = stem_rows(pixels)
    norm_at = row_starts(rows)
    input_at = row_starts(rows[1:])
    skip_at = row_starts(rows[:4])
    spacing = 16
    natural[...] = lax.dot_general(
        image_ref[...],
        first_ref[...],
        (((0,), (0,)), ((), ())),
        preferred_element_type=jnp.float32,
    )
    for start, place in places:
        norm_ref[place : place + 8, :] = natural[pl.ds(start, 8, stride=spacing), :]
    for layer in range(LAYERS):
        height = rows[layer]
        chunk = min(height, PIX_CHUNK)
        base = norm_at[layer]
        total = jnp.zeros((8, 128), jnp.float32)
        if layer > 0:
            weights = weights_ref[layer - 1]
            stacked = jnp.concatenate([weights, weights], axis=0)

            def convolve(index, total):
                at = pl.multiple_of(index * chunk, chunk)
                values = jnp.dot(
                    split_two(input_ref[pl.ds(input_at[layer - 1] + at, chunk), :]),
                    stacked,
                    preferred_element_type=jnp.float32,
                )
                norm_ref[pl.ds(base + at, chunk), :] = values
                return total + jnp.sum(values.reshape(chunk // 8, 8, 128), axis=0)

        else:

            def convolve(index, total):
                at = pl.multiple_of(index * chunk, chunk)
                values = norm_ref[pl.ds(base + at, chunk), :]
                return total + jnp.sum(values.reshape(chunk // 8, 8, 128), axis=0)

        total = lax.fori_loop(0, height // chunk, convolve, total)
        mean = jnp.sum(total, axis=0, keepdims=True) * (1.0 / height)

        def deviate(index, total):
            at = pl.multiple_of(index * chunk, chunk)
            values = norm_ref[pl.ds(base + at, chunk), :] - mean
            return total + jnp.sum((values * values).reshape(chunk // 8, 8, 128), axis=0)

        square = lax.fori_loop(0, height // chunk, deviate, jnp.zeros((8, 128), jnp.float32))
        square = jnp.sum(square, axis=0, keepdims=True)
        stats = jnp.concatenate([mean, square], axis=0)
        source[layer] = stats
        slots[layer, me] = stats
        if layer == 0:
            greeted(count)
        send_all(
            count,
            source.at[layer],
            slots.at[layer, me],
            send_sem.at[layer],
            recv_sem.at[layer],
        )
        wait_all(count, slots.at[layer], recv_sem.at[layer])
        means = slots[layer, :, 0, :]
        centre = group_sum(wide(jnp.sum(means, axis=0, keepdims=True))) * (0.25 / count)
        apart = means - centre[0:1]
        spread = jnp.sum(slots[layer, :, 1, :], axis=0, keepdims=True) + height * jnp.sum(
            apart * apart, axis=0, keepdims=True
        )
        variance = group_sum(wide(spread)) * (1.0 / (4 * height * count))
        inverse = lax.rsqrt(variance + group_eps)[0:1]
        centre = centre[0:1]
        scale_ref[layer : layer + 1, :] = inverse
        gain = gain_ref[layer : layer + 1, :]
        shift = shift_ref[layer : layer + 1, :]

        def activate(start, size):
            normed = (norm_ref[pl.ds(base + start, size), :] - centre) * inverse
            norm_ref[pl.ds(base + start, size), :] = normed
            lifted = normed * gain + shift
            return lifted / (1.0 + jnp.exp(-lifted))

        if layer < 4:
            quarter = height // 4
            part = min(quarter, 64)

            def pool(index, carry):
                at = pl.multiple_of(index * part, part)
                mean_of = jnp.zeros((part, 128), jnp.float32)
                for corner in range(4):
                    value = activate(corner * quarter + at, part)
                    skip[pl.ds(skip_at[layer] + corner * quarter + at, part), :] = value
                    mean_of = mean_of + value
                input_ref[pl.ds(input_at[layer] + at, part), :] = mean_of * 0.25
                return carry

            lax.fori_loop(0, quarter // part, pool, 0)
        elif layer < 8:
            part = min(height, 64)
            skipped = skip_at[7 - layer]

            def grow(index, carry):
                at = pl.multiple_of(index * part, part)
                value = activate(at, part)
                for corner in range(4):
                    place = corner * height + at
                    input_ref[pl.ds(input_at[layer] + place, part), :] = (
                        value + skip[pl.ds(skipped + place, part), :]
                    )
                return carry

            lax.fori_loop(0, height // part, grow, 0)
        else:

            def finish(index, carry):
                at = pl.multiple_of(index * chunk, chunk)
                current[pl.ds(at, chunk), :] = activate(at, chunk)
                return carry

            lax.fori_loop(0, height // chunk, finish, 0)
    for start, place in places:
        feature_ref[pl.ds(start, 8, stride=spacing), :] = current[place : place + 8, :]
    for layer in range(LAYERS):
        wait_all(count, slots.at[layer], send_sem.at[layer])


def stem_backward_kernel(
    count,
    places,
    grad_ref,
    image_ref,
    norm_ref,
    input_ref,
    scale_ref,
    weights_ref,
    gain_ref,
    shift_ref,
    split_ref,
    small_ref,
    first_out,
    weights_out,
    gain_out,
    shift_out,
    split_out,
    small_out,
    natural,
    ordered,
    active,
    grad_conv,
    skip,
    grads,
    product,
    source,
    slots,
    first_source,
    first_slots,
    parts,
    shared,
    send_sem,
    recv_sem,
    part_send,
    part_recv,
    share_send,
    share_recv,
    split_slots,
    split_half,
    small_slots,
    row_send,
    row_recv,
):
    me = my_index()
    row = lax.axis_index("dp")
    core = lax.axis_index("tensor")
    rows_count = count // 2
    greet_all(count)
    pixels = grad_ref.shape[0]
    rows = stem_rows(pixels)
    norm_at = row_starts(rows)
    input_at = row_starts(rows[1:])
    skip_at = row_starts(rows[:4])
    spacing = 16
    owners = count // 8
    owned = parts.shape[1]
    for start, place in places:
        ordered[place : place + 8, :] = grad_ref[pl.ds(start, 8, stride=spacing), :]

    def send_rows(first, last, source_of, target, place):
        def send(step, carry):
            other = lax.rem(row + step, rows_count)
            pltpu.make_async_remote_copy(
                src_ref=source_of(other),
                dst_ref=target.at[row],
                send_sem=row_send.at[place],
                recv_sem=row_recv.at[place],
                device_id=(other, core),
                device_id_type=MESH,
            ).start()
            return carry

        lax.fori_loop(first, last, send, 0)

    def weight_grad(layer):
        height = rows[layer]
        chunk = min(height, 512)

        def add(index, total):
            at = pl.multiple_of(index * chunk, chunk)
            return total + lax.dot_general(
                input_ref[pl.ds(input_at[layer - 1] + at, chunk), :].astype(jnp.bfloat16),
                grad_conv[pl.ds(norm_at[layer] + at, chunk), :].astype(jnp.bfloat16),
                (((0,), (0,)), ((), ())),
                preferred_element_type=jnp.float32,
            )

        product[layer - 1] = lax.fori_loop(
            0, height // chunk, add, jnp.zeros((128, 128), jnp.float32)
        ).reshape(owners, owned, 128)

        def send(index, carry):
            owner = layer - 1 + 8 * index

            @pl.when(owner != me)
            def _():
                pltpu.make_async_remote_copy(
                    src_ref=product.at[layer - 1, index],
                    dst_ref=parts.at[me],
                    send_sem=part_send,
                    recv_sem=part_recv,
                    device_id=(owner // 2, lax.rem(owner, 2)),
                    device_id_type=MESH,
                ).start()

            @pl.when(owner == me)
            def _():
                parts[me] = product[layer - 1, index]

            return carry

        lax.fori_loop(0, owners, send, 0)

    for layer in range(LAYERS - 1, -1, -1):
        height = rows[layer]
        chunk = min(height, PIX_CHUNK)
        base = norm_at[layer]
        gain = gain_ref[layer : layer + 1, :]
        shift = shift_ref[layer : layer + 1, :]
        inverse = scale_ref[layer : layer + 1, :]
        incoming = ordered if layer == 8 else grads

        def activate(index, carry):
            first, second = carry
            at = pl.multiple_of(index * chunk, chunk)
            normed = norm_ref[pl.ds(base + at, chunk), :]
            lifted = normed * gain + shift
            sigma = 1.0 / (1.0 + jnp.exp(-lifted))
            value = incoming[pl.ds(at, chunk), :] * sigma * (1.0 + lifted * (1.0 - sigma))
            active[pl.ds(at, chunk), :] = value
            first = first + jnp.sum(value.reshape(chunk // 8, 8, 128), axis=0)
            second = second + jnp.sum((value * normed).reshape(chunk // 8, 8, 128), axis=0)
            return first, second

        zero = jnp.zeros((8, 128), jnp.float32)
        first, second = lax.fori_loop(0, height // chunk, activate, (zero, zero))
        sums = jnp.concatenate(
            [jnp.sum(first, axis=0, keepdims=True), jnp.sum(second, axis=0, keepdims=True)], axis=0
        )
        source[layer] = sums
        slots[layer, me] = sums
        if layer == 8:
            greeted(count)
        send_all(
            count, source.at[layer], slots.at[layer, me], send_sem.at[layer], recv_sem.at[layer]
        )
        middle = (rows_count + 1) // 2
        if layer == 7:
            small_slots[row] = small_ref[...]
            split_slots[row] = split_ref[row, core]
            send_rows(1, rows_count, lambda other: small_ref, small_slots, 0)
        if layer == 6:
            send_rows(1, middle, lambda other: split_ref.at[other, core], split_slots, 1)
        if layer == 5:
            send_rows(middle, rows_count, lambda other: split_ref.at[other, core], split_slots, 1)
        if layer == 3:
            wait_all(rows_count, small_slots, row_recv.at[0])
            small_out[...] = jnp.sum(small_slots[...], axis=0)
            wait_all(rows_count, split_slots, row_recv.at[1])
            split_half[core] = jnp.sum(split_slots[...], axis=0)
            swap = pltpu.make_async_remote_copy(
                src_ref=split_half.at[core],
                dst_ref=split_half.at[core],
                send_sem=row_send.at[2],
                recv_sem=row_recv.at[2],
                device_id=(row, 1 - core),
                device_id_type=MESH,
            )
            swap.start()
        if layer == 1:
            swap.wait()
            split_out[...] = split_half[...]
        if layer < 8:
            weight_grad(layer + 1)
        wait_all(count, slots.at[layer], recv_sem.at[layer])
        totals = jnp.sum(slots[layer], axis=0)
        shift_out[layer : layer + 1, :] = totals[0:1]
        gain_out[layer : layer + 1, :] = totals[1:2]
        share = 1.0 / (4 * height * count)
        first_mean = group_sum(wide(totals[0:1] * gain))[0:1] * share
        second_mean = group_sum(wide(totals[1:2] * gain))[0:1] * share

        def conv_grad(start, size):
            value = inverse * (
                active[pl.ds(start, size), :] * gain
                - first_mean
                - norm_ref[pl.ds(base + start, size), :] * second_mean
            )
            grad_conv[pl.ds(base + start, size), :] = value
            return value

        if layer > 0:
            weights = weights_ref[layer - 1]
            stacked = jnp.concatenate([weights, weights], axis=1)

            def input_grad(start, size):
                return lax.dot_general(
                    split_two(conv_grad(start, size)),
                    stacked,
                    (((1,), (1,)), ((), ())),
                    preferred_element_type=jnp.float32,
                )

        if layer > 4:
            quarter = height // 4
            part = min(quarter, 64)
            skipped = skip_at[8 - layer]

            def shrink(index, carry):
                at = pl.multiple_of(index * part, part)
                total = jnp.zeros((part, 128), jnp.float32)
                for corner in range(4):
                    place = corner * quarter + at
                    value = input_grad(place, part)
                    skip[pl.ds(skipped + place, part), :] = value
                    total = total + value
                grads[pl.ds(at, part), :] = total
                return carry

            lax.fori_loop(0, quarter // part, shrink, 0)
        elif layer > 0:
            part = min(height, 128)
            skipped = skip_at[layer - 1]

            def spread_out(index, carry):
                at = pl.multiple_of(index * part, part)
                value = input_grad(at, part) * 0.25
                for corner in range(4):
                    place = corner * height + at
                    grads[pl.ds(place, part), :] = value + skip[pl.ds(skipped + place, part), :]
                return carry

            lax.fori_loop(0, height // part, spread_out, 0)
        else:

            def finish(index, carry):
                at = pl.multiple_of(index * chunk, chunk)
                conv_grad(at, chunk)
                return carry

            lax.fori_loop(0, height // chunk, finish, 0)
    for start, place in places:
        natural[pl.ds(start, 8, stride=spacing), :] = grad_conv[place : place + 8, :]
    first_part = jnp.dot(
        image_ref[...], natural[...].astype(jnp.bfloat16), preferred_element_type=jnp.float32
    )
    first_source[...] = first_part
    first_slots[me] = first_part
    send_all(count, first_source, first_slots.at[me], send_sem.at[LAYERS], recv_sem.at[LAYERS])
    wait_all(count, parts, part_recv)
    mine = jnp.sum(parts[...], axis=0)
    shared[me] = mine
    send_all(count, shared.at[me], shared.at[me], share_send, share_recv)
    wait_all(count, first_slots, recv_sem.at[LAYERS])
    first_out[...] = jnp.sum(first_slots[...], axis=0)
    wait_all(count, shared, share_recv)
    for device in range(count):
        weights_out[device % 8, (device // 8) * owned : (device // 8 + 1) * owned, :] = shared[
            device
        ]
    for layer in range(LAYERS):
        wait_all(count, slots.at[layer], send_sem.at[layer])
    wait_all(count, first_slots, send_sem.at[LAYERS])
    wait_all(rows_count, small_slots, row_send.at[0])
    wait_all(rows_count, split_slots, row_send.at[1])
    wait_all(count, parts, part_send)
    wait_all(count, shared, share_send)


def stem_forward(page_image, conv_first, conv_weights, group_gain, group_shift, devices):
    planes, tile_rows, columns = page_image.shape
    pixels = tile_rows * columns
    rows = stem_rows(pixels)
    image = page_image.reshape(planes, pixels)
    places = natural_places(tile_rows, columns)
    whole = pl.BlockSpec(memory_space=pltpu.VMEM)
    return pl.pallas_call(
        functools.partial(stem_forward_kernel, devices, places),
        out_shape=(
            jax.ShapeDtypeStruct((pixels, 128), jnp.float32),
            jax.ShapeDtypeStruct((sum(rows), 128), jnp.float32),
            jax.ShapeDtypeStruct((sum(rows[1:]), 128), jnp.float32),
            jax.ShapeDtypeStruct((LAYERS, 128), jnp.float32),
        ),
        in_specs=[whole] * 5,
        out_specs=(whole,) * 4,
        scratch_shapes=[
            pltpu.VMEM((pixels, 128), jnp.float32),
            pltpu.VMEM((sum(rows[:4]), 128), jnp.float32),
            pltpu.VMEM((pixels, 128), jnp.float32),
            pltpu.VMEM((LAYERS, 2, 128), jnp.float32),
            pltpu.VMEM((LAYERS, devices, 2, 128), jnp.float32),
            pltpu.SemaphoreType.DMA((LAYERS,)),
            pltpu.SemaphoreType.DMA((LAYERS,)),
        ],
        compiler_params=pltpu.CompilerParams(
            collective_id=0, has_side_effects=True, vmem_limit_bytes=40 * 2**20
        ),
        name="stem_forward",
    )(image, conv_first, conv_weights, group_gain, group_shift)


def stem_backward(
    grad_map, page_image, records, conv_weights, group_gain, group_shift, split, small, devices
):
    planes, tile_rows, columns = page_image.shape
    pixels = tile_rows * columns
    rows = stem_rows(pixels)
    norms, inputs, scales = records
    image = page_image.reshape(planes, pixels)
    places = natural_places(tile_rows, columns)
    whole = pl.BlockSpec(memory_space=pltpu.VMEM)
    owned = 1024 // devices
    return pl.pallas_call(
        functools.partial(stem_backward_kernel, devices, places),
        out_shape=(
            jax.ShapeDtypeStruct((planes, 128), jnp.float32),
            jax.ShapeDtypeStruct((8, 128, 128), jnp.float32),
            jax.ShapeDtypeStruct((LAYERS, 128), jnp.float32),
            jax.ShapeDtypeStruct((LAYERS, 128), jnp.float32),
            jax.ShapeDtypeStruct(split.shape[1:], jnp.float32),
            jax.ShapeDtypeStruct(small.shape, jnp.float32),
        ),
        in_specs=[whole] * 10,
        out_specs=(whole,) * 6,
        scratch_shapes=[
            pltpu.VMEM((pixels, 128), jnp.float32),
            pltpu.VMEM((pixels, 128), jnp.float32),
            pltpu.VMEM((pixels, 128), jnp.float32),
            pltpu.VMEM((sum(rows), 128), jnp.float32),
            pltpu.VMEM((sum(rows[:4]), 128), jnp.float32),
            pltpu.VMEM((pixels, 128), jnp.float32),
            pltpu.VMEM((8, devices // 8, owned, 128), jnp.float32),
            pltpu.VMEM((LAYERS, 2, 128), jnp.float32),
            pltpu.VMEM((LAYERS, devices, 2, 128), jnp.float32),
            pltpu.VMEM((planes, 128), jnp.float32),
            pltpu.VMEM((devices, planes, 128), jnp.float32),
            pltpu.VMEM((devices, owned, 128), jnp.float32),
            pltpu.VMEM((devices, owned, 128), jnp.float32),
            pltpu.SemaphoreType.DMA((LAYERS + 1,)),
            pltpu.SemaphoreType.DMA((LAYERS + 1,)),
            pltpu.SemaphoreType.DMA,
            pltpu.SemaphoreType.DMA,
            pltpu.SemaphoreType.DMA,
            pltpu.SemaphoreType.DMA,
            pltpu.VMEM((devices // 2, *split.shape[2:]), jnp.float32),
            pltpu.VMEM(split.shape[1:], jnp.float32),
            pltpu.VMEM((devices // 2, *small.shape), jnp.float32),
            pltpu.SemaphoreType.DMA((3,)),
            pltpu.SemaphoreType.DMA((3,)),
        ],
        compiler_params=pltpu.CompilerParams(
            collective_id=1, has_side_effects=True, vmem_limit_bytes=40 * 2**20
        ),
        name="stem_backward",
    )(
        grad_map, image, norms, inputs, scales, conv_weights, group_gain, group_shift, split, small
    )


def rms_forward(values, gains):
    inverse = lax.rsqrt(jnp.mean(values * values, axis=-1, keepdims=True) + norm_eps)
    normal = values * inverse
    return ((normal * gains).astype(jnp.bfloat16), normal, inverse)


def rms_backward(grads, normal, inverse, gains):
    scaled = grads * gains
    grad_gain = jnp.sum(grads * normal, axis=0)
    back = inverse * (scaled - normal * jnp.mean(scaled * normal, axis=-1, keepdims=True))
    return (back, grad_gain)


def exact_gelu(values):
    return jax.nn.gelu(values, approximate=False)


TILE = 128
QROWS = 256
KIND_ROWS = 8
FAR_LANE = 32
LOW_LANE = 40
PAD_LANE = 48
DOC_LANE = 56


def dot_last(left, right):
    return lax.dot_general(
        left, right, (((1,), (1,)), ((), ())), preferred_element_type=jnp.float32
    )


def dot_plain(left, right):
    return jnp.dot(left, right, preferred_element_type=jnp.float32)


def bucket_vector(tables_ref, table, head, relative):
    buckets = bucket_of(relative)
    values = jnp.zeros(relative.shape, jnp.float32)
    for bucket in range(NBUCKET):
        values = jnp.where(buckets == bucket, tables_ref[table, bucket, head], values)
    return values


def signed_lanes(width):
    lane = lax.broadcasted_iota(jnp.int32, (8, width), 1)
    return jnp.where(lane < width // 2, lane, lane - width)


def rolled(row, height):
    return pltpu.roll(
        jnp.broadcast_to(row[0:1], (height, row.shape[1])), 0, 1, stride=1, stride_axis=0
    )


def token_lanes(info_ref, one_hot_x, query_base, key_base, pad_tiles):
    tokens = info_ref.shape[0]
    lane = lax.broadcasted_iota(jnp.int32, (TILE, 128), 1)
    row = lax.broadcasted_iota(jnp.int32, (TILE, 128), 0)
    for tile in range(tokens // TILE):
        at = slice(tile * TILE, (tile + 1) * TILE)
        left = info_ref[at, 0:1]
        top = info_ref[at, 1:2]
        doc = info_ref[at, 2:3]
        hidden = jnp.where(info_ref[at, 3:4] > 0, 0.0, masked_score)
        one_hot_x[at, :] = (lane == left).astype(jnp.float32).astype(jnp.bfloat16)
        shared = jnp.where((lane == top) | (lane == DOC_LANE + doc), 1.0, 0.0)
        query_base[at, :] = jnp.where(lane == FAR_LANE + tile, 1.0, shared).astype(jnp.bfloat16)
        key = jnp.where((lane == FAR_LANE + tile) | (lane == LOW_LANE + tile), 1.0, shared)
        key = jnp.where(lane == PAD_LANE + tile, hidden, key)
        key_base[1, at, :] = key.astype(jnp.bfloat16)
        key_base[0, at, :] = pltpu.roll(key, 64, 1).astype(jnp.bfloat16)
        pad_tiles[at, :] = jnp.where(lane == row, 0.0, jnp.broadcast_to(hidden, (TILE, 128)))


def head_matrices(tables_ref, head, side):
    first = bucket_vector(tables_ref, 1, head, signed_lanes(256))
    across = rolled(first, 128)[:, :128].astype(jnp.bfloat16)
    second = rolled(bucket_vector(tables_ref, 2, head, signed_lanes(128)), 128)
    row = lax.broadcasted_iota(jnp.int32, (128, 128), 0)
    lane = lax.broadcasted_iota(jnp.int32, (128, 128), 1)
    mixed = jnp.where((row < FAR_LANE) & (lane < FAR_LANE), second, 0.0)
    gap = lane % 8 - (row - FAR_LANE)
    before = jnp.full((128, 128), tables_ref[0, NBUCKET // 2 - 1, head], jnp.float32)
    after = jnp.full((128, 128), tables_ref[0, NBUCKET - 1, head], jnp.float32)
    far = jnp.where(gap <= -2, before, jnp.where(gap >= 2, after, 0.0))
    high = far.astype(jnp.bfloat16).astype(jnp.float32)
    of_tile = (row >= FAR_LANE) & (row < LOW_LANE)
    mixed = jnp.where(of_tile & (lane >= FAR_LANE) & (lane < LOW_LANE), high, mixed)
    mixed = jnp.where(of_tile & (lane >= LOW_LANE) & (lane < PAD_LANE), far - high, mixed)
    mixed = jnp.where(
        of_tile & (lane >= PAD_LANE) & (lane < DOC_LANE) & (gap != 0), 1.0, mixed
    )
    docs = (row >= DOC_LANE) & (row < 64) & (lane >= DOC_LANE) & (lane < 64)
    mixed = jnp.where(docs & (row != lane), masked_score, mixed)
    if side == 0:
        mixed = pltpu.roll(mixed, 64, 1)
    near = rolled(bucket_vector(tables_ref, 0, head, -signed_lanes(512)), 128)
    tiles = {0: near[:, :128], 1: near[:, 384:], -1: near[:, 128:256]}
    return across, mixed.astype(jnp.bfloat16), tiles


def own_half(side, own, other):
    lane = lax.broadcasted_iota(jnp.int32, own.shape, 1)
    return jnp.where((lane < 64) if side == 0 else (lane >= 64), own, other)


def widen_operands(
    side, head, tables_ref, query_ref, key_ref, one_hot_x, query_base, key_base, query_wide, key_wide, near
):
    across, mixed, tiles = head_matrices(tables_ref, head, side)
    for gap in (-1, 0, 1):
        near[side, gap + 1] = tiles[gap]
    scaled = (query_ref[...].astype(jnp.float32) * HDIM ** (-0.5)).astype(jnp.bfloat16)
    query_wide[side, :, :128] = own_half(
        side, scaled, dot_plain(query_base[...], mixed).astype(jnp.bfloat16)
    )
    query_wide[side, :, 128:] = dot_plain(one_hot_x[...], across).astype(jnp.bfloat16)
    key_wide[side, :, :128] = own_half(side, key_ref[...], key_base[side])
    key_wide[side, :, 128:] = one_hot_x[...]


def near_scores(scores, side, block, tile, near, pad_tiles):
    halves = []
    for half in range(QROWS // TILE):
        part = scores[:, half * TILE : (half + 1) * TILE]
        gap = tile - (block * (QROWS // TILE) + half)
        if abs(gap) <= 1:
            part = part + near[side, gap + 1]
        if gap == 0:
            part = part + pad_tiles[tile * TILE : (tile + 1) * TILE, :]
        halves.append(part)
    return jnp.concatenate(halves, axis=1)


def attention_forward_kernel(
    tables_ref,
    info_ref,
    query_ref,
    key_ref,
    value_ref,
    context_ref,
    exact_ref,
    lse_ref,
    one_hot_x,
    query_base,
    key_base,
    pad_tiles,
    query_wide,
    key_wide,
    near,
    scores,
    weights,
):
    pair = pl.program_id(0)
    tokens = query_ref.shape[0]

    @pl.when(pair == 0)
    def _():
        token_lanes(info_ref, one_hot_x, query_base, key_base, pad_tiles)

    for side in range(2):
        widen_operands(
            side, pair * 2 + side, tables_ref, query_ref, key_ref, one_hot_x, query_base, key_base,
            query_wide, key_wide, near,
        )
    values = value_ref[...].T
    for block in range(tokens // QROWS):
        columns = slice(block * QROWS, (block + 1) * QROWS)
        contexts = []
        for side in range(2):
            scores[side] = dot_last(key_wide[side], query_wide[side, columns, :])
            top = jnp.full((8, QROWS), masked_score, jnp.float32)
            for tile in range(tokens // TILE):
                at = slice(tile * TILE, (tile + 1) * TILE)
                part = scores[side, at, :]
                if any(abs(tile - 2 * block - half) <= 1 for half in range(2)):
                    part = near_scores(part, side, block, tile, near, pad_tiles)
                    scores[side, at, :] = part
                top = jnp.maximum(top, jnp.max(part.reshape(TILE // 8, 8, QROWS), axis=0))
            top = jnp.max(top, axis=0, keepdims=True)
            total = jnp.zeros((8, QROWS), jnp.float32)
            for tile in range(tokens // TILE):
                at = slice(tile * TILE, (tile + 1) * TILE)
                part = jnp.exp(scores[side, at, :] - top)
                total = total + jnp.sum(part.reshape(TILE // 8, 8, QROWS), axis=0)
                weights[side, at, :] = part.astype(jnp.bfloat16)
            total = jnp.sum(total, axis=0, keepdims=True)
            context = dot_plain(values[side * 64 : (side + 1) * 64, :], weights[side])
            contexts.append(context * (1.0 / total))
            lse_ref[0, side : side + 1, columns] = top + jnp.log(total)
        context = jnp.concatenate(contexts, axis=0)
        exact_ref[:, columns] = context
        context_ref[columns, :] = context.T.astype(jnp.bfloat16)


def attention_backward_kernel(
    tables_ref,
    info_ref,
    query_ref,
    key_ref,
    value_ref,
    grad_ref,
    exact_ref,
    lse_ref,
    grad_query_ref,
    grad_key_ref,
    grad_value_ref,
    diagonal_ref,
    one_hot_x,
    query_base,
    key_base,
    pad_tiles,
    reverse,
    query_wide,
    key_wide,
    near,
    scores,
    grad_probs,
    probs_low,
    grad_low,
    key_turned,
    grad_near,
    grad_blocks,
    grad_key,
    grad_value,
):
    pair = pl.program_id(0)
    tokens = query_ref.shape[0]

    @pl.when(pair == 0)
    def _():
        token_lanes(info_ref, one_hot_x, query_base, key_base, pad_tiles)
        lane = lax.broadcasted_iota(jnp.int32, (TILE, 128), 1)
        for tile in range(tokens // TILE):
            at = slice(tile * TILE, (tile + 1) * TILE)
            left = info_ref[at, 0:1]
            top = info_ref[at, 1:2]
            reverse[at, :128] = jnp.where(lane == 127 - left, 1.0, 0.0).astype(jnp.bfloat16)
            reverse[at, 128:] = jnp.where(
                (lane == 31 - top) | (lane == FAR_LANE + tile), 1.0, 0.0
            ).astype(jnp.bfloat16)

    for side in range(2):
        widen_operands(
            side, pair * 2 + side, tables_ref, query_ref, key_ref, one_hot_x, query_base, key_base,
            query_wide, key_wide, near,
        )
        key_turned[side] = key_wide[side].T
    grad_near[...] = jnp.zeros_like(grad_near)
    grad_blocks[...] = jnp.zeros_like(grad_blocks)
    values = [
        own_half(side, value_ref[...], jnp.zeros(value_ref.shape, jnp.bfloat16)) for side in range(2)
    ]
    for block in range(tokens // QROWS):
        columns = slice(block * QROWS, (block + 1) * QROWS)
        grad_block = grad_ref[columns, :]
        product = grad_block.astype(jnp.float32).T * exact_ref[:, columns]
        scaled = (query_ref[columns, :].astype(jnp.float32) * HDIM ** (-0.5)).astype(jnp.bfloat16)
        turned = []
        key_terms = []
        value_terms = []
        for side in range(2):
            delta = jnp.sum(product[side * 64 : (side + 1) * 64, :], axis=0, keepdims=True)
            lse = lse_ref[0, side : side + 1, columns]
            scores[side] = dot_last(key_wide[side], query_wide[side, columns, :])
            grad_probs[side] = dot_last(values[side], grad_block)
            for tile in range(tokens // TILE):
                at = slice(tile * TILE, (tile + 1) * TILE)
                part = near_scores(scores[side, at, :], side, block, tile, near, pad_tiles)
                probs = jnp.exp(part - lse)
                grad_part = probs * (grad_probs[side, at, :] - delta)
                probs_low[side, at, :] = probs.astype(jnp.bfloat16)
                grad_low[side, at, :] = grad_part.astype(jnp.bfloat16)
                for half in range(QROWS // TILE):
                    gap = tile - (block * (QROWS // TILE) + half)
                    if abs(gap) <= 1:
                        grad_near[side, gap + 1] += grad_part[:, half * TILE : (half + 1) * TILE]
            value_terms.append(dot_plain(probs_low[side], grad_block))
            key_terms.append(dot_plain(grad_low[side], scaled))
            sums = dot_plain(key_turned[side], grad_low[side])
            turned.append(sums[side * 64 : (side + 1) * 64, :])
            grad_blocks[side] += dot_plain(sums.astype(jnp.bfloat16), reverse[columns, :])
        grad_query_ref[columns, :] = (
            (jnp.concatenate(turned, axis=0) * HDIM ** (-0.5)).T.astype(jnp.bfloat16)
        )
        key_term = own_half(0, key_terms[0], key_terms[1])
        value_term = own_half(0, value_terms[0], value_terms[1])
        if block == 0:
            grad_key[...] = key_term
            grad_value[...] = value_term
        else:
            grad_key[...] += key_term
            grad_value[...] += value_term
    grad_key_ref[...] = grad_key[...].astype(jnp.bfloat16)
    grad_value_ref[...] = grad_value[...].astype(jnp.bfloat16)
    row = lax.broadcasted_iota(jnp.int32, (128, 128), 0)
    lane = lax.broadcasted_iota(jnp.int32, (128, 128), 1)
    flip = jnp.where(row + lane == 127, 1.0, 0.0).astype(jnp.bfloat16)
    blank = jnp.zeros((128, 128), jnp.float32)

    def diagonal_sums(values):
        spread = jnp.concatenate([values, blank], axis=1)
        return jnp.sum(
            pltpu.roll(spread, 0, 1, stride=1, stride_axis=0), axis=0, keepdims=True
        )

    for side in range(2):
        misc = 64 * (1 - side)
        sums = [diagonal_sums(grad_blocks[side, 128:, :128])]
        below = grad_blocks[side, misc : misc + 64, 128:]
        small_row = lax.broadcasted_iota(jnp.int32, (64, 128), 0)
        small_lane = lax.broadcasted_iota(jnp.int32, (64, 128), 1)
        upright = jnp.where((small_row < FAR_LANE) & (small_lane < FAR_LANE), below, 0.0)
        sums.append(diagonal_sums(jnp.concatenate([upright, jnp.zeros((64, 128), jnp.float32)], axis=0)))
        for gap in range(3):
            tile = grad_near[side, gap]
            high = tile.astype(jnp.bfloat16)
            rest = (tile - high.astype(jnp.float32)).astype(jnp.bfloat16)
            sums.append(diagonal_sums(dot_plain(high, flip) + dot_plain(rest, flip)))
        gap = (small_row - FAR_LANE) - (small_lane - FAR_LANE)
        inside = (
            (small_row >= FAR_LANE)
            & (small_row < LOW_LANE)
            & (small_lane >= FAR_LANE)
            & (small_lane < LOW_LANE)
        )
        for chosen in (gap <= -2, gap >= 2):
            far = jnp.sum(jnp.where(inside & chosen, below, 0.0), axis=0, keepdims=True)
            sums.append(jnp.concatenate([far, blank[0:1]], axis=1))
        sums.append(jnp.zeros((1, 256), jnp.float32))
        diagonal_ref[side] = jnp.concatenate(sums, axis=0)


def attention_scratch(tokens):
    return [
        pltpu.VMEM((tokens, 128), jnp.bfloat16),
        pltpu.VMEM((tokens, 128), jnp.bfloat16),
        pltpu.VMEM((2, tokens, 128), jnp.bfloat16),
        pltpu.VMEM((tokens, 128), jnp.float32),
    ], [
        pltpu.VMEM((2, tokens, 256), jnp.bfloat16),
        pltpu.VMEM((2, tokens, 256), jnp.bfloat16),
        pltpu.VMEM((2, 3, TILE, TILE), jnp.float32),
        pltpu.VMEM((2, tokens, QROWS), jnp.float32),
    ]


def attention_forward(tables, info, query, key, value):
    tokens, width = query.shape
    pairs = width // 128
    own = pl.BlockSpec((tokens, 128), lambda pair: (0, pair))
    fixed, moving = attention_scratch(tokens)
    return pl.pallas_call(
        attention_forward_kernel,
        grid=(pairs,),
        out_shape=(
            jax.ShapeDtypeStruct((tokens, width), jnp.bfloat16),
            jax.ShapeDtypeStruct((width, tokens), jnp.float32),
            jax.ShapeDtypeStruct((pairs, 2, tokens), jnp.float32),
        ),
        in_specs=[
            pl.BlockSpec(memory_space=pltpu.SMEM),
            pl.BlockSpec((tokens, 8), lambda pair: (0, 0)),
            own,
            own,
            own,
        ],
        out_specs=(
            own,
            pl.BlockSpec((128, tokens), lambda pair: (pair, 0)),
            pl.BlockSpec((1, 2, tokens), lambda pair: (pair, 0, 0)),
        ),
        scratch_shapes=fixed
        + moving
        + [
            pltpu.VMEM((2, tokens, QROWS), jnp.bfloat16),
        ],
        compiler_params=pltpu.CompilerParams(
            dimension_semantics=("arbitrary",), vmem_limit_bytes=48 * 2**20
        ),
        name="attention_forward",
    )(tables, info, query, key, value)


def attention_backward(tables, info, query, key, value, grad_context, exact, lse):
    tokens, width = query.shape
    pairs = width // 128
    own = pl.BlockSpec((tokens, 128), lambda pair: (0, pair))
    fixed, moving = attention_scratch(tokens)
    low = jax.ShapeDtypeStruct((tokens, width), jnp.bfloat16)
    return pl.pallas_call(
        attention_backward_kernel,
        grid=(pairs,),
        out_shape=(low, low, low, jax.ShapeDtypeStruct((2 * pairs, 8, 256), jnp.float32)),
        in_specs=[
            pl.BlockSpec(memory_space=pltpu.SMEM),
            pl.BlockSpec((tokens, 8), lambda pair: (0, 0)),
            own,
            own,
            own,
            own,
            pl.BlockSpec((128, tokens), lambda pair: (pair, 0)),
            pl.BlockSpec((1, 2, tokens), lambda pair: (pair, 0, 0)),
        ],
        out_specs=(own, own, own, pl.BlockSpec((2, 8, 256), lambda pair: (pair, 0, 0))),
        scratch_shapes=fixed
        + [pltpu.VMEM((tokens, 256), jnp.bfloat16)]
        + moving
        + [
            pltpu.VMEM((2, tokens, QROWS), jnp.float32),
            pltpu.VMEM((2, tokens, QROWS), jnp.bfloat16),
            pltpu.VMEM((2, tokens, QROWS), jnp.bfloat16),
            pltpu.VMEM((2, 256, tokens), jnp.bfloat16),
            pltpu.VMEM((2, 3, TILE, TILE), jnp.float32),
            pltpu.VMEM((2, 256, 256), jnp.float32),
            pltpu.VMEM((tokens, 128), jnp.float32),
            pltpu.VMEM((tokens, 128), jnp.float32),
        ],
        compiler_params=pltpu.CompilerParams(
            dimension_semantics=("arbitrary",), vmem_limit_bytes=48 * 2**20
        ),
        name="attention_backward",
    )(tables, info, query, key, value, grad_context, exact, lse)


def bucket_grads(diagonals):
    lane = jnp.arange(256, dtype=jnp.int32)
    wide_buckets = [
        bucket_of(lane - 127),
        bucket_of(lane - 31),
        bucket_of(lane - 127 - TILE),
        bucket_of(lane - 127),
        bucket_of(lane - 127 + TILE),
        jnp.full((256,), NBUCKET // 2 - 1, jnp.int32),
        jnp.full((256,), NBUCKET - 1, jnp.int32),
    ]
    table_of = (1, 2, 0, 0, 0, 0, 0)
    slots = jnp.stack([bucket + NBUCKET * table for bucket, table in zip(wide_buckets, table_of)])
    chosen = (slots[..., None] == jnp.arange(3 * NBUCKET, dtype=jnp.int32)).astype(jnp.float32)
    sums = jnp.einsum("hrc,rcb->bh", diagonals[:, :7], chosen, precision=highest)
    return sums.reshape(3, NBUCKET, -1)


def on_device(
    page_image,
    embeddings,
    cotangent,
    doc_ids,
    pad_mask,
    token_boxes,
    conv_first,
    conv_weights,
    group_gain,
    group_shift,
    roi_proj,
    attn_norm,
    query_proj,
    key_proj,
    value_proj,
    output_proj,
    bias_tables,
    ffn_norm,
    up_proj,
    down_proj,
):
    devices = lax.axis_size("dp") * lax.axis_size("tensor")
    feature_map, *records = stem_forward(
        page_image, conv_first, conv_weights, group_gain, group_shift, devices
    )
    tile_rows = page_image.shape[1]
    row_ids = lax.axis_index("tensor") * tile_rows + jnp.arange(tile_rows, dtype=jnp.int32)
    col_ids = jnp.arange(page_image.shape[2], dtype=jnp.int32)
    left_edge = token_boxes[0, 0]
    top_edge = token_boxes[1, 0]
    right_edge = token_boxes[2, 0]
    bottom_edge = token_boxes[3, 0]
    row_mask = (
        (row_ids[None, :] >= top_edge[:, None]) & (row_ids[None, :] < bottom_edge[:, None])
    ).astype(jnp.float32)
    col_mask = (
        (col_ids[None, :] >= left_edge[:, None]) & (col_ids[None, :] < right_edge[:, None])
    ).astype(jnp.float32)
    box_area = ((bottom_edge - top_edge) * (right_edge - left_edge)).astype(jnp.float32)
    box_mask = (row_mask[:, :, None] * col_mask[:, None, :]).astype(jnp.bfloat16)
    box_mask = box_mask.reshape(box_mask.shape[0], -1)
    feature_pair = split_two(feature_map)
    box_pair = jnp.dot(box_mask, feature_pair, preferred_element_type=jnp.float32)
    partial_boxes = box_pair[:, :128] + box_pair[:, 128:]
    box_sums = lax.psum(partial_boxes, "tensor")
    pooled = (box_sums / box_area[:, None]).astype(jnp.bfloat16)
    stream = embeddings.astype(jnp.float32) + jnp.dot(
        pooled, roi_proj, preferred_element_type=jnp.float32
    )
    attn_in, attn_hat, attn_inv = rms_forward(stream, attn_norm)
    query = jnp.dot(attn_in, query_proj, preferred_element_type=jnp.float32).astype(jnp.bfloat16)
    key = jnp.dot(attn_in, key_proj, preferred_element_type=jnp.float32).astype(jnp.bfloat16)
    value = jnp.dot(attn_in, value_proj, preferred_element_type=jnp.float32).astype(jnp.bfloat16)
    blank = jnp.zeros_like(left_edge)
    info = jnp.stack(
        [left_edge, top_edge, doc_ids[0], pad_mask[0], blank, blank, blank, blank], axis=1
    )
    context, exact, lse = attention_forward(bias_tables, info, query, key, value)
    attn_out = lax.psum(jnp.dot(context, output_proj, preferred_element_type=jnp.float32), "tensor")
    middle = stream + attn_out
    ffn_in, ffn_hat, ffn_inv = rms_forward(middle, ffn_norm)
    pre_act = jnp.dot(ffn_in, up_proj, preferred_element_type=jnp.float32)
    activated, gelu_pullback = jax.vjp(exact_gelu, pre_act)
    hidden = activated.astype(jnp.bfloat16)
    ffn_out = lax.psum(jnp.dot(hidden, down_proj, preferred_element_type=jnp.float32), "tensor")
    layer_out = (middle + ffn_out).astype(jnp.bfloat16)
    grad_down = jnp.dot(cotangent.T, hidden, preferred_element_type=jnp.float32)
    grad_hidden = jnp.dot(cotangent, down_proj.T, preferred_element_type=jnp.float32)
    grad_pre = gelu_pullback(grad_hidden)[0].astype(jnp.bfloat16)
    grad_up = jnp.dot(ffn_in.T, grad_pre, preferred_element_type=jnp.float32)
    grad_ffn_in = lax.psum(
        jnp.dot(grad_pre, up_proj.T, preferred_element_type=jnp.float32), "tensor"
    )
    grad_mid_norm, grad_ffn_norm = rms_backward(grad_ffn_in, ffn_hat, ffn_inv, ffn_norm)
    grad_middle = cotangent.astype(jnp.float32) + grad_mid_norm
    grad_mid_low = grad_middle.astype(jnp.bfloat16)
    grad_context = jnp.dot(
        grad_mid_low, output_proj.T, preferred_element_type=jnp.float32
    ).astype(jnp.bfloat16)
    grad_query_low, grad_key_low, grad_value_low, diagonals = attention_backward(
        bias_tables, info, query, key, value, grad_context, exact, lse
    )
    grad_tables = bucket_grads(diagonals)
    attn_terms = jnp.dot(grad_query_low, query_proj.T, preferred_element_type=jnp.float32)
    attn_terms = attn_terms + jnp.dot(grad_key_low, key_proj.T, preferred_element_type=jnp.float32)
    attn_terms = attn_terms + jnp.dot(
        grad_value_low, value_proj.T, preferred_element_type=jnp.float32
    )
    grad_attn_in = lax.psum(attn_terms, "tensor")
    grad_stream_norm, grad_attn_norm = rms_backward(grad_attn_in, attn_hat, attn_inv, attn_norm)
    grad_stream = grad_middle + grad_stream_norm
    grad_low = grad_stream.astype(jnp.bfloat16)
    grad_roi = jnp.dot(grad_low.T, pooled, preferred_element_type=jnp.float32)
    grad_pooled = jnp.dot(grad_low, roi_proj.T, preferred_element_type=jnp.float32)
    grad_box = grad_pooled / box_area[:, None]
    map_pair = jnp.dot(box_mask.T, split_two(grad_box), preferred_element_type=jnp.float32)
    grad_map = map_pair[:, :128] + map_pair[:, 128:]
    grad_attn = jnp.concatenate(
        [
            jnp.dot(
                attn_in.T,
                jnp.concatenate([grad_query_low, grad_key_low, grad_value_low], axis=1),
                preferred_element_type=jnp.float32,
            ),
            jnp.dot(grad_mid_low.T, context, preferred_element_type=jnp.float32),
        ],
        axis=1,
    )
    rows_count = lax.axis_size("dp")
    width = grad_attn_norm.shape[0]
    own_rows = width // rows_count
    heads = grad_tables.shape[2]
    small = jnp.concatenate([grad_attn_norm, grad_ffn_norm, grad_tables.reshape(-1)])
    small = jnp.pad(small, (0, -small.shape[0] % 1024)).reshape(-1, 128)
    split = grad_roi.reshape(rows_count, 2, own_rows // 2, grad_roi.shape[1])
    grad_first, grad_convs, grad_gains, grad_offsets, own_roi, small = stem_backward(
        grad_map,
        page_image,
        records,
        conv_weights,
        group_gain,
        group_shift,
        split,
        small,
        devices,
    )
    small = small.reshape(-1)
    start = lax.axis_index("dp") * own_rows
    own_attn_norm = lax.dynamic_slice(small, (start,), (own_rows,))
    own_ffn_norm = lax.dynamic_slice(small, (width + start,), (own_rows,))
    own_tables = small[2 * width : 2 * width + grad_tables.size].reshape(3, NBUCKET, heads)
    own_up = lax.psum_scatter(grad_up, "dp", scatter_dimension=0, tiled=True)
    own_down = lax.psum_scatter(grad_down, "dp", scatter_dimension=0, tiled=True).T
    own_attn = lax.psum_scatter(grad_attn, "dp", scatter_dimension=0, tiled=True)
    part = query_proj.shape[1]
    return (
        layer_out,
        grad_stream,
        grad_first,
        grad_convs,
        grad_gains,
        grad_offsets,
        own_roi.reshape(own_rows, -1).T,
        own_attn_norm,
        own_attn[:, :part],
        own_attn[:, part : 2 * part],
        own_attn[:, 2 * part : 3 * part],
        own_attn[:, 3 * part :].T,
        own_tables,
        own_ffn_norm,
        own_up,
        own_down,
    )


def solution(mesh):
    placed = (
        P(None, ("dp", "tensor"), None),
        P("dp", None),
        P("dp", None),
        P("dp", None),
        P("dp", None),
        P(None, "dp", None),
        P(),
        P(),
        P(),
        P(),
        P(),
        P(),
        P(None, "tensor"),
        P(None, "tensor"),
        P(None, "tensor"),
        P("tensor", None),
        P(None, None, "tensor"),
        P(),
        P(None, "tensor"),
        P("tensor", None),
    )
    return jax.shard_map(
        on_device,
        mesh=mesh,
        in_specs=placed,
        out_specs=(
            P("dp", None),
            P("dp", None),
            P(),
            P(),
            P(),
            P(),
            P(None, "dp"),
            P("dp"),
            P("dp", "tensor"),
            P("dp", "tensor"),
            P("dp", "tensor"),
            P("tensor", "dp"),
            P(None, None, "tensor"),
            P("dp"),
            P("dp", "tensor"),
            P("tensor", "dp"),
        ),
        check_vma=False,
    )
```

```python
import functools

import jax
import jax.numpy as jnp
from jax import lax
from jax.experimental import pallas as pl
from jax.experimental.pallas import tpu as pltpu
from jax.sharding import PartitionSpec as P

HDIM = 64
NBUCKET = 32
GROUPS = 32


bucket_edges = (12, 16, 23, 32, 46, 64, 91)
norm_eps = 1e-06
group_eps = 1e-05
masked_score = -1e30
highest = lax.Precision.HIGHEST


def bucket_of(relative):
    magnitude = jnp.abs(relative)
    coarse = jnp.full(relative.shape, 8, jnp.int32)
    for edge in bucket_edges:
        coarse = coarse + (magnitude >= edge).astype(jnp.int32)
    return jnp.where(magnitude < 8, magnitude, coarse) + jnp.where(relative > 0, 16, 0).astype(
        jnp.int32
    )


MESH = pl.DeviceIdType.MESH
LAYERS = 9
PIX_CHUNK = 256


def level_of(layer):
    return layer if layer <= 4 else 8 - layer


def stem_rows(pixels):
    return [pixels >> (2 * level_of(layer)) for layer in range(LAYERS)]


def row_starts(rows):
    starts = [0]
    for count in rows:
        starts.append(starts[-1] + count)
    return starts


def split_two(values):
    high = values.astype(jnp.bfloat16)
    low = (values - high.astype(jnp.float32)).astype(jnp.bfloat16)
    return jnp.concatenate([high, low], axis=1)


def group_sum(values):
    lane = lax.broadcasted_iota(jnp.int32, values.shape, 1)
    pairs = values + jnp.where(
        lane % 2 == 0, pltpu.roll(values, 127, 1), pltpu.roll(values, 1, 1)
    )
    return pairs + jnp.where(
        (lane // 2) % 2 == 0, pltpu.roll(pairs, 126, 1), pltpu.roll(pairs, 2, 1)
    )


def wide(row):
    return jnp.broadcast_to(row, (8, row.shape[1]))


def my_index():
    return lax.axis_index("dp") * 2 + lax.axis_index("tensor")


def greet_all(count):
    barrier = pltpu.get_barrier_semaphore()
    me = my_index()

    def greet(step, carry):
        other = lax.rem(me + step, count)
        pl.semaphore_signal(
            barrier, inc=1, device_id=(other // 2, lax.rem(other, 2)), device_id_type=MESH
        )
        return carry

    lax.fori_loop(1, count, greet, 0)


def greeted(count):
    pl.semaphore_wait(pltpu.get_barrier_semaphore(), count - 1)


def send_all(count, source, target, send_sem, recv_sem):
    me = my_index()

    def send(step, carry):
        other = lax.rem(me + step, count)
        pltpu.make_async_remote_copy(
            src_ref=source,
            dst_ref=target,
            send_sem=send_sem,
            recv_sem=recv_sem,
            device_id=(other // 2, lax.rem(other, 2)),
            device_id_type=MESH,
        ).start()
        return carry

    lax.fori_loop(1, count, send, 0, unroll=count <= 32)


def wait_all(count, slots, sem):
    part = slots.at[pl.ds(0, count - 1)]
    pltpu.make_async_copy(part, part, sem).wait()


def natural_places(tile_rows, columns):
    spacing = columns // 8
    places = []
    for row in range(tile_rows):
        for col in range(spacing):
            place = 0
            for bit in range(4):
                place = place * 4 + ((row >> bit) & 1) * 2 + ((col >> bit) & 1)
            places.append((row * columns + col, place * 8))
    return places


def stem_forward_kernel(
    count,
    places,
    image_ref,
    first_ref,
    weights_ref,
    gain_ref,
    shift_ref,
    feature_ref,
    norm_ref,
    input_ref,
    scale_ref,
    natural,
    skip,
    current,
    source,
    slots,
    send_sem,
    recv_sem,
):
    me = my_index()
    greet_all(count)
    pixels = feature_ref.shape[0]
    rows = stem_rows(pixels)
    norm_at = row_starts(rows)
    input_at = row_starts(rows[1:])
    skip_at = row_starts(rows[:4])
    spacing = 16
    natural[...] = lax.dot_general(
        image_ref[...],
        first_ref[...],
        (((0,), (0,)), ((), ())),
        preferred_element_type=jnp.float32,
    )
    for start, place in places:
        norm_ref[place : place + 8, :] = natural[pl.ds(start, 8, stride=spacing), :]
    for layer in range(LAYERS):
        height = rows[layer]
        chunk = min(height, PIX_CHUNK)
        base = norm_at[layer]
        total = jnp.zeros((8, 128), jnp.float32)
        if layer > 0:
            weights = weights_ref[layer - 1]
            stacked = jnp.concatenate([weights, weights], axis=0)

            def convolve(index, total):
                at = pl.multiple_of(index * chunk, chunk)
                values = jnp.dot(
                    split_two(input_ref[pl.ds(input_at[layer - 1] + at, chunk), :]),
                    stacked,
                    preferred_element_type=jnp.float32,
                )
                norm_ref[pl.ds(base + at, chunk), :] = values
                return total + jnp.sum(values.reshape(chunk // 8, 8, 128), axis=0)

        else:

            def convolve(index, total):
                at = pl.multiple_of(index * chunk, chunk)
                values = norm_ref[pl.ds(base + at, chunk), :]
                return total + jnp.sum(values.reshape(chunk // 8, 8, 128), axis=0)

        total = lax.fori_loop(0, height // chunk, convolve, total)
        mean = jnp.sum(total, axis=0, keepdims=True) * (1.0 / height)

        def deviate(index, total):
            at = pl.multiple_of(index * chunk, chunk)
            values = norm_ref[pl.ds(base + at, chunk), :] - mean
            return total + jnp.sum((values * values).reshape(chunk // 8, 8, 128), axis=0)

        square = lax.fori_loop(0, height // chunk, deviate, jnp.zeros((8, 128), jnp.float32))
        square = jnp.sum(square, axis=0, keepdims=True)
        stats = jnp.concatenate([mean, square], axis=0)
        source[layer] = stats
        slots[layer, me] = stats
        if layer == 0:
            greeted(count)
        send_all(
            count,
            source.at[layer],
            slots.at[layer, me],
            send_sem.at[layer],
            recv_sem.at[layer],
        )
        wait_all(count, slots.at[layer], recv_sem.at[layer])
        means = slots[layer, :, 0, :]
        centre = group_sum(wide(jnp.sum(means, axis=0, keepdims=True))) * (0.25 / count)
        apart = means - centre[0:1]
        spread = jnp.sum(slots[layer, :, 1, :], axis=0, keepdims=True) + height * jnp.sum(
            apart * apart, axis=0, keepdims=True
        )
        variance = group_sum(wide(spread)) * (1.0 / (4 * height * count))
        inverse = lax.rsqrt(variance + group_eps)[0:1]
        centre = centre[0:1]
        scale_ref[layer : layer + 1, :] = inverse
        gain = gain_ref[layer : layer + 1, :]
        shift = shift_ref[layer : layer + 1, :]

        def activate(start, size):
            normed = (norm_ref[pl.ds(base + start, size), :] - centre) * inverse
            norm_ref[pl.ds(base + start, size), :] = normed
            lifted = normed * gain + shift
            return lifted / (1.0 + jnp.exp(-lifted))

        if layer < 4:
            quarter = height // 4
            part = min(quarter, 64)

            def pool(index, carry):
                at = pl.multiple_of(index * part, part)
                mean_of = jnp.zeros((part, 128), jnp.float32)
                for corner in range(4):
                    value = activate(corner * quarter + at, part)
                    skip[pl.ds(skip_at[layer] + corner * quarter + at, part), :] = value
                    mean_of = mean_of + value
                input_ref[pl.ds(input_at[layer] + at, part), :] = mean_of * 0.25
                return carry

            lax.fori_loop(0, quarter // part, pool, 0)
        elif layer < 8:
            part = min(height, 64)
            skipped = skip_at[7 - layer]

            def grow(index, carry):
                at = pl.multiple_of(index * part, part)
                value = activate(at, part)
                for corner in range(4):
                    place = corner * height + at
                    input_ref[pl.ds(input_at[layer] + place, part), :] = (
                        value + skip[pl.ds(skipped + place, part), :]
                    )
                return carry

            lax.fori_loop(0, height // part, grow, 0)
        else:

            def finish(index, carry):
                at = pl.multiple_of(index * chunk, chunk)
                current[pl.ds(at, chunk), :] = activate(at, chunk)
                return carry

            lax.fori_loop(0, height // chunk, finish, 0)
    for start, place in places:
        feature_ref[pl.ds(start, 8, stride=spacing), :] = current[place : place + 8, :]
    for layer in range(LAYERS):
        wait_all(count, slots.at[layer], send_sem.at[layer])


def stem_backward_kernel(
    count,
    places,
    grad_ref,
    image_ref,
    norm_ref,
    input_ref,
    scale_ref,
    weights_ref,
    gain_ref,
    shift_ref,
    split_ref,
    small_ref,
    first_out,
    weights_out,
    gain_out,
    shift_out,
    split_out,
    small_out,
    natural,
    ordered,
    active,
    grad_conv,
    skip,
    grads,
    product,
    source,
    slots,
    first_source,
    first_slots,
    parts,
    shared,
    send_sem,
    recv_sem,
    part_send,
    part_recv,
    share_send,
    share_recv,
    split_slots,
    split_half,
    small_slots,
    row_send,
    row_recv,
):
    me = my_index()
    row = lax.axis_index("dp")
    core = lax.axis_index("tensor")
    rows_count = count // 2
    greet_all(count)
    pixels = grad_ref.shape[0]
    rows = stem_rows(pixels)
    norm_at = row_starts(rows)
    input_at = row_starts(rows[1:])
    skip_at = row_starts(rows[:4])
    spacing = 16
    owners = count // 8
    owned = parts.shape[1]
    for start, place in places:
        ordered[place : place + 8, :] = grad_ref[pl.ds(start, 8, stride=spacing), :]

    def send_rows(first, last, source_of, target, place):
        def send(step, carry):
            other = lax.rem(row + step, rows_count)
            pltpu.make_async_remote_copy(
                src_ref=source_of(other),
                dst_ref=target.at[row],
                send_sem=row_send.at[place],
                recv_sem=row_recv.at[place],
                device_id=(other, core),
                device_id_type=MESH,
            ).start()
            return carry

        lax.fori_loop(first, last, send, 0)

    def weight_grad(layer):
        height = rows[layer]
        chunk = min(height, 512)

        def add(index, total):
            at = pl.multiple_of(index * chunk, chunk)
            return total + lax.dot_general(
                input_ref[pl.ds(input_at[layer - 1] + at, chunk), :].astype(jnp.bfloat16),
                grad_conv[pl.ds(norm_at[layer] + at, chunk), :].astype(jnp.bfloat16),
                (((0,), (0,)), ((), ())),
                preferred_element_type=jnp.float32,
            )

        product[layer - 1] = lax.fori_loop(
            0, height // chunk, add, jnp.zeros((128, 128), jnp.float32)
        ).reshape(owners, owned, 128)

        def send(index, carry):
            owner = layer - 1 + 8 * index

            @pl.when(owner != me)
            def _():
                pltpu.make_async_remote_copy(
                    src_ref=product.at[layer - 1, index],
                    dst_ref=parts.at[me],
                    send_sem=part_send,
                    recv_sem=part_recv,
                    device_id=(owner // 2, lax.rem(owner, 2)),
                    device_id_type=MESH,
                ).start()

            @pl.when(owner == me)
            def _():
                parts[me] = product[layer - 1, index]

            return carry

        lax.fori_loop(0, owners, send, 0)

    for layer in range(LAYERS - 1, -1, -1):
        height = rows[layer]
        chunk = min(height, PIX_CHUNK)
        base = norm_at[layer]
        gain = gain_ref[layer : layer + 1, :]
        shift = shift_ref[layer : layer + 1, :]
        inverse = scale_ref[layer : layer + 1, :]
        incoming = ordered if layer == 8 else grads

        def activate(index, carry):
            first, second = carry
            at = pl.multiple_of(index * chunk, chunk)
            normed = norm_ref[pl.ds(base + at, chunk), :]
            lifted = normed * gain + shift
            sigma = 1.0 / (1.0 + jnp.exp(-lifted))
            value = incoming[pl.ds(at, chunk), :] * sigma * (1.0 + lifted * (1.0 - sigma))
            active[pl.ds(at, chunk), :] = value
            first = first + jnp.sum(value.reshape(chunk // 8, 8, 128), axis=0)
            second = second + jnp.sum((value * normed).reshape(chunk // 8, 8, 128), axis=0)
            return first, second

        zero = jnp.zeros((8, 128), jnp.float32)
        first, second = lax.fori_loop(0, height // chunk, activate, (zero, zero))
        sums = jnp.concatenate(
            [jnp.sum(first, axis=0, keepdims=True), jnp.sum(second, axis=0, keepdims=True)], axis=0
        )
        source[layer] = sums
        slots[layer, me] = sums
        if layer == 8:
            greeted(count)
        send_all(
            count, source.at[layer], slots.at[layer, me], send_sem.at[layer], recv_sem.at[layer]
        )
        middle = (rows_count + 1) // 2
        if layer == 7:
            small_slots[row] = small_ref[...]
            split_slots[row] = split_ref[row, core]
            send_rows(1, rows_count, lambda other: small_ref, small_slots, 0)
        if layer == 6:
            send_rows(1, middle, lambda other: split_ref.at[other, core], split_slots, 1)
        if layer == 5:
            send_rows(middle, rows_count, lambda other: split_ref.at[other, core], split_slots, 1)
        if layer == 3:
            wait_all(rows_count, small_slots, row_recv.at[0])
            small_out[...] = jnp.sum(small_slots[...], axis=0)
            wait_all(rows_count, split_slots, row_recv.at[1])
            split_half[core] = jnp.sum(split_slots[...], axis=0)
            swap = pltpu.make_async_remote_copy(
                src_ref=split_half.at[core],
                dst_ref=split_half.at[core],
                send_sem=row_send.at[2],
                recv_sem=row_recv.at[2],
                device_id=(row, 1 - core),
                device_id_type=MESH,
            )
            swap.start()
        if layer == 1:
            swap.wait()
            split_out[...] = split_half[...]
        if layer < 8:
            weight_grad(layer + 1)
        wait_all(count, slots.at[layer], recv_sem.at[layer])
        totals = jnp.sum(slots[layer], axis=0)
        shift_out[layer : layer + 1, :] = totals[0:1]
        gain_out[layer : layer + 1, :] = totals[1:2]
        share = 1.0 / (4 * height * count)
        first_mean = group_sum(wide(totals[0:1] * gain))[0:1] * share
        second_mean = group_sum(wide(totals[1:2] * gain))[0:1] * share

        def conv_grad(start, size):
            value = inverse * (
                active[pl.ds(start, size), :] * gain
                - first_mean
                - norm_ref[pl.ds(base + start, size), :] * second_mean
            )
            grad_conv[pl.ds(base + start, size), :] = value
            return value

        if layer > 0:
            weights = weights_ref[layer - 1]
            stacked = jnp.concatenate([weights, weights], axis=1)

            def input_grad(start, size):
                return lax.dot_general(
                    split_two(conv_grad(start, size)),
                    stacked,
                    (((1,), (1,)), ((), ())),
                    preferred_element_type=jnp.float32,
                )

        if layer > 4:
            quarter = height // 4
            part = min(quarter, 64)
            skipped = skip_at[8 - layer]

            def shrink(index, carry):
                at = pl.multiple_of(index * part, part)
                total = jnp.zeros((part, 128), jnp.float32)
                for corner in range(4):
                    place = corner * quarter + at
                    value = input_grad(place, part)
                    skip[pl.ds(skipped + place, part), :] = value
                    total = total + value
                grads[pl.ds(at, part), :] = total
                return carry

            lax.fori_loop(0, quarter // part, shrink, 0)
        elif layer > 0:
            part = min(height, 128)
            skipped = skip_at[layer - 1]

            def spread_out(index, carry):
                at = pl.multiple_of(index * part, part)
                value = input_grad(at, part) * 0.25
                for corner in range(4):
                    place = corner * height + at
                    grads[pl.ds(place, part), :] = value + skip[pl.ds(skipped + place, part), :]
                return carry

            lax.fori_loop(0, height // part, spread_out, 0)
        else:

            def finish(index, carry):
                at = pl.multiple_of(index * chunk, chunk)
                conv_grad(at, chunk)
                return carry

            lax.fori_loop(0, height // chunk, finish, 0)
    for start, place in places:
        natural[pl.ds(start, 8, stride=spacing), :] = grad_conv[place : place + 8, :]
    first_part = jnp.dot(
        image_ref[...], natural[...].astype(jnp.bfloat16), preferred_element_type=jnp.float32
    )
    first_source[...] = first_part
    first_slots[me] = first_part
    send_all(count, first_source, first_slots.at[me], send_sem.at[LAYERS], recv_sem.at[LAYERS])
    wait_all(count, parts, part_recv)
    mine = jnp.sum(parts[...], axis=0)
    shared[me] = mine
    send_all(count, shared.at[me], shared.at[me], share_send, share_recv)
    wait_all(count, first_slots, recv_sem.at[LAYERS])
    first_out[...] = jnp.sum(first_slots[...], axis=0)
    wait_all(count, shared, share_recv)
    for device in range(count):
        weights_out[device % 8, (device // 8) * owned : (device // 8 + 1) * owned, :] = shared[
            device
        ]
    for layer in range(LAYERS):
        wait_all(count, slots.at[layer], send_sem.at[layer])
    wait_all(count, first_slots, send_sem.at[LAYERS])
    wait_all(rows_count, small_slots, row_send.at[0])
    wait_all(rows_count, split_slots, row_send.at[1])
    wait_all(count, parts, part_send)
    wait_all(count, shared, share_send)


def stem_forward(page_image, conv_first, conv_weights, group_gain, group_shift, devices):
    planes, tile_rows, columns = page_image.shape
    pixels = tile_rows * columns
    rows = stem_rows(pixels)
    image = page_image.reshape(planes, pixels)
    places = natural_places(tile_rows, columns)
    whole = pl.BlockSpec(memory_space=pltpu.VMEM)
    return pl.pallas_call(
        functools.partial(stem_forward_kernel, devices, places),
        out_shape=(
            jax.ShapeDtypeStruct((pixels, 128), jnp.float32),
            jax.ShapeDtypeStruct((sum(rows), 128), jnp.float32),
            jax.ShapeDtypeStruct((sum(rows[1:]), 128), jnp.float32),
            jax.ShapeDtypeStruct((LAYERS, 128), jnp.float32),
        ),
        in_specs=[whole] * 5,
        out_specs=(whole,) * 4,
        scratch_shapes=[
            pltpu.VMEM((pixels, 128), jnp.float32),
            pltpu.VMEM((sum(rows[:4]), 128), jnp.float32),
            pltpu.VMEM((pixels, 128), jnp.float32),
            pltpu.VMEM((LAYERS, 2, 128), jnp.float32),
            pltpu.VMEM((LAYERS, devices, 2, 128), jnp.float32),
            pltpu.SemaphoreType.DMA((LAYERS,)),
            pltpu.SemaphoreType.DMA((LAYERS,)),
        ],
        compiler_params=pltpu.CompilerParams(
            collective_id=0, has_side_effects=True, vmem_limit_bytes=40 * 2**20
        ),
        cost_estimate=pl.CostEstimate(
            flops=54 * 10**9, bytes_accessed=2 * 10**7, transcendentals=0
        ),
        name="stem_forward",
    )(image, conv_first, conv_weights, group_gain, group_shift)


def stem_backward(
    grad_map, page_image, records, conv_weights, group_gain, group_shift, split, small, devices
):
    planes, tile_rows, columns = page_image.shape
    pixels = tile_rows * columns
    rows = stem_rows(pixels)
    norms, inputs, scales = records
    image = page_image.reshape(planes, pixels)
    places = natural_places(tile_rows, columns)
    whole = pl.BlockSpec(memory_space=pltpu.VMEM)
    owned = 1024 // devices
    return pl.pallas_call(
        functools.partial(stem_backward_kernel, devices, places),
        out_shape=(
            jax.ShapeDtypeStruct((planes, 128), jnp.float32),
            jax.ShapeDtypeStruct((8, 128, 128), jnp.float32),
            jax.ShapeDtypeStruct((LAYERS, 128), jnp.float32),
            jax.ShapeDtypeStruct((LAYERS, 128), jnp.float32),
            jax.ShapeDtypeStruct(split.shape[1:], jnp.float32),
            jax.ShapeDtypeStruct(small.shape, jnp.float32),
        ),
        in_specs=[whole] * 10,
        out_specs=(whole,) * 6,
        scratch_shapes=[
            pltpu.VMEM((pixels, 128), jnp.float32),
            pltpu.VMEM((pixels, 128), jnp.float32),
            pltpu.VMEM((pixels, 128), jnp.float32),
            pltpu.VMEM((sum(rows), 128), jnp.float32),
            pltpu.VMEM((sum(rows[:4]), 128), jnp.float32),
            pltpu.VMEM((pixels, 128), jnp.float32),
            pltpu.VMEM((8, devices // 8, owned, 128), jnp.float32),
            pltpu.VMEM((LAYERS, 2, 128), jnp.float32),
            pltpu.VMEM((LAYERS, devices, 2, 128), jnp.float32),
            pltpu.VMEM((planes, 128), jnp.float32),
            pltpu.VMEM((devices, planes, 128), jnp.float32),
            pltpu.VMEM((devices, owned, 128), jnp.float32),
            pltpu.VMEM((devices, owned, 128), jnp.float32),
            pltpu.SemaphoreType.DMA((LAYERS + 1,)),
            pltpu.SemaphoreType.DMA((LAYERS + 1,)),
            pltpu.SemaphoreType.DMA,
            pltpu.SemaphoreType.DMA,
            pltpu.SemaphoreType.DMA,
            pltpu.SemaphoreType.DMA,
            pltpu.VMEM((devices // 2, *split.shape[2:]), jnp.float32),
            pltpu.VMEM(split.shape[1:], jnp.float32),
            pltpu.VMEM((devices // 2, *small.shape), jnp.float32),
            pltpu.SemaphoreType.DMA((3,)),
            pltpu.SemaphoreType.DMA((3,)),
        ],
        compiler_params=pltpu.CompilerParams(
            collective_id=1, has_side_effects=True, vmem_limit_bytes=40 * 2**20
        ),
        cost_estimate=pl.CostEstimate(
            flops=65 * 10**9, bytes_accessed=2 * 10**7, transcendentals=0
        ),
        name="stem_backward",
    )(
        grad_map, image, norms, inputs, scales, conv_weights, group_gain, group_shift, split, small
    )


TILE = 128
QROWS = 256
KIND_ROWS = 8
FAR_LANE = 32
LOW_LANE = 40
PAD_LANE = 48
DOC_LANE = 56


def dot_last(left, right):
    return lax.dot_general(
        left, right, (((1,), (1,)), ((), ())), preferred_element_type=jnp.float32
    )


def dot_plain(left, right):
    return jnp.dot(left, right, preferred_element_type=jnp.float32)


def bucket_vector(tables_ref, table, head, relative):
    buckets = bucket_of(relative)
    values = jnp.zeros(relative.shape, jnp.float32)
    for bucket in range(NBUCKET):
        values = jnp.where(buckets == bucket, tables_ref[table, bucket, head], values)
    return values


def signed_lanes(width):
    lane = lax.broadcasted_iota(jnp.int32, (8, width), 1)
    return jnp.where(lane < width // 2, lane, lane - width)


def rolled(row, height):
    return pltpu.roll(
        jnp.broadcast_to(row[0:1], (height, row.shape[1])), 0, 1, stride=1, stride_axis=0
    )


def token_lanes(info_ref, one_hot_x, query_base, key_base, pad_tiles):
    tokens = info_ref.shape[0]
    lane = lax.broadcasted_iota(jnp.int32, (TILE, 128), 1)
    row = lax.broadcasted_iota(jnp.int32, (TILE, 128), 0)
    for tile in range(tokens // TILE):
        at = slice(tile * TILE, (tile + 1) * TILE)
        left = info_ref[at, 0:1]
        top = info_ref[at, 1:2]
        doc = info_ref[at, 2:3]
        hidden = jnp.where(info_ref[at, 3:4] > 0, 0.0, masked_score)
        one_hot_x[at, :] = (lane == left).astype(jnp.float32).astype(jnp.bfloat16)
        shared = jnp.where((lane == top) | (lane == DOC_LANE + doc), 1.0, 0.0)
        query_base[at, :] = jnp.where(lane == FAR_LANE + tile, 1.0, shared).astype(jnp.bfloat16)
        key = jnp.where((lane == FAR_LANE + tile) | (lane == LOW_LANE + tile), 1.0, shared)
        key = jnp.where(lane == PAD_LANE + tile, hidden, key)
        key_base[1, at, :] = key.astype(jnp.bfloat16)
        key_base[0, at, :] = pltpu.roll(key, 64, 1).astype(jnp.bfloat16)
        pad_tiles[at, :] = jnp.where(lane == row, 0.0, jnp.broadcast_to(hidden, (TILE, 128)))


def head_matrices(tables_ref, head, side):
    first = bucket_vector(tables_ref, 1, head, signed_lanes(256))
    across = rolled(first, 128)[:, :128].astype(jnp.bfloat16)
    second = rolled(bucket_vector(tables_ref, 2, head, signed_lanes(128)), 128)
    row = lax.broadcasted_iota(jnp.int32, (128, 128), 0)
    lane = lax.broadcasted_iota(jnp.int32, (128, 128), 1)
    mixed = jnp.where((row < FAR_LANE) & (lane < FAR_LANE), second, 0.0)
    gap = lane % 8 - (row - FAR_LANE)
    before = jnp.full((128, 128), tables_ref[0, NBUCKET // 2 - 1, head], jnp.float32)
    after = jnp.full((128, 128), tables_ref[0, NBUCKET - 1, head], jnp.float32)
    far = jnp.where(gap <= -2, before, jnp.where(gap >= 2, after, 0.0))
    high = far.astype(jnp.bfloat16).astype(jnp.float32)
    of_tile = (row >= FAR_LANE) & (row < LOW_LANE)
    mixed = jnp.where(of_tile & (lane >= FAR_LANE) & (lane < LOW_LANE), high, mixed)
    mixed = jnp.where(of_tile & (lane >= LOW_LANE) & (lane < PAD_LANE), far - high, mixed)
    mixed = jnp.where(
        of_tile & (lane >= PAD_LANE) & (lane < DOC_LANE) & (gap != 0), 1.0, mixed
    )
    docs = (row >= DOC_LANE) & (row < 64) & (lane >= DOC_LANE) & (lane < 64)
    mixed = jnp.where(docs & (row != lane), masked_score, mixed)
    if side == 0:
        mixed = pltpu.roll(mixed, 64, 1)
    near = rolled(bucket_vector(tables_ref, 0, head, -signed_lanes(512)), 128)
    tiles = {0: near[:, :128], 1: near[:, 384:], -1: near[:, 128:256]}
    return across, mixed.astype(jnp.bfloat16), tiles


def own_half(side, own, other):
    lane = lax.broadcasted_iota(jnp.int32, own.shape, 1)
    return jnp.where((lane < 64) if side == 0 else (lane >= 64), own, other)


def widen_operands(
    side, head, tables_ref, query_ref, key_ref, one_hot_x, query_base, key_base, query_wide, key_wide, near
):
    across, mixed, tiles = head_matrices(tables_ref, head, side)
    for gap in (-1, 0, 1):
        near[side, gap + 1] = tiles[gap]
    scaled = (query_ref[...].astype(jnp.float32) * HDIM ** (-0.5)).astype(jnp.bfloat16)
    query_wide[side, :, :128] = own_half(
        side, scaled, dot_plain(query_base[...], mixed).astype(jnp.bfloat16)
    )
    query_wide[side, :, 128:] = dot_plain(one_hot_x[...], across).astype(jnp.bfloat16)
    key_wide[side, :, :128] = own_half(side, key_ref[...], key_base[side])
    key_wide[side, :, 128:] = one_hot_x[...]


def near_scores(scores, side, block, tile, near, pad_tiles):
    halves = []
    for half in range(QROWS // TILE):
        part = scores[:, half * TILE : (half + 1) * TILE]
        gap = tile - (block * (QROWS // TILE) + half)
        if abs(gap) <= 1:
            part = part + near[side, gap + 1]
        if gap == 0:
            part = part + pad_tiles[tile * TILE : (tile + 1) * TILE, :]
        halves.append(part)
    return jnp.concatenate(halves, axis=1)


def attention_forward_kernel(
    tables_ref,
    info_ref,
    query_ref,
    key_ref,
    value_ref,
    context_ref,
    exact_ref,
    lse_ref,
    one_hot_x,
    query_base,
    key_base,
    pad_tiles,
    query_wide,
    key_wide,
    near,
    scores,
    weights,
):
    pair = pl.program_id(0)
    tokens = query_ref.shape[0]

    @pl.when(pair == 0)
    def _():
        token_lanes(info_ref, one_hot_x, query_base, key_base, pad_tiles)

    for side in range(2):
        widen_operands(
            side, pair * 2 + side, tables_ref, query_ref, key_ref, one_hot_x, query_base, key_base,
            query_wide, key_wide, near,
        )
    values = value_ref[...].T
    for block in range(tokens // QROWS):
        columns = slice(block * QROWS, (block + 1) * QROWS)
        contexts = []
        for side in range(2):
            scores[side] = dot_last(key_wide[side], query_wide[side, columns, :])
            top = jnp.full((8, QROWS), masked_score, jnp.float32)
            for tile in range(tokens // TILE):
                at = slice(tile * TILE, (tile + 1) * TILE)
                part = scores[side, at, :]
                if any(abs(tile - 2 * block - half) <= 1 for half in range(2)):
                    part = near_scores(part, side, block, tile, near, pad_tiles)
                    scores[side, at, :] = part
                top = jnp.maximum(top, jnp.max(part.reshape(TILE // 8, 8, QROWS), axis=0))
            top = jnp.max(top, axis=0, keepdims=True)
            total = jnp.zeros((8, QROWS), jnp.float32)
            for tile in range(tokens // TILE):
                at = slice(tile * TILE, (tile + 1) * TILE)
                part = jnp.exp(scores[side, at, :] - top)
                total = total + jnp.sum(part.reshape(TILE // 8, 8, QROWS), axis=0)
                weights[side, at, :] = part.astype(jnp.bfloat16)
            total = jnp.sum(total, axis=0, keepdims=True)
            context = dot_plain(values[side * 64 : (side + 1) * 64, :], weights[side])
            contexts.append(context * (1.0 / total))
            lse_ref[0, side : side + 1, columns] = top + jnp.log(total)
        context = jnp.concatenate(contexts, axis=0)
        exact_ref[:, columns] = context
        context_ref[columns, :] = context.T.astype(jnp.bfloat16)


def attention_backward_kernel(
    tables_ref,
    info_ref,
    query_ref,
    key_ref,
    value_ref,
    grad_ref,
    exact_ref,
    lse_ref,
    grad_query_ref,
    grad_key_ref,
    grad_value_ref,
    diagonal_ref,
    one_hot_x,
    query_base,
    key_base,
    pad_tiles,
    reverse,
    query_wide,
    key_wide,
    near,
    scores,
    grad_probs,
    probs_low,
    grad_low,
    key_turned,
    grad_near,
    grad_blocks,
    grad_key,
    grad_value,
):
    pair = pl.program_id(0)
    tokens = query_ref.shape[0]

    @pl.when(pair == 0)
    def _():
        token_lanes(info_ref, one_hot_x, query_base, key_base, pad_tiles)
        lane = lax.broadcasted_iota(jnp.int32, (TILE, 128), 1)
        for tile in range(tokens // TILE):
            at = slice(tile * TILE, (tile + 1) * TILE)
            left = info_ref[at, 0:1]
            top = info_ref[at, 1:2]
            reverse[at, :128] = jnp.where(lane == 127 - left, 1.0, 0.0).astype(jnp.bfloat16)
            reverse[at, 128:] = jnp.where(
                (lane == 31 - top) | (lane == FAR_LANE + tile), 1.0, 0.0
            ).astype(jnp.bfloat16)

    for side in range(2):
        widen_operands(
            side, pair * 2 + side, tables_ref, query_ref, key_ref, one_hot_x, query_base, key_base,
            query_wide, key_wide, near,
        )
        key_turned[side] = key_wide[side].T
    grad_near[...] = jnp.zeros_like(grad_near)
    grad_blocks[...] = jnp.zeros_like(grad_blocks)
    values = [
        own_half(side, value_ref[...], jnp.zeros(value_ref.shape, jnp.bfloat16)) for side in range(2)
    ]
    for block in range(tokens // QROWS):
        columns = slice(block * QROWS, (block + 1) * QROWS)
        grad_block = grad_ref[columns, :]
        product = grad_block.astype(jnp.float32).T * exact_ref[:, columns]
        scaled = (query_ref[columns, :].astype(jnp.float32) * HDIM ** (-0.5)).astype(jnp.bfloat16)
        turned = []
        key_terms = []
        value_terms = []
        for side in range(2):
            delta = jnp.sum(product[side * 64 : (side + 1) * 64, :], axis=0, keepdims=True)
            lse = lse_ref[0, side : side + 1, columns]
            scores[side] = dot_last(key_wide[side], query_wide[side, columns, :])
            grad_probs[side] = dot_last(values[side], grad_block)
            for tile in range(tokens // TILE):
                at = slice(tile * TILE, (tile + 1) * TILE)
                part = near_scores(scores[side, at, :], side, block, tile, near, pad_tiles)
                probs = jnp.exp(part - lse)
                grad_part = probs * (grad_probs[side, at, :] - delta)
                probs_low[side, at, :] = probs.astype(jnp.bfloat16)
                grad_low[side, at, :] = grad_part.astype(jnp.bfloat16)
                for half in range(QROWS // TILE):
                    gap = tile - (block * (QROWS // TILE) + half)
                    if abs(gap) <= 1:
                        grad_near[side, gap + 1] += grad_part[:, half * TILE : (half + 1) * TILE]
            value_terms.append(dot_plain(probs_low[side], grad_block))
            key_terms.append(dot_plain(grad_low[side], scaled))
            sums = dot_plain(key_turned[side], grad_low[side])
            turned.append(sums[side * 64 : (side + 1) * 64, :])
            grad_blocks[side] += dot_plain(sums.astype(jnp.bfloat16), reverse[columns, :])
        grad_query_ref[columns, :] = (
            (jnp.concatenate(turned, axis=0) * HDIM ** (-0.5)).T.astype(jnp.bfloat16)
        )
        key_term = own_half(0, key_terms[0], key_terms[1])
        value_term = own_half(0, value_terms[0], value_terms[1])
        if block == 0:
            grad_key[...] = key_term
            grad_value[...] = value_term
        else:
            grad_key[...] += key_term
            grad_value[...] += value_term
    grad_key_ref[...] = grad_key[...].astype(jnp.bfloat16)
    grad_value_ref[...] = grad_value[...].astype(jnp.bfloat16)
    row = lax.broadcasted_iota(jnp.int32, (128, 128), 0)
    lane = lax.broadcasted_iota(jnp.int32, (128, 128), 1)
    flip = jnp.where(row + lane == 127, 1.0, 0.0).astype(jnp.bfloat16)
    blank = jnp.zeros((128, 128), jnp.float32)

    def diagonal_sums(values):
        spread = jnp.concatenate([values, blank], axis=1)
        return jnp.sum(
            pltpu.roll(spread, 0, 1, stride=1, stride_axis=0), axis=0, keepdims=True
        )

    for side in range(2):
        misc = 64 * (1 - side)
        sums = [diagonal_sums(grad_blocks[side, 128:, :128])]
        below = grad_blocks[side, misc : misc + 64, 128:]
        small_row = lax.broadcasted_iota(jnp.int32, (64, 128), 0)
        small_lane = lax.broadcasted_iota(jnp.int32, (64, 128), 1)
        upright = jnp.where((small_row < FAR_LANE) & (small_lane < FAR_LANE), below, 0.0)
        sums.append(diagonal_sums(jnp.concatenate([upright, jnp.zeros((64, 128), jnp.float32)], axis=0)))
        for gap in range(3):
            tile = grad_near[side, gap]
            high = tile.astype(jnp.bfloat16)
            rest = (tile - high.astype(jnp.float32)).astype(jnp.bfloat16)
            sums.append(diagonal_sums(dot_plain(high, flip) + dot_plain(rest, flip)))
        gap = (small_row - FAR_LANE) - (small_lane - FAR_LANE)
        inside = (
            (small_row >= FAR_LANE)
            & (small_row < LOW_LANE)
            & (small_lane >= FAR_LANE)
            & (small_lane < LOW_LANE)
        )
        for chosen in (gap <= -2, gap >= 2):
            far = jnp.sum(jnp.where(inside & chosen, below, 0.0), axis=0, keepdims=True)
            sums.append(jnp.concatenate([far, blank[0:1]], axis=1))
        sums.append(jnp.zeros((1, 256), jnp.float32))
        diagonal_ref[side] = jnp.concatenate(sums, axis=0)


def attention_scratch(tokens):
    return [
        pltpu.VMEM((tokens, 128), jnp.bfloat16),
        pltpu.VMEM((tokens, 128), jnp.bfloat16),
        pltpu.VMEM((2, tokens, 128), jnp.bfloat16),
        pltpu.VMEM((tokens, 128), jnp.float32),
    ], [
        pltpu.VMEM((2, tokens, 256), jnp.bfloat16),
        pltpu.VMEM((2, tokens, 256), jnp.bfloat16),
        pltpu.VMEM((2, 3, TILE, TILE), jnp.float32),
        pltpu.VMEM((2, tokens, QROWS), jnp.float32),
    ]


def attention_forward(tables, info, heads):
    tokens, width = heads.shape[0], heads.shape[1] // 3
    pairs = width // 128
    own = pl.BlockSpec((tokens, 128), lambda pair: (0, pair))
    fixed, moving = attention_scratch(tokens)
    return pl.pallas_call(
        attention_forward_kernel,
        grid=(pairs,),
        out_shape=(
            jax.ShapeDtypeStruct((tokens, width), jnp.bfloat16),
            jax.ShapeDtypeStruct((width, tokens), jnp.float32),
            jax.ShapeDtypeStruct((pairs, 2, tokens), jnp.float32),
        ),
        in_specs=[
            pl.BlockSpec(memory_space=pltpu.SMEM),
            pl.BlockSpec((tokens, 8), lambda pair: (0, 0)),
            own,
            pl.BlockSpec((tokens, 128), lambda pair: (0, pairs + pair)),
            pl.BlockSpec((tokens, 128), lambda pair: (0, 2 * pairs + pair)),
        ],
        out_specs=(
            own,
            pl.BlockSpec((128, tokens), lambda pair: (pair, 0)),
            pl.BlockSpec((1, 2, tokens), lambda pair: (pair, 0, 0)),
        ),
        scratch_shapes=fixed
        + moving
        + [
            pltpu.VMEM((2, tokens, QROWS), jnp.bfloat16),
        ],
        compiler_params=pltpu.CompilerParams(
            dimension_semantics=("arbitrary",), vmem_limit_bytes=48 * 2**20
        ),
        cost_estimate=pl.CostEstimate(
            flops=23 * 10**9, bytes_accessed=2 * 10**7, transcendentals=0
        ),
        name="attention_forward",
    )(tables, info, heads, heads, heads)


def attention_backward(tables, info, heads, grad_context, exact, lse):
    tokens, width = grad_context.shape
    pairs = width // 128
    own = pl.BlockSpec((tokens, 128), lambda pair: (0, pair))
    fixed, moving = attention_scratch(tokens)
    low = jax.ShapeDtypeStruct((tokens, width), jnp.bfloat16)
    return pl.pallas_call(
        attention_backward_kernel,
        grid=(pairs,),
        out_shape=(low, low, low, jax.ShapeDtypeStruct((2 * pairs, 8, 256), jnp.float32)),
        in_specs=[
            pl.BlockSpec(memory_space=pltpu.SMEM),
            pl.BlockSpec((tokens, 8), lambda pair: (0, 0)),
            own,
            pl.BlockSpec((tokens, 128), lambda pair: (0, pairs + pair)),
            pl.BlockSpec((tokens, 128), lambda pair: (0, 2 * pairs + pair)),
            own,
            pl.BlockSpec((128, tokens), lambda pair: (pair, 0)),
            pl.BlockSpec((1, 2, tokens), lambda pair: (pair, 0, 0)),
        ],
        out_specs=(own, own, own, pl.BlockSpec((2, 8, 256), lambda pair: (pair, 0, 0))),
        scratch_shapes=fixed
        + [pltpu.VMEM((tokens, 256), jnp.bfloat16)]
        + moving
        + [
            pltpu.VMEM((2, tokens, QROWS), jnp.float32),
            pltpu.VMEM((2, tokens, QROWS), jnp.bfloat16),
            pltpu.VMEM((2, tokens, QROWS), jnp.bfloat16),
            pltpu.VMEM((2, 256, tokens), jnp.bfloat16),
            pltpu.VMEM((2, 3, TILE, TILE), jnp.float32),
            pltpu.VMEM((2, 256, 256), jnp.float32),
            pltpu.VMEM((tokens, 128), jnp.float32),
            pltpu.VMEM((tokens, 128), jnp.float32),
        ],
        compiler_params=pltpu.CompilerParams(
            dimension_semantics=("arbitrary",), vmem_limit_bytes=48 * 2**20
        ),
        cost_estimate=pl.CostEstimate(
            flops=30 * 10**9, bytes_accessed=2 * 10**7, transcendentals=0
        ),
        name="attention_backward",
    )(tables, info, heads, heads, heads, grad_context, exact, lse)


def bucket_grads(diagonals):
    lane = jnp.arange(256, dtype=jnp.int32)
    wide_buckets = [
        bucket_of(lane - 127),
        bucket_of(lane - 31),
        bucket_of(lane - 127 - TILE),
        bucket_of(lane - 127),
        bucket_of(lane - 127 + TILE),
        jnp.full((256,), NBUCKET // 2 - 1, jnp.int32),
        jnp.full((256,), NBUCKET - 1, jnp.int32),
    ]
    table_of = (1, 2, 0, 0, 0, 0, 0)
    slots = jnp.stack([bucket + NBUCKET * table for bucket, table in zip(wide_buckets, table_of)])
    chosen = (slots[..., None] == jnp.arange(3 * NBUCKET, dtype=jnp.int32)).astype(jnp.float32)
    sums = jnp.einsum("hrc,rcb->bh", diagonals[:, :7], chosen, precision=highest)
    return sums.reshape(3, NBUCKET, -1)


ROWS = 256


def greet_partner():
    pl.semaphore_signal(
        pltpu.get_barrier_semaphore(),
        inc=1,
        device_id=(lax.axis_index("dp"), 1 - lax.axis_index("tensor")),
        device_id_type=MESH,
    )


def partner_copy(source, target, send_sem, recv_sem):
    return pltpu.make_async_remote_copy(
        src_ref=source,
        dst_ref=target,
        send_sem=send_sem,
        recv_sem=recv_sem,
        device_id=(lax.axis_index("dp"), 1 - lax.axis_index("tensor")),
        device_id_type=MESH,
    )


def dot_rows(left, right):
    return lax.dot_general(
        left, right, (((0,), (0,)), ((), ())), preferred_element_type=jnp.float32
    )


def inverse_rms(values):
    return lax.rsqrt(jnp.mean(values * values, axis=1, keepdims=True) + norm_eps)


def box_kernel(
    feature_ref,
    info_ref,
    embedded_ref,
    roi_ref,
    norm_ref,
    query_proj_ref,
    key_proj_ref,
    value_proj_ref,
    pooled_ref,
    stream_ref,
    input_ref,
    heads_ref,
    features,
    mask,
    part,
    received,
    projections,
    send_sem,
    recv_sem,
):
    greet_partner()
    tokens = info_ref.shape[0]
    pixels = feature_ref.shape[0]
    tile_rows = pixels // 128
    first_row = lax.axis_index("tensor") * tile_rows
    features[...] = split_two(feature_ref[...])
    lane = lax.broadcasted_iota(jnp.int32, (ROWS, 128), 1)
    copies = []
    for block in range(tokens // ROWS):
        at = slice(block * ROWS, (block + 1) * ROWS)
        column = (lane >= info_ref[at, 0:1]) & (lane < info_ref[at, 4:5])
        column = jnp.where(column, 1.0, 0.0)
        top = jnp.broadcast_to(info_ref[at, 1:2], (ROWS, 128)) - first_row
        bottom = jnp.broadcast_to(info_ref[at, 5:6], (ROWS, 128)) - first_row
        for row in range(tile_rows):
            inside = jnp.where((top <= row) & (bottom > row), column, 0.0)
            mask[block % 2, :, row * 128 : (row + 1) * 128] = inside.astype(jnp.bfloat16)
        sums = dot_plain(mask[block % 2], features[...])
        part[at, :] = sums[:, :128] + sums[:, 128:]
        if block == 0:
            pl.semaphore_wait(pltpu.get_barrier_semaphore(), 1)
        copy = partner_copy(
            part.at[pl.ds(block * ROWS, ROWS)],
            received.at[pl.ds(block * ROWS, ROWS)],
            send_sem.at[block],
            recv_sem.at[block],
        )
        copy.start()
        copies.append(copy)
    width = query_proj_ref.shape[1]
    for index, ref in enumerate((query_proj_ref, key_proj_ref, value_proj_ref)):
        projections[:, index * width : (index + 1) * width] = ref[...]
    for block in range(tokens // ROWS):
        at = slice(block * ROWS, (block + 1) * ROWS)
        copies[block].wait_recv()
        area = (info_ref[at, 5:6] - info_ref[at, 1:2]) * (info_ref[at, 4:5] - info_ref[at, 0:1])
        pooled = ((part[at, :] + received[at, :]) / area.astype(jnp.float32)).astype(jnp.bfloat16)
        pooled_ref[at, :] = pooled
        stream = embedded_ref[at, :].astype(jnp.float32) + dot_plain(pooled, roi_ref[...])
        stream_ref[at, :] = stream
        attn_in = (stream * inverse_rms(stream) * norm_ref[...]).astype(jnp.bfloat16)
        input_ref[at, :] = attn_in
        heads_ref[at, :] = dot_plain(attn_in, projections[...]).astype(jnp.bfloat16)
    for copy in copies:
        copy.wait_send()


def box_forward(
    feature_map, info, embeddings, roi_proj, attn_norm, query_proj, key_proj, value_proj
):
    tokens, width = embeddings.shape
    local = query_proj.shape[1]
    blocks = tokens // ROWS
    whole = pl.BlockSpec(memory_space=pltpu.VMEM)
    return pl.pallas_call(
        box_kernel,
        out_shape=(
            jax.ShapeDtypeStruct((tokens, 128), jnp.bfloat16),
            jax.ShapeDtypeStruct((tokens, width), jnp.float32),
            jax.ShapeDtypeStruct((tokens, width), jnp.bfloat16),
            jax.ShapeDtypeStruct((tokens, 3 * local), jnp.bfloat16),
        ),
        in_specs=[whole] * 8,
        out_specs=(whole,) * 4,
        scratch_shapes=[
            pltpu.VMEM((feature_map.shape[0], 256), jnp.bfloat16),
            pltpu.VMEM((2, ROWS, feature_map.shape[0]), jnp.bfloat16),
            pltpu.VMEM((tokens, 128), jnp.float32),
            pltpu.VMEM((tokens, 128), jnp.float32),
            pltpu.VMEM((width, 3 * local), jnp.bfloat16),
            pltpu.SemaphoreType.DMA((blocks,)),
            pltpu.SemaphoreType.DMA((blocks,)),
        ],
        compiler_params=pltpu.CompilerParams(
            collective_id=2, has_side_effects=True, vmem_limit_bytes=48 * 2**20
        ),
        cost_estimate=pl.CostEstimate(
            flops=12 * 10**9, bytes_accessed=2 * 10**7, transcendentals=0
        ),
        name="box_forward",
    )(
        feature_map,
        info,
        embeddings,
        roi_proj,
        attn_norm.reshape(1, -1),
        query_proj,
        key_proj,
        value_proj,
    )


def middle_kernel(
    context_ref,
    stream_hbm,
    cotangent_hbm,
    output_ref,
    norm_ref,
    up_hbm,
    down_hbm,
    layer_hbm,
    grad_middle_hbm,
    grad_context_hbm,
    grad_up_hbm,
    grad_down_hbm,
    grad_output_ref,
    grad_norm_ref,
    middle,
    cotangent,
    up,
    down,
    part,
    other,
    part_out,
    other_out,
    other_grad,
    ffn_in,
    hidden,
    grad_pre,
    staged,
    grad_low,
    layer_low,
    grad_context,
    load_sem,
    store_sem,
    grad_sem,
    send_sem,
    recv_sem,
):
    greet_partner()
    tokens, width = stream_hbm.shape
    units = up_hbm.shape[1]
    blocks = tokens // ROWS
    loads = [
        pltpu.make_async_copy(source, target, load_sem.at[index])
        for index, (source, target) in enumerate(
            [(cotangent_hbm, cotangent), (down_hbm, down), (stream_hbm, middle), (up_hbm, up)]
        )
    ]
    for load in loads:
        load.start()
    attn_copies = []
    for block in range(blocks):
        at = slice(block * ROWS, (block + 1) * ROWS)
        part[at, :] = dot_plain(context_ref[at, :], output_ref[...])
        if block == 0:
            pl.semaphore_wait(pltpu.get_barrier_semaphore(), 1)
        copy = partner_copy(
            part.at[pl.ds(block * ROWS, ROWS)],
            other.at[pl.ds(block * ROWS, ROWS)],
            send_sem.at[0, block],
            recv_sem.at[0, block],
        )
        copy.start()
        attn_copies.append(copy)
    for load in loads:
        load.wait()
    out_copies = []
    grad_copies = []
    for block in range(blocks):
        at = slice(block * ROWS, (block + 1) * ROWS)
        grad_hidden = dot_last(cotangent[at, :], down[...])
        attn_copies[block].wait()
        values = middle[at, :] + (part[at, :] + other[at, :])
        middle[at, :] = values
        inner = (values * inverse_rms(values) * norm_ref[...]).astype(jnp.bfloat16)
        ffn_in[at, :] = inner
        pre_act = dot_plain(inner, up[...])
        below = 0.5 * (1.0 + lax.erf(pre_act * (0.5**0.5)))
        density = jnp.exp(-0.5 * (pre_act * pre_act)) * 0.3989422804014327
        hidden[at, :] = (pre_act * below).astype(jnp.bfloat16)
        grad_pre[at, :] = (grad_hidden * (below + pre_act * density)).astype(jnp.bfloat16)
        part[at, :] = dot_last(grad_pre[at, :], up[...])
        copy = partner_copy(
            part.at[pl.ds(block * ROWS, ROWS)],
            other_grad.at[pl.ds(block * ROWS, ROWS)],
            send_sem.at[1, block],
            recv_sem.at[1, block],
        )
        copy.start()
        grad_copies.append(copy)
        part_out[at, :] = dot_plain(hidden[at, :], down[...])
        copy = partner_copy(
            part_out.at[pl.ds(block * ROWS, ROWS)],
            other_out.at[pl.ds(block * ROWS, ROWS)],
            send_sem.at[2, block],
            recv_sem.at[2, block],
        )
        copy.start()
        out_copies.append(copy)
    half = width // 2
    stores = []
    for index in range(4):
        rows = slice((index % 2) * half, (index % 2 + 1) * half)
        if index >= 2:
            stores[index - 2].wait()
        if index < 2:
            staged[index % 2] = dot_rows(ffn_in[:, rows], grad_pre[...])
            target = grad_up_hbm
        else:
            staged[index % 2] = dot_rows(cotangent[:, rows], hidden[...])
            target = grad_down_hbm
        store = pltpu.make_async_copy(
            staged.at[index % 2], target.at[pl.ds((index % 2) * half, half)], grad_sem.at[index]
        )
        store.start()
        stores.append(store)
    norm_total = jnp.zeros((8, width), jnp.float32)
    for block in range(blocks):
        at = slice(block * ROWS, (block + 1) * ROWS)
        values = middle[at, :]
        inverse = inverse_rms(values)
        hat = values * inverse
        grad_copies[block].wait()
        grad_inner = part[at, :] + other_grad[at, :]
        norm_total = norm_total + jnp.sum((grad_inner * hat).reshape(ROWS // 8, 8, width), axis=0)
        scaled = grad_inner * norm_ref[...]
        back = inverse * (scaled - hat * jnp.mean(scaled * hat, axis=1, keepdims=True))
        grad_values = cotangent[at, :].astype(jnp.float32) + back
        out_copies[block].wait()
        layer_low[at, :] = (values + (part_out[at, :] + other_out[at, :])).astype(jnp.bfloat16)
        middle[at, :] = grad_values
        low = grad_values.astype(jnp.bfloat16)
        grad_low[at, :] = low
        grad_context[at, :] = dot_last(low, output_ref[...]).astype(jnp.bfloat16)
        for index, (source, target) in enumerate(
            [
                (layer_low, layer_hbm),
                (middle, grad_middle_hbm),
                (grad_context, grad_context_hbm),
            ]
        ):
            rows = pl.ds(block * ROWS, ROWS)
            store = pltpu.make_async_copy(
                source.at[rows], target.at[rows], store_sem.at[index, block]
            )
            store.start()
            stores.append(store)
    grad_norm_ref[...] = jnp.sum(norm_total, axis=0, keepdims=True)
    grad_output_ref[...] = dot_rows(grad_low[...], context_ref[...])
    for store in stores[2:]:
        store.wait()


def middle_layer(context, stream, cotangent, output_proj, ffn_norm, up_proj, down_proj):
    tokens, width = stream.shape
    units = up_proj.shape[1]
    local = context.shape[1]
    blocks = tokens // ROWS
    whole = pl.BlockSpec(memory_space=pltpu.VMEM)
    far = pl.BlockSpec(memory_space=pl.ANY)
    wide_sum = pltpu.VMEM((tokens, width), jnp.float32)
    wide_low = pltpu.VMEM((tokens, width), jnp.bfloat16)
    unit_low = pltpu.VMEM((tokens, units), jnp.bfloat16)
    return pl.pallas_call(
        middle_kernel,
        out_shape=(
            jax.ShapeDtypeStruct((tokens, width), jnp.bfloat16),
            jax.ShapeDtypeStruct((tokens, width), jnp.float32),
            jax.ShapeDtypeStruct((tokens, local), jnp.bfloat16),
            jax.ShapeDtypeStruct((width, units), jnp.float32),
            jax.ShapeDtypeStruct((width, units), jnp.float32),
            jax.ShapeDtypeStruct((width, local), jnp.float32),
            jax.ShapeDtypeStruct((1, width), jnp.float32),
        ),
        in_specs=[whole, far, far, whole, whole, far, far],
        out_specs=(far, far, far, far, far, whole, whole),
        scratch_shapes=[
            wide_sum,
            wide_low,
            pltpu.VMEM((width, units), jnp.bfloat16),
            pltpu.VMEM((units, width), jnp.bfloat16),
            wide_sum,
            wide_sum,
            wide_sum,
            wide_sum,
            wide_sum,
            wide_low,
            unit_low,
            unit_low,
            pltpu.VMEM((2, width // 2, units), jnp.float32),
            wide_low,
            wide_low,
            pltpu.VMEM((tokens, local), jnp.bfloat16),
            pltpu.SemaphoreType.DMA((4,)),
            pltpu.SemaphoreType.DMA((3, blocks)),
            pltpu.SemaphoreType.DMA((4,)),
            pltpu.SemaphoreType.DMA((3, blocks)),
            pltpu.SemaphoreType.DMA((3, blocks)),
        ],
        compiler_params=pltpu.CompilerParams(
            collective_id=3, has_side_effects=True, vmem_limit_bytes=60 * 2**20
        ),
        cost_estimate=pl.CostEstimate(
            flops=32 * 10**9, bytes_accessed=2 * 10**7, transcendentals=0
        ),
        name="middle_layer",
    )(context, stream, cotangent, output_proj, ffn_norm.reshape(1, -1), up_proj, down_proj)


def end_kernel(
    grad_query_ref,
    grad_key_ref,
    grad_value_ref,
    query_proj_ref,
    key_proj_ref,
    value_proj_ref,
    input_ref,
    stream_hbm,
    grad_middle_hbm,
    norm_ref,
    roi_ref,
    pooled_ref,
    info_ref,
    boxes_ref,
    grad_stream_hbm,
    grad_heads_hbm,
    grad_roi_ref,
    grad_map_ref,
    grad_norm_ref,
    grad_heads,
    projections,
    stream,
    grad_stream,
    part,
    other,
    weight_grad,
    grad_low,
    grad_box,
    load_sem,
    store_sem,
    grad_sem,
    send_sem,
    recv_sem,
):
    greet_partner()
    tokens, width = stream_hbm.shape
    local = grad_query_ref.shape[1]
    blocks = tokens // ROWS
    loads = [
        pltpu.make_async_copy(stream_hbm, stream, load_sem.at[0]),
        pltpu.make_async_copy(grad_middle_hbm, grad_stream, load_sem.at[1]),
    ]
    for load in loads:
        load.start()
    for index, (grad, proj) in enumerate(
        (
            (grad_query_ref, query_proj_ref),
            (grad_key_ref, key_proj_ref),
            (grad_value_ref, value_proj_ref),
        )
    ):
        columns = slice(index * local, (index + 1) * local)
        grad_heads[:, columns] = grad[...]
        projections[:, columns] = proj[...]
    copies = []
    for block in range(blocks):
        at = slice(block * ROWS, (block + 1) * ROWS)
        part[at, :] = dot_last(grad_heads[at, :], projections[...])
        if block == 0:
            pl.semaphore_wait(pltpu.get_barrier_semaphore(), 1)
        copy = partner_copy(
            part.at[pl.ds(block * ROWS, ROWS)],
            other.at[pl.ds(block * ROWS, ROWS)],
            send_sem.at[block],
            recv_sem.at[block],
        )
        copy.start()
        copies.append(copy)
    weight_grad[...] = dot_rows(input_ref[...], grad_heads[...])
    weight_store = pltpu.make_async_copy(weight_grad, grad_heads_hbm, grad_sem)
    weight_store.start()
    for load in loads:
        load.wait()
    stores = []
    norm_total = jnp.zeros((8, width), jnp.float32)
    for block in range(blocks):
        at = slice(block * ROWS, (block + 1) * ROWS)
        values = stream[at, :]
        inverse = inverse_rms(values)
        hat = values * inverse
        copies[block].wait()
        grad_inner = part[at, :] + other[at, :]
        norm_total = norm_total + jnp.sum((grad_inner * hat).reshape(ROWS // 8, 8, width), axis=0)
        scaled = grad_inner * norm_ref[...]
        back = inverse * (scaled - hat * jnp.mean(scaled * hat, axis=1, keepdims=True))
        grad_values = grad_stream[at, :] + back
        grad_stream[at, :] = grad_values
        rows = pl.ds(block * ROWS, ROWS)
        store = pltpu.make_async_copy(
            grad_stream.at[rows], grad_stream_hbm.at[rows], store_sem.at[block]
        )
        store.start()
        stores.append(store)
        low = grad_values.astype(jnp.bfloat16)
        grad_low[at, :] = low
        area = (info_ref[at, 5:6] - info_ref[at, 1:2]) * (info_ref[at, 4:5] - info_ref[at, 0:1])
        grad_box[at, :] = split_two(dot_last(low, roi_ref[...]) / area.astype(jnp.float32))
    grad_norm_ref[...] = jnp.sum(norm_total, axis=0, keepdims=True)
    tile_rows = grad_map_ref.shape[0] // 128
    first_row = lax.axis_index("tensor") * tile_rows
    column = lax.broadcasted_iota(jnp.int32, (128, tokens), 0)
    inside = jnp.where(
        (column >= boxes_ref[0:1, :]) & (column < boxes_ref[2:3, :]), 1.0, 0.0
    ).astype(jnp.bfloat16)
    top = boxes_ref[1:2, :] - first_row
    bottom = boxes_ref[3:4, :] - first_row
    for row in range(tile_rows):
        chosen = jnp.where((top <= row) & (bottom > row), 1.0, 0.0).astype(jnp.bfloat16)
        sums = dot_plain(inside * chosen, grad_box[...])
        grad_map_ref[row * 128 : (row + 1) * 128, :] = sums[:, :128] + sums[:, 128:]
    grad_roi_ref[...] = dot_rows(grad_low[...], pooled_ref[...])
    weight_store.wait()
    for store in stores:
        store.wait()


def end_layer(
    grad_heads,
    projections,
    attn_in,
    stream,
    grad_middle,
    attn_norm,
    roi_proj,
    pooled,
    info,
    boxes,
    pixels,
):
    tokens, width = stream.shape
    local = grad_heads[0].shape[1]
    blocks = tokens // ROWS
    whole = pl.BlockSpec(memory_space=pltpu.VMEM)
    far = pl.BlockSpec(memory_space=pl.ANY)
    wide_sum = pltpu.VMEM((tokens, width), jnp.float32)
    return pl.pallas_call(
        end_kernel,
        out_shape=(
            jax.ShapeDtypeStruct((tokens, width), jnp.float32),
            jax.ShapeDtypeStruct((width, 3 * local), jnp.float32),
            jax.ShapeDtypeStruct((width, 128), jnp.float32),
            jax.ShapeDtypeStruct((pixels, 128), jnp.float32),
            jax.ShapeDtypeStruct((1, width), jnp.float32),
        ),
        in_specs=[whole] * 7 + [far, far] + [whole] * 5,
        out_specs=(far, far, whole, whole, whole),
        scratch_shapes=[
            pltpu.VMEM((tokens, 3 * local), jnp.bfloat16),
            pltpu.VMEM((width, 3 * local), jnp.bfloat16),
            wide_sum,
            wide_sum,
            wide_sum,
            wide_sum,
            pltpu.VMEM((width, 3 * local), jnp.float32),
            pltpu.VMEM((tokens, width), jnp.bfloat16),
            pltpu.VMEM((tokens, 256), jnp.bfloat16),
            pltpu.SemaphoreType.DMA((2,)),
            pltpu.SemaphoreType.DMA((blocks,)),
            pltpu.SemaphoreType.DMA,
            pltpu.SemaphoreType.DMA((blocks,)),
            pltpu.SemaphoreType.DMA((blocks,)),
        ],
        compiler_params=pltpu.CompilerParams(
            collective_id=4, has_side_effects=True, vmem_limit_bytes=56 * 2**20
        ),
        cost_estimate=pl.CostEstimate(
            flops=15 * 10**9, bytes_accessed=2 * 10**7, transcendentals=0
        ),
        name="end_layer",
    )(
        *grad_heads,
        *projections,
        attn_in,
        stream,
        grad_middle,
        attn_norm.reshape(1, -1),
        roi_proj,
        pooled,
        info,
        boxes,
    )


def on_device(
    page_image,
    embeddings,
    cotangent,
    doc_ids,
    pad_mask,
    token_boxes,
    conv_first,
    conv_weights,
    group_gain,
    group_shift,
    roi_proj,
    attn_norm,
    query_proj,
    key_proj,
    value_proj,
    output_proj,
    bias_tables,
    ffn_norm,
    up_proj,
    down_proj,
):
    devices = lax.axis_size("dp") * lax.axis_size("tensor")
    feature_map, *records = stem_forward(
        page_image, conv_first, conv_weights, group_gain, group_shift, devices
    )
    left_edge, top_edge, right_edge, bottom_edge = token_boxes[:, 0]
    blank = jnp.zeros_like(left_edge)
    info = jnp.stack(
        [left_edge, top_edge, doc_ids[0], pad_mask[0], right_edge, bottom_edge, blank, blank],
        axis=1,
    )
    pooled, stream, attn_in, heads = box_forward(
        feature_map, info, embeddings, roi_proj, attn_norm, query_proj, key_proj, value_proj
    )
    context, exact, lse = attention_forward(bias_tables, info, heads)
    layer_out, grad_middle, grad_context, grad_up, grad_down, grad_output, grad_ffn_norm = (
        middle_layer(context, stream, cotangent, output_proj, ffn_norm, up_proj, down_proj)
    )
    *grad_heads, diagonals = attention_backward(
        bias_tables, info, heads, grad_context, exact, lse
    )
    grad_tables = bucket_grads(diagonals)
    grad_stream, grad_projections, grad_roi, grad_map, grad_attn_norm = end_layer(
        grad_heads,
        (query_proj, key_proj, value_proj),
        attn_in,
        stream,
        grad_middle,
        attn_norm,
        roi_proj,
        pooled,
        info,
        token_boxes[:, 0],
        feature_map.shape[0],
    )
    grad_attn = jnp.concatenate([grad_projections, grad_output], axis=1)
    rows_count = lax.axis_size("dp")
    width = grad_attn_norm.shape[1]
    own_rows = width // rows_count
    local_heads = grad_tables.shape[2]
    small = jnp.concatenate([grad_attn_norm[0], grad_ffn_norm[0], grad_tables.reshape(-1)])
    small = jnp.pad(small, (0, -small.shape[0] % 1024)).reshape(-1, 128)
    split = grad_roi.reshape(rows_count, 2, own_rows // 2, grad_roi.shape[1])
    grad_first, grad_convs, grad_gains, grad_offsets, own_roi, small = stem_backward(
        grad_map,
        page_image,
        records,
        conv_weights,
        group_gain,
        group_shift,
        split,
        small,
        devices,
    )
    small = small.reshape(-1)
    start = lax.axis_index("dp") * own_rows
    own_attn_norm = lax.dynamic_slice(small, (start,), (own_rows,))
    own_ffn_norm = lax.dynamic_slice(small, (width + start,), (own_rows,))
    own_tables = small[2 * width : 2 * width + grad_tables.size].reshape(3, NBUCKET, local_heads)
    own_up = lax.psum_scatter(grad_up, "dp", scatter_dimension=0, tiled=True)
    own_down = lax.psum_scatter(grad_down, "dp", scatter_dimension=0, tiled=True).T
    own_attn = lax.psum_scatter(grad_attn, "dp", scatter_dimension=0, tiled=True)
    part = query_proj.shape[1]
    return (
        layer_out,
        grad_stream,
        grad_first,
        grad_convs,
        grad_gains,
        grad_offsets,
        own_roi.reshape(own_rows, -1).T,
        own_attn_norm,
        own_attn[:, :part],
        own_attn[:, part : 2 * part],
        own_attn[:, 2 * part : 3 * part],
        own_attn[:, 3 * part :].T,
        own_tables,
        own_ffn_norm,
        own_up,
        own_down,
    )


def solution(mesh):
    placed = (
        P(None, ("dp", "tensor"), None),
        P("dp", None),
        P("dp", None),
        P("dp", None),
        P("dp", None),
        P(None, "dp", None),
        P(),
        P(),
        P(),
        P(),
        P(),
        P(),
        P(None, "tensor"),
        P(None, "tensor"),
        P(None, "tensor"),
        P("tensor", None),
        P(None, None, "tensor"),
        P(),
        P(None, "tensor"),
        P("tensor", None),
    )
    return jax.shard_map(
        on_device,
        mesh=mesh,
        in_specs=placed,
        out_specs=(
            P("dp", None),
            P("dp", None),
            P(),
            P(),
            P(),
            P(),
            P(None, "dp"),
            P("dp"),
            P("dp", "tensor"),
            P("dp", "tensor"),
            P("dp", "tensor"),
            P("tensor", "dp"),
            P(None, None, "tensor"),
            P("dp"),
            P("dp", "tensor"),
            P("tensor", "dp"),
        ),
        check_vma=False,
    )
```

```python
import functools

import jax
import jax.numpy as jnp
from jax import lax
from jax.experimental import pallas as pl
from jax.experimental.pallas import tpu as pltpu
from jax.sharding import PartitionSpec as P

HDIM = 64
NBUCKET = 32
GROUPS = 32


bucket_edges = (12, 16, 23, 32, 46, 64, 91)
norm_eps = 1e-06
group_eps = 1e-05
masked_score = -1e30
highest = lax.Precision.HIGHEST


def bucket_of(relative):
    magnitude = jnp.abs(relative)
    coarse = jnp.full(relative.shape, 8, jnp.int32)
    for edge in bucket_edges:
        coarse = coarse + (magnitude >= edge).astype(jnp.int32)
    return jnp.where(magnitude < 8, magnitude, coarse) + jnp.where(relative > 0, 16, 0).astype(
        jnp.int32
    )


MESH = pl.DeviceIdType.MESH
LAYERS = 9
PIX_CHUNK = 256


def level_of(layer):
    return layer if layer <= 4 else 8 - layer


def stem_rows(pixels):
    return [pixels >> (2 * level_of(layer)) for layer in range(LAYERS)]


def row_starts(rows):
    starts = [0]
    for count in rows:
        starts.append(starts[-1] + count)
    return starts


def split_two(values):
    high = values.astype(jnp.bfloat16)
    low = (values - high.astype(jnp.float32)).astype(jnp.bfloat16)
    return jnp.concatenate([high, low], axis=1)


def group_sum(values):
    lane = lax.broadcasted_iota(jnp.int32, values.shape, 1)
    pairs = values + jnp.where(
        lane % 2 == 0, pltpu.roll(values, 127, 1), pltpu.roll(values, 1, 1)
    )
    return pairs + jnp.where(
        (lane // 2) % 2 == 0, pltpu.roll(pairs, 126, 1), pltpu.roll(pairs, 2, 1)
    )


def wide(row):
    return jnp.broadcast_to(row, (8, row.shape[1]))


def my_index():
    return lax.axis_index("dp") * 2 + lax.axis_index("tensor")


def greet_all(count):
    barrier = pltpu.get_barrier_semaphore()
    me = my_index()

    def greet(step, carry):
        other = lax.rem(me + step, count)
        pl.semaphore_signal(
            barrier, inc=1, device_id=(other // 2, lax.rem(other, 2)), device_id_type=MESH
        )
        return carry

    lax.fori_loop(1, count, greet, 0)


def greeted(count):
    pl.semaphore_wait(pltpu.get_barrier_semaphore(), count - 1)


def send_all(count, source, target, send_sem, recv_sem):
    me = my_index()

    def send(step, carry):
        other = lax.rem(me + step, count)
        pltpu.make_async_remote_copy(
            src_ref=source,
            dst_ref=target,
            send_sem=send_sem,
            recv_sem=recv_sem,
            device_id=(other // 2, lax.rem(other, 2)),
            device_id_type=MESH,
        ).start()
        return carry

    lax.fori_loop(1, count, send, 0, unroll=count <= 32)


def wait_all(count, slots, sem):
    part = slots.at[pl.ds(0, count - 1)]
    pltpu.make_async_copy(part, part, sem).wait()


def natural_places(tile_rows, columns):
    spacing = columns // 8
    places = []
    for row in range(tile_rows):
        for col in range(spacing):
            place = 0
            for bit in range(4):
                place = place * 4 + ((row >> bit) & 1) * 2 + ((col >> bit) & 1)
            places.append((row * columns + col, place * 8))
    return places


SCATTER_COPIES = 5


def place_of(row):
    return row // 4, lax.rem(row // 2, 2), lax.rem(row, 2)


def start_remote(source, target, send_sem, recv_sem, row):
    copy = pltpu.make_async_remote_copy(
        src_ref=source,
        dst_ref=target,
        send_sem=send_sem,
        recv_sem=recv_sem,
        device_id=(row, lax.axis_index("tensor")),
        device_id_type=MESH,
    )
    copy.start()


def await_bytes(buffer, sem):
    pltpu.make_async_copy(buffer, buffer, sem).wait()


def greet_rows(rows):
    for row in rows:
        pl.semaphore_signal(
            pltpu.get_barrier_semaphore(),
            inc=1,
            device_id=(row, lax.axis_index("tensor")),
            device_id_type=MESH,
        )


class Scatter:
    def __init__(self, send_sem, recv_sem, load_sem=None):
        self.row = lax.axis_index("dp")
        self.z, self.y, self.x = place_of(self.row)
        self.across_x = self.row + 1 - 2 * self.x
        self.across_y = self.row + 2 - 4 * self.y
        self.send_sem, self.recv_sem, self.load_sem = send_sem, recv_sem, load_sem

    def load_own(self, source, own):
        half = source.shape[-1] // 2
        self.loads = [
            pltpu.make_async_copy(
                source.at[:, :, self.x, :, pl.ds(0, half)], own.at[0], self.load_sem.at[0]
            ),
            pltpu.make_async_copy(
                source.at[:, self.y, :, :, pl.ds(half, half)], own.at[1], self.load_sem.at[1]
            ),
        ]
        for load in self.loads:
            load.start()

    def send_first(self, source, target, part, parts):
        half = source.shape[-1] // 2
        size = source.shape[0] // parts
        depth = pl.ds(part * size, size)
        start_remote(
            source.at[depth, :, 1 - self.x, :, pl.ds(0, half)],
            target.at[0, depth],
            self.send_sem.at[0],
            self.recv_sem.at[0],
            self.across_x,
        )
        start_remote(
            source.at[depth, 1 - self.y, :, :, pl.ds(half, half)],
            target.at[1, depth],
            self.send_sem.at[1],
            self.recv_sem.at[1],
            self.across_y,
        )

    def add_first(self, own, target):
        for load in self.loads:
            load.wait()
        for side in range(2):
            await_bytes(target.at[side], self.recv_sem.at[side])
            for depth in range(own.shape[1]):
                own[side, depth] = own[side, depth] + target[side, depth]

    def send_second(self, source, target, part, parts):
        size = source.shape[1] // parts
        depth = pl.ds(part * size, size)
        start_remote(
            source.at[0, depth, 1 - self.y],
            target.at[0, depth],
            self.send_sem.at[2],
            self.recv_sem.at[2],
            self.across_y,
        )
        start_remote(
            source.at[1, depth, 1 - self.x],
            target.at[1, depth],
            self.send_sem.at[3],
            self.recv_sem.at[3],
            self.across_x,
        )

    def add_second(self, own, target, total):
        half = target.shape[-1]
        for side in range(2):
            await_bytes(target.at[side], self.recv_sem.at[2 + side])
            kept = self.y if side == 0 else self.x
            for depth in range(total.shape[0]):
                total[depth, :, side * half : (side + 1) * half] = (
                    own[side, depth, kept] + target[side, depth]
                )

    def send_third(self, total, target):
        depths = total.shape[0]
        below = lax.rem(self.row, 4)

        def send(step, carry):
            other = lax.rem(self.z + step, depths)
            start_remote(
                total.at[other],
                target.at[self.z],
                self.send_sem.at[4],
                self.recv_sem.at[4],
                other * 4 + below,
            )
            return carry

        lax.fori_loop(1, depths, send, 0)

    def add_third(self, total, target, result):
        depths = total.shape[0]
        target[self.z] = total[self.z]
        await_bytes(target.at[pl.ds(0, depths - 1)], self.recv_sem.at[4])
        values = target[0]
        for depth in range(1, depths):
            values = values + target[depth]
        result[...] = values

    def sent(self, first=None, second=None, third=None):
        if first is not None:
            await_bytes(first.at[0], self.send_sem.at[0])
            await_bytes(first.at[1], self.send_sem.at[1])
        if second is not None:
            await_bytes(second.at[0], self.send_sem.at[2])
            await_bytes(second.at[1], self.send_sem.at[3])
        if third is not None:
            await_bytes(third.at[pl.ds(0, third.shape[0] - 1)], self.send_sem.at[4])


def scatter_semaphores(copies=SCATTER_COPIES):
    return [pltpu.SemaphoreType.DMA((copies,)), pltpu.SemaphoreType.DMA((copies,))]


def stem_forward_kernel(
    count,
    places,
    image_ref,
    first_ref,
    weights_ref,
    gain_ref,
    shift_ref,
    feature_ref,
    norm_ref,
    input_ref,
    scale_ref,
    natural,
    skip,
    current,
    source,
    slots,
    send_sem,
    recv_sem,
):
    me = my_index()
    greet_all(count)
    pixels = feature_ref.shape[0]
    rows = stem_rows(pixels)
    norm_at = row_starts(rows)
    input_at = row_starts(rows[1:])
    skip_at = row_starts(rows[:4])
    spacing = 16
    natural[...] = lax.dot_general(
        image_ref[...],
        first_ref[...],
        (((0,), (0,)), ((), ())),
        preferred_element_type=jnp.float32,
    )
    for start, place in places:
        norm_ref[place : place + 8, :] = natural[pl.ds(start, 8, stride=spacing), :]
    for layer in range(LAYERS):
        height = rows[layer]
        chunk = min(height, PIX_CHUNK)
        base = norm_at[layer]
        total = jnp.zeros((8, 128), jnp.float32)
        if layer > 0:
            weights = weights_ref[layer - 1]
            stacked = jnp.concatenate([weights, weights], axis=0)

            def convolve(index, total):
                at = pl.multiple_of(index * chunk, chunk)
                values = jnp.dot(
                    split_two(input_ref[pl.ds(input_at[layer - 1] + at, chunk), :]),
                    stacked,
                    preferred_element_type=jnp.float32,
                )
                norm_ref[pl.ds(base + at, chunk), :] = values
                return total + jnp.sum(values.reshape(chunk // 8, 8, 128), axis=0)

        else:

            def convolve(index, total):
                at = pl.multiple_of(index * chunk, chunk)
                values = norm_ref[pl.ds(base + at, chunk), :]
                return total + jnp.sum(values.reshape(chunk // 8, 8, 128), axis=0)

        total = lax.fori_loop(0, height // chunk, convolve, total)
        mean = jnp.sum(total, axis=0, keepdims=True) * (1.0 / height)

        def deviate(index, total):
            at = pl.multiple_of(index * chunk, chunk)
            values = norm_ref[pl.ds(base + at, chunk), :] - mean
            return total + jnp.sum((values * values).reshape(chunk // 8, 8, 128), axis=0)

        square = lax.fori_loop(0, height // chunk, deviate, jnp.zeros((8, 128), jnp.float32))
        square = jnp.sum(square, axis=0, keepdims=True)
        stats = jnp.concatenate([mean, square], axis=0)
        source[layer] = stats
        slots[layer, me] = stats
        if layer == 0:
            greeted(count)
        send_all(
            count,
            source.at[layer],
            slots.at[layer, me],
            send_sem.at[layer],
            recv_sem.at[layer],
        )
        wait_all(count, slots.at[layer], recv_sem.at[layer])
        means = slots[layer, :, 0, :]
        centre = group_sum(wide(jnp.sum(means, axis=0, keepdims=True))) * (0.25 / count)
        apart = means - centre[0:1]
        spread = jnp.sum(slots[layer, :, 1, :], axis=0, keepdims=True) + height * jnp.sum(
            apart * apart, axis=0, keepdims=True
        )
        variance = group_sum(wide(spread)) * (1.0 / (4 * height * count))
        inverse = lax.rsqrt(variance + group_eps)[0:1]
        centre = centre[0:1]
        scale_ref[layer : layer + 1, :] = inverse
        gain = gain_ref[layer : layer + 1, :]
        shift = shift_ref[layer : layer + 1, :]

        def activate(start, size):
            normed = (norm_ref[pl.ds(base + start, size), :] - centre) * inverse
            norm_ref[pl.ds(base + start, size), :] = normed
            lifted = normed * gain + shift
            return lifted / (1.0 + jnp.exp(-lifted))

        if layer < 4:
            quarter = height // 4
            part = min(quarter, 64)

            def pool(index, carry):
                at = pl.multiple_of(index * part, part)
                mean_of = jnp.zeros((part, 128), jnp.float32)
                for corner in range(4):
                    value = activate(corner * quarter + at, part)
                    skip[pl.ds(skip_at[layer] + corner * quarter + at, part), :] = value
                    mean_of = mean_of + value
                input_ref[pl.ds(input_at[layer] + at, part), :] = mean_of * 0.25
                return carry

            lax.fori_loop(0, quarter // part, pool, 0)
        elif layer < 8:
            part = min(height, 64)
            skipped = skip_at[7 - layer]

            def grow(index, carry):
                at = pl.multiple_of(index * part, part)
                value = activate(at, part)
                for corner in range(4):
                    place = corner * height + at
                    input_ref[pl.ds(input_at[layer] + place, part), :] = (
                        value + skip[pl.ds(skipped + place, part), :]
                    )
                return carry

            lax.fori_loop(0, height // part, grow, 0)
        else:

            def finish(index, carry):
                at = pl.multiple_of(index * chunk, chunk)
                current[pl.ds(at, chunk), :] = activate(at, chunk)
                return carry

            lax.fori_loop(0, height // chunk, finish, 0)
    for start, place in places:
        feature_ref[pl.ds(start, 8, stride=spacing), :] = current[place : place + 8, :]
    for layer in range(LAYERS):
        wait_all(count, slots.at[layer], send_sem.at[layer])


def stem_backward_kernel(
    count,
    places,
    grad_ref,
    image_ref,
    norm_ref,
    input_ref,
    scale_ref,
    weights_ref,
    gain_ref,
    shift_ref,
    split_ref,
    small_ref,
    up_ref,
    attn_ref,
    down_ref,
    first_out,
    weights_out,
    gain_out,
    shift_out,
    split_out,
    small_out,
    up_out,
    attn_out,
    down_out,
    natural,
    ordered,
    active,
    grad_conv,
    skip,
    grads,
    product,
    source,
    slots,
    first_source,
    first_slots,
    parts,
    shared,
    send_sem,
    recv_sem,
    part_send,
    part_recv,
    share_send,
    share_recv,
    split_slots,
    split_half,
    small_slots,
    row_send,
    row_recv,
    up_own,
    up_first,
    up_second,
    up_total,
    up_third,
    attn_own,
    attn_first,
    attn_second,
    attn_total,
    attn_third,
    down_total,
    down_third,
    up_load,
    up_send,
    up_recv,
    attn_load,
    attn_send,
    attn_recv,
    down_load,
    down_send,
    down_recv,
):
    me = my_index()
    up = Scatter(up_send, up_recv, up_load)
    attn = Scatter(attn_send, attn_recv, attn_load)
    down = Scatter(down_send, down_recv)
    up.load_own(up_ref, up_own)
    attn.load_own(attn_ref, attn_own)
    load_down = pltpu.make_async_copy(down_ref, down_total, down_load)
    load_down.start()
    row = lax.axis_index("dp")
    core = lax.axis_index("tensor")
    rows_count = count // 2
    greet_all(count)
    pixels = grad_ref.shape[0]
    rows = stem_rows(pixels)
    norm_at = row_starts(rows)
    input_at = row_starts(rows[1:])
    skip_at = row_starts(rows[:4])
    spacing = 16
    owners = count // 8
    owned = parts.shape[1]
    for start, place in places:
        ordered[place : place + 8, :] = grad_ref[pl.ds(start, 8, stride=spacing), :]

    def send_rows(first, last, source_of, target, place):
        def send(step, carry):
            other = lax.rem(row + step, rows_count)
            pltpu.make_async_remote_copy(
                src_ref=source_of(other),
                dst_ref=target.at[row],
                send_sem=row_send.at[place],
                recv_sem=row_recv.at[place],
                device_id=(other, core),
                device_id_type=MESH,
            ).start()
            return carry

        lax.fori_loop(first, last, send, 0)

    def weight_grad(layer):
        height = rows[layer]
        chunk = min(height, 512)

        def add(index, total):
            at = pl.multiple_of(index * chunk, chunk)
            return total + lax.dot_general(
                input_ref[pl.ds(input_at[layer - 1] + at, chunk), :].astype(jnp.bfloat16),
                grad_conv[pl.ds(norm_at[layer] + at, chunk), :].astype(jnp.bfloat16),
                (((0,), (0,)), ((), ())),
                preferred_element_type=jnp.float32,
            )

        product[layer - 1] = lax.fori_loop(
            0, height // chunk, add, jnp.zeros((128, 128), jnp.float32)
        ).reshape(owners, owned, 128)

        def send(index, carry):
            owner = layer - 1 + 8 * index

            @pl.when(owner != me)
            def _():
                pltpu.make_async_remote_copy(
                    src_ref=product.at[layer - 1, index],
                    dst_ref=parts.at[me],
                    send_sem=part_send,
                    recv_sem=part_recv,
                    device_id=(owner // 2, lax.rem(owner, 2)),
                    device_id_type=MESH,
                ).start()

            @pl.when(owner == me)
            def _():
                parts[me] = product[layer - 1, index]

            return carry

        lax.fori_loop(0, owners, send, 0)

    for layer in range(LAYERS - 1, -1, -1):
        height = rows[layer]
        chunk = min(height, PIX_CHUNK)
        base = norm_at[layer]
        gain = gain_ref[layer : layer + 1, :]
        shift = shift_ref[layer : layer + 1, :]
        inverse = scale_ref[layer : layer + 1, :]
        incoming = ordered if layer == 8 else grads

        def activate(index, carry):
            first, second = carry
            at = pl.multiple_of(index * chunk, chunk)
            normed = norm_ref[pl.ds(base + at, chunk), :]
            lifted = normed * gain + shift
            sigma = 1.0 / (1.0 + jnp.exp(-lifted))
            value = incoming[pl.ds(at, chunk), :] * sigma * (1.0 + lifted * (1.0 - sigma))
            active[pl.ds(at, chunk), :] = value
            first = first + jnp.sum(value.reshape(chunk // 8, 8, 128), axis=0)
            second = second + jnp.sum((value * normed).reshape(chunk // 8, 8, 128), axis=0)
            return first, second

        zero = jnp.zeros((8, 128), jnp.float32)
        first, second = lax.fori_loop(0, height // chunk, activate, (zero, zero))
        sums = jnp.concatenate(
            [jnp.sum(first, axis=0, keepdims=True), jnp.sum(second, axis=0, keepdims=True)], axis=0
        )
        source[layer] = sums
        slots[layer, me] = sums
        if layer == 8:
            greeted(count)
        send_all(
            count, source.at[layer], slots.at[layer, me], send_sem.at[layer], recv_sem.at[layer]
        )
        middle = (rows_count + 1) // 2
        if layer == 8:
            load_down.wait()
            down.send_third(down_total, down_third)
        if layer >= 5:
            up.send_first(up_ref, up_first, 8 - layer, 4)
        if layer == 4:
            attn.send_first(attn_ref, attn_first, 0, 4)
        if layer == 3:
            up.add_first(up_own, up_first)
            up.send_second(up_own, up_second, 0, 2)
        if layer == 2:
            up.send_second(up_own, up_second, 1, 2)
            attn.send_first(attn_ref, attn_first, 1, 4)
        if layer == 1:
            attn.send_first(attn_ref, attn_first, 2, 4)
            up.add_second(up_own, up_second, up_total)
            up.send_third(up_total, up_third)
        if layer == 0:
            attn.send_first(attn_ref, attn_first, 3, 4)
            down.add_third(down_total, down_third, down_out)
        if layer == 7:
            small_slots[row] = small_ref[...]
            split_slots[row] = split_ref[row, core]
            send_rows(1, rows_count, lambda other: small_ref, small_slots, 0)
        if layer == 6:
            send_rows(1, middle, lambda other: split_ref.at[other, core], split_slots, 1)
        if layer == 5:
            send_rows(middle, rows_count, lambda other: split_ref.at[other, core], split_slots, 1)
        if layer == 3:
            wait_all(rows_count, small_slots, row_recv.at[0])
            small_out[...] = jnp.sum(small_slots[...], axis=0)
            wait_all(rows_count, split_slots, row_recv.at[1])
            split_half[core] = jnp.sum(split_slots[...], axis=0)
            swap = pltpu.make_async_remote_copy(
                src_ref=split_half.at[core],
                dst_ref=split_half.at[core],
                send_sem=row_send.at[2],
                recv_sem=row_recv.at[2],
                device_id=(row, 1 - core),
                device_id_type=MESH,
            )
            swap.start()
        if layer == 1:
            swap.wait()
            split_out[...] = split_half[...]
        if layer < 8:
            weight_grad(layer + 1)
        wait_all(count, slots.at[layer], recv_sem.at[layer])
        totals = jnp.sum(slots[layer], axis=0)
        shift_out[layer : layer + 1, :] = totals[0:1]
        gain_out[layer : layer + 1, :] = totals[1:2]
        share = 1.0 / (4 * height * count)
        first_mean = group_sum(wide(totals[0:1] * gain))[0:1] * share
        second_mean = group_sum(wide(totals[1:2] * gain))[0:1] * share

        def conv_grad(start, size):
            value = inverse * (
                active[pl.ds(start, size), :] * gain
                - first_mean
                - norm_ref[pl.ds(base + start, size), :] * second_mean
            )
            grad_conv[pl.ds(base + start, size), :] = value
            return value

        if layer > 0:
            weights = weights_ref[layer - 1]
            stacked = jnp.concatenate([weights, weights], axis=1)

            def input_grad(start, size):
                return lax.dot_general(
                    split_two(conv_grad(start, size)),
                    stacked,
                    (((1,), (1,)), ((), ())),
                    preferred_element_type=jnp.float32,
                )

        if layer > 4:
            quarter = height // 4
            part = min(quarter, 64)
            skipped = skip_at[8 - layer]

            def shrink(index, carry):
                at = pl.multiple_of(index * part, part)
                total = jnp.zeros((part, 128), jnp.float32)
                for corner in range(4):
                    place = corner * quarter + at
                    value = input_grad(place, part)
                    skip[pl.ds(skipped + place, part), :] = value
                    total = total + value
                grads[pl.ds(at, part), :] = total
                return carry

            lax.fori_loop(0, quarter // part, shrink, 0)
        elif layer > 0:
            part = min(height, 128)
            skipped = skip_at[layer - 1]

            def spread_out(index, carry):
                at = pl.multiple_of(index * part, part)
                value = input_grad(at, part) * 0.25
                for corner in range(4):
                    place = corner * height + at
                    grads[pl.ds(place, part), :] = value + skip[pl.ds(skipped + place, part), :]
                return carry

            lax.fori_loop(0, height // part, spread_out, 0)
        else:

            def finish(index, carry):
                at = pl.multiple_of(index * chunk, chunk)
                conv_grad(at, chunk)
                return carry

            lax.fori_loop(0, height // chunk, finish, 0)
    for start, place in places:
        natural[pl.ds(start, 8, stride=spacing), :] = grad_conv[place : place + 8, :]
    first_part = jnp.dot(
        image_ref[...], natural[...].astype(jnp.bfloat16), preferred_element_type=jnp.float32
    )
    first_source[...] = first_part
    first_slots[me] = first_part
    send_all(count, first_source, first_slots.at[me], send_sem.at[LAYERS], recv_sem.at[LAYERS])
    attn.add_first(attn_own, attn_first)
    attn.send_second(attn_own, attn_second, 0, 1)
    wait_all(count, parts, part_recv)
    mine = jnp.sum(parts[...], axis=0)
    shared[me] = mine
    send_all(count, shared.at[me], shared.at[me], share_send, share_recv)
    attn.add_second(attn_own, attn_second, attn_total)
    attn.send_third(attn_total, attn_third)
    up.add_third(up_total, up_third, up_out)
    wait_all(count, first_slots, recv_sem.at[LAYERS])
    first_out[...] = jnp.sum(first_slots[...], axis=0)
    wait_all(count, shared, share_recv)
    for device in range(count):
        weights_out[device % 8, (device // 8) * owned : (device // 8 + 1) * owned, :] = shared[
            device
        ]
    attn.add_third(attn_total, attn_third, attn_out)
    up.sent(up_first, up_second, up_third)
    attn.sent(attn_first, attn_second, attn_third)
    down.sent(third=down_third)
    for layer in range(LAYERS):
        wait_all(count, slots.at[layer], send_sem.at[layer])
    wait_all(count, first_slots, send_sem.at[LAYERS])
    wait_all(rows_count, small_slots, row_send.at[0])
    wait_all(rows_count, split_slots, row_send.at[1])
    wait_all(count, parts, part_send)
    wait_all(count, shared, share_send)


def stem_forward(page_image, conv_first, conv_weights, group_gain, group_shift, devices):
    planes, tile_rows, columns = page_image.shape
    pixels = tile_rows * columns
    rows = stem_rows(pixels)
    image = page_image.reshape(planes, pixels)
    places = natural_places(tile_rows, columns)
    whole = pl.BlockSpec(memory_space=pltpu.VMEM)
    return pl.pallas_call(
        functools.partial(stem_forward_kernel, devices, places),
        out_shape=(
            jax.ShapeDtypeStruct((pixels, 128), jnp.float32),
            jax.ShapeDtypeStruct((sum(rows), 128), jnp.float32),
            jax.ShapeDtypeStruct((sum(rows[1:]), 128), jnp.float32),
            jax.ShapeDtypeStruct((LAYERS, 128), jnp.float32),
        ),
        in_specs=[whole] * 5,
        out_specs=(whole,) * 4,
        scratch_shapes=[
            pltpu.VMEM((pixels, 128), jnp.float32),
            pltpu.VMEM((sum(rows[:4]), 128), jnp.float32),
            pltpu.VMEM((pixels, 128), jnp.float32),
            pltpu.VMEM((LAYERS, 2, 128), jnp.float32),
            pltpu.VMEM((LAYERS, devices, 2, 128), jnp.float32),
            pltpu.SemaphoreType.DMA((LAYERS,)),
            pltpu.SemaphoreType.DMA((LAYERS,)),
        ],
        compiler_params=pltpu.CompilerParams(
            collective_id=0, has_side_effects=True, vmem_limit_bytes=40 * 2**20
        ),
        cost_estimate=pl.CostEstimate(
            flops=54 * 10**9, bytes_accessed=2 * 10**7, transcendentals=0
        ),
        name="stem_forward",
    )(image, conv_first, conv_weights, group_gain, group_shift)


def stem_backward(
    grad_map,
    page_image,
    records,
    conv_weights,
    group_gain,
    group_shift,
    split,
    small,
    up,
    attn,
    down,
    devices,
):
    planes, tile_rows, columns = page_image.shape
    pixels = tile_rows * columns
    rows = stem_rows(pixels)
    norms, inputs, scales = records
    image = page_image.reshape(planes, pixels)
    places = natural_places(tile_rows, columns)
    whole = pl.BlockSpec(memory_space=pltpu.VMEM)
    owned = 1024 // devices
    far = pl.BlockSpec(memory_space=pl.ANY)
    depths, _, _, own_rows, columns = up.shape
    own = pltpu.VMEM((2, depths, 2, own_rows, columns // 2), jnp.float32)
    after = pltpu.VMEM((2, depths, own_rows, columns // 2), jnp.float32)
    total = pltpu.VMEM((depths, own_rows, columns), jnp.float32)
    return pl.pallas_call(
        functools.partial(stem_backward_kernel, devices, places),
        out_shape=(
            jax.ShapeDtypeStruct((planes, 128), jnp.float32),
            jax.ShapeDtypeStruct((8, 128, 128), jnp.float32),
            jax.ShapeDtypeStruct((LAYERS, 128), jnp.float32),
            jax.ShapeDtypeStruct((LAYERS, 128), jnp.float32),
            jax.ShapeDtypeStruct(split.shape[1:], jnp.float32),
            jax.ShapeDtypeStruct(small.shape, jnp.float32),
            *[jax.ShapeDtypeStruct((own_rows, columns), jnp.float32)] * 3,
        ),
        in_specs=[whole] * 10 + [far] * 3,
        out_specs=(whole,) * 9,
        scratch_shapes=[
            pltpu.VMEM((pixels, 128), jnp.float32),
            pltpu.VMEM((pixels, 128), jnp.float32),
            pltpu.VMEM((pixels, 128), jnp.float32),
            pltpu.VMEM((sum(rows), 128), jnp.float32),
            pltpu.VMEM((sum(rows[:4]), 128), jnp.float32),
            pltpu.VMEM((pixels, 128), jnp.float32),
            pltpu.VMEM((8, devices // 8, owned, 128), jnp.float32),
            pltpu.VMEM((LAYERS, 2, 128), jnp.float32),
            pltpu.VMEM((LAYERS, devices, 2, 128), jnp.float32),
            pltpu.VMEM((planes, 128), jnp.float32),
            pltpu.VMEM((devices, planes, 128), jnp.float32),
            pltpu.VMEM((devices, owned, 128), jnp.float32),
            pltpu.VMEM((devices, owned, 128), jnp.float32),
            pltpu.SemaphoreType.DMA((LAYERS + 1,)),
            pltpu.SemaphoreType.DMA((LAYERS + 1,)),
            pltpu.SemaphoreType.DMA,
            pltpu.SemaphoreType.DMA,
            pltpu.SemaphoreType.DMA,
            pltpu.SemaphoreType.DMA,
            pltpu.VMEM((devices // 2, *split.shape[2:]), jnp.float32),
            pltpu.VMEM(split.shape[1:], jnp.float32),
            pltpu.VMEM((devices // 2, *small.shape), jnp.float32),
            pltpu.SemaphoreType.DMA((3,)),
            pltpu.SemaphoreType.DMA((3,)),
            own,
            own,
            after,
            total,
            total,
            own,
            own,
            after,
            total,
            total,
            total,
            total,
            pltpu.SemaphoreType.DMA((2,)),
            *scatter_semaphores(),
            pltpu.SemaphoreType.DMA((2,)),
            *scatter_semaphores(),
            pltpu.SemaphoreType.DMA,
            *scatter_semaphores(),
        ],
        compiler_params=pltpu.CompilerParams(
            collective_id=1, has_side_effects=True, vmem_limit_bytes=56 * 2**20
        ),
        cost_estimate=pl.CostEstimate(
            flops=65 * 10**9, bytes_accessed=2 * 10**7, transcendentals=0
        ),
        name="stem_backward",
    )(
        grad_map,
        image,
        norms,
        inputs,
        scales,
        conv_weights,
        group_gain,
        group_shift,
        split,
        small,
        up,
        attn,
        down,
    )


TILE = 128
QROWS = 256
KIND_ROWS = 8
FAR_LANE = 32
LOW_LANE = 40
PAD_LANE = 48
DOC_LANE = 56


def dot_last(left, right):
    return lax.dot_general(
        left, right, (((1,), (1,)), ((), ())), preferred_element_type=jnp.float32
    )


def dot_plain(left, right):
    return jnp.dot(left, right, preferred_element_type=jnp.float32)


def bucket_vector(tables_ref, table, head, relative):
    buckets = bucket_of(relative)
    values = jnp.zeros(relative.shape, jnp.float32)
    for bucket in range(NBUCKET):
        values = jnp.where(buckets == bucket, tables_ref[table, bucket, head], values)
    return values


def signed_lanes(width):
    lane = lax.broadcasted_iota(jnp.int32, (8, width), 1)
    return jnp.where(lane < width // 2, lane, lane - width)


def rolled(row, height):
    return pltpu.roll(
        jnp.broadcast_to(row[0:1], (height, row.shape[1])), 0, 1, stride=1, stride_axis=0
    )


def token_lanes(info_ref, one_hot_x, query_base, key_base, pad_tiles):
    tokens = info_ref.shape[0]
    lane = lax.broadcasted_iota(jnp.int32, (TILE, 128), 1)
    row = lax.broadcasted_iota(jnp.int32, (TILE, 128), 0)
    for tile in range(tokens // TILE):
        at = slice(tile * TILE, (tile + 1) * TILE)
        left = info_ref[at, 0:1]
        top = info_ref[at, 1:2]
        doc = info_ref[at, 2:3]
        hidden = jnp.where(info_ref[at, 3:4] > 0, 0.0, masked_score)
        one_hot_x[at, :] = (lane == left).astype(jnp.float32).astype(jnp.bfloat16)
        shared = jnp.where((lane == top) | (lane == DOC_LANE + doc), 1.0, 0.0)
        query_base[at, :] = jnp.where(lane == FAR_LANE + tile, 1.0, shared).astype(jnp.bfloat16)
        key = jnp.where((lane == FAR_LANE + tile) | (lane == LOW_LANE + tile), 1.0, shared)
        key = jnp.where(lane == PAD_LANE + tile, hidden, key)
        key_base[1, at, :] = key.astype(jnp.bfloat16)
        key_base[0, at, :] = pltpu.roll(key, 64, 1).astype(jnp.bfloat16)
        pad_tiles[at, :] = jnp.where(lane == row, 0.0, jnp.broadcast_to(hidden, (TILE, 128)))


def head_matrices(tables_ref, head, side):
    first = bucket_vector(tables_ref, 1, head, signed_lanes(256))
    across = rolled(first, 128)[:, :128].astype(jnp.bfloat16)
    second = rolled(bucket_vector(tables_ref, 2, head, signed_lanes(128)), 128)
    row = lax.broadcasted_iota(jnp.int32, (128, 128), 0)
    lane = lax.broadcasted_iota(jnp.int32, (128, 128), 1)
    mixed = jnp.where((row < FAR_LANE) & (lane < FAR_LANE), second, 0.0)
    gap = lane % 8 - (row - FAR_LANE)
    before = jnp.full((128, 128), tables_ref[0, NBUCKET // 2 - 1, head], jnp.float32)
    after = jnp.full((128, 128), tables_ref[0, NBUCKET - 1, head], jnp.float32)
    far = jnp.where(gap <= -2, before, jnp.where(gap >= 2, after, 0.0))
    high = far.astype(jnp.bfloat16).astype(jnp.float32)
    of_tile = (row >= FAR_LANE) & (row < LOW_LANE)
    mixed = jnp.where(of_tile & (lane >= FAR_LANE) & (lane < LOW_LANE), high, mixed)
    mixed = jnp.where(of_tile & (lane >= LOW_LANE) & (lane < PAD_LANE), far - high, mixed)
    mixed = jnp.where(
        of_tile & (lane >= PAD_LANE) & (lane < DOC_LANE) & (gap != 0), 1.0, mixed
    )
    docs = (row >= DOC_LANE) & (row < 64) & (lane >= DOC_LANE) & (lane < 64)
    mixed = jnp.where(docs & (row != lane), masked_score, mixed)
    if side == 0:
        mixed = pltpu.roll(mixed, 64, 1)
    near = rolled(bucket_vector(tables_ref, 0, head, -signed_lanes(512)), 128)
    tiles = {0: near[:, :128], 1: near[:, 384:], -1: near[:, 128:256]}
    return across, mixed.astype(jnp.bfloat16), tiles


def own_half(side, own, other):
    lane = lax.broadcasted_iota(jnp.int32, own.shape, 1)
    return jnp.where((lane < 64) if side == 0 else (lane >= 64), own, other)


def widen_operands(
    side, head, tables_ref, query_ref, key_ref, one_hot_x, query_base, key_base, query_wide, key_wide, near
):
    across, mixed, tiles = head_matrices(tables_ref, head, side)
    for gap in (-1, 0, 1):
        near[side, gap + 1] = tiles[gap]
    scaled = (query_ref[...].astype(jnp.float32) * HDIM ** (-0.5)).astype(jnp.bfloat16)
    query_wide[side, :, :128] = own_half(
        side, scaled, dot_plain(query_base[...], mixed).astype(jnp.bfloat16)
    )
    query_wide[side, :, 128:] = dot_plain(one_hot_x[...], across).astype(jnp.bfloat16)
    key_wide[side, :, :128] = own_half(side, key_ref[...], key_base[side])
    key_wide[side, :, 128:] = one_hot_x[...]


def near_scores(scores, side, block, tile, near, pad_tiles):
    halves = []
    for half in range(QROWS // TILE):
        part = scores[:, half * TILE : (half + 1) * TILE]
        gap = tile - (block * (QROWS // TILE) + half)
        if abs(gap) <= 1:
            part = part + near[side, gap + 1]
        if gap == 0:
            part = part + pad_tiles[tile * TILE : (tile + 1) * TILE, :]
        halves.append(part)
    return jnp.concatenate(halves, axis=1)


def attention_forward_kernel(
    tables_ref,
    info_ref,
    query_ref,
    key_ref,
    value_ref,
    context_ref,
    exact_ref,
    lse_ref,
    one_hot_x,
    query_base,
    key_base,
    pad_tiles,
    query_wide,
    key_wide,
    near,
    scores,
    weights,
):
    pair = pl.program_id(0)
    tokens = query_ref.shape[0]

    @pl.when(pair == 0)
    def _():
        token_lanes(info_ref, one_hot_x, query_base, key_base, pad_tiles)

    for side in range(2):
        widen_operands(
            side, pair * 2 + side, tables_ref, query_ref, key_ref, one_hot_x, query_base, key_base,
            query_wide, key_wide, near,
        )
    values = value_ref[...].T
    for block in range(tokens // QROWS):
        columns = slice(block * QROWS, (block + 1) * QROWS)
        contexts = []
        for side in range(2):
            scores[side] = dot_last(key_wide[side], query_wide[side, columns, :])
            top = jnp.full((8, QROWS), masked_score, jnp.float32)
            for tile in range(tokens // TILE):
                at = slice(tile * TILE, (tile + 1) * TILE)
                part = scores[side, at, :]
                if any(abs(tile - 2 * block - half) <= 1 for half in range(2)):
                    part = near_scores(part, side, block, tile, near, pad_tiles)
                    scores[side, at, :] = part
                top = jnp.maximum(top, jnp.max(part.reshape(TILE // 8, 8, QROWS), axis=0))
            top = jnp.max(top, axis=0, keepdims=True)
            total = jnp.zeros((8, QROWS), jnp.float32)
            for tile in range(tokens // TILE):
                at = slice(tile * TILE, (tile + 1) * TILE)
                part = jnp.exp(scores[side, at, :] - top)
                total = total + jnp.sum(part.reshape(TILE // 8, 8, QROWS), axis=0)
                weights[side, at, :] = part.astype(jnp.bfloat16)
            total = jnp.sum(total, axis=0, keepdims=True)
            context = dot_plain(values[side * 64 : (side + 1) * 64, :], weights[side])
            contexts.append(context * (1.0 / total))
            lse_ref[0, side : side + 1, columns] = top + jnp.log(total)
        context = jnp.concatenate(contexts, axis=0)
        exact_ref[:, columns] = context
        context_ref[columns, :] = context.T.astype(jnp.bfloat16)


def attention_backward_kernel(
    tables_ref,
    info_ref,
    query_ref,
    key_ref,
    value_ref,
    grad_ref,
    exact_ref,
    lse_ref,
    scatter_ref,
    grad_query_ref,
    grad_key_ref,
    grad_value_ref,
    diagonal_ref,
    first_ref,
    one_hot_x,
    query_base,
    key_base,
    pad_tiles,
    reverse,
    query_wide,
    key_wide,
    near,
    scores,
    grad_probs,
    probs_low,
    grad_low,
    key_turned,
    grad_near,
    grad_blocks,
    grad_key,
    grad_value,
    own,
    arrived,
    load_sem,
    send_sem,
    recv_sem,
):
    pair = pl.program_id(0)
    tokens = query_ref.shape[0]
    scatter = Scatter(send_sem, recv_sem, load_sem)

    @pl.when(pair == 0)
    def _():
        greet_rows((scatter.across_x, scatter.across_y))
        scatter.load_own(scatter_ref, own)
        for load in scatter.loads:
            load.wait()
        pl.semaphore_wait(pltpu.get_barrier_semaphore(), 2)
        scatter.send_first(scatter_ref, arrived, 0, 1)
        token_lanes(info_ref, one_hot_x, query_base, key_base, pad_tiles)
        lane = lax.broadcasted_iota(jnp.int32, (TILE, 128), 1)
        for tile in range(tokens // TILE):
            at = slice(tile * TILE, (tile + 1) * TILE)
            left = info_ref[at, 0:1]
            top = info_ref[at, 1:2]
            reverse[at, :128] = jnp.where(lane == 127 - left, 1.0, 0.0).astype(jnp.bfloat16)
            reverse[at, 128:] = jnp.where(
                (lane == 31 - top) | (lane == FAR_LANE + tile), 1.0, 0.0
            ).astype(jnp.bfloat16)

    for side in range(2):
        widen_operands(
            side, pair * 2 + side, tables_ref, query_ref, key_ref, one_hot_x, query_base, key_base,
            query_wide, key_wide, near,
        )
        key_turned[side] = key_wide[side].T
    grad_near[...] = jnp.zeros_like(grad_near)
    grad_blocks[...] = jnp.zeros_like(grad_blocks)
    values = [
        own_half(side, value_ref[...], jnp.zeros(value_ref.shape, jnp.bfloat16)) for side in range(2)
    ]
    for block in range(tokens // QROWS):
        columns = slice(block * QROWS, (block + 1) * QROWS)
        grad_block = grad_ref[columns, :]
        product = grad_block.astype(jnp.float32).T * exact_ref[:, columns]
        scaled = (query_ref[columns, :].astype(jnp.float32) * HDIM ** (-0.5)).astype(jnp.bfloat16)
        turned = []
        key_terms = []
        value_terms = []
        for side in range(2):
            delta = jnp.sum(product[side * 64 : (side + 1) * 64, :], axis=0, keepdims=True)
            lse = lse_ref[0, side : side + 1, columns]
            scores[side] = dot_last(key_wide[side], query_wide[side, columns, :])
            grad_probs[side] = dot_last(values[side], grad_block)
            for tile in range(tokens // TILE):
                at = slice(tile * TILE, (tile + 1) * TILE)
                part = near_scores(scores[side, at, :], side, block, tile, near, pad_tiles)
                probs = jnp.exp(part - lse)
                grad_part = probs * (grad_probs[side, at, :] - delta)
                probs_low[side, at, :] = probs.astype(jnp.bfloat16)
                grad_low[side, at, :] = grad_part.astype(jnp.bfloat16)
                for half in range(QROWS // TILE):
                    gap = tile - (block * (QROWS // TILE) + half)
                    if abs(gap) <= 1:
                        grad_near[side, gap + 1] += grad_part[:, half * TILE : (half + 1) * TILE]
            value_terms.append(dot_plain(probs_low[side], grad_block))
            key_terms.append(dot_plain(grad_low[side], scaled))
            sums = dot_plain(key_turned[side], grad_low[side])
            turned.append(sums[side * 64 : (side + 1) * 64, :])
            grad_blocks[side] += dot_plain(sums.astype(jnp.bfloat16), reverse[columns, :])
        grad_query_ref[columns, :] = (
            (jnp.concatenate(turned, axis=0) * HDIM ** (-0.5)).T.astype(jnp.bfloat16)
        )
        key_term = own_half(0, key_terms[0], key_terms[1])
        value_term = own_half(0, value_terms[0], value_terms[1])
        if block == 0:
            grad_key[...] = key_term
            grad_value[...] = value_term
        else:
            grad_key[...] += key_term
            grad_value[...] += value_term
    grad_key_ref[...] = grad_key[...].astype(jnp.bfloat16)
    grad_value_ref[...] = grad_value[...].astype(jnp.bfloat16)
    row = lax.broadcasted_iota(jnp.int32, (128, 128), 0)
    lane = lax.broadcasted_iota(jnp.int32, (128, 128), 1)
    flip = jnp.where(row + lane == 127, 1.0, 0.0).astype(jnp.bfloat16)
    blank = jnp.zeros((128, 128), jnp.float32)

    def diagonal_sums(values):
        spread = jnp.concatenate([values, blank], axis=1)
        return jnp.sum(
            pltpu.roll(spread, 0, 1, stride=1, stride_axis=0), axis=0, keepdims=True
        )

    for side in range(2):
        misc = 64 * (1 - side)
        sums = [diagonal_sums(grad_blocks[side, 128:, :128])]
        below = grad_blocks[side, misc : misc + 64, 128:]
        small_row = lax.broadcasted_iota(jnp.int32, (64, 128), 0)
        small_lane = lax.broadcasted_iota(jnp.int32, (64, 128), 1)
        upright = jnp.where((small_row < FAR_LANE) & (small_lane < FAR_LANE), below, 0.0)
        sums.append(diagonal_sums(jnp.concatenate([upright, jnp.zeros((64, 128), jnp.float32)], axis=0)))
        for gap in range(3):
            tile = grad_near[side, gap]
            high = tile.astype(jnp.bfloat16)
            rest = (tile - high.astype(jnp.float32)).astype(jnp.bfloat16)
            sums.append(diagonal_sums(dot_plain(high, flip) + dot_plain(rest, flip)))
        gap = (small_row - FAR_LANE) - (small_lane - FAR_LANE)
        inside = (
            (small_row >= FAR_LANE)
            & (small_row < LOW_LANE)
            & (small_lane >= FAR_LANE)
            & (small_lane < LOW_LANE)
        )
        for chosen in (gap <= -2, gap >= 2):
            far = jnp.sum(jnp.where(inside & chosen, below, 0.0), axis=0, keepdims=True)
            sums.append(jnp.concatenate([far, blank[0:1]], axis=1))
        sums.append(jnp.zeros((1, 256), jnp.float32))
        diagonal_ref[side] = jnp.concatenate(sums, axis=0)

    @pl.when(pair == pl.num_programs(0) - 1)
    def _():
        scatter.loads = []
        scatter.add_first(own, arrived)
        store = pltpu.make_async_copy(own, first_ref, load_sem.at[0])
        store.start()
        scatter.sent(first=arrived)
        store.wait()


def attention_scratch(tokens):
    return [
        pltpu.VMEM((tokens, 128), jnp.bfloat16),
        pltpu.VMEM((tokens, 128), jnp.bfloat16),
        pltpu.VMEM((2, tokens, 128), jnp.bfloat16),
        pltpu.VMEM((tokens, 128), jnp.float32),
    ], [
        pltpu.VMEM((2, tokens, 256), jnp.bfloat16),
        pltpu.VMEM((2, tokens, 256), jnp.bfloat16),
        pltpu.VMEM((2, 3, TILE, TILE), jnp.float32),
        pltpu.VMEM((2, tokens, QROWS), jnp.float32),
    ]


def attention_forward(tables, info, heads):
    tokens, width = heads.shape[0], heads.shape[1] // 3
    pairs = width // 128
    own = pl.BlockSpec((tokens, 128), lambda pair: (0, pair))
    fixed, moving = attention_scratch(tokens)
    return pl.pallas_call(
        attention_forward_kernel,
        grid=(pairs,),
        out_shape=(
            jax.ShapeDtypeStruct((tokens, width), jnp.bfloat16),
            jax.ShapeDtypeStruct((width, tokens), jnp.float32),
            jax.ShapeDtypeStruct((pairs, 2, tokens), jnp.float32),
        ),
        in_specs=[
            pl.BlockSpec(memory_space=pltpu.SMEM),
            pl.BlockSpec((tokens, 8), lambda pair: (0, 0)),
            own,
            pl.BlockSpec((tokens, 128), lambda pair: (0, pairs + pair)),
            pl.BlockSpec((tokens, 128), lambda pair: (0, 2 * pairs + pair)),
        ],
        out_specs=(
            own,
            pl.BlockSpec((128, tokens), lambda pair: (pair, 0)),
            pl.BlockSpec((1, 2, tokens), lambda pair: (pair, 0, 0)),
        ),
        scratch_shapes=fixed
        + moving
        + [
            pltpu.VMEM((2, tokens, QROWS), jnp.bfloat16),
        ],
        compiler_params=pltpu.CompilerParams(
            dimension_semantics=("arbitrary",), vmem_limit_bytes=48 * 2**20
        ),
        cost_estimate=pl.CostEstimate(
            flops=23 * 10**9, bytes_accessed=2 * 10**7, transcendentals=0
        ),
        name="attention_forward",
    )(tables, info, heads, heads, heads)


def attention_backward(tables, info, heads, grad_context, exact, lse, scatter):
    tokens, width = grad_context.shape
    pairs = width // 128
    own = pl.BlockSpec((tokens, 128), lambda pair: (0, pair))
    fixed, moving = attention_scratch(tokens)
    low = jax.ShapeDtypeStruct((tokens, width), jnp.bfloat16)
    halves = (2, scatter.shape[0], 2, scatter.shape[3], scatter.shape[4] // 2)
    return pl.pallas_call(
        attention_backward_kernel,
        grid=(pairs,),
        out_shape=(
            low,
            low,
            low,
            jax.ShapeDtypeStruct((2 * pairs, 8, 256), jnp.float32),
            jax.ShapeDtypeStruct(halves, jnp.float32),
        ),
        in_specs=[
            pl.BlockSpec(memory_space=pltpu.SMEM),
            pl.BlockSpec((tokens, 8), lambda pair: (0, 0)),
            own,
            pl.BlockSpec((tokens, 128), lambda pair: (0, pairs + pair)),
            pl.BlockSpec((tokens, 128), lambda pair: (0, 2 * pairs + pair)),
            own,
            pl.BlockSpec((128, tokens), lambda pair: (pair, 0)),
            pl.BlockSpec((1, 2, tokens), lambda pair: (pair, 0, 0)),
            pl.BlockSpec(memory_space=pl.ANY),
        ],
        out_specs=(
            own,
            own,
            own,
            pl.BlockSpec((2, 8, 256), lambda pair: (pair, 0, 0)),
            pl.BlockSpec(memory_space=pl.ANY),
        ),
        scratch_shapes=fixed
        + [pltpu.VMEM((tokens, 256), jnp.bfloat16)]
        + moving
        + [
            pltpu.VMEM((2, tokens, QROWS), jnp.float32),
            pltpu.VMEM((2, tokens, QROWS), jnp.bfloat16),
            pltpu.VMEM((2, tokens, QROWS), jnp.bfloat16),
            pltpu.VMEM((2, 256, tokens), jnp.bfloat16),
            pltpu.VMEM((2, 3, TILE, TILE), jnp.float32),
            pltpu.VMEM((2, 256, 256), jnp.float32),
            pltpu.VMEM((tokens, 128), jnp.float32),
            pltpu.VMEM((tokens, 128), jnp.float32),
            pltpu.VMEM(halves, jnp.float32),
            pltpu.VMEM(halves, jnp.float32),
            pltpu.SemaphoreType.DMA((2,)),
            *scatter_semaphores(2),
        ],
        compiler_params=pltpu.CompilerParams(
            dimension_semantics=("arbitrary",),
            collective_id=5,
            has_side_effects=True,
            vmem_limit_bytes=52 * 2**20,
        ),
        cost_estimate=pl.CostEstimate(
            flops=30 * 10**9, bytes_accessed=2 * 10**7, transcendentals=0
        ),
        name="attention_backward",
    )(tables, info, heads, heads, heads, grad_context, exact, lse, scatter)


def bucket_grads(diagonals):
    lane = jnp.arange(256, dtype=jnp.int32)
    wide_buckets = [
        bucket_of(lane - 127),
        bucket_of(lane - 31),
        bucket_of(lane - 127 - TILE),
        bucket_of(lane - 127),
        bucket_of(lane - 127 + TILE),
        jnp.full((256,), NBUCKET // 2 - 1, jnp.int32),
        jnp.full((256,), NBUCKET - 1, jnp.int32),
    ]
    table_of = (1, 2, 0, 0, 0, 0, 0)
    slots = jnp.stack([bucket + NBUCKET * table for bucket, table in zip(wide_buckets, table_of)])
    chosen = (slots[..., None] == jnp.arange(3 * NBUCKET, dtype=jnp.int32)).astype(jnp.float32)
    sums = jnp.einsum("hrc,rcb->bh", diagonals[:, :7], chosen, precision=highest)
    return sums.reshape(3, NBUCKET, -1)


ROWS = 256


def greet_partner():
    pl.semaphore_signal(
        pltpu.get_barrier_semaphore(),
        inc=1,
        device_id=(lax.axis_index("dp"), 1 - lax.axis_index("tensor")),
        device_id_type=MESH,
    )


def partner_copy(source, target, send_sem, recv_sem):
    return pltpu.make_async_remote_copy(
        src_ref=source,
        dst_ref=target,
        send_sem=send_sem,
        recv_sem=recv_sem,
        device_id=(lax.axis_index("dp"), 1 - lax.axis_index("tensor")),
        device_id_type=MESH,
    )


def dot_rows(left, right):
    return lax.dot_general(
        left, right, (((0,), (0,)), ((), ())), preferred_element_type=jnp.float32
    )


def inverse_rms(values):
    return lax.rsqrt(jnp.mean(values * values, axis=1, keepdims=True) + norm_eps)


def box_kernel(
    feature_ref,
    info_ref,
    embedded_ref,
    roi_ref,
    norm_ref,
    query_proj_ref,
    key_proj_ref,
    value_proj_ref,
    pooled_ref,
    stream_ref,
    input_ref,
    heads_ref,
    features,
    mask,
    part,
    received,
    projections,
    send_sem,
    recv_sem,
):
    greet_partner()
    tokens = info_ref.shape[0]
    pixels = feature_ref.shape[0]
    tile_rows = pixels // 128
    first_row = lax.axis_index("tensor") * tile_rows
    features[...] = split_two(feature_ref[...])
    lane = lax.broadcasted_iota(jnp.int32, (ROWS, 128), 1)
    copies = []
    for block in range(tokens // ROWS):
        at = slice(block * ROWS, (block + 1) * ROWS)
        column = (lane >= info_ref[at, 0:1]) & (lane < info_ref[at, 4:5])
        column = jnp.where(column, 1.0, 0.0)
        top = jnp.broadcast_to(info_ref[at, 1:2], (ROWS, 128)) - first_row
        bottom = jnp.broadcast_to(info_ref[at, 5:6], (ROWS, 128)) - first_row
        for row in range(tile_rows):
            inside = jnp.where((top <= row) & (bottom > row), column, 0.0)
            mask[block % 2, :, row * 128 : (row + 1) * 128] = inside.astype(jnp.bfloat16)
        sums = dot_plain(mask[block % 2], features[...])
        part[at, :] = sums[:, :128] + sums[:, 128:]
        if block == 0:
            pl.semaphore_wait(pltpu.get_barrier_semaphore(), 1)
        copy = partner_copy(
            part.at[pl.ds(block * ROWS, ROWS)],
            received.at[pl.ds(block * ROWS, ROWS)],
            send_sem.at[block],
            recv_sem.at[block],
        )
        copy.start()
        copies.append(copy)
    width = query_proj_ref.shape[1]
    for index, ref in enumerate((query_proj_ref, key_proj_ref, value_proj_ref)):
        projections[:, index * width : (index + 1) * width] = ref[...]
    for block in range(tokens // ROWS):
        at = slice(block * ROWS, (block + 1) * ROWS)
        copies[block].wait_recv()
        area = (info_ref[at, 5:6] - info_ref[at, 1:2]) * (info_ref[at, 4:5] - info_ref[at, 0:1])
        pooled = ((part[at, :] + received[at, :]) / area.astype(jnp.float32)).astype(jnp.bfloat16)
        pooled_ref[at, :] = pooled
        stream = embedded_ref[at, :].astype(jnp.float32) + dot_plain(pooled, roi_ref[...])
        stream_ref[at, :] = stream
        attn_in = (stream * inverse_rms(stream) * norm_ref[...]).astype(jnp.bfloat16)
        input_ref[at, :] = attn_in
        heads_ref[at, :] = dot_plain(attn_in, projections[...]).astype(jnp.bfloat16)
    for copy in copies:
        copy.wait_send()


def box_forward(
    feature_map, info, embeddings, roi_proj, attn_norm, query_proj, key_proj, value_proj
):
    tokens, width = embeddings.shape
    local = query_proj.shape[1]
    blocks = tokens // ROWS
    whole = pl.BlockSpec(memory_space=pltpu.VMEM)
    return pl.pallas_call(
        box_kernel,
        out_shape=(
            jax.ShapeDtypeStruct((tokens, 128), jnp.bfloat16),
            jax.ShapeDtypeStruct((tokens, width), jnp.float32),
            jax.ShapeDtypeStruct((tokens, width), jnp.bfloat16),
            jax.ShapeDtypeStruct((tokens, 3 * local), jnp.bfloat16),
        ),
        in_specs=[whole] * 8,
        out_specs=(whole,) * 4,
        scratch_shapes=[
            pltpu.VMEM((feature_map.shape[0], 256), jnp.bfloat16),
            pltpu.VMEM((2, ROWS, feature_map.shape[0]), jnp.bfloat16),
            pltpu.VMEM((tokens, 128), jnp.float32),
            pltpu.VMEM((tokens, 128), jnp.float32),
            pltpu.VMEM((width, 3 * local), jnp.bfloat16),
            pltpu.SemaphoreType.DMA((blocks,)),
            pltpu.SemaphoreType.DMA((blocks,)),
        ],
        compiler_params=pltpu.CompilerParams(
            collective_id=2, has_side_effects=True, vmem_limit_bytes=48 * 2**20
        ),
        cost_estimate=pl.CostEstimate(
            flops=12 * 10**9, bytes_accessed=2 * 10**7, transcendentals=0
        ),
        name="box_forward",
    )(
        feature_map,
        info,
        embeddings,
        roi_proj,
        attn_norm.reshape(1, -1),
        query_proj,
        key_proj,
        value_proj,
    )


def middle_kernel(
    context_ref,
    stream_hbm,
    cotangent_hbm,
    output_ref,
    norm_ref,
    up_hbm,
    down_hbm,
    layer_hbm,
    grad_middle_hbm,
    grad_context_hbm,
    grad_up_hbm,
    grad_down_hbm,
    grad_output_ref,
    grad_norm_ref,
    middle,
    cotangent,
    up,
    down,
    part,
    other,
    part_out,
    other_out,
    other_grad,
    ffn_in,
    hidden,
    grad_pre,
    staged,
    grad_low,
    layer_low,
    grad_context,
    load_sem,
    store_sem,
    grad_sem,
    send_sem,
    recv_sem,
):
    greet_partner()
    tokens, width = stream_hbm.shape
    units = up_hbm.shape[1]
    blocks = tokens // ROWS
    loads = [
        pltpu.make_async_copy(source, target, load_sem.at[index])
        for index, (source, target) in enumerate(
            [(cotangent_hbm, cotangent), (down_hbm, down), (stream_hbm, middle), (up_hbm, up)]
        )
    ]
    for load in loads:
        load.start()
    attn_copies = []
    for block in range(blocks):
        at = slice(block * ROWS, (block + 1) * ROWS)
        part[at, :] = dot_plain(context_ref[at, :], output_ref[...])
        if block == 0:
            pl.semaphore_wait(pltpu.get_barrier_semaphore(), 1)
        copy = partner_copy(
            part.at[pl.ds(block * ROWS, ROWS)],
            other.at[pl.ds(block * ROWS, ROWS)],
            send_sem.at[0, block],
            recv_sem.at[0, block],
        )
        copy.start()
        attn_copies.append(copy)
    for load in loads:
        load.wait()
    out_copies = []
    grad_copies = []
    for block in range(blocks):
        at = slice(block * ROWS, (block + 1) * ROWS)
        grad_hidden = dot_last(cotangent[at, :], down[...])
        attn_copies[block].wait()
        values = middle[at, :] + (part[at, :] + other[at, :])
        middle[at, :] = values
        inner = (values * inverse_rms(values) * norm_ref[...]).astype(jnp.bfloat16)
        ffn_in[at, :] = inner
        pre_act = dot_plain(inner, up[...])
        below = 0.5 * (1.0 + lax.erf(pre_act * (0.5**0.5)))
        density = jnp.exp(-0.5 * (pre_act * pre_act)) * 0.3989422804014327
        hidden[at, :] = (pre_act * below).astype(jnp.bfloat16)
        grad_pre[at, :] = (grad_hidden * (below + pre_act * density)).astype(jnp.bfloat16)
        part[at, :] = dot_last(grad_pre[at, :], up[...])
        copy = partner_copy(
            part.at[pl.ds(block * ROWS, ROWS)],
            other_grad.at[pl.ds(block * ROWS, ROWS)],
            send_sem.at[1, block],
            recv_sem.at[1, block],
        )
        copy.start()
        grad_copies.append(copy)
        part_out[at, :] = dot_plain(hidden[at, :], down[...])
        copy = partner_copy(
            part_out.at[pl.ds(block * ROWS, ROWS)],
            other_out.at[pl.ds(block * ROWS, ROWS)],
            send_sem.at[2, block],
            recv_sem.at[2, block],
        )
        copy.start()
        out_copies.append(copy)
    half = width // 2
    stores = []
    for index in range(4):
        rows = slice((index % 2) * half, (index % 2 + 1) * half)
        if index >= 2:
            stores[index - 2].wait()
        if index < 2:
            staged[index % 2] = dot_rows(ffn_in[:, rows], grad_pre[...])
            target = grad_up_hbm
        else:
            staged[index % 2] = dot_rows(cotangent[:, rows], hidden[...])
            target = grad_down_hbm
        store = pltpu.make_async_copy(
            staged.at[index % 2], target.at[pl.ds((index % 2) * half, half)], grad_sem.at[index]
        )
        store.start()
        stores.append(store)
    norm_total = jnp.zeros((8, width), jnp.float32)
    for block in range(blocks):
        at = slice(block * ROWS, (block + 1) * ROWS)
        values = middle[at, :]
        inverse = inverse_rms(values)
        hat = values * inverse
        grad_copies[block].wait()
        grad_inner = part[at, :] + other_grad[at, :]
        norm_total = norm_total + jnp.sum((grad_inner * hat).reshape(ROWS // 8, 8, width), axis=0)
        scaled = grad_inner * norm_ref[...]
        back = inverse * (scaled - hat * jnp.mean(scaled * hat, axis=1, keepdims=True))
        grad_values = cotangent[at, :].astype(jnp.float32) + back
        out_copies[block].wait()
        layer_low[at, :] = (values + (part_out[at, :] + other_out[at, :])).astype(jnp.bfloat16)
        middle[at, :] = grad_values
        low = grad_values.astype(jnp.bfloat16)
        grad_low[at, :] = low
        grad_context[at, :] = dot_last(low, output_ref[...]).astype(jnp.bfloat16)
        for index, (source, target) in enumerate(
            [
                (layer_low, layer_hbm),
                (middle, grad_middle_hbm),
                (grad_context, grad_context_hbm),
            ]
        ):
            rows = pl.ds(block * ROWS, ROWS)
            store = pltpu.make_async_copy(
                source.at[rows], target.at[rows], store_sem.at[index, block]
            )
            store.start()
            stores.append(store)
    grad_norm_ref[...] = jnp.sum(norm_total, axis=0, keepdims=True)
    grad_output_ref[...] = dot_rows(grad_low[...], context_ref[...])
    for store in stores[2:]:
        store.wait()


def middle_layer(context, stream, cotangent, output_proj, ffn_norm, up_proj, down_proj):
    tokens, width = stream.shape
    units = up_proj.shape[1]
    local = context.shape[1]
    blocks = tokens // ROWS
    whole = pl.BlockSpec(memory_space=pltpu.VMEM)
    far = pl.BlockSpec(memory_space=pl.ANY)
    wide_sum = pltpu.VMEM((tokens, width), jnp.float32)
    wide_low = pltpu.VMEM((tokens, width), jnp.bfloat16)
    unit_low = pltpu.VMEM((tokens, units), jnp.bfloat16)
    return pl.pallas_call(
        middle_kernel,
        out_shape=(
            jax.ShapeDtypeStruct((tokens, width), jnp.bfloat16),
            jax.ShapeDtypeStruct((tokens, width), jnp.float32),
            jax.ShapeDtypeStruct((tokens, local), jnp.bfloat16),
            jax.ShapeDtypeStruct((width, units), jnp.float32),
            jax.ShapeDtypeStruct((width, units), jnp.float32),
            jax.ShapeDtypeStruct((width, local), jnp.float32),
            jax.ShapeDtypeStruct((1, width), jnp.float32),
        ),
        in_specs=[whole, far, far, whole, whole, far, far],
        out_specs=(far, far, far, far, far, whole, whole),
        scratch_shapes=[
            wide_sum,
            wide_low,
            pltpu.VMEM((width, units), jnp.bfloat16),
            pltpu.VMEM((units, width), jnp.bfloat16),
            wide_sum,
            wide_sum,
            wide_sum,
            wide_sum,
            wide_sum,
            wide_low,
            unit_low,
            unit_low,
            pltpu.VMEM((2, width // 2, units), jnp.float32),
            wide_low,
            wide_low,
            pltpu.VMEM((tokens, local), jnp.bfloat16),
            pltpu.SemaphoreType.DMA((4,)),
            pltpu.SemaphoreType.DMA((3, blocks)),
            pltpu.SemaphoreType.DMA((4,)),
            pltpu.SemaphoreType.DMA((3, blocks)),
            pltpu.SemaphoreType.DMA((3, blocks)),
        ],
        compiler_params=pltpu.CompilerParams(
            collective_id=3, has_side_effects=True, vmem_limit_bytes=60 * 2**20
        ),
        cost_estimate=pl.CostEstimate(
            flops=32 * 10**9, bytes_accessed=2 * 10**7, transcendentals=0
        ),
        name="middle_layer",
    )(context, stream, cotangent, output_proj, ffn_norm.reshape(1, -1), up_proj, down_proj)


def end_kernel(
    grad_query_ref,
    grad_key_ref,
    grad_value_ref,
    query_proj_ref,
    key_proj_ref,
    value_proj_ref,
    input_ref,
    stream_hbm,
    grad_middle_hbm,
    norm_ref,
    roi_ref,
    pooled_ref,
    info_ref,
    boxes_ref,
    grad_output_ref,
    first_hbm,
    grad_stream_hbm,
    grad_heads_hbm,
    second_hbm,
    grad_roi_ref,
    grad_map_ref,
    grad_norm_ref,
    grad_heads,
    projections,
    stream,
    grad_stream,
    part,
    other,
    weight_grad,
    grad_low,
    grad_box,
    first,
    arrived,
    second,
    load_sem,
    store_sem,
    grad_sem,
    send_sem,
    recv_sem,
    scatter_send,
    scatter_recv,
):
    scatter = Scatter(scatter_send, scatter_recv)
    greet_partner()
    greet_rows((scatter.across_x, scatter.across_y))
    first_load = pltpu.make_async_copy(first_hbm, first, load_sem.at[2])
    first_load.start()
    tokens, width = stream_hbm.shape
    local = grad_query_ref.shape[1]
    blocks = tokens // ROWS
    loads = [
        pltpu.make_async_copy(stream_hbm, stream, load_sem.at[0]),
        pltpu.make_async_copy(grad_middle_hbm, grad_stream, load_sem.at[1]),
    ]
    for load in loads:
        load.start()
    for index, (grad, proj) in enumerate(
        (
            (grad_query_ref, query_proj_ref),
            (grad_key_ref, key_proj_ref),
            (grad_value_ref, value_proj_ref),
        )
    ):
        columns = slice(index * local, (index + 1) * local)
        grad_heads[:, columns] = grad[...]
        projections[:, columns] = proj[...]
    copies = []
    for block in range(blocks):
        at = slice(block * ROWS, (block + 1) * ROWS)
        part[at, :] = dot_last(grad_heads[at, :], projections[...])
        if block == 0:
            pl.semaphore_wait(pltpu.get_barrier_semaphore(), 3)
            scatter.send_second(first_hbm, arrived, 0, 1)
        copy = partner_copy(
            part.at[pl.ds(block * ROWS, ROWS)],
            other.at[pl.ds(block * ROWS, ROWS)],
            send_sem.at[block],
            recv_sem.at[block],
        )
        copy.start()
        copies.append(copy)
    weight_grad[:, : 3 * local] = dot_rows(input_ref[...], grad_heads[...])
    weight_grad[:, 3 * local :] = grad_output_ref[...]
    weight_store = pltpu.make_async_copy(weight_grad, grad_heads_hbm, grad_sem)
    weight_store.start()
    for load in loads:
        load.wait()
    stores = []
    norm_total = jnp.zeros((8, width), jnp.float32)
    for block in range(blocks):
        at = slice(block * ROWS, (block + 1) * ROWS)
        values = stream[at, :]
        inverse = inverse_rms(values)
        hat = values * inverse
        copies[block].wait()
        grad_inner = part[at, :] + other[at, :]
        norm_total = norm_total + jnp.sum((grad_inner * hat).reshape(ROWS // 8, 8, width), axis=0)
        scaled = grad_inner * norm_ref[...]
        back = inverse * (scaled - hat * jnp.mean(scaled * hat, axis=1, keepdims=True))
        grad_values = grad_stream[at, :] + back
        grad_stream[at, :] = grad_values
        rows = pl.ds(block * ROWS, ROWS)
        store = pltpu.make_async_copy(
            grad_stream.at[rows], grad_stream_hbm.at[rows], store_sem.at[block]
        )
        store.start()
        stores.append(store)
        low = grad_values.astype(jnp.bfloat16)
        grad_low[at, :] = low
        area = (info_ref[at, 5:6] - info_ref[at, 1:2]) * (info_ref[at, 4:5] - info_ref[at, 0:1])
        grad_box[at, :] = split_two(dot_last(low, roi_ref[...]) / area.astype(jnp.float32))
    grad_norm_ref[...] = jnp.sum(norm_total, axis=0, keepdims=True)
    tile_rows = grad_map_ref.shape[0] // 128
    first_row = lax.axis_index("tensor") * tile_rows
    column = lax.broadcasted_iota(jnp.int32, (128, tokens), 0)
    inside = jnp.where(
        (column >= boxes_ref[0:1, :]) & (column < boxes_ref[2:3, :]), 1.0, 0.0
    ).astype(jnp.bfloat16)
    top = boxes_ref[1:2, :] - first_row
    bottom = boxes_ref[3:4, :] - first_row
    for row in range(tile_rows):
        chosen = jnp.where((top <= row) & (bottom > row), 1.0, 0.0).astype(jnp.bfloat16)
        sums = dot_plain(inside * chosen, grad_box[...])
        grad_map_ref[row * 128 : (row + 1) * 128, :] = sums[:, :128] + sums[:, 128:]
    grad_roi_ref[...] = dot_rows(grad_low[...], pooled_ref[...])
    first_load.wait()
    scatter.add_second(first, arrived, second)
    second_store = pltpu.make_async_copy(second, second_hbm, load_sem.at[2])
    second_store.start()
    scatter.sent(second=arrived)
    second_store.wait()
    weight_store.wait()
    for store in stores:
        store.wait()


def end_layer(
    grad_heads,
    projections,
    attn_in,
    stream,
    grad_middle,
    attn_norm,
    roi_proj,
    pooled,
    info,
    boxes,
    grad_output,
    first,
    pixels,
):
    tokens, width = stream.shape
    local = grad_heads[0].shape[1]
    blocks = tokens // ROWS
    whole = pl.BlockSpec(memory_space=pltpu.VMEM)
    far = pl.BlockSpec(memory_space=pl.ANY)
    wide_sum = pltpu.VMEM((tokens, width), jnp.float32)
    _, depths, _, rows, half = first.shape
    total = (depths, rows, 2 * half)
    return pl.pallas_call(
        end_kernel,
        out_shape=(
            jax.ShapeDtypeStruct((tokens, width), jnp.float32),
            jax.ShapeDtypeStruct((width, 4 * local), jnp.float32),
            jax.ShapeDtypeStruct(total, jnp.float32),
            jax.ShapeDtypeStruct((width, 128), jnp.float32),
            jax.ShapeDtypeStruct((pixels, 128), jnp.float32),
            jax.ShapeDtypeStruct((1, width), jnp.float32),
        ),
        in_specs=[whole] * 7 + [far, far] + [whole] * 6 + [far],
        out_specs=(far, far, far, whole, whole, whole),
        scratch_shapes=[
            pltpu.VMEM((tokens, 3 * local), jnp.bfloat16),
            pltpu.VMEM((width, 3 * local), jnp.bfloat16),
            wide_sum,
            wide_sum,
            wide_sum,
            wide_sum,
            pltpu.VMEM((width, 4 * local), jnp.float32),
            pltpu.VMEM((tokens, width), jnp.bfloat16),
            pltpu.VMEM((tokens, 256), jnp.bfloat16),
            pltpu.VMEM(first.shape, jnp.float32),
            pltpu.VMEM((2, depths, rows, half), jnp.float32),
            pltpu.VMEM(total, jnp.float32),
            pltpu.SemaphoreType.DMA((3,)),
            pltpu.SemaphoreType.DMA((blocks,)),
            pltpu.SemaphoreType.DMA,
            pltpu.SemaphoreType.DMA((blocks,)),
            pltpu.SemaphoreType.DMA((blocks,)),
            *scatter_semaphores(4),
        ],
        compiler_params=pltpu.CompilerParams(
            collective_id=4, has_side_effects=True, vmem_limit_bytes=56 * 2**20
        ),
        cost_estimate=pl.CostEstimate(
            flops=15 * 10**9, bytes_accessed=2 * 10**7, transcendentals=0
        ),
        name="end_layer",
    )(
        *grad_heads,
        *projections,
        attn_in,
        stream,
        grad_middle,
        attn_norm.reshape(1, -1),
        roi_proj,
        pooled,
        info,
        boxes,
        grad_output,
        first,
    )


def on_device(
    page_image,
    embeddings,
    cotangent,
    doc_ids,
    pad_mask,
    token_boxes,
    conv_first,
    conv_weights,
    group_gain,
    group_shift,
    roi_proj,
    attn_norm,
    query_proj,
    key_proj,
    value_proj,
    output_proj,
    bias_tables,
    ffn_norm,
    up_proj,
    down_proj,
):
    devices = lax.axis_size("dp") * lax.axis_size("tensor")
    feature_map, *records = stem_forward(
        page_image, conv_first, conv_weights, group_gain, group_shift, devices
    )
    left_edge, top_edge, right_edge, bottom_edge = token_boxes[:, 0]
    blank = jnp.zeros_like(left_edge)
    info = jnp.stack(
        [left_edge, top_edge, doc_ids[0], pad_mask[0], right_edge, bottom_edge, blank, blank],
        axis=1,
    )
    pooled, stream, attn_in, heads = box_forward(
        feature_map, info, embeddings, roi_proj, attn_norm, query_proj, key_proj, value_proj
    )
    context, exact, lse = attention_forward(bias_tables, info, heads)
    layer_out, grad_middle, grad_context, grad_up, grad_down, grad_output, grad_ffn_norm = (
        middle_layer(context, stream, cotangent, output_proj, ffn_norm, up_proj, down_proj)
    )
    rows_count = lax.axis_size("dp")
    width = stream.shape[1]
    own_rows = width // rows_count

    def by_place(values):
        return values.reshape(rows_count // 4, 2, 2, own_rows, values.shape[1])

    *grad_heads, diagonals, down_first = attention_backward(
        bias_tables, info, heads, grad_context, exact, lse, by_place(grad_down)
    )
    grad_tables = bucket_grads(diagonals)
    grad_stream, grad_attn, down_second, grad_roi, grad_map, grad_attn_norm = end_layer(
        grad_heads,
        (query_proj, key_proj, value_proj),
        attn_in,
        stream,
        grad_middle,
        attn_norm,
        roi_proj,
        pooled,
        info,
        token_boxes[:, 0],
        grad_output,
        down_first,
        feature_map.shape[0],
    )
    local_heads = grad_tables.shape[2]
    small = jnp.concatenate([grad_attn_norm[0], grad_ffn_norm[0], grad_tables.reshape(-1)])
    small = jnp.pad(small, (0, -small.shape[0] % 1024)).reshape(-1, 128)
    split = grad_roi.reshape(rows_count, 2, own_rows // 2, grad_roi.shape[1])
    (
        grad_first,
        grad_convs,
        grad_gains,
        grad_offsets,
        own_roi,
        small,
        own_up,
        own_attn,
        own_down,
    ) = stem_backward(
        grad_map,
        page_image,
        records,
        conv_weights,
        group_gain,
        group_shift,
        split,
        small,
        by_place(grad_up),
        by_place(grad_attn),
        down_second,
        devices,
    )
    small = small.reshape(-1)
    start = lax.axis_index("dp") * own_rows
    own_attn_norm = lax.dynamic_slice(small, (start,), (own_rows,))
    own_ffn_norm = lax.dynamic_slice(small, (width + start,), (own_rows,))
    own_tables = small[2 * width : 2 * width + grad_tables.size].reshape(3, NBUCKET, local_heads)
    part = query_proj.shape[1]
    return (
        layer_out,
        grad_stream,
        grad_first,
        grad_convs,
        grad_gains,
        grad_offsets,
        own_roi.reshape(own_rows, -1).T,
        own_attn_norm,
        own_attn[:, :part],
        own_attn[:, part : 2 * part],
        own_attn[:, 2 * part : 3 * part],
        own_attn[:, 3 * part :].T,
        own_tables,
        own_ffn_norm,
        own_up,
        own_down.T,
    )


def solution(mesh):
    placed = (
        P(None, ("dp", "tensor"), None),
        P("dp", None),
        P("dp", None),
        P("dp", None),
        P("dp", None),
        P(None, "dp", None),
        P(),
        P(),
        P(),
        P(),
        P(),
        P(),
        P(None, "tensor"),
        P(None, "tensor"),
        P(None, "tensor"),
        P("tensor", None),
        P(None, None, "tensor"),
        P(),
        P(None, "tensor"),
        P("tensor", None),
    )
    return jax.shard_map(
        on_device,
        mesh=mesh,
        in_specs=placed,
        out_specs=(
            P("dp", None),
            P("dp", None),
            P(),
            P(),
            P(),
            P(),
            P(None, "dp"),
            P("dp"),
            P("dp", "tensor"),
            P("dp", "tensor"),
            P("dp", "tensor"),
            P("tensor", "dp"),
            P(None, None, "tensor"),
            P("dp"),
            P("dp", "tensor"),
            P("tensor", "dp"),
        ),
        check_vma=False,
    )
```

```python
import functools

import jax
import jax.numpy as jnp
import numpy as np
from jax import lax
from jax.experimental import pallas as pl
from jax.experimental.pallas import tpu as pltpu
from jax.sharding import PartitionSpec as P

HDIM = 64
NBUCKET = 32
VMEM_LIMIT = 63 * 2**20
GROUPS = 32


bucket_edges = (12, 16, 23, 32, 46, 64, 91)
norm_eps = 1e-06
group_eps = 1e-05
masked_score = -1e30
highest = lax.Precision.HIGHEST


def bucket_of(relative):
    magnitude = jnp.abs(relative)
    coarse = jnp.full(relative.shape, 8, jnp.int32)
    for edge in bucket_edges:
        coarse = coarse + (magnitude >= edge).astype(jnp.int32)
    return jnp.where(magnitude < 8, magnitude, coarse) + jnp.where(relative > 0, 16, 0).astype(
        jnp.int32
    )


MESH = pl.DeviceIdType.MESH
LAYERS = 9
PIX_CHUNK = 256


def level_of(layer):
    return layer if layer <= 4 else 8 - layer


def stem_rows(pixels):
    return [pixels >> (2 * level_of(layer)) for layer in range(LAYERS)]


def row_starts(rows):
    starts = [0]
    for count in rows:
        starts.append(starts[-1] + count)
    return starts


def split_two(values):
    high = values.astype(jnp.bfloat16)
    low = (values - high.astype(jnp.float32)).astype(jnp.bfloat16)
    return jnp.concatenate([high, low], axis=1)


def group_sum(values):
    lane = lax.broadcasted_iota(jnp.int32, values.shape, 1)
    pairs = values + jnp.where(
        lane % 2 == 0, pltpu.roll(values, 127, 1), pltpu.roll(values, 1, 1)
    )
    return pairs + jnp.where(
        (lane // 2) % 2 == 0, pltpu.roll(pairs, 126, 1), pltpu.roll(pairs, 2, 1)
    )


def wide(row):
    return jnp.broadcast_to(row, (8, row.shape[1]))


def my_index():
    return lax.axis_index("dp") * 2 + lax.axis_index("tensor")


def greet_all(count):
    barrier = pltpu.get_barrier_semaphore()
    me = my_index()

    def greet(step, carry):
        other = lax.rem(me + step, count)
        pl.semaphore_signal(
            barrier, inc=1, device_id=(other // 2, lax.rem(other, 2)), device_id_type=MESH
        )
        return carry

    lax.fori_loop(1, count, greet, 0)


def greeted(count):
    pl.semaphore_wait(pltpu.get_barrier_semaphore(), count - 1)


def send_all(count, source, target, send_sem, recv_sem):
    me = my_index()

    def send(step, carry):
        other = lax.rem(me + step, count)
        pltpu.make_async_remote_copy(
            src_ref=source,
            dst_ref=target,
            send_sem=send_sem,
            recv_sem=recv_sem,
            device_id=(other // 2, lax.rem(other, 2)),
            device_id_type=MESH,
        ).start()
        return carry

    lax.fori_loop(1, count, send, 0, unroll=count <= 32)


def wait_all(count, slots, sem):
    part = slots.at[pl.ds(0, count - 1)]
    pltpu.make_async_copy(part, part, sem).wait()


def natural_places(tile_rows, columns):
    spacing = columns // 8
    places = []
    for row in range(tile_rows):
        for col in range(spacing):
            place = 0
            for bit in range(4):
                place = place * 4 + ((row >> bit) & 1) * 2 + ((col >> bit) & 1)
            places.append((row * columns + col, place * 8))
    return places


SCHEDULE = {
    8: 'u1b v1a d3a',
    7: 'v1b d3b small',
    6: 'u2 e3a split',
    5: 'a1a e3b',
    4: 'a1b v2 u3a',
    3: 'u3b b1a rows',
    2: 'v3a b1b',
    1: 'v3b a2 kept',
    0: 'a3a b2',
    'end': 'a3b',
    'last': 'b3a b3b',
}


def place_of(row):
    return row // 4, lax.rem(row // 2, 2), lax.rem(row, 2)


def start_remote(source, target, send_sem, recv_sem, row):
    pltpu.make_async_remote_copy(
        src_ref=source,
        dst_ref=target,
        send_sem=send_sem,
        recv_sem=recv_sem,
        device_id=(row, lax.axis_index("tensor")),
        device_id_type=MESH,
    ).start()


def await_bytes(buffer, sem):
    pltpu.make_async_copy(buffer, buffer, sem).wait()


def greet_rows(rows):
    for row in rows:
        pl.semaphore_signal(
            pltpu.get_barrier_semaphore(),
            inc=1,
            device_id=(row, lax.axis_index("tensor")),
            device_id_type=MESH,
        )


class Scatter:
    def __init__(self, width, left, send_sem, recv_sem):
        self.row = lax.axis_index("dp")
        self.z, self.y, self.x = place_of(self.row)
        self.across_x = self.row + 1 - 2 * self.x
        self.across_y = self.row + 2 - 4 * self.y
        self.width, self.left = width, left
        self.send_sem, self.recv_sem = send_sem, recv_sem

    def columns(self, source):
        half = source.shape[-1] // 2
        return pl.ds(self.left, self.width), pl.ds(half + self.left, self.width)

    def own_loads(self, source, own, sem):
        first, second = self.columns(source)
        return [
            pltpu.make_async_copy(source.at[:, :, self.x, :, first], own.at[0], sem.at[0]),
            pltpu.make_async_copy(source.at[:, self.y, :, :, second], own.at[1], sem.at[1]),
        ]

    def send_first(self, source, target, begin, size, shift=0):
        first, second = self.columns(source)
        depth = pl.ds(begin, size)
        landing = pl.ds(begin - shift, size)
        start_remote(
            source.at[depth, :, 1 - self.x, :, first],
            target.at[0, landing],
            self.send_sem.at[0],
            self.recv_sem.at[0],
            self.across_x,
        )
        start_remote(
            source.at[depth, 1 - self.y, :, :, second],
            target.at[1, landing],
            self.send_sem.at[1],
            self.recv_sem.at[1],
            self.across_y,
        )

    def await_first(self, landed):
        for side in range(2):
            await_bytes(landed.at[side], self.recv_sem.at[side])

    def sent_first(self, landed):
        for side in range(2):
            await_bytes(landed.at[side], self.send_sem.at[side])

    def send_second(self, source, target):
        start_remote(
            source.at[0, :, 1 - self.y],
            target.at[0],
            self.send_sem.at[2],
            self.recv_sem.at[2],
            self.across_y,
        )
        start_remote(
            source.at[1, :, 1 - self.x],
            target.at[1],
            self.send_sem.at[3],
            self.recv_sem.at[3],
            self.across_x,
        )

    def await_second(self, landed):
        for side in range(2):
            await_bytes(landed.at[side], self.recv_sem.at[2 + side])

    def sent_second(self, landed):
        for side in range(2):
            await_bytes(landed.at[side], self.send_sem.at[2 + side])

    def along_z(self, total, target, step):
        depths = total.shape[1]
        begins = [0]
        for index in range(step):
            begins.append(begins[-1] + (depths >> (index + 1)))
        bit = lax.rem(self.z // (1 << step), 2)
        if step == 0:
            return total, 0, begins[0], depths >> 1, bit
        return target, begins[step - 1], begins[step], depths >> (step + 1), bit

    def send_along(self, total, target, step):
        source, begin, landing, blocks, bit = self.along_z(total, target, step)
        other = self.row + (1 - 2 * bit) * (4 << step)
        for block in range(blocks):
            start_remote(
                source.at[:, begin + 2 * block + 1 - bit],
                target.at[:, landing + block],
                self.send_sem.at[4 + step],
                self.recv_sem.at[4 + step],
                other,
            )

    def add_along(self, total, target, step):
        source, begin, landing, blocks, bit = self.along_z(total, target, step)
        await_bytes(target.at[:, pl.ds(landing, blocks)], self.recv_sem.at[4 + step])
        for side in range(2):
            for block in range(blocks):
                target[side, landing + block] = (
                    target[side, landing + block] + source[side, begin + 2 * block + bit]
                )

    def finish(self, total, target, result, base, step):
        steps = z_steps(total.shape[1])
        for index in range(step, steps):
            if index > step:
                self.send_along(total, target, index)
            self.add_along(total, target, index)
        landing = self.along_z(total, target, steps - 1)[2]
        half = result.shape[-1] // 2
        for side in range(2):
            at = side * half + self.left
            result[base, :, at : at + self.width] = target[side, landing]

    def sent_along(self, total, target):
        for step in range(z_steps(total.shape[1])):
            _, _, landing, blocks, _ = self.along_z(total, target, step)
            await_bytes(target.at[:, pl.ds(landing, blocks)], self.send_sem.at[4 + step])


def z_steps(depths):
    return depths.bit_length() - 1


def add_pairs(left, right):
    for side in range(left.shape[0]):
        for depth in range(left.shape[1]):
            left[side, depth] = left[side, depth] + right[side, depth]


def scatter_semaphores(copies):
    return [pltpu.SemaphoreType.DMA((copies,)), pltpu.SemaphoreType.DMA((copies,))]


class ScatterHere(Scatter):
    refs = 8

    @staticmethod
    def scratch(depths, rows, width):
        pair = pltpu.VMEM((2, depths, 2, rows, width), jnp.float32)
        one = pltpu.VMEM((2, depths, rows, width), jnp.float32)
        return [pair, pair, one, one, one, pltpu.SemaphoreType.DMA((2,)), *scatter_semaphores(4 + z_steps(depths))]

    def __init__(self, source, left, refs):
        self.source = source
        self.own, self.first, self.second, self.total, self.third, load_sem, send, recv = refs
        super().__init__(self.own.shape[-1], left, send, recv)
        self.loads = self.own_loads(source, self.own, load_sem)
        for load in self.loads:
            load.start()

    def start_first(self, part):
        size = self.own.shape[1] // 2
        self.send_first(self.source, self.first, part * size, size)

    def start_second(self, landed=None):
        for load in self.loads:
            load.wait()
        self.await_first(self.first if landed is None else landed)
        add_pairs(self.own, self.first)
        self.send_second(self.own, self.second)

    def add_second(self):
        self.await_second(self.second)
        for side in range(2):
            kept = self.y if side == 0 else self.x
            for depth in range(self.total.shape[1]):
                self.total[side, depth] = self.own[side, depth, kept] + self.second[side, depth]

    def third_first(self):
        self.add_second()
        self.send_along(self.total, self.third, 0)

    def third_next(self):
        self.add_along(self.total, self.third, 0)
        self.send_along(self.total, self.third, 1)

    def end(self, result, base):
        self.finish(self.total, self.third, result, base, 1)

    def sent(self, landed=None):
        self.sent_first(self.first if landed is None else landed)
        self.sent_second(self.second)
        self.sent_along(self.total, self.third)


class ScatterRest(Scatter):
    refs = 6

    @staticmethod
    def scratch(depths, rows, width):
        one = pltpu.VMEM((2, depths, rows, width), jnp.float32)
        return [one, one, one, pltpu.SemaphoreType.DMA((2,)), *scatter_semaphores(4 + z_steps(depths))]

    def __init__(self, kept, arrived, left, refs):
        self.total, self.second, self.third, load_sem, send, recv = refs
        width = self.total.shape[-1]
        super().__init__(width, left, send, recv)
        columns = pl.ds(left, width)
        self.loads = [
            pltpu.make_async_copy(kept.at[:, :, :, columns], self.total, load_sem.at[0]),
            pltpu.make_async_copy(arrived.at[:, :, :, columns], self.second, load_sem.at[1]),
        ]
        for load in self.loads:
            load.start()

    def third_first(self):
        for load in self.loads:
            load.wait()
        add_pairs(self.total, self.second)
        self.send_along(self.total, self.third, 0)

    third_next = ScatterHere.third_next
    end = ScatterHere.end

    def sent(self):
        self.sent_along(self.total, self.third)


def stem_forward_kernel(
    count,
    places,
    image_ref,
    first_ref,
    weights_ref,
    gain_ref,
    shift_ref,
    feature_ref,
    norm_hbm,
    input_hbm,
    scale_ref,
    norm_ref,
    input_ref,
    natural,
    skip,
    current,
    source,
    slots,
    send_sem,
    recv_sem,
    store_sem,
):
    me = my_index()
    greet_all(count)
    pixels = feature_ref.shape[0]
    rows = stem_rows(pixels)
    norm_at = row_starts(rows)
    input_at = row_starts(rows[1:])
    skip_at = row_starts(rows[:4])
    spacing = 16
    for row in range(image_ref.shape[1]):
        natural[row * 128 : (row + 1) * 128, :] = lax.dot_general(
            image_ref[:, row, :],
            first_ref[...],
            (((0,), (0,)), ((), ())),
            preferred_element_type=jnp.float32,
        )
    for start, place in places:
        norm_ref[place : place + 8, :] = natural[pl.ds(start, 8, stride=spacing), :]
    stores = []
    for layer in range(LAYERS):
        height = rows[layer]
        chunk = min(height, PIX_CHUNK)
        base = norm_at[layer]
        total = jnp.zeros((8, 128), jnp.float32)
        if layer > 0:
            weights = weights_ref[layer - 1]
            stacked = jnp.concatenate([weights, weights], axis=0)

            def convolve(index, total):
                at = pl.multiple_of(index * chunk, chunk)
                values = jnp.dot(
                    split_two(input_ref[pl.ds(input_at[layer - 1] + at, chunk), :]),
                    stacked,
                    preferred_element_type=jnp.float32,
                )
                norm_ref[pl.ds(base + at, chunk), :] = values
                return total + jnp.sum(values.reshape(chunk // 8, 8, 128), axis=0)

        else:

            def convolve(index, total):
                at = pl.multiple_of(index * chunk, chunk)
                values = norm_ref[pl.ds(base + at, chunk), :]
                return total + jnp.sum(values.reshape(chunk // 8, 8, 128), axis=0)

        total = lax.fori_loop(0, height // chunk, convolve, total)
        mean = jnp.sum(total, axis=0, keepdims=True) * (1.0 / height)

        def deviate(index, total):
            at = pl.multiple_of(index * chunk, chunk)
            values = norm_ref[pl.ds(base + at, chunk), :] - mean
            return total + jnp.sum((values * values).reshape(chunk // 8, 8, 128), axis=0)

        square = lax.fori_loop(0, height // chunk, deviate, jnp.zeros((8, 128), jnp.float32))
        square = jnp.sum(square, axis=0, keepdims=True)
        stats = jnp.concatenate([mean, square], axis=0)
        source[layer] = stats
        slots[layer, me] = stats
        if layer == 0:
            greeted(count)
        send_all(
            count,
            source.at[layer],
            slots.at[layer, me],
            send_sem.at[layer],
            recv_sem.at[layer],
        )
        wait_all(count, slots.at[layer], recv_sem.at[layer])
        means = slots[layer, :, 0, :]
        centre = group_sum(wide(jnp.sum(means, axis=0, keepdims=True))) * (0.25 / count)
        apart = means - centre[0:1]
        spread = jnp.sum(slots[layer, :, 1, :], axis=0, keepdims=True) + height * jnp.sum(
            apart * apart, axis=0, keepdims=True
        )
        variance = group_sum(wide(spread)) * (1.0 / (4 * height * count))
        inverse = lax.rsqrt(variance + group_eps)[0:1]
        centre = centre[0:1]
        scale_ref[layer : layer + 1, :] = inverse
        gain = gain_ref[layer : layer + 1, :]
        shift = shift_ref[layer : layer + 1, :]

        def activate(start, size):
            normed = (norm_ref[pl.ds(base + start, size), :] - centre) * inverse
            norm_ref[pl.ds(base + start, size), :] = normed
            lifted = normed * gain + shift
            return lifted / (1.0 + jnp.exp(-lifted))

        if layer < 4:
            quarter = height // 4
            part = min(quarter, 64)

            def pool(index, carry):
                at = pl.multiple_of(index * part, part)
                mean_of = jnp.zeros((part, 128), jnp.float32)
                for corner in range(4):
                    value = activate(corner * quarter + at, part)
                    skip[pl.ds(skip_at[layer] + corner * quarter + at, part), :] = value
                    mean_of = mean_of + value
                input_ref[pl.ds(input_at[layer] + at, part), :] = mean_of * 0.25
                return carry

            lax.fori_loop(0, quarter // part, pool, 0)
        elif layer < 8:
            part = min(height, 64)
            skipped = skip_at[7 - layer]

            def grow(index, carry):
                at = pl.multiple_of(index * part, part)
                value = activate(at, part)
                for corner in range(4):
                    place = corner * height + at
                    input_ref[pl.ds(input_at[layer] + place, part), :] = (
                        value + skip[pl.ds(skipped + place, part), :]
                    )
                return carry

            lax.fori_loop(0, height // part, grow, 0)
        else:

            def finish(index, carry):
                at = pl.multiple_of(index * chunk, chunk)
                current[pl.ds(at, chunk), :] = activate(at, chunk)
                return carry

            lax.fori_loop(0, height // chunk, finish, 0)
        parts = [(norm_ref, norm_hbm, base, height)]
        if layer < 8:
            parts.append((input_ref, input_hbm, input_at[layer], rows[layer + 1]))
        for index, (source_ref, target, begin, size) in enumerate(parts):
            store = pltpu.make_async_copy(
                source_ref.at[pl.ds(begin, size)],
                target.at[pl.ds(begin, size)],
                store_sem.at[index, layer],
            )
            store.start()
            stores.append(store)
    for start, place in places:
        feature_ref[pl.ds(start, 8, stride=spacing), :] = current[place : place + 8, :]
    for layer in range(LAYERS):
        wait_all(count, slots.at[layer], send_sem.at[layer])
    for store in stores:
        store.wait()


def stem_backward_kernel(
    count,
    places,
    grad_ref,
    image_ref,
    norm_hbm,
    input_hbm,
    scale_ref,
    weights_ref,
    gain_ref,
    shift_ref,
    split_ref,
    attn_norm_ref,
    ffn_norm_ref,
    tables_ref,
    up_ref,
    attn_ref,
    kept_ref,
    second_ref,
    early_ref,
    small_out,
    large_out,
    norm_ref,
    input_ref,
    natural,
    ordered,
    active,
    grad_conv,
    skip,
    grads,
    product,
    source,
    slots,
    first_source,
    first_slots,
    parts,
    shared,
    send_sem,
    recv_sem,
    part_send,
    part_recv,
    share_send,
    share_recv,
    split_slots,
    split_half,
    small_ref,
    small_slots,
    row_send,
    row_recv,
    load_sem,
    *scatter_refs,
):
    me = my_index()
    row = lax.axis_index("dp")
    core = lax.axis_index("tensor")
    rows_count = count // 2
    greet_all(count)
    pixels = grad_ref.shape[0]
    rows = stem_rows(pixels)
    norm_at = row_starts(rows)
    input_at = row_starts(rows[1:])
    loads = []
    for index, (source_ref, target, begin, size) in enumerate(
        [
            (norm_hbm, norm_ref, norm_at[8], rows[8]),
            (input_hbm, input_ref, input_at[7], rows[8]),
            (norm_hbm, norm_ref, 0, norm_at[8]),
            (input_hbm, input_ref, 0, input_at[7]),
        ]
    ):
        loads.append(
            pltpu.make_async_copy(
                source_ref.at[pl.ds(begin, size)], target.at[pl.ds(begin, size)], load_sem.at[index]
            )
        )
        loads[-1].start()
    jobs = []
    for index, (source_ref, left) in enumerate(
        [(up_ref, 0), (up_ref, 1), (attn_ref, 0), (attn_ref, 1)]
    ):
        refs = scatter_refs[index * ScatterHere.refs : (index + 1) * ScatterHere.refs]
        jobs.append(ScatterHere(source_ref, left * refs[0].shape[-1], refs))
    rest = 4 * ScatterHere.refs
    for index in range(2):
        refs = scatter_refs[rest + index * ScatterRest.refs : rest + (index + 1) * ScatterRest.refs]
        jobs.append(ScatterRest(kept_ref, second_ref, index * refs[0].shape[-1], refs))
    up_left, up_right, attn_left, attn_right, down_left, down_right = jobs
    early = up_left.first.shape[1] // 2
    early_load = pltpu.make_async_copy(
        early_ref, up_left.first.at[:, pl.ds(0, early)], load_sem.at[4]
    )
    early_load.start()
    up_landed = up_left.first.at[:, pl.ds(early, early)]
    small_rows, split_rows = 1064, 1072
    own_rows = 2 * split_half.shape[1]
    small_ref[...] = jnp.zeros_like(small_ref)
    for device in range(rows_count):
        lanes = slice(device * own_rows, (device + 1) * own_rows)
        small_ref[device, 0:1, :own_rows] = attn_norm_ref[:, lanes]
        small_ref[device, 1:2, :own_rows] = ffn_norm_ref[:, lanes]
        small_ref[device, 2 : 2 + tables_ref.shape[0], : tables_ref.shape[1]] = tables_ref[...]
    skip_at = row_starts(rows[:4])
    spacing = 16
    owners = count // 8
    owned = parts.shape[1]
    for start, place in places:
        ordered[place : place + 8, :] = grad_ref[pl.ds(start, 8, stride=spacing), :]

    def send_rows(first, last, source_of, target, place):
        def send(step, carry):
            other = lax.rem(row + step, rows_count)
            pltpu.make_async_remote_copy(
                src_ref=source_of(other),
                dst_ref=target.at[row],
                send_sem=row_send.at[place],
                recv_sem=row_recv.at[place],
                device_id=(other, core),
                device_id_type=MESH,
            ).start()
            return carry

        lax.fori_loop(first, last, send, 0)

    def weight_grad(layer):
        height = rows[layer]
        chunk = min(height, 512)

        def add(index, total):
            at = pl.multiple_of(index * chunk, chunk)
            return total + lax.dot_general(
                input_ref[pl.ds(input_at[layer - 1] + at, chunk), :].astype(jnp.bfloat16),
                grad_conv[pl.ds(norm_at[layer] + at, chunk), :].astype(jnp.bfloat16),
                (((0,), (0,)), ((), ())),
                preferred_element_type=jnp.float32,
            )

        product[layer - 1] = lax.fori_loop(
            0, height // chunk, add, jnp.zeros((128, 128), jnp.float32)
        ).reshape(owners, owned, 128)

        def send(index, carry):
            owner = layer - 1 + 8 * index

            @pl.when(owner != me)
            def _():
                pltpu.make_async_remote_copy(
                    src_ref=product.at[layer - 1, index],
                    dst_ref=parts.at[me],
                    send_sem=part_send,
                    recv_sem=part_recv,
                    device_id=(owner // 2, lax.rem(owner, 2)),
                    device_id_type=MESH,
                ).start()

            @pl.when(owner == me)
            def _():
                parts[me] = product[layer - 1, index]

            return carry

        lax.fori_loop(0, owners, send, 0)

    def send_small():
        small_slots[row] = small_ref[row]
        send_rows(1, rows_count, lambda other: small_ref.at[other], small_slots, 0)

    def send_split():
        split_slots[row] = split_ref[row, core]
        send_rows(1, rows_count, lambda other: split_ref.at[other, core], split_slots, 1)

    def add_rows():
        wait_all(rows_count, small_slots, row_recv.at[0])
        small_out[small_rows : small_rows + 8, :] = jnp.sum(small_slots[...], axis=0)
        wait_all(rows_count, split_slots, row_recv.at[1])
        split_half[core] = jnp.sum(split_slots[...], axis=0)
        swap.start()

    def keep_rows():
        swap.wait()
        size = split_half.shape[1]
        for part in range(2):
            begin = split_rows + part * size
            small_out[begin : begin + size, :] = split_half[part]

    swap = pltpu.make_async_remote_copy(
        src_ref=split_half.at[core],
        dst_ref=split_half.at[core],
        send_sem=row_send.at[2],
        recv_sem=row_recv.at[2],
        device_id=(row, 1 - core),
        device_id_type=MESH,
    )

    def second_of_up():
        early_load.wait()
        up_left.start_second(up_landed)

    steps = {
        "small": send_small,
        "split": send_split,
        "rows": add_rows,
        "kept": keep_rows,
        "u1b": lambda: up_left.start_first(1),
        "u2": second_of_up,
    }
    for mark, job in zip("uvabde", jobs):
        if mark in "vab":
            steps[mark + "1a"] = functools.partial(job.start_first, 0)
            steps[mark + "1b"] = functools.partial(job.start_first, 1)
            steps[mark + "2"] = job.start_second
        steps[mark + "3a"] = job.third_first
        steps[mark + "3b"] = job.third_next

    for layer in range(LAYERS - 1, -1, -1):
        height = rows[layer]
        chunk = min(height, PIX_CHUNK)
        base = norm_at[layer]
        gain = gain_ref[layer : layer + 1, :]
        shift = shift_ref[layer : layer + 1, :]
        inverse = scale_ref[layer : layer + 1, :]
        incoming = ordered if layer == 8 else grads
        if layer == 8:
            loads[0].wait()
        if layer == 7:
            loads[2].wait()
        if layer == 6:
            loads[3].wait()

        def activate(index, carry):
            first, second = carry
            at = pl.multiple_of(index * chunk, chunk)
            normed = norm_ref[pl.ds(base + at, chunk), :]
            lifted = normed * gain + shift
            sigma = 1.0 / (1.0 + jnp.exp(-lifted))
            value = incoming[pl.ds(at, chunk), :] * sigma * (1.0 + lifted * (1.0 - sigma))
            active[pl.ds(at, chunk), :] = value
            first = first + jnp.sum(value.reshape(chunk // 8, 8, 128), axis=0)
            second = second + jnp.sum((value * normed).reshape(chunk // 8, 8, 128), axis=0)
            return first, second

        zero = jnp.zeros((8, 128), jnp.float32)
        first, second = lax.fori_loop(0, height // chunk, activate, (zero, zero))
        sums = jnp.concatenate(
            [jnp.sum(first, axis=0, keepdims=True), jnp.sum(second, axis=0, keepdims=True)], axis=0
        )
        source[layer] = sums
        slots[layer, me] = sums
        if layer == 8:
            greeted(count)
        send_all(
            count, source.at[layer], slots.at[layer, me], send_sem.at[layer], recv_sem.at[layer]
        )
        for name in SCHEDULE[layer].split():
            steps[name]()
        if layer == 7:
            loads[1].wait()
        if layer < 8:
            weight_grad(layer + 1)
        wait_all(count, slots.at[layer], recv_sem.at[layer])
        totals = jnp.sum(slots[layer], axis=0)
        small_out[1032 + layer : 1033 + layer, :] = totals[1:2]
        small_out[1048 + layer : 1049 + layer, :] = totals[0:1]
        share = 1.0 / (4 * height * count)
        first_mean = group_sum(wide(totals[0:1] * gain))[0:1] * share
        second_mean = group_sum(wide(totals[1:2] * gain))[0:1] * share

        def conv_grad(start, size):
            value = inverse * (
                active[pl.ds(start, size), :] * gain
                - first_mean
                - norm_ref[pl.ds(base + start, size), :] * second_mean
            )
            grad_conv[pl.ds(base + start, size), :] = value
            return value

        if layer > 0:
            weights = weights_ref[layer - 1]
            stacked = jnp.concatenate([weights, weights], axis=1)

            def input_grad(start, size):
                return lax.dot_general(
                    split_two(conv_grad(start, size)),
                    stacked,
                    (((1,), (1,)), ((), ())),
                    preferred_element_type=jnp.float32,
                )

        if layer > 4:
            quarter = height // 4
            part = min(quarter, 64)
            skipped = skip_at[8 - layer]

            def shrink(index, carry):
                at = pl.multiple_of(index * part, part)
                total = jnp.zeros((part, 128), jnp.float32)
                for corner in range(4):
                    place = corner * quarter + at
                    value = input_grad(place, part)
                    skip[pl.ds(skipped + place, part), :] = value
                    total = total + value
                grads[pl.ds(at, part), :] = total
                return carry

            lax.fori_loop(0, quarter // part, shrink, 0)
        elif layer > 0:
            part = min(height, 128)
            skipped = skip_at[layer - 1]

            def spread_out(index, carry):
                at = pl.multiple_of(index * part, part)
                value = input_grad(at, part) * 0.25
                for corner in range(4):
                    place = corner * height + at
                    grads[pl.ds(place, part), :] = value + skip[pl.ds(skipped + place, part), :]
                return carry

            lax.fori_loop(0, height // part, spread_out, 0)
        else:

            def finish(index, carry):
                at = pl.multiple_of(index * chunk, chunk)
                conv_grad(at, chunk)
                return carry

            lax.fori_loop(0, height // chunk, finish, 0)
    for start, place in places:
        natural[pl.ds(start, 8, stride=spacing), :] = grad_conv[place : place + 8, :]
    first_part = jnp.zeros(first_source.shape, jnp.float32)
    for line in range(image_ref.shape[1]):
        first_part = first_part + dot_plain(
            image_ref[:, line, :],
            natural[line * 128 : (line + 1) * 128, :].astype(jnp.bfloat16),
        )
    first_source[...] = first_part
    first_slots[me] = first_part
    send_all(count, first_source, first_slots.at[me], send_sem.at[LAYERS], recv_sem.at[LAYERS])
    for name in SCHEDULE["end"].split():
        steps[name]()
    wait_all(count, parts, part_recv)
    shared[me] = jnp.sum(parts[...], axis=0)
    send_all(count, shared.at[me], shared.at[me], share_send, share_recv)
    for job, base in ((down_left, 2), (down_right, 2), (up_left, 0), (up_right, 0)):
        job.end(large_out, base)
    for name in SCHEDULE["last"].split():
        steps[name]()
    wait_all(count, first_slots, recv_sem.at[LAYERS])
    small_out[1024 : 1024 + first_slots.shape[1], :] = jnp.sum(first_slots[...], axis=0)
    wait_all(count, shared, share_recv)
    for device in range(count):
        begin = (device % 8) * 128 + (device // 8) * owned
        small_out[begin : begin + owned, :] = shared[device]
    attn_left.end(large_out, 1)
    for layer in range(LAYERS):
        wait_all(count, slots.at[layer], send_sem.at[layer])
    wait_all(count, first_slots, send_sem.at[LAYERS])
    wait_all(rows_count, small_slots, row_send.at[0])
    wait_all(rows_count, split_slots, row_send.at[1])
    wait_all(count, parts, part_send)
    wait_all(count, shared, share_send)
    up_left.sent(up_landed)
    for job in jobs[1:]:
        job.sent()
    attn_right.end(large_out, 1)


def stem_forward(page_image, conv_first, conv_weights, group_gain, group_shift, devices):
    planes, tile_rows, columns = page_image.shape
    pixels = tile_rows * columns
    rows = stem_rows(pixels)
    places = natural_places(tile_rows, columns)
    whole = pl.BlockSpec(memory_space=pltpu.VMEM)
    far = pl.BlockSpec(memory_space=pltpu.HBM)
    return pl.pallas_call(
        functools.partial(stem_forward_kernel, devices, places),
        out_shape=(
            jax.ShapeDtypeStruct((pixels, 128), jnp.float32),
            jax.ShapeDtypeStruct((sum(rows), 128), jnp.float32),
            jax.ShapeDtypeStruct((sum(rows[1:]), 128), jnp.float32),
            jax.ShapeDtypeStruct((LAYERS, 128), jnp.float32),
        ),
        in_specs=[whole] * 5,
        out_specs=(whole, far, far, whole),
        scratch_shapes=[
            pltpu.VMEM((sum(rows), 128), jnp.float32),
            pltpu.VMEM((sum(rows[1:]), 128), jnp.float32),
            pltpu.VMEM((pixels, 128), jnp.float32),
            pltpu.VMEM((sum(rows[:4]), 128), jnp.float32),
            pltpu.VMEM((pixels, 128), jnp.float32),
            pltpu.VMEM((LAYERS, 2, 128), jnp.float32),
            pltpu.VMEM((LAYERS, devices, 2, 128), jnp.float32),
            pltpu.SemaphoreType.DMA((LAYERS,)),
            pltpu.SemaphoreType.DMA((LAYERS,)),
            pltpu.SemaphoreType.DMA((2, LAYERS)),
        ],
        compiler_params=pltpu.CompilerParams(
            collective_id=0, has_side_effects=True, vmem_limit_bytes=VMEM_LIMIT
        ),
        cost_estimate=pl.CostEstimate(
            flops=54 * 10**9, bytes_accessed=2 * 10**7, transcendentals=0
        ),
        name="stem_forward",
    )(page_image, conv_first, conv_weights, group_gain, group_shift)


def stem_backward(
    grad_map,
    page_image,
    records,
    conv_weights,
    group_gain,
    group_shift,
    split,
    norm_grads,
    tables,
    up,
    attn,
    kept,
    second,
    early,
    devices,
):
    planes, tile_rows, columns = page_image.shape
    pixels = tile_rows * columns
    rows = stem_rows(pixels)
    norms, inputs, scales = records
    places = natural_places(tile_rows, columns)
    whole = pl.BlockSpec(memory_space=pltpu.VMEM)
    owned = 1024 // devices
    far = pl.BlockSpec(memory_space=pltpu.HBM)
    depths, _, _, own_rows, columns = up.shape
    return pl.pallas_call(
        functools.partial(stem_backward_kernel, devices, places),
        out_shape=(
            jax.ShapeDtypeStruct((1072 + 2 * split.shape[2], 128), jnp.float32),
            jax.ShapeDtypeStruct((3, own_rows, columns), jnp.float32),
        ),
        in_specs=[whole, whole, far, far] + [whole] * 8 + [far] * 5,
        out_specs=(whole,) * 2,
        scratch_shapes=[
            pltpu.VMEM((sum(rows), 128), jnp.float32),
            pltpu.VMEM((sum(rows[1:]), 128), jnp.float32),
            pltpu.VMEM((pixels, 128), jnp.float32),
            pltpu.VMEM((pixels, 128), jnp.float32),
            pltpu.VMEM((pixels, 128), jnp.float32),
            pltpu.VMEM((sum(rows), 128), jnp.float32),
            pltpu.VMEM((sum(rows[:4]), 128), jnp.float32),
            pltpu.VMEM((pixels, 128), jnp.float32),
            pltpu.VMEM((8, devices // 8, owned, 128), jnp.float32),
            pltpu.VMEM((LAYERS, 2, 128), jnp.float32),
            pltpu.VMEM((LAYERS, devices, 2, 128), jnp.float32),
            pltpu.VMEM((planes, 128), jnp.float32),
            pltpu.VMEM((devices, planes, 128), jnp.float32),
            pltpu.VMEM((devices, owned, 128), jnp.float32),
            pltpu.VMEM((devices, owned, 128), jnp.float32),
            pltpu.SemaphoreType.DMA((LAYERS + 1,)),
            pltpu.SemaphoreType.DMA((LAYERS + 1,)),
            pltpu.SemaphoreType.DMA,
            pltpu.SemaphoreType.DMA,
            pltpu.SemaphoreType.DMA,
            pltpu.SemaphoreType.DMA,
            pltpu.VMEM((devices // 2, *split.shape[2:]), jnp.float32),
            pltpu.VMEM(split.shape[1:], jnp.float32),
            pltpu.VMEM((devices // 2, 8, 128), jnp.float32),
            pltpu.VMEM((devices // 2, 8, 128), jnp.float32),
            pltpu.SemaphoreType.DMA((3,)),
            pltpu.SemaphoreType.DMA((3,)),
            pltpu.SemaphoreType.DMA((5,)),
            *(ScatterHere.scratch(depths, own_rows, columns // 4) * 4),
            *(ScatterRest.scratch(depths, own_rows, columns // 4) * 2),
        ],
        compiler_params=pltpu.CompilerParams(
            collective_id=1, has_side_effects=True, vmem_limit_bytes=VMEM_LIMIT
        ),
        cost_estimate=pl.CostEstimate(
            flops=65 * 10**9, bytes_accessed=2 * 10**7, transcendentals=0
        ),
        name="stem_backward",
    )(
        grad_map,
        page_image,
        norms,
        inputs,
        scales,
        conv_weights,
        group_gain,
        group_shift,
        split,
        *norm_grads,
        tables,
        up,
        attn,
        kept,
        second,
        early,
    )


TILE = 128
QROWS = 256
KIND_ROWS = 8
FAR_LANE = 32
LOW_LANE = 40
PAD_LANE = 48
DOC_LANE = 56


def dot_last(left, right):
    return lax.dot_general(
        left, right, (((1,), (1,)), ((), ())), preferred_element_type=jnp.float32
    )


def dot_plain(left, right):
    return jnp.dot(left, right, preferred_element_type=jnp.float32)


def bucket_vector(tables_ref, table, head, relative):
    buckets = bucket_of(relative)
    values = jnp.zeros(relative.shape, jnp.float32)
    for bucket in range(NBUCKET):
        values = jnp.where(buckets == bucket, tables_ref[table, head, bucket], values)
    return values


def signed_lanes(width):
    lane = lax.broadcasted_iota(jnp.int32, (8, width), 1)
    return jnp.where(lane < width // 2, lane, lane - width)


def rolled(row, height):
    return pltpu.roll(
        jnp.broadcast_to(row[0:1], (height, row.shape[1])), 0, 1, stride=1, stride_axis=0
    )


def token_columns(boxes_ref, docs_ref, pads_ref, info):
    rows = [boxes_ref[0], boxes_ref[1], docs_ref[...], pads_ref[...], boxes_ref[2], boxes_ref[3]]
    rows = rows + [jnp.zeros_like(rows[0])] * 2
    info[...] = jnp.concatenate(rows, axis=0).astype(jnp.float32).T.astype(jnp.int32)


def token_lanes(info_ref, one_hot_x, query_base, key_base, pad_tiles):
    tokens = info_ref.shape[0]
    lane = lax.broadcasted_iota(jnp.int32, (TILE, 128), 1)
    row = lax.broadcasted_iota(jnp.int32, (TILE, 128), 0)
    for tile in range(tokens // TILE):
        at = slice(tile * TILE, (tile + 1) * TILE)
        left = info_ref[at, 0:1]
        top = info_ref[at, 1:2]
        doc = info_ref[at, 2:3]
        hidden = jnp.where(info_ref[at, 3:4] > 0, 0.0, masked_score)
        one_hot_x[at, :] = (lane == left).astype(jnp.float32).astype(jnp.bfloat16)
        shared = jnp.where((lane == top) | (lane == DOC_LANE + doc), 1.0, 0.0)
        query_base[at, :] = jnp.where(lane == FAR_LANE + tile, 1.0, shared).astype(jnp.bfloat16)
        key = jnp.where((lane == FAR_LANE + tile) | (lane == LOW_LANE + tile), 1.0, shared)
        key = jnp.where(lane == PAD_LANE + tile, hidden, key)
        key_base[1, at, :] = key.astype(jnp.bfloat16)
        key_base[0, at, :] = pltpu.roll(key, 64, 1).astype(jnp.bfloat16)
        pad_tiles[at, :] = jnp.where(lane == row, 0.0, jnp.broadcast_to(hidden, (TILE, 128)))


def head_matrices(tables_ref, head, side):
    first = bucket_vector(tables_ref, 1, head, signed_lanes(256))
    across = rolled(first, 128)[:, :128].astype(jnp.bfloat16)
    second = rolled(bucket_vector(tables_ref, 2, head, signed_lanes(128)), 128)
    row = lax.broadcasted_iota(jnp.int32, (128, 128), 0)
    lane = lax.broadcasted_iota(jnp.int32, (128, 128), 1)
    mixed = jnp.where((row < FAR_LANE) & (lane < FAR_LANE), second, 0.0)
    gap = lane % 8 - (row - FAR_LANE)
    before = jnp.full((128, 128), tables_ref[0, head, NBUCKET // 2 - 1], jnp.float32)
    after = jnp.full((128, 128), tables_ref[0, head, NBUCKET - 1], jnp.float32)
    far = jnp.where(gap <= -2, before, jnp.where(gap >= 2, after, 0.0))
    high = far.astype(jnp.bfloat16).astype(jnp.float32)
    of_tile = (row >= FAR_LANE) & (row < LOW_LANE)
    mixed = jnp.where(of_tile & (lane >= FAR_LANE) & (lane < LOW_LANE), high, mixed)
    mixed = jnp.where(of_tile & (lane >= LOW_LANE) & (lane < PAD_LANE), far - high, mixed)
    mixed = jnp.where(
        of_tile & (lane >= PAD_LANE) & (lane < DOC_LANE) & (gap != 0), 1.0, mixed
    )
    docs = (row >= DOC_LANE) & (row < 64) & (lane >= DOC_LANE) & (lane < 64)
    mixed = jnp.where(docs & (row != lane), masked_score, mixed)
    if side == 0:
        mixed = pltpu.roll(mixed, 64, 1)
    near = rolled(bucket_vector(tables_ref, 0, head, -signed_lanes(512)), 128)
    tiles = {0: near[:, :128], 1: near[:, 384:], -1: near[:, 128:256]}
    return across, mixed.astype(jnp.bfloat16), tiles


def own_half(side, own, other):
    lane = lax.broadcasted_iota(jnp.int32, own.shape, 1)
    return jnp.where((lane < 64) if side == 0 else (lane >= 64), own, other)


def widen_operands(
    side, head, tables_ref, query_ref, key_ref, one_hot_x, query_base, key_base, query_wide, key_wide, near
):
    across, mixed, tiles = head_matrices(tables_ref, head, side)
    for gap in (-1, 0, 1):
        near[side, gap + 1] = tiles[gap]
    scaled = (query_ref[...].astype(jnp.float32) * HDIM ** (-0.5)).astype(jnp.bfloat16)
    query_wide[side, :, :128] = own_half(
        side, scaled, dot_plain(query_base[...], mixed).astype(jnp.bfloat16)
    )
    query_wide[side, :, 128:] = dot_plain(one_hot_x[...], across).astype(jnp.bfloat16)
    key_wide[side, :, :128] = own_half(side, key_ref[...], key_base[side])
    key_wide[side, :, 128:] = one_hot_x[...]


def near_scores(scores, side, block, tile, near, pad_tiles):
    halves = []
    for half in range(QROWS // TILE):
        part = scores[:, half * TILE : (half + 1) * TILE]
        gap = tile - (block * (QROWS // TILE) + half)
        if abs(gap) <= 1:
            part = part + near[side, gap + 1]
        if gap == 0:
            part = part + pad_tiles[tile * TILE : (tile + 1) * TILE, :]
        halves.append(part)
    return jnp.concatenate(halves, axis=1)


def attention_forward_kernel(
    tables_ref,
    boxes_ref,
    docs_ref,
    pads_ref,
    query_ref,
    key_ref,
    value_ref,
    context_ref,
    exact_ref,
    lse_ref,
    info_ref,
    one_hot_x,
    query_base,
    key_base,
    pad_tiles,
    query_wide,
    key_wide,
    near,
    scores,
    weights,
):
    pair = pl.program_id(0)
    tokens = query_ref.shape[0]

    @pl.when(pair == 0)
    def _():
        token_columns(boxes_ref, docs_ref, pads_ref, info_ref)
        token_lanes(info_ref, one_hot_x, query_base, key_base, pad_tiles)

    for side in range(2):
        widen_operands(
            side, pair * 2 + side, tables_ref, query_ref, key_ref, one_hot_x, query_base, key_base,
            query_wide, key_wide, near,
        )
    values = value_ref[...].T
    for block in range(tokens // QROWS):
        columns = slice(block * QROWS, (block + 1) * QROWS)
        contexts = []
        for side in range(2):
            scores[side] = dot_last(key_wide[side], query_wide[side, columns, :])
            top = jnp.full((8, QROWS), masked_score, jnp.float32)
            for tile in range(tokens // TILE):
                at = slice(tile * TILE, (tile + 1) * TILE)
                part = scores[side, at, :]
                if any(abs(tile - 2 * block - half) <= 1 for half in range(2)):
                    part = near_scores(part, side, block, tile, near, pad_tiles)
                    scores[side, at, :] = part
                top = jnp.maximum(top, jnp.max(part.reshape(TILE // 8, 8, QROWS), axis=0))
            top = jnp.max(top, axis=0, keepdims=True)
            total = jnp.zeros((8, QROWS), jnp.float32)
            for tile in range(tokens // TILE):
                at = slice(tile * TILE, (tile + 1) * TILE)
                part = jnp.exp(scores[side, at, :] - top)
                total = total + jnp.sum(part.reshape(TILE // 8, 8, QROWS), axis=0)
                weights[side, at, :] = part.astype(jnp.bfloat16)
            total = jnp.sum(total, axis=0, keepdims=True)
            context = dot_plain(values[side * 64 : (side + 1) * 64, :], weights[side])
            contexts.append(context * (1.0 / total))
            lse_ref[0, side : side + 1, columns] = top + jnp.log(total)
        context = jnp.concatenate(contexts, axis=0)
        exact_ref[:, columns] = context
        context_ref[columns, :] = context.T.astype(jnp.bfloat16)


def attention_backward_kernel(
    tables_ref,
    boxes_ref,
    docs_ref,
    pads_ref,
    query_ref,
    key_ref,
    value_ref,
    grad_ref,
    exact_ref,
    lse_ref,
    down_ref,
    up_ref,
    grad_query_ref,
    grad_key_ref,
    grad_value_ref,
    diagonal_ref,
    down_landed,
    up_landed,
    info_ref,
    one_hot_x,
    query_base,
    key_base,
    pad_tiles,
    reverse,
    query_wide,
    key_wide,
    near,
    scores,
    grad_probs,
    probs_low,
    grad_low,
    key_turned,
    grad_near,
    grad_blocks,
    grad_key,
    grad_value,
    down_send,
    down_recv,
    up_send,
    up_recv,
):
    pair = pl.program_id(0)
    tokens = query_ref.shape[0]
    down = Scatter(down_landed.shape[-1], 0, down_send, down_recv)
    up = Scatter(up_landed.shape[-1], 0, up_send, up_recv)

    @pl.when(pair == 0)
    def _():
        greet_rows((down.across_x, down.across_y))
        pl.semaphore_wait(pltpu.get_barrier_semaphore(), 2)
        down.send_first(down_ref, down_landed, 0, down_landed.shape[1])
        up.send_first(up_ref, up_landed, 0, up_landed.shape[1])
        token_columns(boxes_ref, docs_ref, pads_ref, info_ref)
        token_lanes(info_ref, one_hot_x, query_base, key_base, pad_tiles)
        lane = lax.broadcasted_iota(jnp.int32, (TILE, 128), 1)
        for tile in range(tokens // TILE):
            at = slice(tile * TILE, (tile + 1) * TILE)
            left = info_ref[at, 0:1]
            top = info_ref[at, 1:2]
            reverse[at, :128] = jnp.where(lane == 127 - left, 1.0, 0.0).astype(jnp.bfloat16)
            reverse[at, 128:] = jnp.where(
                (lane == 31 - top) | (lane == FAR_LANE + tile), 1.0, 0.0
            ).astype(jnp.bfloat16)

    for side in range(2):
        widen_operands(
            side, pair * 2 + side, tables_ref, query_ref, key_ref, one_hot_x, query_base, key_base,
            query_wide, key_wide, near,
        )
        key_turned[side] = key_wide[side].T
    grad_near[...] = jnp.zeros_like(grad_near)
    grad_blocks[...] = jnp.zeros_like(grad_blocks)
    values = [
        own_half(side, value_ref[...], jnp.zeros(value_ref.shape, jnp.bfloat16)) for side in range(2)
    ]
    for block in range(tokens // QROWS):
        columns = slice(block * QROWS, (block + 1) * QROWS)
        grad_block = grad_ref[columns, :]
        product = grad_block.astype(jnp.float32).T * exact_ref[:, columns]
        scaled = (query_ref[columns, :].astype(jnp.float32) * HDIM ** (-0.5)).astype(jnp.bfloat16)
        turned = []
        key_terms = []
        value_terms = []
        for side in range(2):
            delta = jnp.sum(product[side * 64 : (side + 1) * 64, :], axis=0, keepdims=True)
            lse = lse_ref[0, side : side + 1, columns]
            scores[side] = dot_last(key_wide[side], query_wide[side, columns, :])
            grad_probs[side] = dot_last(values[side], grad_block)
            for tile in range(tokens // TILE):
                at = slice(tile * TILE, (tile + 1) * TILE)
                part = near_scores(scores[side, at, :], side, block, tile, near, pad_tiles)
                probs = jnp.exp(part - lse)
                grad_part = probs * (grad_probs[side, at, :] - delta)
                probs_low[side, at, :] = probs.astype(jnp.bfloat16)
                grad_low[side, at, :] = grad_part.astype(jnp.bfloat16)
                for half in range(QROWS // TILE):
                    gap = tile - (block * (QROWS // TILE) + half)
                    if abs(gap) <= 1:
                        grad_near[side, gap + 1] += grad_part[:, half * TILE : (half + 1) * TILE]
            value_terms.append(dot_plain(probs_low[side], grad_block))
            key_terms.append(dot_plain(grad_low[side], scaled))
            sums = dot_plain(key_turned[side], grad_low[side])
            turned.append(sums[side * 64 : (side + 1) * 64, :])
            grad_blocks[side] += dot_plain(sums.astype(jnp.bfloat16), reverse[columns, :])
        grad_query_ref[columns, :] = (
            (jnp.concatenate(turned, axis=0) * HDIM ** (-0.5)).T.astype(jnp.bfloat16)
        )
        key_term = own_half(0, key_terms[0], key_terms[1])
        value_term = own_half(0, value_terms[0], value_terms[1])
        if block == 0:
            grad_key[...] = key_term
            grad_value[...] = value_term
        else:
            grad_key[...] += key_term
            grad_value[...] += value_term
    grad_key_ref[...] = grad_key[...].astype(jnp.bfloat16)
    grad_value_ref[...] = grad_value[...].astype(jnp.bfloat16)
    row = lax.broadcasted_iota(jnp.int32, (128, 128), 0)
    lane = lax.broadcasted_iota(jnp.int32, (128, 128), 1)
    flip = jnp.where(row + lane == 127, 1.0, 0.0).astype(jnp.bfloat16)
    blank = jnp.zeros((128, 128), jnp.float32)

    def diagonal_sums(values):
        spread = jnp.concatenate([values, blank], axis=1)
        return jnp.sum(
            pltpu.roll(spread, 0, 1, stride=1, stride_axis=0), axis=0, keepdims=True
        )

    for side in range(2):
        misc = 64 * (1 - side)
        sums = [diagonal_sums(grad_blocks[side, 128:, :128])]
        below = grad_blocks[side, misc : misc + 64, 128:]
        small_row = lax.broadcasted_iota(jnp.int32, (64, 128), 0)
        small_lane = lax.broadcasted_iota(jnp.int32, (64, 128), 1)
        upright = jnp.where((small_row < FAR_LANE) & (small_lane < FAR_LANE), below, 0.0)
        sums.append(diagonal_sums(jnp.concatenate([upright, jnp.zeros((64, 128), jnp.float32)], axis=0)))
        for gap in range(3):
            tile = grad_near[side, gap]
            high = tile.astype(jnp.bfloat16)
            rest = (tile - high.astype(jnp.float32)).astype(jnp.bfloat16)
            sums.append(diagonal_sums(dot_plain(high, flip) + dot_plain(rest, flip)))
        gap = (small_row - FAR_LANE) - (small_lane - FAR_LANE)
        inside = (
            (small_row >= FAR_LANE)
            & (small_row < LOW_LANE)
            & (small_lane >= FAR_LANE)
            & (small_lane < LOW_LANE)
        )
        for chosen in (gap <= -2, gap >= 2):
            far = jnp.sum(jnp.where(inside & chosen, below, 0.0), axis=0, keepdims=True)
            sums.append(jnp.concatenate([far, blank[0:1]], axis=1))
        sums.append(jnp.zeros((1, 256), jnp.float32))
        diagonal_ref[side] = jnp.concatenate(sums, axis=0)

    @pl.when(pair == pl.num_programs(0) - 1)
    def _():
        for scatter, landed in ((down, down_landed), (up, up_landed)):
            scatter.await_first(landed)
            scatter.sent_first(landed)


def attention_scratch(tokens):
    return [
        pltpu.VMEM((tokens, 8), jnp.int32),
        pltpu.VMEM((tokens, 128), jnp.bfloat16),
        pltpu.VMEM((tokens, 128), jnp.bfloat16),
        pltpu.VMEM((2, tokens, 128), jnp.bfloat16),
        pltpu.VMEM((tokens, 128), jnp.float32),
    ], [
        pltpu.VMEM((2, tokens, 256), jnp.bfloat16),
        pltpu.VMEM((2, tokens, 256), jnp.bfloat16),
        pltpu.VMEM((2, 3, TILE, TILE), jnp.float32),
        pltpu.VMEM((2, tokens, QROWS), jnp.float32),
    ]


def attention_forward(tables, places, heads):
    tokens, width = heads.shape[0], heads.shape[1] // 3
    pairs = width // 128
    own = pl.BlockSpec((tokens, 128), lambda pair: (0, pair))
    fixed, moving = attention_scratch(tokens)
    return pl.pallas_call(
        attention_forward_kernel,
        grid=(pairs,),
        out_shape=(
            jax.ShapeDtypeStruct((tokens, width), jnp.bfloat16),
            jax.ShapeDtypeStruct((width, tokens), jnp.float32),
            jax.ShapeDtypeStruct((pairs, 2, tokens), jnp.float32),
        ),
        in_specs=[
            pl.BlockSpec(memory_space=pltpu.SMEM),
            *[pl.BlockSpec(memory_space=pltpu.VMEM)] * 3,
            own,
            pl.BlockSpec((tokens, 128), lambda pair: (0, pairs + pair)),
            pl.BlockSpec((tokens, 128), lambda pair: (0, 2 * pairs + pair)),
        ],
        out_specs=(
            own,
            pl.BlockSpec((128, tokens), lambda pair: (pair, 0)),
            pl.BlockSpec((1, 2, tokens), lambda pair: (pair, 0, 0)),
        ),
        scratch_shapes=fixed
        + moving
        + [
            pltpu.VMEM((2, tokens, QROWS), jnp.bfloat16),
        ],
        compiler_params=pltpu.CompilerParams(
            dimension_semantics=("arbitrary",), vmem_limit_bytes=VMEM_LIMIT
        ),
        cost_estimate=pl.CostEstimate(
            flops=23 * 10**9, bytes_accessed=2 * 10**7, transcendentals=0
        ),
        name="attention_forward",
    )(tables, *places, heads, heads, heads)


def attention_backward(tables, places, heads, grad_context, exact, lse, down, up):
    tokens, width = grad_context.shape
    pairs = width // 128
    own = pl.BlockSpec((tokens, 128), lambda pair: (0, pair))
    fixed, moving = attention_scratch(tokens)
    low = jax.ShapeDtypeStruct((tokens, width), jnp.bfloat16)
    depths, _, _, rows, columns = down.shape
    return pl.pallas_call(
        attention_backward_kernel,
        grid=(pairs,),
        out_shape=(
            low,
            low,
            low,
            jax.ShapeDtypeStruct((2 * pairs, 8, 256), jnp.float32),
            jax.ShapeDtypeStruct((2, depths, 2, rows, columns // 2), jnp.float32),
            jax.ShapeDtypeStruct((2, depths // 2, 2, rows, columns // 4), jnp.float32),
        ),
        in_specs=[
            pl.BlockSpec(memory_space=pltpu.SMEM),
            *[pl.BlockSpec(memory_space=pltpu.VMEM)] * 3,
            own,
            pl.BlockSpec((tokens, 128), lambda pair: (0, pairs + pair)),
            pl.BlockSpec((tokens, 128), lambda pair: (0, 2 * pairs + pair)),
            own,
            pl.BlockSpec((128, tokens), lambda pair: (pair, 0)),
            pl.BlockSpec((1, 2, tokens), lambda pair: (pair, 0, 0)),
            pl.BlockSpec(memory_space=pltpu.HBM),
            pl.BlockSpec(memory_space=pltpu.HBM),
        ],
        out_specs=(
            own,
            own,
            own,
            pl.BlockSpec((2, 8, 256), lambda pair: (pair, 0, 0)),
            pl.BlockSpec(memory_space=pltpu.HBM),
            pl.BlockSpec(memory_space=pltpu.HBM),
        ),
        scratch_shapes=fixed
        + [pltpu.VMEM((tokens, 256), jnp.bfloat16)]
        + moving
        + [
            pltpu.VMEM((2, tokens, QROWS), jnp.float32),
            pltpu.VMEM((2, tokens, QROWS), jnp.bfloat16),
            pltpu.VMEM((2, tokens, QROWS), jnp.bfloat16),
            pltpu.VMEM((2, 256, tokens), jnp.bfloat16),
            pltpu.VMEM((2, 3, TILE, TILE), jnp.float32),
            pltpu.VMEM((2, 256, 256), jnp.float32),
            pltpu.VMEM((tokens, 128), jnp.float32),
            pltpu.VMEM((tokens, 128), jnp.float32),
            *scatter_semaphores(2),
            *scatter_semaphores(2),
        ],
        compiler_params=pltpu.CompilerParams(
            dimension_semantics=("arbitrary",),
            collective_id=5,
            has_side_effects=True,
            vmem_limit_bytes=VMEM_LIMIT,
        ),
        cost_estimate=pl.CostEstimate(
            flops=30 * 10**9, bytes_accessed=2 * 10**7, transcendentals=0
        ),
        name="attention_backward",
    )(tables, *places, heads, heads, heads, grad_context, exact, lse, down, up)


def known_bucket(relative):
    magnitude = np.abs(relative)
    coarse = 8 + sum((magnitude >= edge).astype(int) for edge in bucket_edges)
    return np.where(magnitude < 8, magnitude, coarse) + np.where(relative > 0, 16, 0)


def bucket_grads(diagonals):
    lane = np.arange(256)
    far = np.zeros(256, int)
    wide_buckets = [
        known_bucket(lane - 127),
        known_bucket(lane - 31),
        known_bucket(lane - 127 - TILE),
        known_bucket(lane - 127),
        known_bucket(lane - 127 + TILE),
        far + NBUCKET // 2 - 1,
        far + NBUCKET - 1,
    ]
    table_of = (1, 2, 0, 0, 0, 0, 0)
    slots = np.stack([bucket + NBUCKET * table for bucket, table in zip(wide_buckets, table_of)])
    slots = jnp.asarray(slots, jnp.int32)
    chosen = (slots[..., None] == jnp.arange(3 * NBUCKET, dtype=jnp.int32)).astype(jnp.float32)
    return jnp.einsum("hrc,rcb->hb", diagonals[:, :7], chosen, precision=highest)


ROWS = 256


def greet_partner():
    pl.semaphore_signal(
        pltpu.get_barrier_semaphore(),
        inc=1,
        device_id=(lax.axis_index("dp"), 1 - lax.axis_index("tensor")),
        device_id_type=MESH,
    )


def partner_copy(source, target, send_sem, recv_sem):
    return pltpu.make_async_remote_copy(
        src_ref=source,
        dst_ref=target,
        send_sem=send_sem,
        recv_sem=recv_sem,
        device_id=(lax.axis_index("dp"), 1 - lax.axis_index("tensor")),
        device_id_type=MESH,
    )


def dot_rows(left, right):
    return lax.dot_general(
        left, right, (((0,), (0,)), ((), ())), preferred_element_type=jnp.float32
    )


def inverse_rms(values):
    return lax.rsqrt(jnp.mean(values * values, axis=1, keepdims=True) + norm_eps)


def box_kernel(
    feature_ref,
    boxes_ref,
    docs_ref,
    pads_ref,
    embedded_ref,
    roi_ref,
    norm_ref,
    query_proj_ref,
    key_proj_ref,
    value_proj_ref,
    pooled_ref,
    stream_ref,
    input_ref,
    heads_ref,
    info_ref,
    features,
    mask,
    part,
    received,
    projections,
    send_sem,
    recv_sem,
):
    greet_partner()
    token_columns(boxes_ref, docs_ref, pads_ref, info_ref)
    tokens = info_ref.shape[0]
    pixels = feature_ref.shape[0]
    tile_rows = pixels // 128
    first_row = lax.axis_index("tensor") * tile_rows
    features[...] = split_two(feature_ref[...])
    lane = lax.broadcasted_iota(jnp.int32, (ROWS, 128), 1)
    copies = []
    for block in range(tokens // ROWS):
        at = slice(block * ROWS, (block + 1) * ROWS)
        column = (lane >= info_ref[at, 0:1]) & (lane < info_ref[at, 4:5])
        column = jnp.where(column, 1.0, 0.0)
        top = jnp.broadcast_to(info_ref[at, 1:2], (ROWS, 128)) - first_row
        bottom = jnp.broadcast_to(info_ref[at, 5:6], (ROWS, 128)) - first_row
        for row in range(tile_rows):
            inside = jnp.where((top <= row) & (bottom > row), column, 0.0)
            mask[block % 2, :, row * 128 : (row + 1) * 128] = inside.astype(jnp.bfloat16)
        sums = dot_plain(mask[block % 2], features[...])
        part[at, :] = sums[:, :128] + sums[:, 128:]
        if block == 0:
            pl.semaphore_wait(pltpu.get_barrier_semaphore(), 1)
        copy = partner_copy(
            part.at[pl.ds(block * ROWS, ROWS)],
            received.at[pl.ds(block * ROWS, ROWS)],
            send_sem.at[block],
            recv_sem.at[block],
        )
        copy.start()
        copies.append(copy)
    width = query_proj_ref.shape[1]
    for index, ref in enumerate((query_proj_ref, key_proj_ref, value_proj_ref)):
        projections[:, index * width : (index + 1) * width] = ref[...]
    for block in range(tokens // ROWS):
        at = slice(block * ROWS, (block + 1) * ROWS)
        copies[block].wait_recv()
        area = (info_ref[at, 5:6] - info_ref[at, 1:2]) * (info_ref[at, 4:5] - info_ref[at, 0:1])
        pooled = ((part[at, :] + received[at, :]) / area.astype(jnp.float32)).astype(jnp.bfloat16)
        pooled_ref[at, :] = pooled
        stream = embedded_ref[at, :].astype(jnp.float32) + dot_plain(pooled, roi_ref[...])
        stream_ref[at, :] = stream
        attn_in = (stream * inverse_rms(stream) * norm_ref[...].reshape(1, -1)).astype(jnp.bfloat16)
        input_ref[at, :] = attn_in
        heads_ref[at, :] = dot_plain(attn_in, projections[...]).astype(jnp.bfloat16)
    for copy in copies:
        copy.wait_send()


def box_forward(
    feature_map, places, embeddings, roi_proj, attn_norm, query_proj, key_proj, value_proj
):
    tokens, width = embeddings.shape
    local = query_proj.shape[1]
    blocks = tokens // ROWS
    whole = pl.BlockSpec(memory_space=pltpu.VMEM)
    return pl.pallas_call(
        box_kernel,
        out_shape=(
            jax.ShapeDtypeStruct((tokens, 128), jnp.bfloat16),
            jax.ShapeDtypeStruct((tokens, width), jnp.float32),
            jax.ShapeDtypeStruct((tokens, width), jnp.bfloat16),
            jax.ShapeDtypeStruct((tokens, 3 * local), jnp.bfloat16),
        ),
        in_specs=[whole] * 10,
        out_specs=(whole,) * 4,
        scratch_shapes=[
            pltpu.VMEM((tokens, 8), jnp.int32),
            pltpu.VMEM((feature_map.shape[0], 256), jnp.bfloat16),
            pltpu.VMEM((2, ROWS, feature_map.shape[0]), jnp.bfloat16),
            pltpu.VMEM((tokens, 128), jnp.float32),
            pltpu.VMEM((tokens, 128), jnp.float32),
            pltpu.VMEM((width, 3 * local), jnp.bfloat16),
            pltpu.SemaphoreType.DMA((blocks,)),
            pltpu.SemaphoreType.DMA((blocks,)),
        ],
        compiler_params=pltpu.CompilerParams(
            collective_id=2, has_side_effects=True, vmem_limit_bytes=VMEM_LIMIT
        ),
        cost_estimate=pl.CostEstimate(
            flops=12 * 10**9, bytes_accessed=2 * 10**7, transcendentals=0
        ),
        name="box_forward",
    )(
        feature_map,
        *places,
        embeddings,
        roi_proj,
        attn_norm,
        query_proj,
        key_proj,
        value_proj,
    )


def middle_kernel(
    context_ref,
    stream_hbm,
    cotangent_hbm,
    output_ref,
    norm_ref,
    up_hbm,
    down_hbm,
    layer_hbm,
    grad_middle_hbm,
    grad_context_hbm,
    grad_up_hbm,
    grad_down_hbm,
    grad_output_ref,
    grad_norm_ref,
    middle,
    cotangent,
    up,
    down,
    part,
    other,
    part_out,
    other_out,
    other_grad,
    ffn_in,
    hidden,
    grad_pre,
    staged,
    grad_low,
    layer_low,
    grad_context,
    load_sem,
    store_sem,
    grad_sem,
    send_sem,
    recv_sem,
):
    greet_partner()
    norm = norm_ref[...].reshape(1, -1)
    tokens, width = stream_hbm.shape
    units = up_hbm.shape[1]
    blocks = tokens // ROWS
    loads = [
        pltpu.make_async_copy(source, target, load_sem.at[index])
        for index, (source, target) in enumerate(
            [(cotangent_hbm, cotangent), (down_hbm, down), (stream_hbm, middle), (up_hbm, up)]
        )
    ]
    for load in loads:
        load.start()
    attn_copies = []
    for block in range(blocks):
        at = slice(block * ROWS, (block + 1) * ROWS)
        part[at, :] = dot_plain(context_ref[at, :], output_ref[...])
        if block == 0:
            pl.semaphore_wait(pltpu.get_barrier_semaphore(), 1)
        copy = partner_copy(
            part.at[pl.ds(block * ROWS, ROWS)],
            other.at[pl.ds(block * ROWS, ROWS)],
            send_sem.at[0, block],
            recv_sem.at[0, block],
        )
        copy.start()
        attn_copies.append(copy)
    for load in loads:
        load.wait()
    out_copies = []
    grad_copies = []
    for block in range(blocks):
        at = slice(block * ROWS, (block + 1) * ROWS)
        grad_hidden = dot_last(cotangent[at, :], down[...])
        attn_copies[block].wait()
        values = middle[at, :] + (part[at, :] + other[at, :])
        middle[at, :] = values
        inner = (values * inverse_rms(values) * norm).astype(jnp.bfloat16)
        ffn_in[at, :] = inner
        pre_act = dot_plain(inner, up[...])
        below = 0.5 * (1.0 + lax.erf(pre_act * (0.5**0.5)))
        density = jnp.exp(-0.5 * (pre_act * pre_act)) * 0.3989422804014327
        hidden[at, :] = (pre_act * below).astype(jnp.bfloat16)
        grad_pre[at, :] = (grad_hidden * (below + pre_act * density)).astype(jnp.bfloat16)
        part[at, :] = dot_last(grad_pre[at, :], up[...])
        copy = partner_copy(
            part.at[pl.ds(block * ROWS, ROWS)],
            other_grad.at[pl.ds(block * ROWS, ROWS)],
            send_sem.at[1, block],
            recv_sem.at[1, block],
        )
        copy.start()
        grad_copies.append(copy)
        part_out[at, :] = dot_plain(hidden[at, :], down[...])
        copy = partner_copy(
            part_out.at[pl.ds(block * ROWS, ROWS)],
            other_out.at[pl.ds(block * ROWS, ROWS)],
            send_sem.at[2, block],
            recv_sem.at[2, block],
        )
        copy.start()
        out_copies.append(copy)
    half = width // 2
    stores = []
    for index in range(4):
        rows = slice((index % 2) * half, (index % 2 + 1) * half)
        if index >= 2:
            stores[index - 2].wait()
        if index < 2:
            staged[index % 2] = dot_rows(ffn_in[:, rows], grad_pre[...])
            target = grad_up_hbm
        else:
            staged[index % 2] = dot_rows(cotangent[:, rows], hidden[...])
            target = grad_down_hbm
        store = pltpu.make_async_copy(
            staged.at[index % 2], target.at[pl.ds((index % 2) * half, half)], grad_sem.at[index]
        )
        store.start()
        stores.append(store)
    norm_total = jnp.zeros((8, width), jnp.float32)
    for block in range(blocks):
        at = slice(block * ROWS, (block + 1) * ROWS)
        values = middle[at, :]
        inverse = inverse_rms(values)
        hat = values * inverse
        grad_copies[block].wait()
        grad_inner = part[at, :] + other_grad[at, :]
        norm_total = norm_total + jnp.sum((grad_inner * hat).reshape(ROWS // 8, 8, width), axis=0)
        scaled = grad_inner * norm
        back = inverse * (scaled - hat * jnp.mean(scaled * hat, axis=1, keepdims=True))
        grad_values = cotangent[at, :].astype(jnp.float32) + back
        out_copies[block].wait()
        layer_low[at, :] = (values + (part_out[at, :] + other_out[at, :])).astype(jnp.bfloat16)
        middle[at, :] = grad_values
        low = grad_values.astype(jnp.bfloat16)
        grad_low[at, :] = low
        grad_context[at, :] = dot_last(low, output_ref[...]).astype(jnp.bfloat16)
        for index, (source, target) in enumerate(
            [
                (layer_low, layer_hbm),
                (middle, grad_middle_hbm),
                (grad_context, grad_context_hbm),
            ]
        ):
            rows = pl.ds(block * ROWS, ROWS)
            store = pltpu.make_async_copy(
                source.at[rows], target.at[rows], store_sem.at[index, block]
            )
            store.start()
            stores.append(store)
    grad_norm_ref[...] = jnp.sum(norm_total, axis=0, keepdims=True)
    grad_output_ref[...] = dot_rows(grad_low[...], context_ref[...])
    for store in stores[2:]:
        store.wait()


def middle_layer(context, stream, cotangent, output_proj, ffn_norm, up_proj, down_proj):
    tokens, width = stream.shape
    units = up_proj.shape[1]
    local = context.shape[1]
    blocks = tokens // ROWS
    whole = pl.BlockSpec(memory_space=pltpu.VMEM)
    far = pl.BlockSpec(memory_space=pl.ANY)
    wide_sum = pltpu.VMEM((tokens, width), jnp.float32)
    wide_low = pltpu.VMEM((tokens, width), jnp.bfloat16)
    unit_low = pltpu.VMEM((tokens, units), jnp.bfloat16)
    return pl.pallas_call(
        middle_kernel,
        out_shape=(
            jax.ShapeDtypeStruct((tokens, width), jnp.bfloat16),
            jax.ShapeDtypeStruct((tokens, width), jnp.float32),
            jax.ShapeDtypeStruct((tokens, local), jnp.bfloat16),
            jax.ShapeDtypeStruct((width, units), jnp.float32),
            jax.ShapeDtypeStruct((width, units), jnp.float32),
            jax.ShapeDtypeStruct((width, local), jnp.float32),
            jax.ShapeDtypeStruct((1, width), jnp.float32),
        ),
        in_specs=[whole, far, far, whole, whole, far, far],
        out_specs=(far, far, far, far, far, whole, whole),
        scratch_shapes=[
            wide_sum,
            wide_low,
            pltpu.VMEM((width, units), jnp.bfloat16),
            pltpu.VMEM((units, width), jnp.bfloat16),
            wide_sum,
            wide_sum,
            wide_sum,
            wide_sum,
            wide_sum,
            wide_low,
            unit_low,
            unit_low,
            pltpu.VMEM((2, width // 2, units), jnp.float32),
            wide_low,
            wide_low,
            pltpu.VMEM((tokens, local), jnp.bfloat16),
            pltpu.SemaphoreType.DMA((4,)),
            pltpu.SemaphoreType.DMA((3, blocks)),
            pltpu.SemaphoreType.DMA((4,)),
            pltpu.SemaphoreType.DMA((3, blocks)),
            pltpu.SemaphoreType.DMA((3, blocks)),
        ],
        compiler_params=pltpu.CompilerParams(
            collective_id=3, has_side_effects=True, vmem_limit_bytes=VMEM_LIMIT
        ),
        cost_estimate=pl.CostEstimate(
            flops=32 * 10**9, bytes_accessed=2 * 10**7, transcendentals=0
        ),
        name="middle_layer",
    )(context, stream, cotangent, output_proj, ffn_norm, up_proj, down_proj)


def end_kernel(
    grad_query_ref,
    grad_key_ref,
    grad_value_ref,
    query_proj_ref,
    key_proj_ref,
    value_proj_ref,
    input_ref,
    stream_hbm,
    grad_middle_hbm,
    norm_ref,
    roi_ref,
    pooled_ref,
    boxes_ref,
    docs_ref,
    pads_ref,
    grad_output_ref,
    down_hbm,
    landed_hbm,
    grad_stream_hbm,
    grad_heads_hbm,
    kept_hbm,
    second_hbm,
    grad_roi_ref,
    grad_map_ref,
    grad_norm_ref,
    info_ref,
    grad_heads,
    projections,
    stream,
    grad_stream,
    part,
    other,
    weight_grad,
    grad_low,
    grad_box,
    first,
    landed,
    load_sem,
    store_sem,
    grad_sem,
    send_sem,
    recv_sem,
    scatter_sem,
    scatter_send,
    scatter_recv,
):
    scatter = Scatter(first.shape[-1], 0, scatter_send, scatter_recv)
    greet_partner()
    norm = norm_ref[...].reshape(1, -1)
    greet_rows((scatter.across_x, scatter.across_y))
    first_loads = scatter.own_loads(down_hbm, first, scatter_sem)
    first_loads.append(pltpu.make_async_copy(landed_hbm, landed, scatter_sem.at[2]))
    for load in first_loads:
        load.start()
    tokens, width = stream_hbm.shape
    local = grad_query_ref.shape[1]
    blocks = tokens // ROWS
    loads = [
        pltpu.make_async_copy(stream_hbm, stream, load_sem.at[0]),
        pltpu.make_async_copy(grad_middle_hbm, grad_stream, load_sem.at[1]),
    ]
    for load in loads:
        load.start()
    for index, (grad, proj) in enumerate(
        (
            (grad_query_ref, query_proj_ref),
            (grad_key_ref, key_proj_ref),
            (grad_value_ref, value_proj_ref),
        )
    ):
        columns = slice(index * local, (index + 1) * local)
        grad_heads[:, columns] = grad[...]
        projections[:, columns] = proj[...]
    token_columns(boxes_ref, docs_ref, pads_ref, info_ref)
    copies = []
    for block in range(blocks):
        at = slice(block * ROWS, (block + 1) * ROWS)
        part[at, :] = dot_last(grad_heads[at, :], projections[...])
        if block == 0:
            for load in first_loads:
                load.wait()
            add_pairs(first, landed)
            pl.semaphore_wait(pltpu.get_barrier_semaphore(), 3)
            scatter.send_second(first, second_hbm)
            kept_stores = [
                pltpu.make_async_copy(first.at[0, :, scatter.y], kept_hbm.at[0], scatter_sem.at[0]),
                pltpu.make_async_copy(first.at[1, :, scatter.x], kept_hbm.at[1], scatter_sem.at[1]),
            ]
            for store in kept_stores:
                store.start()
        copy = partner_copy(
            part.at[pl.ds(block * ROWS, ROWS)],
            other.at[pl.ds(block * ROWS, ROWS)],
            send_sem.at[block],
            recv_sem.at[block],
        )
        copy.start()
        copies.append(copy)
    weight_grad[:, : 3 * local] = dot_rows(input_ref[...], grad_heads[...])
    weight_grad[:, 3 * local :] = grad_output_ref[...]
    weight_store = pltpu.make_async_copy(weight_grad, grad_heads_hbm, grad_sem)
    weight_store.start()
    for load in loads:
        load.wait()
    stores = []
    norm_total = jnp.zeros((8, width), jnp.float32)
    for block in range(blocks):
        at = slice(block * ROWS, (block + 1) * ROWS)
        values = stream[at, :]
        inverse = inverse_rms(values)
        hat = values * inverse
        copies[block].wait()
        grad_inner = part[at, :] + other[at, :]
        norm_total = norm_total + jnp.sum((grad_inner * hat).reshape(ROWS // 8, 8, width), axis=0)
        scaled = grad_inner * norm
        back = inverse * (scaled - hat * jnp.mean(scaled * hat, axis=1, keepdims=True))
        grad_values = grad_stream[at, :] + back
        grad_stream[at, :] = grad_values
        rows = pl.ds(block * ROWS, ROWS)
        store = pltpu.make_async_copy(
            grad_stream.at[rows], grad_stream_hbm.at[rows], store_sem.at[block]
        )
        store.start()
        stores.append(store)
        low = grad_values.astype(jnp.bfloat16)
        grad_low[at, :] = low
        area = (info_ref[at, 5:6] - info_ref[at, 1:2]) * (info_ref[at, 4:5] - info_ref[at, 0:1])
        grad_box[at, :] = split_two(dot_last(low, roi_ref[...]) / area.astype(jnp.float32))
    grad_norm_ref[...] = jnp.sum(norm_total, axis=0, keepdims=True)
    tile_rows = grad_map_ref.shape[0] // 128
    first_row = lax.axis_index("tensor") * tile_rows
    column = lax.broadcasted_iota(jnp.int32, (128, tokens), 0)
    inside = jnp.where(
        (column >= boxes_ref[0]) & (column < boxes_ref[2]), 1.0, 0.0
    ).astype(jnp.bfloat16)
    top = boxes_ref[1] - first_row
    bottom = boxes_ref[3] - first_row
    for row in range(tile_rows):
        chosen = jnp.where((top <= row) & (bottom > row), 1.0, 0.0).astype(jnp.bfloat16)
        sums = dot_plain(inside * chosen, grad_box[...])
        grad_map_ref[row * 128 : (row + 1) * 128, :] = sums[:, :128] + sums[:, 128:]
    grad_roi_ref[...] = dot_rows(grad_low[...], pooled_ref[...])
    for store in kept_stores:
        store.wait()
    scatter.await_second(second_hbm)
    scatter.sent_second(second_hbm)
    weight_store.wait()
    for store in stores:
        store.wait()


def end_layer(
    grad_heads,
    projections,
    attn_in,
    stream,
    grad_middle,
    attn_norm,
    roi_proj,
    pooled,
    places,
    grad_output,
    down,
    landed,
    pixels,
):
    tokens, width = stream.shape
    local = grad_heads[0].shape[1]
    blocks = tokens // ROWS
    whole = pl.BlockSpec(memory_space=pltpu.VMEM)
    far = pl.BlockSpec(memory_space=pltpu.HBM)
    wide_sum = pltpu.VMEM((tokens, width), jnp.float32)
    _, depths, _, rows, half = landed.shape
    return pl.pallas_call(
        end_kernel,
        out_shape=(
            jax.ShapeDtypeStruct((tokens, width), jnp.float32),
            jax.ShapeDtypeStruct((width, 4 * local), jnp.float32),
            jax.ShapeDtypeStruct((2, depths, rows, half), jnp.float32),
            jax.ShapeDtypeStruct((2, depths, rows, half), jnp.float32),
            jax.ShapeDtypeStruct((width, 128), jnp.float32),
            jax.ShapeDtypeStruct((pixels, 128), jnp.float32),
            jax.ShapeDtypeStruct((1, width), jnp.float32),
        ),
        in_specs=[whole] * 7 + [far, far] + [whole] * 7 + [far, far],
        out_specs=(far, far, far, far, whole, whole, whole),
        scratch_shapes=[
            pltpu.VMEM((tokens, 8), jnp.int32),
            pltpu.VMEM((tokens, 3 * local), jnp.bfloat16),
            pltpu.VMEM((width, 3 * local), jnp.bfloat16),
            wide_sum,
            wide_sum,
            wide_sum,
            wide_sum,
            pltpu.VMEM((width, 4 * local), jnp.float32),
            pltpu.VMEM((tokens, width), jnp.bfloat16),
            pltpu.VMEM((tokens, 256), jnp.bfloat16),
            pltpu.VMEM(landed.shape, jnp.float32),
            pltpu.VMEM(landed.shape, jnp.float32),
            pltpu.SemaphoreType.DMA((2,)),
            pltpu.SemaphoreType.DMA((blocks,)),
            pltpu.SemaphoreType.DMA,
            pltpu.SemaphoreType.DMA((blocks,)),
            pltpu.SemaphoreType.DMA((blocks,)),
            pltpu.SemaphoreType.DMA((3,)),
            *scatter_semaphores(4),
        ],
        compiler_params=pltpu.CompilerParams(
            collective_id=4, has_side_effects=True, vmem_limit_bytes=VMEM_LIMIT
        ),
        cost_estimate=pl.CostEstimate(
            flops=15 * 10**9, bytes_accessed=2 * 10**7, transcendentals=0
        ),
        name="end_layer",
    )(
        *grad_heads,
        *projections,
        attn_in,
        stream,
        grad_middle,
        attn_norm,
        roi_proj,
        pooled,
        *places,
        grad_output,
        down,
        landed,
    )


def unpack_kernel(
    places,
    sums_ref,
    own_ref,
    layer_in,
    stream_in,
    layer_out,
    stream_out,
    first_out,
    convs_out,
    gain_out,
    shift_out,
    roi_out,
    attn_norm_out,
    query_out,
    key_out,
    value_out,
    output_out,
    tables_out,
    ffn_norm_out,
    up_out,
    down_out,
    layer_kept,
    stream_kept,
    sem,
):
    loads = [
        pltpu.make_async_copy(layer_in, layer_kept, sem.at[0]),
        pltpu.make_async_copy(stream_in, stream_kept, sem.at[1]),
    ]
    copies = [
        pltpu.make_async_copy(layer_kept, layer_out, sem.at[0]),
        pltpu.make_async_copy(stream_kept, stream_out, sem.at[1]),
    ]
    for load in loads:
        load.start()
    for target, begin in places:
        if target == "first":
            first_out[...] = sums_ref[begin : begin + first_out.shape[0], :]
        if target == "gain":
            gain_out[...] = sums_ref[begin : begin + LAYERS, :]
        if target == "shift":
            shift_out[...] = sums_ref[begin : begin + LAYERS, :]
        if target == "roi":
            roi_out[...] = sums_ref[begin : begin + roi_out.shape[0], :]
        if target == "small":
            attn_norm_out[...] = sums_ref[begin : begin + 1, : attn_norm_out.shape[1]]
            ffn_norm_out[...] = sums_ref[begin + 1 : begin + 2, : ffn_norm_out.shape[1]]
            for table in range(3):
                tables_out[table] = sums_ref[
                    begin + 2 : begin + 2 + tables_out.shape[1],
                    table * NBUCKET : (table + 1) * NBUCKET,
                ]
    for level in range(8):
        convs_out[level] = sums_ref[level * 128 : (level + 1) * 128, :]
    up_out[...] = own_ref[0]
    down_out[...] = own_ref[2]
    part = query_out.shape[1]
    for index, target in enumerate((query_out, key_out, value_out, output_out)):
        target[...] = own_ref[1, :, index * part : (index + 1) * part]
    for load, copy in zip(loads, copies):
        load.wait()
        copy.start()
    for copy in copies:
        copy.wait()


def unpack(sums, own, layer_out, grad_stream, planes, heads):
    _, own_rows, columns = own.shape
    whole = pl.BlockSpec(memory_space=pltpu.VMEM)
    far = pl.BlockSpec(memory_space=pl.ANY)
    places = (("first", 1024), ("gain", 1032), ("shift", 1048), ("small", 1064), ("roi", 1072))

    def sized(*shape):
        return jax.ShapeDtypeStruct(shape, jnp.float32)

    return pl.pallas_call(
        functools.partial(unpack_kernel, places),
        out_shape=(
            jax.ShapeDtypeStruct(layer_out.shape, layer_out.dtype),
            jax.ShapeDtypeStruct(grad_stream.shape, grad_stream.dtype),
            sized(planes, 128),
            sized(8, 128, 128),
            sized(LAYERS, 128),
            sized(LAYERS, 128),
            sized(own_rows, 128),
            sized(1, own_rows),
            *[sized(own_rows, columns // 4)] * 4,
            sized(3, heads, NBUCKET),
            sized(1, own_rows),
            sized(own_rows, columns),
            sized(own_rows, columns),
        ),
        in_specs=[whole, whole, far, far],
        out_specs=(far, far) + (whole,) * 14,
        scratch_shapes=[
            pltpu.VMEM(layer_out.shape, layer_out.dtype),
            pltpu.VMEM(grad_stream.shape, grad_stream.dtype),
            pltpu.SemaphoreType.DMA((2,)),
        ],
        compiler_params=pltpu.CompilerParams(vmem_limit_bytes=VMEM_LIMIT),
        name="unpack",
    )(sums, own, layer_out, grad_stream)


def on_device(
    page_image,
    embeddings,
    cotangent,
    doc_ids,
    pad_mask,
    token_boxes,
    conv_first,
    conv_weights,
    group_gain,
    group_shift,
    roi_proj,
    attn_norm,
    query_proj,
    key_proj,
    value_proj,
    output_proj,
    bias_tables,
    ffn_norm,
    up_proj,
    down_proj,
):
    devices = lax.axis_size("dp") * lax.axis_size("tensor")
    feature_map, *records = stem_forward(
        page_image, conv_first, conv_weights, group_gain, group_shift, devices
    )
    places = (token_boxes, doc_ids, pad_mask)
    tables = bias_tables.swapaxes(1, 2)
    pooled, stream, attn_in, heads = box_forward(
        feature_map, places, embeddings, roi_proj, attn_norm, query_proj, key_proj, value_proj
    )
    context, exact, lse = attention_forward(tables, places, heads)
    layer_out, grad_middle, grad_context, grad_up, grad_down, grad_output, grad_ffn_norm = (
        middle_layer(context, stream, cotangent, output_proj, ffn_norm, up_proj, down_proj)
    )
    rows_count = lax.axis_size("dp")
    width = stream.shape[1]
    own_rows = width // rows_count

    def by_place(values):
        return values.reshape(rows_count // 4, 2, 2, own_rows, values.shape[1])

    down, up = by_place(grad_down), by_place(grad_up)
    *grad_heads, diagonals, landed, early = attention_backward(
        tables, places, heads, grad_context, exact, lse, down, up
    )
    grad_tables = bucket_grads(diagonals)
    grad_stream, grad_attn, kept, second, grad_roi, grad_map, grad_attn_norm = end_layer(
        grad_heads,
        (query_proj, key_proj, value_proj),
        attn_in,
        stream,
        grad_middle,
        attn_norm,
        roi_proj,
        pooled,
        places,
        grad_output,
        down,
        landed,
        feature_map.shape[0],
    )
    local_heads = grad_tables.shape[0]
    split = grad_roi.reshape(rows_count, 2, own_rows // 2, grad_roi.shape[1])
    sums, own = stem_backward(
        grad_map,
        page_image,
        records,
        conv_weights,
        group_gain,
        group_shift,
        split,
        (grad_attn_norm, grad_ffn_norm),
        grad_tables,
        up,
        by_place(grad_attn),
        kept,
        second,
        early,
        devices,
    )
    outs = list(
        unpack(sums, own, layer_out, grad_stream, conv_first.shape[0], local_heads)
    )
    outs[6] = outs[6].T
    outs[7] = outs[7][0]
    outs[11] = outs[11].T
    outs[12] = outs[12].swapaxes(1, 2)
    outs[13] = outs[13][0]
    outs[15] = outs[15].T
    return tuple(outs)


def solution(mesh):
    placed = (
        P(None, ("dp", "tensor"), None),
        P("dp", None),
        P("dp", None),
        P("dp", None),
        P("dp", None),
        P(None, "dp", None),
        P(),
        P(),
        P(),
        P(),
        P(),
        P(),
        P(None, "tensor"),
        P(None, "tensor"),
        P(None, "tensor"),
        P("tensor", None),
        P(None, None, "tensor"),
        P(),
        P(None, "tensor"),
        P("tensor", None),
    )
    return jax.shard_map(
        on_device,
        mesh=mesh,
        in_specs=placed,
        out_specs=(
            P("dp", None),
            P("dp", None),
            P(),
            P(),
            P(),
            P(),
            P(None, "dp"),
            P("dp"),
            P("dp", "tensor"),
            P("dp", "tensor"),
            P("dp", "tensor"),
            P("tensor", "dp"),
            P(None, None, "tensor"),
            P("dp"),
            P("dp", "tensor"),
            P("tensor", "dp"),
        ),
        check_vma=False,
    )
```

```python
import functools

import jax
import jax.numpy as jnp
import numpy as np
from jax import lax
from jax.experimental import pallas as pl
from jax.experimental.pallas import tpu as pltpu
from jax.sharding import PartitionSpec as P

HDIM = 64
NBUCKET = 32
VMEM_LIMIT = 63 * 2**20
GROUPS = 32


bucket_edges = (12, 16, 23, 32, 46, 64, 91)
norm_eps = 1e-06
group_eps = 1e-05
masked_score = -1e30
highest = lax.Precision.HIGHEST


def bucket_of(relative):
    magnitude = jnp.abs(relative)
    coarse = jnp.full(relative.shape, 8, jnp.int32)
    for edge in bucket_edges:
        coarse = coarse + (magnitude >= edge).astype(jnp.int32)
    return jnp.where(magnitude < 8, magnitude, coarse) + jnp.where(relative > 0, 16, 0).astype(
        jnp.int32
    )


MESH = pl.DeviceIdType.MESH
LAYERS = 9
PIX_CHUNK = 256


def level_of(layer):
    return layer if layer <= 4 else 8 - layer


def stem_rows(pixels):
    return [pixels >> (2 * level_of(layer)) for layer in range(LAYERS)]


def row_starts(rows):
    starts = [0]
    for count in rows:
        starts.append(starts[-1] + count)
    return starts


def split_two(values):
    high = values.astype(jnp.bfloat16)
    low = (values - high.astype(jnp.float32)).astype(jnp.bfloat16)
    return jnp.concatenate([high, low], axis=1)


def group_sum(values):
    lane = lax.broadcasted_iota(jnp.int32, values.shape, 1)
    pairs = values + jnp.where(
        lane % 2 == 0, pltpu.roll(values, 127, 1), pltpu.roll(values, 1, 1)
    )
    return pairs + jnp.where(
        (lane // 2) % 2 == 0, pltpu.roll(pairs, 126, 1), pltpu.roll(pairs, 2, 1)
    )


def wide(row):
    return jnp.broadcast_to(row, (8, row.shape[1]))


def my_index():
    return lax.axis_index("dp") * 2 + lax.axis_index("tensor")


def greet_all(count):
    barrier = pltpu.get_barrier_semaphore()
    me = my_index()

    def greet(step, carry):
        other = lax.rem(me + step, count)
        pl.semaphore_signal(
            barrier, inc=1, device_id=(other // 2, lax.rem(other, 2)), device_id_type=MESH
        )
        return carry

    lax.fori_loop(1, count, greet, 0)


def greeted(count):
    pl.semaphore_wait(pltpu.get_barrier_semaphore(), count - 1)


def send_all(count, source, target, send_sem, recv_sem):
    me = my_index()

    def send(step, carry):
        other = lax.rem(me + step, count)
        pltpu.make_async_remote_copy(
            src_ref=source,
            dst_ref=target,
            send_sem=send_sem,
            recv_sem=recv_sem,
            device_id=(other // 2, lax.rem(other, 2)),
            device_id_type=MESH,
        ).start()
        return carry

    lax.fori_loop(1, count, send, 0, unroll=count <= 32)


def wait_all(count, slots, sem):
    part = slots.at[pl.ds(0, count - 1)]
    pltpu.make_async_copy(part, part, sem).wait()


def natural_places(tile_rows, columns):
    spacing = columns // 8
    places = []
    for row in range(tile_rows):
        for col in range(spacing):
            place = 0
            for bit in range(4):
                place = place * 4 + ((row >> bit) & 1) * 2 + ((col >> bit) & 1)
            places.append((row * columns + col, place * 8))
    return places


SCHEDULE = {
    8: 'u1b v1a d3a',
    7: 'v1b d3b small',
    6: 'u2 e3a split',
    5: 'a1a e3b',
    4: 'a1b v2 u3a',
    3: 'u3b b1a rows',
    2: 'v3a b1b',
    1: 'v3b a2 kept',
    0: 'a3a b2',
    'end': 'a3b',
    'last': 'b3a b3b',
}


def place_of(row):
    return row // 4, lax.rem(row // 2, 2), lax.rem(row, 2)


def start_remote(source, target, send_sem, recv_sem, row):
    pltpu.make_async_remote_copy(
        src_ref=source,
        dst_ref=target,
        send_sem=send_sem,
        recv_sem=recv_sem,
        device_id=(row, lax.axis_index("tensor")),
        device_id_type=MESH,
    ).start()


def await_bytes(buffer, sem):
    pltpu.make_async_copy(buffer, buffer, sem).wait()


def greet_rows(rows):
    for row in rows:
        pl.semaphore_signal(
            pltpu.get_barrier_semaphore(),
            inc=1,
            device_id=(row, lax.axis_index("tensor")),
            device_id_type=MESH,
        )


class Scatter:
    def __init__(self, width, left, send_sem, recv_sem):
        self.row = lax.axis_index("dp")
        self.z, self.y, self.x = place_of(self.row)
        self.across_x = self.row + 1 - 2 * self.x
        self.across_y = self.row + 2 - 4 * self.y
        self.width, self.left = width, left
        self.send_sem, self.recv_sem = send_sem, recv_sem

    def columns(self, source):
        half = source.shape[-1] // 2
        return pl.ds(self.left, self.width), pl.ds(half + self.left, self.width)

    def own_loads(self, source, own, sem):
        first, second = self.columns(source)
        return [
            pltpu.make_async_copy(source.at[:, :, self.x, :, first], own.at[0], sem.at[0]),
            pltpu.make_async_copy(source.at[:, self.y, :, :, second], own.at[1], sem.at[1]),
        ]

    def send_first(self, source, target, begin, size, shift=0):
        first, second = self.columns(source)
        depth = pl.ds(begin, size)
        landing = pl.ds(begin - shift, size)
        start_remote(
            source.at[depth, :, 1 - self.x, :, first],
            target.at[0, landing],
            self.send_sem.at[0],
            self.recv_sem.at[0],
            self.across_x,
        )
        start_remote(
            source.at[depth, 1 - self.y, :, :, second],
            target.at[1, landing],
            self.send_sem.at[1],
            self.recv_sem.at[1],
            self.across_y,
        )

    def await_first(self, landed):
        for side in range(2):
            await_bytes(landed.at[side], self.recv_sem.at[side])

    def sent_first(self, landed):
        for side in range(2):
            await_bytes(landed.at[side], self.send_sem.at[side])

    def send_second(self, source, target):
        start_remote(
            source.at[0, :, 1 - self.y],
            target.at[0],
            self.send_sem.at[2],
            self.recv_sem.at[2],
            self.across_y,
        )
        start_remote(
            source.at[1, :, 1 - self.x],
            target.at[1],
            self.send_sem.at[3],
            self.recv_sem.at[3],
            self.across_x,
        )

    def await_second(self, landed):
        for side in range(2):
            await_bytes(landed.at[side], self.recv_sem.at[2 + side])

    def sent_second(self, landed):
        for side in range(2):
            await_bytes(landed.at[side], self.send_sem.at[2 + side])

    def along_z(self, total, target, step):
        depths = total.shape[1]
        begins = [0]
        for index in range(step):
            begins.append(begins[-1] + (depths >> (index + 1)))
        bit = lax.rem(self.z // (1 << step), 2)
        if step == 0:
            return total, 0, begins[0], depths >> 1, bit
        return target, begins[step - 1], begins[step], depths >> (step + 1), bit

    def send_along(self, total, target, step):
        source, begin, landing, blocks, bit = self.along_z(total, target, step)
        other = self.row + (1 - 2 * bit) * (4 << step)
        for block in range(blocks):
            start_remote(
                source.at[:, begin + 2 * block + 1 - bit],
                target.at[:, landing + block],
                self.send_sem.at[4 + step],
                self.recv_sem.at[4 + step],
                other,
            )

    def add_along(self, total, target, step):
        source, begin, landing, blocks, bit = self.along_z(total, target, step)
        await_bytes(target.at[:, pl.ds(landing, blocks)], self.recv_sem.at[4 + step])
        for side in range(2):
            for block in range(blocks):
                target[side, landing + block] = (
                    target[side, landing + block] + source[side, begin + 2 * block + bit]
                )

    def finish(self, total, target, result, base, step):
        steps = z_steps(total.shape[1])
        for index in range(step, steps):
            if index > step:
                self.send_along(total, target, index)
            self.add_along(total, target, index)
        landing = self.along_z(total, target, steps - 1)[2]
        half = result.shape[-1] // 2
        for side in range(2):
            at = side * half + self.left
            result[base, :, at : at + self.width] = target[side, landing]

    def sent_along(self, total, target):
        for step in range(z_steps(total.shape[1])):
            _, _, landing, blocks, _ = self.along_z(total, target, step)
            await_bytes(target.at[:, pl.ds(landing, blocks)], self.send_sem.at[4 + step])


def z_steps(depths):
    return depths.bit_length() - 1


def add_pairs(left, right):
    for side in range(left.shape[0]):
        for depth in range(left.shape[1]):
            left[side, depth] = left[side, depth] + right[side, depth]


def scatter_semaphores(copies):
    return [pltpu.SemaphoreType.DMA((copies,)), pltpu.SemaphoreType.DMA((copies,))]


class ScatterHere(Scatter):
    refs = 8

    @staticmethod
    def scratch(depths, rows, width):
        pair = pltpu.VMEM((2, depths, 2, rows, width), jnp.float32)
        one = pltpu.VMEM((2, depths, rows, width), jnp.float32)
        return [pair, pair, one, one, one, pltpu.SemaphoreType.DMA((2,)), *scatter_semaphores(4 + z_steps(depths))]

    def __init__(self, source, left, refs):
        self.source = source
        self.own, self.first, self.second, self.total, self.third, load_sem, send, recv = refs
        super().__init__(self.own.shape[-1], left, send, recv)
        self.loads = self.own_loads(source, self.own, load_sem)
        for load in self.loads:
            load.start()

    def start_first(self, part):
        size = self.own.shape[1] // 2
        self.send_first(self.source, self.first, part * size, size)

    def start_second(self, landed=None):
        for load in self.loads:
            load.wait()
        self.await_first(self.first if landed is None else landed)
        add_pairs(self.own, self.first)
        self.send_second(self.own, self.second)

    def add_second(self):
        self.await_second(self.second)
        for side in range(2):
            kept = self.y if side == 0 else self.x
            for depth in range(self.total.shape[1]):
                self.total[side, depth] = self.own[side, depth, kept] + self.second[side, depth]

    def third_first(self):
        self.add_second()
        self.send_along(self.total, self.third, 0)

    def third_next(self):
        self.add_along(self.total, self.third, 0)
        self.send_along(self.total, self.third, 1)

    def end(self, result, base):
        self.finish(self.total, self.third, result, base, 1)

    def sent(self, landed=None):
        self.sent_first(self.first if landed is None else landed)
        self.sent_second(self.second)
        self.sent_along(self.total, self.third)


class ScatterRest(Scatter):
    refs = 6

    @staticmethod
    def scratch(depths, rows, width):
        one = pltpu.VMEM((2, depths, rows, width), jnp.float32)
        return [one, one, one, pltpu.SemaphoreType.DMA((2,)), *scatter_semaphores(4 + z_steps(depths))]

    def __init__(self, kept, arrived, left, refs):
        self.total, self.second, self.third, load_sem, send, recv = refs
        width = self.total.shape[-1]
        super().__init__(width, left, send, recv)
        columns = pl.ds(left, width)
        self.loads = [
            pltpu.make_async_copy(kept.at[:, :, :, columns], self.total, load_sem.at[0]),
            pltpu.make_async_copy(arrived.at[:, :, :, columns], self.second, load_sem.at[1]),
        ]
        for load in self.loads:
            load.start()

    def third_first(self):
        for load in self.loads:
            load.wait()
        add_pairs(self.total, self.second)
        self.send_along(self.total, self.third, 0)

    third_next = ScatterHere.third_next
    end = ScatterHere.end

    def sent(self):
        self.sent_along(self.total, self.third)


def stem_forward_kernel(
    count,
    places,
    image_ref,
    first_ref,
    weights_ref,
    gain_ref,
    shift_ref,
    feature_ref,
    norm_hbm,
    input_hbm,
    scale_ref,
    norm_ref,
    input_ref,
    natural,
    skip,
    current,
    source,
    slots,
    send_sem,
    recv_sem,
    store_sem,
):
    me = my_index()
    greet_all(count)
    pixels = feature_ref.shape[0]
    rows = stem_rows(pixels)
    norm_at = row_starts(rows)
    input_at = row_starts(rows[1:])
    skip_at = row_starts(rows[:4])
    spacing = 16
    for row in range(image_ref.shape[1]):
        natural[row * 128 : (row + 1) * 128, :] = lax.dot_general(
            image_ref[:, row, :],
            first_ref[...],
            (((0,), (0,)), ((), ())),
            preferred_element_type=jnp.float32,
        )
    for start, place in places:
        norm_ref[place : place + 8, :] = natural[pl.ds(start, 8, stride=spacing), :]
    stores = []
    for layer in range(LAYERS):
        height = rows[layer]
        chunk = min(height, PIX_CHUNK)
        base = norm_at[layer]
        total = jnp.zeros((8, 128), jnp.float32)
        if layer > 0:
            weights = weights_ref[layer - 1]
            stacked = jnp.concatenate([weights, weights], axis=0)

            def convolve(index, total):
                at = pl.multiple_of(index * chunk, chunk)
                values = jnp.dot(
                    split_two(input_ref[pl.ds(input_at[layer - 1] + at, chunk), :]),
                    stacked,
                    preferred_element_type=jnp.float32,
                )
                norm_ref[pl.ds(base + at, chunk), :] = values
                return total + jnp.sum(values.reshape(chunk // 8, 8, 128), axis=0)

        else:

            def convolve(index, total):
                at = pl.multiple_of(index * chunk, chunk)
                values = norm_ref[pl.ds(base + at, chunk), :]
                return total + jnp.sum(values.reshape(chunk // 8, 8, 128), axis=0)

        total = lax.fori_loop(0, height // chunk, convolve, total, unroll=True)
        mean = jnp.sum(total, axis=0, keepdims=True) * (1.0 / height)

        def deviate(index, total):
            at = pl.multiple_of(index * chunk, chunk)
            values = norm_ref[pl.ds(base + at, chunk), :] - mean
            return total + jnp.sum((values * values).reshape(chunk // 8, 8, 128), axis=0)

        square = lax.fori_loop(0, height // chunk, deviate, jnp.zeros((8, 128), jnp.float32), unroll=True)
        square = jnp.sum(square, axis=0, keepdims=True)
        stats = jnp.concatenate([mean, square], axis=0)
        source[layer] = stats
        slots[layer, me] = stats
        if layer == 0:
            greeted(count)
        send_all(
            count,
            source.at[layer],
            slots.at[layer, me],
            send_sem.at[layer],
            recv_sem.at[layer],
        )
        wait_all(count, slots.at[layer], recv_sem.at[layer])
        means = slots[layer, :, 0, :]
        centre = group_sum(wide(jnp.sum(means, axis=0, keepdims=True))) * (0.25 / count)
        apart = means - centre[0:1]
        spread = jnp.sum(slots[layer, :, 1, :], axis=0, keepdims=True) + height * jnp.sum(
            apart * apart, axis=0, keepdims=True
        )
        variance = group_sum(wide(spread)) * (1.0 / (4 * height * count))
        inverse = lax.rsqrt(variance + group_eps)[0:1]
        centre = centre[0:1]
        scale_ref[layer : layer + 1, :] = inverse
        gain = gain_ref[layer : layer + 1, :]
        shift = shift_ref[layer : layer + 1, :]

        def activate(start, size):
            normed = (norm_ref[pl.ds(base + start, size), :] - centre) * inverse
            norm_ref[pl.ds(base + start, size), :] = normed
            lifted = normed * gain + shift
            return lifted / (1.0 + jnp.exp(-lifted))

        if layer < 4:
            quarter = height // 4
            part = min(quarter, 64)

            def pool(index, carry):
                at = pl.multiple_of(index * part, part)
                mean_of = jnp.zeros((part, 128), jnp.float32)
                for corner in range(4):
                    value = activate(corner * quarter + at, part)
                    skip[pl.ds(skip_at[layer] + corner * quarter + at, part), :] = value
                    mean_of = mean_of + value
                input_ref[pl.ds(input_at[layer] + at, part), :] = mean_of * 0.25
                return carry

            lax.fori_loop(0, quarter // part, pool, 0, unroll=True)
        elif layer < 8:
            part = min(height, 64)
            skipped = skip_at[7 - layer]

            def grow(index, carry):
                at = pl.multiple_of(index * part, part)
                value = activate(at, part)
                for corner in range(4):
                    place = corner * height + at
                    input_ref[pl.ds(input_at[layer] + place, part), :] = (
                        value + skip[pl.ds(skipped + place, part), :]
                    )
                return carry

            lax.fori_loop(0, height // part, grow, 0, unroll=True)
        else:

            def finish(index, carry):
                at = pl.multiple_of(index * chunk, chunk)
                current[pl.ds(at, chunk), :] = activate(at, chunk)
                return carry

            lax.fori_loop(0, height // chunk, finish, 0, unroll=True)
        parts = [(norm_ref, norm_hbm, base, height)]
        if layer < 8:
            parts.append((input_ref, input_hbm, input_at[layer], rows[layer + 1]))
        for index, (source_ref, target, begin, size) in enumerate(parts):
            store = pltpu.make_async_copy(
                source_ref.at[pl.ds(begin, size)],
                target.at[pl.ds(begin, size)],
                store_sem.at[index, layer],
            )
            store.start()
            stores.append(store)
    for start, place in places:
        feature_ref[pl.ds(start, 8, stride=spacing), :] = current[place : place + 8, :]
    for layer in range(LAYERS):
        wait_all(count, slots.at[layer], send_sem.at[layer])
    for store in stores:
        store.wait()


def stem_backward_kernel(
    count,
    places,
    grad_ref,
    image_ref,
    norm_hbm,
    input_hbm,
    scale_ref,
    weights_ref,
    gain_ref,
    shift_ref,
    split_ref,
    attn_norm_ref,
    ffn_norm_ref,
    tables_ref,
    up_ref,
    attn_ref,
    kept_ref,
    second_ref,
    early_ref,
    small_out,
    large_out,
    norm_ref,
    input_ref,
    natural,
    ordered,
    active,
    grad_conv,
    skip,
    grads,
    product,
    source,
    slots,
    first_source,
    first_slots,
    parts,
    shared,
    send_sem,
    recv_sem,
    part_send,
    part_recv,
    share_send,
    share_recv,
    split_slots,
    split_half,
    small_ref,
    small_slots,
    row_send,
    row_recv,
    load_sem,
    *scatter_refs,
):
    me = my_index()
    row = lax.axis_index("dp")
    core = lax.axis_index("tensor")
    rows_count = count // 2
    greet_all(count)
    pixels = grad_ref.shape[0]
    rows = stem_rows(pixels)
    norm_at = row_starts(rows)
    input_at = row_starts(rows[1:])
    loads = []
    for index, (source_ref, target, begin, size) in enumerate(
        [
            (norm_hbm, norm_ref, norm_at[8], rows[8]),
            (input_hbm, input_ref, input_at[7], rows[8]),
            (norm_hbm, norm_ref, 0, norm_at[8]),
            (input_hbm, input_ref, 0, input_at[7]),
        ]
    ):
        loads.append(
            pltpu.make_async_copy(
                source_ref.at[pl.ds(begin, size)], target.at[pl.ds(begin, size)], load_sem.at[index]
            )
        )
        loads[-1].start()
    jobs = []
    for index, (source_ref, left) in enumerate(
        [(up_ref, 0), (up_ref, 1), (attn_ref, 0), (attn_ref, 1)]
    ):
        refs = scatter_refs[index * ScatterHere.refs : (index + 1) * ScatterHere.refs]
        jobs.append(ScatterHere(source_ref, left * refs[0].shape[-1], refs))
    rest = 4 * ScatterHere.refs
    for index in range(2):
        refs = scatter_refs[rest + index * ScatterRest.refs : rest + (index + 1) * ScatterRest.refs]
        jobs.append(ScatterRest(kept_ref, second_ref, index * refs[0].shape[-1], refs))
    up_left, up_right, attn_left, attn_right, down_left, down_right = jobs
    early = up_left.first.shape[1] // 2
    early_load = pltpu.make_async_copy(
        early_ref, up_left.first.at[:, pl.ds(0, early)], load_sem.at[4]
    )
    early_load.start()
    up_landed = up_left.first.at[:, pl.ds(early, early)]
    small_rows, split_rows = 1064, 1072
    own_rows = 2 * split_half.shape[1]
    small_ref[...] = jnp.zeros_like(small_ref)
    for device in range(rows_count):
        lanes = slice(device * own_rows, (device + 1) * own_rows)
        small_ref[device, 0:1, :own_rows] = attn_norm_ref[:, lanes]
        small_ref[device, 1:2, :own_rows] = ffn_norm_ref[:, lanes]
        small_ref[device, 2 : 2 + tables_ref.shape[0], : tables_ref.shape[1]] = tables_ref[...]
    skip_at = row_starts(rows[:4])
    spacing = 16
    owners = count // 8
    owned = parts.shape[1]
    for start, place in places:
        ordered[place : place + 8, :] = grad_ref[pl.ds(start, 8, stride=spacing), :]

    def send_rows(first, last, source_of, target, place):
        def send(step, carry):
            other = lax.rem(row + step, rows_count)
            pltpu.make_async_remote_copy(
                src_ref=source_of(other),
                dst_ref=target.at[row],
                send_sem=row_send.at[place],
                recv_sem=row_recv.at[place],
                device_id=(other, core),
                device_id_type=MESH,
            ).start()
            return carry

        lax.fori_loop(first, last, send, 0)

    def weight_grad(layer):
        height = rows[layer]
        chunk = min(height, 512)

        def add(index, total):
            at = pl.multiple_of(index * chunk, chunk)
            return total + lax.dot_general(
                input_ref[pl.ds(input_at[layer - 1] + at, chunk), :].astype(jnp.bfloat16),
                grad_conv[pl.ds(norm_at[layer] + at, chunk), :].astype(jnp.bfloat16),
                (((0,), (0,)), ((), ())),
                preferred_element_type=jnp.float32,
            )

        product[layer - 1] = lax.fori_loop(
            0, height // chunk, add, jnp.zeros((128, 128), jnp.float32), unroll=True
        ).reshape(owners, owned, 128)

        def send(index, carry):
            owner = layer - 1 + 8 * index

            @pl.when(owner != me)
            def _():
                pltpu.make_async_remote_copy(
                    src_ref=product.at[layer - 1, index],
                    dst_ref=parts.at[me],
                    send_sem=part_send,
                    recv_sem=part_recv,
                    device_id=(owner // 2, lax.rem(owner, 2)),
                    device_id_type=MESH,
                ).start()

            @pl.when(owner == me)
            def _():
                parts[me] = product[layer - 1, index]

            return carry

        lax.fori_loop(0, owners, send, 0)

    def send_small():
        small_slots[row] = small_ref[row]
        send_rows(1, rows_count, lambda other: small_ref.at[other], small_slots, 0)

    def send_split():
        split_slots[row] = split_ref[row, core]
        send_rows(1, rows_count, lambda other: split_ref.at[other, core], split_slots, 1)

    def add_rows():
        wait_all(rows_count, small_slots, row_recv.at[0])
        small_out[small_rows : small_rows + 8, :] = jnp.sum(small_slots[...], axis=0)
        wait_all(rows_count, split_slots, row_recv.at[1])
        split_half[core] = jnp.sum(split_slots[...], axis=0)
        swap.start()

    def keep_rows():
        swap.wait()
        size = split_half.shape[1]
        for part in range(2):
            begin = split_rows + part * size
            small_out[begin : begin + size, :] = split_half[part]

    swap = pltpu.make_async_remote_copy(
        src_ref=split_half.at[core],
        dst_ref=split_half.at[core],
        send_sem=row_send.at[2],
        recv_sem=row_recv.at[2],
        device_id=(row, 1 - core),
        device_id_type=MESH,
    )

    def second_of_up():
        early_load.wait()
        up_left.start_second(up_landed)

    steps = {
        "small": send_small,
        "split": send_split,
        "rows": add_rows,
        "kept": keep_rows,
        "u1b": lambda: up_left.start_first(1),
        "u2": second_of_up,
    }
    for mark, job in zip("uvabde", jobs):
        if mark in "vab":
            steps[mark + "1a"] = functools.partial(job.start_first, 0)
            steps[mark + "1b"] = functools.partial(job.start_first, 1)
            steps[mark + "2"] = job.start_second
        steps[mark + "3a"] = job.third_first
        steps[mark + "3b"] = job.third_next

    for layer in range(LAYERS - 1, -1, -1):
        height = rows[layer]
        chunk = min(height, PIX_CHUNK)
        base = norm_at[layer]
        gain = gain_ref[layer : layer + 1, :]
        shift = shift_ref[layer : layer + 1, :]
        inverse = scale_ref[layer : layer + 1, :]
        incoming = ordered if layer == 8 else grads
        if layer == 8:
            loads[0].wait()
        if layer == 7:
            loads[2].wait()
        if layer == 6:
            loads[3].wait()

        def activate(index, carry):
            first, second = carry
            at = pl.multiple_of(index * chunk, chunk)
            normed = norm_ref[pl.ds(base + at, chunk), :]
            lifted = normed * gain + shift
            sigma = 1.0 / (1.0 + jnp.exp(-lifted))
            value = incoming[pl.ds(at, chunk), :] * sigma * (1.0 + lifted * (1.0 - sigma))
            active[pl.ds(at, chunk), :] = value
            first = first + jnp.sum(value.reshape(chunk // 8, 8, 128), axis=0)
            second = second + jnp.sum((value * normed).reshape(chunk // 8, 8, 128), axis=0)
            return first, second

        zero = jnp.zeros((8, 128), jnp.float32)
        first, second = lax.fori_loop(0, height // chunk, activate, (zero, zero), unroll=True)
        sums = jnp.concatenate(
            [jnp.sum(first, axis=0, keepdims=True), jnp.sum(second, axis=0, keepdims=True)], axis=0
        )
        source[layer] = sums
        slots[layer, me] = sums
        if layer == 8:
            greeted(count)
        send_all(
            count, source.at[layer], slots.at[layer, me], send_sem.at[layer], recv_sem.at[layer]
        )
        for name in SCHEDULE[layer].split():
            steps[name]()
        if layer == 7:
            loads[1].wait()
        if layer < 8:
            weight_grad(layer + 1)
        wait_all(count, slots.at[layer], recv_sem.at[layer])
        totals = jnp.sum(slots[layer], axis=0)
        small_out[1032 + layer : 1033 + layer, :] = totals[1:2]
        small_out[1048 + layer : 1049 + layer, :] = totals[0:1]
        share = 1.0 / (4 * height * count)
        first_mean = group_sum(wide(totals[0:1] * gain))[0:1] * share
        second_mean = group_sum(wide(totals[1:2] * gain))[0:1] * share

        def conv_grad(start, size):
            value = inverse * (
                active[pl.ds(start, size), :] * gain
                - first_mean
                - norm_ref[pl.ds(base + start, size), :] * second_mean
            )
            grad_conv[pl.ds(base + start, size), :] = value
            return value

        if layer > 0:
            weights = weights_ref[layer - 1]
            stacked = jnp.concatenate([weights, weights], axis=1)

            def input_grad(start, size):
                return lax.dot_general(
                    split_two(conv_grad(start, size)),
                    stacked,
                    (((1,), (1,)), ((), ())),
                    preferred_element_type=jnp.float32,
                )

        if layer > 4:
            quarter = height // 4
            part = min(quarter, 64)
            skipped = skip_at[8 - layer]

            def shrink(index, carry):
                at = pl.multiple_of(index * part, part)
                total = jnp.zeros((part, 128), jnp.float32)
                for corner in range(4):
                    place = corner * quarter + at
                    value = input_grad(place, part)
                    skip[pl.ds(skipped + place, part), :] = value
                    total = total + value
                grads[pl.ds(at, part), :] = total
                return carry

            lax.fori_loop(0, quarter // part, shrink, 0, unroll=True)
        elif layer > 0:
            part = min(height, 128)
            skipped = skip_at[layer - 1]

            def spread_out(index, carry):
                at = pl.multiple_of(index * part, part)
                value = input_grad(at, part) * 0.25
                for corner in range(4):
                    place = corner * height + at
                    grads[pl.ds(place, part), :] = value + skip[pl.ds(skipped + place, part), :]
                return carry

            lax.fori_loop(0, height // part, spread_out, 0, unroll=True)
        else:

            def finish(index, carry):
                at = pl.multiple_of(index * chunk, chunk)
                conv_grad(at, chunk)
                return carry

            lax.fori_loop(0, height // chunk, finish, 0, unroll=True)
    for start, place in places:
        natural[pl.ds(start, 8, stride=spacing), :] = grad_conv[place : place + 8, :]
    first_part = jnp.zeros(first_source.shape, jnp.float32)
    for line in range(image_ref.shape[1]):
        first_part = first_part + dot_plain(
            image_ref[:, line, :],
            natural[line * 128 : (line + 1) * 128, :].astype(jnp.bfloat16),
        )
    first_source[...] = first_part
    first_slots[me] = first_part
    send_all(count, first_source, first_slots.at[me], send_sem.at[LAYERS], recv_sem.at[LAYERS])
    for name in SCHEDULE["end"].split():
        steps[name]()
    wait_all(count, parts, part_recv)
    shared[me] = jnp.sum(parts[...], axis=0)
    send_all(count, shared.at[me], shared.at[me], share_send, share_recv)
    for job, base in ((down_left, 2), (down_right, 2), (up_left, 0), (up_right, 0)):
        job.end(large_out, base)
    for name in SCHEDULE["last"].split():
        steps[name]()
    wait_all(count, first_slots, recv_sem.at[LAYERS])
    small_out[1024 : 1024 + first_slots.shape[1], :] = jnp.sum(first_slots[...], axis=0)
    wait_all(count, shared, share_recv)
    for device in range(count):
        begin = (device % 8) * 128 + (device // 8) * owned
        small_out[begin : begin + owned, :] = shared[device]
    attn_left.end(large_out, 1)
    for layer in range(LAYERS):
        wait_all(count, slots.at[layer], send_sem.at[layer])
    wait_all(count, first_slots, send_sem.at[LAYERS])
    wait_all(rows_count, small_slots, row_send.at[0])
    wait_all(rows_count, split_slots, row_send.at[1])
    wait_all(count, parts, part_send)
    wait_all(count, shared, share_send)
    up_left.sent(up_landed)
    for job in jobs[1:]:
        job.sent()
    attn_right.end(large_out, 1)


def stem_forward(page_image, conv_first, conv_weights, group_gain, group_shift, devices):
    planes, tile_rows, columns = page_image.shape
    pixels = tile_rows * columns
    rows = stem_rows(pixels)
    places = natural_places(tile_rows, columns)
    whole = pl.BlockSpec(memory_space=pltpu.VMEM)
    far = pl.BlockSpec(memory_space=pltpu.HBM)
    return pl.pallas_call(
        functools.partial(stem_forward_kernel, devices, places),
        out_shape=(
            jax.ShapeDtypeStruct((pixels, 128), jnp.float32),
            jax.ShapeDtypeStruct((sum(rows), 128), jnp.float32),
            jax.ShapeDtypeStruct((sum(rows[1:]), 128), jnp.float32),
            jax.ShapeDtypeStruct((LAYERS, 128), jnp.float32),
        ),
        in_specs=[whole] * 5,
        out_specs=(whole, far, far, whole),
        scratch_shapes=[
            pltpu.VMEM((sum(rows), 128), jnp.float32),
            pltpu.VMEM((sum(rows[1:]), 128), jnp.float32),
            pltpu.VMEM((pixels, 128), jnp.float32),
            pltpu.VMEM((sum(rows[:4]), 128), jnp.float32),
            pltpu.VMEM((pixels, 128), jnp.float32),
            pltpu.VMEM((LAYERS, 2, 128), jnp.float32),
            pltpu.VMEM((LAYERS, devices, 2, 128), jnp.float32),
            pltpu.SemaphoreType.DMA((LAYERS,)),
            pltpu.SemaphoreType.DMA((LAYERS,)),
            pltpu.SemaphoreType.DMA((2, LAYERS)),
        ],
        compiler_params=pltpu.CompilerParams(
            collective_id=0, has_side_effects=True, vmem_limit_bytes=VMEM_LIMIT
        ),
        cost_estimate=pl.CostEstimate(
            flops=54 * 10**9, bytes_accessed=2 * 10**7, transcendentals=0
        ),
        name="stem_forward",
    )(page_image, conv_first, conv_weights, group_gain, group_shift)


def stem_backward(
    grad_map,
    page_image,
    records,
    conv_weights,
    group_gain,
    group_shift,
    split,
    norm_grads,
    tables,
    up,
    attn,
    kept,
    second,
    early,
    devices,
):
    planes, tile_rows, columns = page_image.shape
    pixels = tile_rows * columns
    rows = stem_rows(pixels)
    norms, inputs, scales = records
    places = natural_places(tile_rows, columns)
    whole = pl.BlockSpec(memory_space=pltpu.VMEM)
    owned = 1024 // devices
    far = pl.BlockSpec(memory_space=pltpu.HBM)
    depths, _, _, own_rows, columns = up.shape
    return pl.pallas_call(
        functools.partial(stem_backward_kernel, devices, places),
        out_shape=(
            jax.ShapeDtypeStruct((1072 + 2 * split.shape[2], 128), jnp.float32),
            jax.ShapeDtypeStruct((3, own_rows, columns), jnp.float32),
        ),
        in_specs=[whole, whole, far, far] + [whole] * 8 + [far] * 5,
        out_specs=(whole,) * 2,
        scratch_shapes=[
            pltpu.VMEM((sum(rows), 128), jnp.float32),
            pltpu.VMEM((sum(rows[1:]), 128), jnp.float32),
            pltpu.VMEM((pixels, 128), jnp.float32),
            pltpu.VMEM((pixels, 128), jnp.float32),
            pltpu.VMEM((pixels, 128), jnp.float32),
            pltpu.VMEM((sum(rows), 128), jnp.float32),
            pltpu.VMEM((sum(rows[:4]), 128), jnp.float32),
            pltpu.VMEM((pixels, 128), jnp.float32),
            pltpu.VMEM((8, devices // 8, owned, 128), jnp.float32),
            pltpu.VMEM((LAYERS, 2, 128), jnp.float32),
            pltpu.VMEM((LAYERS, devices, 2, 128), jnp.float32),
            pltpu.VMEM((planes, 128), jnp.float32),
            pltpu.VMEM((devices, planes, 128), jnp.float32),
            pltpu.VMEM((devices, owned, 128), jnp.float32),
            pltpu.VMEM((devices, owned, 128), jnp.float32),
            pltpu.SemaphoreType.DMA((LAYERS + 1,)),
            pltpu.SemaphoreType.DMA((LAYERS + 1,)),
            pltpu.SemaphoreType.DMA,
            pltpu.SemaphoreType.DMA,
            pltpu.SemaphoreType.DMA,
            pltpu.SemaphoreType.DMA,
            pltpu.VMEM((devices // 2, *split.shape[2:]), jnp.float32),
            pltpu.VMEM(split.shape[1:], jnp.float32),
            pltpu.VMEM((devices // 2, 8, 128), jnp.float32),
            pltpu.VMEM((devices // 2, 8, 128), jnp.float32),
            pltpu.SemaphoreType.DMA((3,)),
            pltpu.SemaphoreType.DMA((3,)),
            pltpu.SemaphoreType.DMA((5,)),
            *(ScatterHere.scratch(depths, own_rows, columns // 4) * 4),
            *(ScatterRest.scratch(depths, own_rows, columns // 4) * 2),
        ],
        compiler_params=pltpu.CompilerParams(
            collective_id=1, has_side_effects=True, vmem_limit_bytes=VMEM_LIMIT
        ),
        cost_estimate=pl.CostEstimate(
            flops=65 * 10**9, bytes_accessed=2 * 10**7, transcendentals=0
        ),
        name="stem_backward",
    )(
        grad_map,
        page_image,
        norms,
        inputs,
        scales,
        conv_weights,
        group_gain,
        group_shift,
        split,
        *norm_grads,
        tables,
        up,
        attn,
        kept,
        second,
        early,
    )


TILE = 128
QROWS = 256
KIND_ROWS = 8
FAR_LANE = 32
LOW_LANE = 40
PAD_LANE = 48
DOC_LANE = 56


def dot_last(left, right):
    return lax.dot_general(
        left, right, (((1,), (1,)), ((), ())), preferred_element_type=jnp.float32
    )


def dot_plain(left, right):
    return jnp.dot(left, right, preferred_element_type=jnp.float32)


def bucket_vector(tables_ref, table, head, relative):
    buckets = bucket_of(relative)
    values = jnp.zeros(relative.shape, jnp.float32)
    for bucket in range(NBUCKET):
        values = jnp.where(buckets == bucket, tables_ref[table, head, bucket], values)
    return values


def signed_lanes(width):
    lane = lax.broadcasted_iota(jnp.int32, (8, width), 1)
    return jnp.where(lane < width // 2, lane, lane - width)


def rolled(row, height):
    return pltpu.roll(
        jnp.broadcast_to(row[0:1], (height, row.shape[1])), 0, 1, stride=1, stride_axis=0
    )


def token_columns(boxes_ref, docs_ref, pads_ref, info):
    rows = [boxes_ref[0], boxes_ref[1], docs_ref[...], pads_ref[...], boxes_ref[2], boxes_ref[3]]
    rows = rows + [jnp.zeros_like(rows[0])] * 2
    info[...] = jnp.concatenate(rows, axis=0).astype(jnp.float32).T.astype(jnp.int32)


def token_lanes(info_ref, one_hot_x, query_base, key_base, pad_tiles):
    tokens = info_ref.shape[0]
    lane = lax.broadcasted_iota(jnp.int32, (TILE, 128), 1)
    row = lax.broadcasted_iota(jnp.int32, (TILE, 128), 0)
    for tile in range(tokens // TILE):
        at = slice(tile * TILE, (tile + 1) * TILE)
        left = info_ref[at, 0:1]
        top = info_ref[at, 1:2]
        doc = info_ref[at, 2:3]
        hidden = jnp.where(info_ref[at, 3:4] > 0, 0.0, masked_score)
        one_hot_x[at, :] = (lane == left).astype(jnp.float32).astype(jnp.bfloat16)
        shared = jnp.where((lane == top) | (lane == DOC_LANE + doc), 1.0, 0.0)
        query_base[at, :] = jnp.where(lane == FAR_LANE + tile, 1.0, shared).astype(jnp.bfloat16)
        key = jnp.where((lane == FAR_LANE + tile) | (lane == LOW_LANE + tile), 1.0, shared)
        key = jnp.where(lane == PAD_LANE + tile, hidden, key)
        key_base[1, at, :] = key.astype(jnp.bfloat16)
        key_base[0, at, :] = pltpu.roll(key, 64, 1).astype(jnp.bfloat16)
        pad_tiles[at, :] = jnp.where(lane == row, 0.0, jnp.broadcast_to(hidden, (TILE, 128)))


def head_matrices(tables_ref, head, side):
    first = bucket_vector(tables_ref, 1, head, signed_lanes(256))
    across = rolled(first, 128)[:, :128].astype(jnp.bfloat16)
    second = rolled(bucket_vector(tables_ref, 2, head, signed_lanes(128)), 128)
    row = lax.broadcasted_iota(jnp.int32, (128, 128), 0)
    lane = lax.broadcasted_iota(jnp.int32, (128, 128), 1)
    mixed = jnp.where((row < FAR_LANE) & (lane < FAR_LANE), second, 0.0)
    gap = lane % 8 - (row - FAR_LANE)
    before = jnp.full((128, 128), tables_ref[0, head, NBUCKET // 2 - 1], jnp.float32)
    after = jnp.full((128, 128), tables_ref[0, head, NBUCKET - 1], jnp.float32)
    far = jnp.where(gap <= -2, before, jnp.where(gap >= 2, after, 0.0))
    high = far.astype(jnp.bfloat16).astype(jnp.float32)
    of_tile = (row >= FAR_LANE) & (row < LOW_LANE)
    mixed = jnp.where(of_tile & (lane >= FAR_LANE) & (lane < LOW_LANE), high, mixed)
    mixed = jnp.where(of_tile & (lane >= LOW_LANE) & (lane < PAD_LANE), far - high, mixed)
    mixed = jnp.where(
        of_tile & (lane >= PAD_LANE) & (lane < DOC_LANE) & (gap != 0), 1.0, mixed
    )
    docs = (row >= DOC_LANE) & (row < 64) & (lane >= DOC_LANE) & (lane < 64)
    mixed = jnp.where(docs & (row != lane), masked_score, mixed)
    if side == 0:
        mixed = pltpu.roll(mixed, 64, 1)
    near = rolled(bucket_vector(tables_ref, 0, head, -signed_lanes(512)), 128)
    tiles = {0: near[:, :128], 1: near[:, 384:], -1: near[:, 128:256]}
    return across, mixed.astype(jnp.bfloat16), tiles


def own_half(side, own, other):
    lane = lax.broadcasted_iota(jnp.int32, own.shape, 1)
    return jnp.where((lane < 64) if side == 0 else (lane >= 64), own, other)


def widen_operands(
    side, head, tables_ref, query_ref, key_ref, one_hot_x, query_base, key_base, query_wide, key_wide, near
):
    across, mixed, tiles = head_matrices(tables_ref, head, side)
    for gap in (-1, 0, 1):
        near[side, gap + 1] = tiles[gap]
    scaled = (query_ref[...].astype(jnp.float32) * HDIM ** (-0.5)).astype(jnp.bfloat16)
    query_wide[side, :, :128] = own_half(
        side, scaled, dot_plain(query_base[...], mixed).astype(jnp.bfloat16)
    )
    query_wide[side, :, 128:] = dot_plain(one_hot_x[...], across).astype(jnp.bfloat16)
    key_wide[side, :, :128] = own_half(side, key_ref[...], key_base[side])
    key_wide[side, :, 128:] = one_hot_x[...]


def near_scores(scores, side, block, tile, near, pad_tiles):
    halves = []
    for half in range(QROWS // TILE):
        part = scores[:, half * TILE : (half + 1) * TILE]
        gap = tile - (block * (QROWS // TILE) + half)
        if abs(gap) <= 1:
            part = part + near[side, gap + 1]
        if gap == 0:
            part = part + pad_tiles[tile * TILE : (tile + 1) * TILE, :]
        halves.append(part)
    return jnp.concatenate(halves, axis=1)


def attention_forward_kernel(
    tables_ref,
    boxes_ref,
    docs_ref,
    pads_ref,
    query_ref,
    key_ref,
    value_ref,
    context_ref,
    exact_ref,
    lse_ref,
    info_ref,
    one_hot_x,
    query_base,
    key_base,
    pad_tiles,
    query_wide,
    key_wide,
    near,
    scores,
    weights,
):
    pair = pl.program_id(0)
    tokens = query_ref.shape[0]

    @pl.when(pair == 0)
    def _():
        token_columns(boxes_ref, docs_ref, pads_ref, info_ref)
        token_lanes(info_ref, one_hot_x, query_base, key_base, pad_tiles)

    def widen(side):
        widen_operands(
            side, pair * 2 + side, tables_ref, query_ref, key_ref, one_hot_x, query_base, key_base,
            query_wide, key_wide, near,
        )

    widen(0)
    values = value_ref[...].T
    steps = [(block, side) for block in range(tokens // QROWS) for side in range(2)]

    def products(step):
        block, side = step
        scores[side] = dot_last(
            key_wide[side], query_wide[side, block * QROWS : (block + 1) * QROWS, :]
        )

    def collect():
        block, side, total = waiting.pop(0)
        columns = slice(block * QROWS, (block + 1) * QROWS)
        context = dot_plain(values[side * 64 : (side + 1) * 64, :], weights[side])
        contexts.append(context * (1.0 / total))
        if side == 1:
            context = jnp.concatenate(contexts, axis=0)
            contexts.clear()
            exact_ref[:, columns] = context
            context_ref[columns, :] = context.T.astype(jnp.bfloat16)

    products(steps[0])
    widen(1)
    contexts = []
    waiting = []
    for index, (block, side) in enumerate(steps):
        columns = slice(block * QROWS, (block + 1) * QROWS)
        if index + 1 < len(steps):
            products(steps[index + 1])
        if waiting:
            collect()
        top = jnp.full((8, QROWS), masked_score, jnp.float32)
        for tile in range(tokens // TILE):
            at = slice(tile * TILE, (tile + 1) * TILE)
            part = scores[side, at, :]
            if any(abs(tile - 2 * block - half) <= 1 for half in range(2)):
                part = near_scores(part, side, block, tile, near, pad_tiles)
                scores[side, at, :] = part
            top = jnp.maximum(top, jnp.max(part.reshape(TILE // 8, 8, QROWS), axis=0))
        top = jnp.max(top, axis=0, keepdims=True)
        total = jnp.zeros((8, QROWS), jnp.float32)
        for tile in range(tokens // TILE):
            at = slice(tile * TILE, (tile + 1) * TILE)
            part = jnp.exp(scores[side, at, :] - top)
            total = total + jnp.sum(part.reshape(TILE // 8, 8, QROWS), axis=0)
            weights[side, at, :] = part.astype(jnp.bfloat16)
        total = jnp.sum(total, axis=0, keepdims=True)
        lse_ref[0, side : side + 1, columns] = top + jnp.log(total)
        waiting.append((block, side, total))
        if index + 1 == len(steps):
            collect()


def attention_backward_kernel(
    tables_ref,
    boxes_ref,
    docs_ref,
    pads_ref,
    query_ref,
    key_ref,
    value_ref,
    grad_ref,
    exact_ref,
    lse_ref,
    down_ref,
    up_ref,
    part_out,
    grad_query_ref,
    grad_key_ref,
    grad_value_ref,
    diagonal_ref,
    down_landed,
    up_landed,
    other_out,
    info_ref,
    one_hot_x,
    query_base,
    key_base,
    pad_tiles,
    reverse,
    query_wide,
    key_wide,
    near,
    scores,
    grad_probs,
    probs_low,
    grad_low,
    key_turned,
    grad_near,
    grad_blocks,
    grad_key,
    grad_value,
    down_send,
    down_recv,
    up_send,
    up_recv,
    out_send,
    out_recv,
):
    pair = pl.program_id(0)
    tokens = query_ref.shape[0]
    down = Scatter(down_landed.shape[-1], 0, down_send, down_recv)
    up = Scatter(up_landed.shape[-1], 0, up_send, up_recv)

    @pl.when(pair == 0)
    def _():
        greet_partner()
        greet_rows((down.across_x, down.across_y))
        pl.semaphore_wait(pltpu.get_barrier_semaphore(), 3)
        down.send_first(down_ref, down_landed, 0, down_landed.shape[1])
        up.send_first(up_ref, up_landed, 0, up_landed.shape[1])
        partner_copy(part_out, other_out, out_send, out_recv).start()
        token_columns(boxes_ref, docs_ref, pads_ref, info_ref)
        token_lanes(info_ref, one_hot_x, query_base, key_base, pad_tiles)
        lane = lax.broadcasted_iota(jnp.int32, (TILE, 128), 1)
        for tile in range(tokens // TILE):
            at = slice(tile * TILE, (tile + 1) * TILE)
            left = info_ref[at, 0:1]
            top = info_ref[at, 1:2]
            reverse[at, :128] = jnp.where(lane == 127 - left, 1.0, 0.0).astype(jnp.bfloat16)
            reverse[at, 128:] = jnp.where(
                (lane == 31 - top) | (lane == FAR_LANE + tile), 1.0, 0.0
            ).astype(jnp.bfloat16)

    for side in range(2):
        widen_operands(
            side, pair * 2 + side, tables_ref, query_ref, key_ref, one_hot_x, query_base, key_base,
            query_wide, key_wide, near,
        )
        key_turned[side] = key_wide[side].T
    grad_near[...] = jnp.zeros_like(grad_near)
    grad_blocks[...] = jnp.zeros_like(grad_blocks)
    values = [
        own_half(side, value_ref[...], jnp.zeros(value_ref.shape, jnp.bfloat16)) for side in range(2)
    ]
    for block in range(tokens // QROWS):
        columns = slice(block * QROWS, (block + 1) * QROWS)
        grad_block = grad_ref[columns, :]
        product = grad_block.astype(jnp.float32).T * exact_ref[:, columns]
        scaled = (query_ref[columns, :].astype(jnp.float32) * HDIM ** (-0.5)).astype(jnp.bfloat16)
        turned = []
        key_terms = []
        value_terms = []
        for side in range(2):
            delta = jnp.sum(product[side * 64 : (side + 1) * 64, :], axis=0, keepdims=True)
            lse = lse_ref[0, side : side + 1, columns]
            scores[side] = dot_last(key_wide[side], query_wide[side, columns, :])
            grad_probs[side] = dot_last(values[side], grad_block)
            for tile in range(tokens // TILE):
                at = slice(tile * TILE, (tile + 1) * TILE)
                part = near_scores(scores[side, at, :], side, block, tile, near, pad_tiles)
                probs = jnp.exp(part - lse)
                grad_part = probs * (grad_probs[side, at, :] - delta)
                probs_low[side, at, :] = probs.astype(jnp.bfloat16)
                grad_low[side, at, :] = grad_part.astype(jnp.bfloat16)
                for half in range(QROWS // TILE):
                    gap = tile - (block * (QROWS // TILE) + half)
                    if abs(gap) <= 1:
                        grad_near[side, gap + 1] += grad_part[:, half * TILE : (half + 1) * TILE]
            value_terms.append(dot_plain(probs_low[side], grad_block))
            key_terms.append(dot_plain(grad_low[side], scaled))
            sums = dot_plain(key_turned[side], grad_low[side])
            turned.append(sums[side * 64 : (side + 1) * 64, :])
            grad_blocks[side] += dot_plain(sums.astype(jnp.bfloat16), reverse[columns, :])
        grad_query_ref[columns, :] = (
            (jnp.concatenate(turned, axis=0) * HDIM ** (-0.5)).T.astype(jnp.bfloat16)
        )
        key_term = own_half(0, key_terms[0], key_terms[1])
        value_term = own_half(0, value_terms[0], value_terms[1])
        if block == 0:
            grad_key[...] = key_term
            grad_value[...] = value_term
        else:
            grad_key[...] += key_term
            grad_value[...] += value_term
    grad_key_ref[...] = grad_key[...].astype(jnp.bfloat16)
    grad_value_ref[...] = grad_value[...].astype(jnp.bfloat16)
    row = lax.broadcasted_iota(jnp.int32, (128, 128), 0)
    lane = lax.broadcasted_iota(jnp.int32, (128, 128), 1)
    flip = jnp.where(row + lane == 127, 1.0, 0.0).astype(jnp.bfloat16)
    blank = jnp.zeros((128, 128), jnp.float32)

    def diagonal_sums(values):
        spread = jnp.concatenate([values, blank], axis=1)
        return jnp.sum(
            pltpu.roll(spread, 0, 1, stride=1, stride_axis=0), axis=0, keepdims=True
        )

    for side in range(2):
        misc = 64 * (1 - side)
        sums = [diagonal_sums(grad_blocks[side, 128:, :128])]
        below = grad_blocks[side, misc : misc + 64, 128:]
        small_row = lax.broadcasted_iota(jnp.int32, (64, 128), 0)
        small_lane = lax.broadcasted_iota(jnp.int32, (64, 128), 1)
        upright = jnp.where((small_row < FAR_LANE) & (small_lane < FAR_LANE), below, 0.0)
        sums.append(diagonal_sums(jnp.concatenate([upright, jnp.zeros((64, 128), jnp.float32)], axis=0)))
        for gap in range(3):
            tile = grad_near[side, gap]
            high = tile.astype(jnp.bfloat16)
            rest = (tile - high.astype(jnp.float32)).astype(jnp.bfloat16)
            sums.append(diagonal_sums(dot_plain(high, flip) + dot_plain(rest, flip)))
        gap = (small_row - FAR_LANE) - (small_lane - FAR_LANE)
        inside = (
            (small_row >= FAR_LANE)
            & (small_row < LOW_LANE)
            & (small_lane >= FAR_LANE)
            & (small_lane < LOW_LANE)
        )
        for chosen in (gap <= -2, gap >= 2):
            far = jnp.sum(jnp.where(inside & chosen, below, 0.0), axis=0, keepdims=True)
            sums.append(jnp.concatenate([far, blank[0:1]], axis=1))
        sums.append(jnp.zeros((1, 256), jnp.float32))
        diagonal_ref[side] = jnp.concatenate(sums, axis=0)

    @pl.when(pair == pl.num_programs(0) - 1)
    def _():
        for scatter, landed in ((down, down_landed), (up, up_landed)):
            scatter.await_first(landed)
            scatter.sent_first(landed)
        await_bytes(other_out, out_recv)
        await_bytes(other_out, out_send)


def attention_scratch(tokens):
    return [
        pltpu.VMEM((tokens, 8), jnp.int32),
        pltpu.VMEM((tokens, 128), jnp.bfloat16),
        pltpu.VMEM((tokens, 128), jnp.bfloat16),
        pltpu.VMEM((2, tokens, 128), jnp.bfloat16),
        pltpu.VMEM((tokens, 128), jnp.float32),
    ], [
        pltpu.VMEM((2, tokens, 256), jnp.bfloat16),
        pltpu.VMEM((2, tokens, 256), jnp.bfloat16),
        pltpu.VMEM((2, 3, TILE, TILE), jnp.float32),
        pltpu.VMEM((2, tokens, QROWS), jnp.float32),
    ]


def attention_forward(tables, places, heads):
    tokens, width = heads.shape[0], heads.shape[1] // 3
    pairs = width // 128
    own = pl.BlockSpec((tokens, 128), lambda pair: (0, pair))
    fixed, moving = attention_scratch(tokens)
    return pl.pallas_call(
        attention_forward_kernel,
        grid=(pairs,),
        out_shape=(
            jax.ShapeDtypeStruct((tokens, width), jnp.bfloat16),
            jax.ShapeDtypeStruct((width, tokens), jnp.float32),
            jax.ShapeDtypeStruct((pairs, 2, tokens), jnp.float32),
        ),
        in_specs=[
            pl.BlockSpec(memory_space=pltpu.SMEM),
            *[pl.BlockSpec(memory_space=pltpu.VMEM)] * 3,
            own,
            pl.BlockSpec((tokens, 128), lambda pair: (0, pairs + pair)),
            pl.BlockSpec((tokens, 128), lambda pair: (0, 2 * pairs + pair)),
        ],
        out_specs=(
            own,
            pl.BlockSpec((128, tokens), lambda pair: (pair, 0)),
            pl.BlockSpec((1, 2, tokens), lambda pair: (pair, 0, 0)),
        ),
        scratch_shapes=fixed
        + moving
        + [
            pltpu.VMEM((2, tokens, QROWS), jnp.bfloat16),
        ],
        compiler_params=pltpu.CompilerParams(
            dimension_semantics=("arbitrary",), vmem_limit_bytes=VMEM_LIMIT
        ),
        cost_estimate=pl.CostEstimate(
            flops=23 * 10**9, bytes_accessed=2 * 10**7, transcendentals=0
        ),
        name="attention_forward",
    )(tables, *places, heads, heads, heads)


def attention_backward(tables, places, heads, grad_context, exact, lse, down, up, part_out):
    tokens, width = grad_context.shape
    pairs = width // 128
    own = pl.BlockSpec((tokens, 128), lambda pair: (0, pair))
    fixed, moving = attention_scratch(tokens)
    low = jax.ShapeDtypeStruct((tokens, width), jnp.bfloat16)
    depths, _, _, rows, columns = down.shape
    return pl.pallas_call(
        attention_backward_kernel,
        grid=(pairs,),
        out_shape=(
            low,
            low,
            low,
            jax.ShapeDtypeStruct((2 * pairs, 8, 256), jnp.float32),
            jax.ShapeDtypeStruct((2, depths, 2, rows, columns // 2), jnp.float32),
            jax.ShapeDtypeStruct((2, depths // 2, 2, rows, columns // 4), jnp.float32),
            jax.ShapeDtypeStruct(part_out.shape, jnp.float32),
        ),
        in_specs=[
            pl.BlockSpec(memory_space=pltpu.SMEM),
            *[pl.BlockSpec(memory_space=pltpu.VMEM)] * 3,
            own,
            pl.BlockSpec((tokens, 128), lambda pair: (0, pairs + pair)),
            pl.BlockSpec((tokens, 128), lambda pair: (0, 2 * pairs + pair)),
            own,
            pl.BlockSpec((128, tokens), lambda pair: (pair, 0)),
            pl.BlockSpec((1, 2, tokens), lambda pair: (pair, 0, 0)),
            *[pl.BlockSpec(memory_space=pltpu.HBM)] * 3,
        ],
        out_specs=(
            own,
            own,
            own,
            pl.BlockSpec((2, 8, 256), lambda pair: (pair, 0, 0)),
            *[pl.BlockSpec(memory_space=pltpu.HBM)] * 3,
        ),
        scratch_shapes=fixed
        + [pltpu.VMEM((tokens, 256), jnp.bfloat16)]
        + moving
        + [
            pltpu.VMEM((2, tokens, QROWS), jnp.float32),
            pltpu.VMEM((2, tokens, QROWS), jnp.bfloat16),
            pltpu.VMEM((2, tokens, QROWS), jnp.bfloat16),
            pltpu.VMEM((2, 256, tokens), jnp.bfloat16),
            pltpu.VMEM((2, 3, TILE, TILE), jnp.float32),
            pltpu.VMEM((2, 256, 256), jnp.float32),
            pltpu.VMEM((tokens, 128), jnp.float32),
            pltpu.VMEM((tokens, 128), jnp.float32),
            *scatter_semaphores(2),
            *scatter_semaphores(2),
            pltpu.SemaphoreType.DMA,
            pltpu.SemaphoreType.DMA,
        ],
        compiler_params=pltpu.CompilerParams(
            dimension_semantics=("arbitrary",),
            collective_id=5,
            has_side_effects=True,
            vmem_limit_bytes=VMEM_LIMIT,
        ),
        cost_estimate=pl.CostEstimate(
            flops=30 * 10**9, bytes_accessed=2 * 10**7, transcendentals=0
        ),
        name="attention_backward",
    )(tables, *places, heads, heads, heads, grad_context, exact, lse, down, up, part_out)


def known_bucket(relative):
    magnitude = np.abs(relative)
    coarse = 8 + sum((magnitude >= edge).astype(int) for edge in bucket_edges)
    return np.where(magnitude < 8, magnitude, coarse) + np.where(relative > 0, 16, 0)


def bucket_grads(diagonals):
    lane = np.arange(256)
    far = np.zeros(256, int)
    wide_buckets = [
        known_bucket(lane - 127),
        known_bucket(lane - 31),
        known_bucket(lane - 127 - TILE),
        known_bucket(lane - 127),
        known_bucket(lane - 127 + TILE),
        far + NBUCKET // 2 - 1,
        far + NBUCKET - 1,
    ]
    table_of = (1, 2, 0, 0, 0, 0, 0)
    slots = np.stack([bucket + NBUCKET * table for bucket, table in zip(wide_buckets, table_of)])
    slots = jnp.asarray(slots, jnp.int32)
    chosen = (slots[..., None] == jnp.arange(3 * NBUCKET, dtype=jnp.int32)).astype(jnp.float32)
    return jnp.einsum("hrc,rcb->hb", diagonals[:, :7], chosen, precision=highest)


ROWS = 256
MIDDLE_ROWS = 256


def greet_partner():
    pl.semaphore_signal(
        pltpu.get_barrier_semaphore(),
        inc=1,
        device_id=(lax.axis_index("dp"), 1 - lax.axis_index("tensor")),
        device_id_type=MESH,
    )


def partner_copy(source, target, send_sem, recv_sem):
    return pltpu.make_async_remote_copy(
        src_ref=source,
        dst_ref=target,
        send_sem=send_sem,
        recv_sem=recv_sem,
        device_id=(lax.axis_index("dp"), 1 - lax.axis_index("tensor")),
        device_id_type=MESH,
    )


def dot_rows(left, right):
    return lax.dot_general(
        left, right, (((0,), (0,)), ((), ())), preferred_element_type=jnp.float32
    )


def inverse_rms(values):
    return lax.rsqrt(jnp.mean(values * values, axis=1, keepdims=True) + norm_eps)


def box_kernel(
    feature_ref,
    boxes_ref,
    docs_ref,
    pads_ref,
    embedded_ref,
    roi_ref,
    norm_ref,
    query_proj_ref,
    key_proj_ref,
    value_proj_ref,
    pooled_ref,
    stream_ref,
    input_ref,
    heads_ref,
    info_ref,
    features,
    mask,
    part,
    received,
    projections,
    send_sem,
    recv_sem,
):
    greet_partner()
    token_columns(boxes_ref, docs_ref, pads_ref, info_ref)
    tokens = info_ref.shape[0]
    pixels = feature_ref.shape[0]
    tile_rows = pixels // 128
    first_row = lax.axis_index("tensor") * tile_rows
    features[...] = split_two(feature_ref[...])
    lane = lax.broadcasted_iota(jnp.int32, (ROWS, 128), 1)
    copies = []
    for block in range(tokens // ROWS):
        at = slice(block * ROWS, (block + 1) * ROWS)
        column = (lane >= info_ref[at, 0:1]) & (lane < info_ref[at, 4:5])
        column = jnp.where(column, 1.0, 0.0)
        top = jnp.broadcast_to(info_ref[at, 1:2], (ROWS, 128)) - first_row
        bottom = jnp.broadcast_to(info_ref[at, 5:6], (ROWS, 128)) - first_row
        for row in range(tile_rows):
            inside = jnp.where((top <= row) & (bottom > row), column, 0.0)
            mask[block % 2, :, row * 128 : (row + 1) * 128] = inside.astype(jnp.bfloat16)
        sums = dot_plain(mask[block % 2], features[...])
        part[at, :] = sums[:, :128] + sums[:, 128:]
        if block == 0:
            pl.semaphore_wait(pltpu.get_barrier_semaphore(), 1)
        copy = partner_copy(
            part.at[pl.ds(block * ROWS, ROWS)],
            received.at[pl.ds(block * ROWS, ROWS)],
            send_sem.at[block],
            recv_sem.at[block],
        )
        copy.start()
        copies.append(copy)
    width = query_proj_ref.shape[1]
    for index, ref in enumerate((query_proj_ref, key_proj_ref, value_proj_ref)):
        projections[:, index * width : (index + 1) * width] = ref[...]
    for block in range(tokens // ROWS):
        at = slice(block * ROWS, (block + 1) * ROWS)
        copies[block].wait_recv()
        area = (info_ref[at, 5:6] - info_ref[at, 1:2]) * (info_ref[at, 4:5] - info_ref[at, 0:1])
        pooled = ((part[at, :] + received[at, :]) / area.astype(jnp.float32)).astype(jnp.bfloat16)
        pooled_ref[at, :] = pooled
        stream = embedded_ref[at, :].astype(jnp.float32) + dot_plain(pooled, roi_ref[...])
        stream_ref[at, :] = stream
        attn_in = (stream * inverse_rms(stream) * norm_ref[...].reshape(1, -1)).astype(jnp.bfloat16)
        input_ref[at, :] = attn_in
        heads_ref[at, :] = dot_plain(attn_in, projections[...]).astype(jnp.bfloat16)
    for copy in copies:
        copy.wait_send()


def box_forward(
    feature_map, places, embeddings, roi_proj, attn_norm, query_proj, key_proj, value_proj
):
    tokens, width = embeddings.shape
    local = query_proj.shape[1]
    blocks = tokens // ROWS
    whole = pl.BlockSpec(memory_space=pltpu.VMEM)
    return pl.pallas_call(
        box_kernel,
        out_shape=(
            jax.ShapeDtypeStruct((tokens, 128), jnp.bfloat16),
            jax.ShapeDtypeStruct((tokens, width), jnp.float32),
            jax.ShapeDtypeStruct((tokens, width), jnp.bfloat16),
            jax.ShapeDtypeStruct((tokens, 3 * local), jnp.bfloat16),
        ),
        in_specs=[whole] * 10,
        out_specs=(whole,) * 4,
        scratch_shapes=[
            pltpu.VMEM((tokens, 8), jnp.int32),
            pltpu.VMEM((feature_map.shape[0], 256), jnp.bfloat16),
            pltpu.VMEM((2, ROWS, feature_map.shape[0]), jnp.bfloat16),
            pltpu.VMEM((tokens, 128), jnp.float32),
            pltpu.VMEM((tokens, 128), jnp.float32),
            pltpu.VMEM((width, 3 * local), jnp.bfloat16),
            pltpu.SemaphoreType.DMA((blocks,)),
            pltpu.SemaphoreType.DMA((blocks,)),
        ],
        compiler_params=pltpu.CompilerParams(
            collective_id=2, has_side_effects=True, vmem_limit_bytes=VMEM_LIMIT
        ),
        cost_estimate=pl.CostEstimate(
            flops=12 * 10**9, bytes_accessed=2 * 10**7, transcendentals=0
        ),
        name="box_forward",
    )(
        feature_map,
        *places,
        embeddings,
        roi_proj,
        attn_norm,
        query_proj,
        key_proj,
        value_proj,
    )


def middle_kernel(
    context_ref,
    stream_hbm,
    cotangent_hbm,
    output_ref,
    norm_ref,
    up_hbm,
    down_hbm,
    middle_hbm,
    part_out_hbm,
    grad_middle_hbm,
    grad_context_hbm,
    grad_up_hbm,
    grad_down_hbm,
    grad_output_ref,
    grad_norm_ref,
    middle,
    cotangent,
    up,
    down,
    part,
    other,
    part_out,
    other_grad,
    ffn_in,
    hidden,
    grad_pre,
    staged,
    grad_low,
    grad_context,
    load_sem,
    store_sem,
    grad_sem,
    send_sem,
    recv_sem,
):
    greet_partner()
    norm = norm_ref[...].reshape(1, -1)
    tokens, width = stream_hbm.shape
    units = up_hbm.shape[1]
    blocks = tokens // MIDDLE_ROWS
    loads = [
        pltpu.make_async_copy(source, target, load_sem.at[index])
        for index, (source, target) in enumerate(
            [(cotangent_hbm, cotangent), (down_hbm, down), (stream_hbm, middle), (up_hbm, up)]
        )
    ]
    for load in loads:
        load.start()
    attn_copies = []
    for block in range(blocks):
        at = slice(block * MIDDLE_ROWS, (block + 1) * MIDDLE_ROWS)
        part[at, :] = dot_plain(context_ref[at, :], output_ref[...])
        if block == 0:
            pl.semaphore_wait(pltpu.get_barrier_semaphore(), 1)
        copy = partner_copy(
            part.at[pl.ds(block * MIDDLE_ROWS, MIDDLE_ROWS)],
            other.at[pl.ds(block * MIDDLE_ROWS, MIDDLE_ROWS)],
            send_sem.at[0, block],
            recv_sem.at[0, block],
        )
        copy.start()
        attn_copies.append(copy)
    for load in loads:
        load.wait()
    out_stores = []
    grad_copies = []
    for block in range(blocks):
        at = slice(block * MIDDLE_ROWS, (block + 1) * MIDDLE_ROWS)
        grad_hidden = dot_last(cotangent[at, :], down[...])
        attn_copies[block].wait()
        values = middle[at, :] + (part[at, :] + other[at, :])
        middle[at, :] = values
        inner = (values * inverse_rms(values) * norm).astype(jnp.bfloat16)
        ffn_in[at, :] = inner
        pre_act = dot_plain(inner, up[...])
        below = 0.5 * (1.0 + lax.erf(pre_act * (0.5**0.5)))
        density = jnp.exp(-0.5 * (pre_act * pre_act)) * 0.3989422804014327
        hidden[at, :] = (pre_act * below).astype(jnp.bfloat16)
        grad_pre[at, :] = (grad_hidden * (below + pre_act * density)).astype(jnp.bfloat16)
        part[at, :] = dot_last(grad_pre[at, :], up[...])
        copy = partner_copy(
            part.at[pl.ds(block * MIDDLE_ROWS, MIDDLE_ROWS)],
            other_grad.at[pl.ds(block * MIDDLE_ROWS, MIDDLE_ROWS)],
            send_sem.at[1, block],
            recv_sem.at[1, block],
        )
        copy.start()
        grad_copies.append(copy)
        part_out[at, :] = dot_plain(hidden[at, :], down[...])
        for index, (source, target) in enumerate([(middle, middle_hbm), (part_out, part_out_hbm)]):
            rows = pl.ds(block * MIDDLE_ROWS, MIDDLE_ROWS)
            store = pltpu.make_async_copy(
                source.at[rows], target.at[rows], store_sem.at[2 + index, block]
            )
            store.start()
            out_stores.append(store)
    half = width // 2
    stores = []
    for index in range(4):
        rows = slice((index % 2) * half, (index % 2 + 1) * half)
        if index >= 2:
            stores[index - 2].wait()
        if index < 2:
            staged[index % 2] = dot_rows(ffn_in[:, rows], grad_pre[...])
            target = grad_up_hbm
        else:
            staged[index % 2] = dot_rows(cotangent[:, rows], hidden[...])
            target = grad_down_hbm
        store = pltpu.make_async_copy(
            staged.at[index % 2], target.at[pl.ds((index % 2) * half, half)], grad_sem.at[index]
        )
        store.start()
        stores.append(store)
    norm_total = jnp.zeros((8, width), jnp.float32)
    for block in range(blocks):
        at = slice(block * MIDDLE_ROWS, (block + 1) * MIDDLE_ROWS)
        values = middle[at, :]
        inverse = inverse_rms(values)
        hat = values * inverse
        grad_copies[block].wait()
        grad_inner = part[at, :] + other_grad[at, :]
        norm_total = norm_total + jnp.sum((grad_inner * hat).reshape(MIDDLE_ROWS // 8, 8, width), axis=0)
        scaled = grad_inner * norm
        back = inverse * (scaled - hat * jnp.mean(scaled * hat, axis=1, keepdims=True))
        grad_values = cotangent[at, :].astype(jnp.float32) + back
        out_stores[2 * block].wait()
        middle[at, :] = grad_values
        low = grad_values.astype(jnp.bfloat16)
        grad_low[at, :] = low
        grad_context[at, :] = dot_last(low, output_ref[...]).astype(jnp.bfloat16)
        for index, (source, target) in enumerate(
            [
                (middle, grad_middle_hbm),
                (grad_context, grad_context_hbm),
            ]
        ):
            rows = pl.ds(block * MIDDLE_ROWS, MIDDLE_ROWS)
            store = pltpu.make_async_copy(
                source.at[rows], target.at[rows], store_sem.at[index, block]
            )
            store.start()
            stores.append(store)
    grad_norm_ref[...] = jnp.sum(norm_total, axis=0, keepdims=True)
    grad_output_ref[...] = dot_rows(grad_low[...], context_ref[...])
    for store in stores[2:] + out_stores[1::2]:
        store.wait()


def middle_layer(context, stream, cotangent, output_proj, ffn_norm, up_proj, down_proj):
    tokens, width = stream.shape
    units = up_proj.shape[1]
    local = context.shape[1]
    blocks = tokens // MIDDLE_ROWS
    whole = pl.BlockSpec(memory_space=pltpu.VMEM)
    far = pl.BlockSpec(memory_space=pl.ANY)
    wide_sum = pltpu.VMEM((tokens, width), jnp.float32)
    wide_low = pltpu.VMEM((tokens, width), jnp.bfloat16)
    unit_low = pltpu.VMEM((tokens, units), jnp.bfloat16)
    return pl.pallas_call(
        middle_kernel,
        out_shape=(
            jax.ShapeDtypeStruct((tokens, width), jnp.float32),
            jax.ShapeDtypeStruct((tokens, width), jnp.float32),
            jax.ShapeDtypeStruct((tokens, width), jnp.float32),
            jax.ShapeDtypeStruct((tokens, local), jnp.bfloat16),
            jax.ShapeDtypeStruct((width, units), jnp.float32),
            jax.ShapeDtypeStruct((width, units), jnp.float32),
            jax.ShapeDtypeStruct((width, local), jnp.float32),
            jax.ShapeDtypeStruct((1, width), jnp.float32),
        ),
        in_specs=[whole, far, far, whole, whole, far, far],
        out_specs=(far,) * 6 + (whole, whole),
        scratch_shapes=[
            wide_sum,
            wide_low,
            pltpu.VMEM((width, units), jnp.bfloat16),
            pltpu.VMEM((units, width), jnp.bfloat16),
            wide_sum,
            wide_sum,
            wide_sum,
            wide_sum,
            wide_low,
            unit_low,
            unit_low,
            pltpu.VMEM((2, width // 2, units), jnp.float32),
            wide_low,
            pltpu.VMEM((tokens, local), jnp.bfloat16),
            pltpu.SemaphoreType.DMA((4,)),
            pltpu.SemaphoreType.DMA((4, blocks)),
            pltpu.SemaphoreType.DMA((4,)),
            pltpu.SemaphoreType.DMA((2, blocks)),
            pltpu.SemaphoreType.DMA((2, blocks)),
        ],
        compiler_params=pltpu.CompilerParams(
            collective_id=3, has_side_effects=True, vmem_limit_bytes=VMEM_LIMIT
        ),
        cost_estimate=pl.CostEstimate(
            flops=32 * 10**9, bytes_accessed=2 * 10**7, transcendentals=0
        ),
        name="middle_layer",
    )(context, stream, cotangent, output_proj, ffn_norm, up_proj, down_proj)


def end_kernel(
    grad_query_ref,
    grad_key_ref,
    grad_value_ref,
    query_proj_ref,
    key_proj_ref,
    value_proj_ref,
    input_ref,
    stream_hbm,
    grad_middle_hbm,
    norm_ref,
    roi_ref,
    pooled_ref,
    boxes_ref,
    docs_ref,
    pads_ref,
    grad_output_ref,
    down_hbm,
    landed_hbm,
    middle_hbm,
    part_out_hbm,
    other_out_hbm,
    grad_stream_hbm,
    grad_heads_hbm,
    kept_hbm,
    second_hbm,
    layer_hbm,
    grad_roi_ref,
    grad_map_ref,
    grad_norm_ref,
    info_ref,
    grad_heads,
    projections,
    stream,
    grad_stream,
    part,
    other,
    weight_grad,
    grad_low,
    grad_box,
    first,
    landed,
    middle,
    part_out,
    other_out,
    layer_low,
    load_sem,
    store_sem,
    grad_sem,
    send_sem,
    recv_sem,
    scatter_sem,
    scatter_send,
    scatter_recv,
):
    scatter = Scatter(first.shape[-1], 0, scatter_send, scatter_recv)
    greet_partner()
    norm = norm_ref[...].reshape(1, -1)
    greet_rows((scatter.across_x, scatter.across_y))
    first_loads = scatter.own_loads(down_hbm, first, scatter_sem)
    first_loads.append(pltpu.make_async_copy(landed_hbm, landed, scatter_sem.at[2]))
    for load in first_loads:
        load.start()
    tokens, width = stream_hbm.shape
    local = grad_query_ref.shape[1]
    blocks = tokens // ROWS
    loads = [
        pltpu.make_async_copy(stream_hbm, stream, load_sem.at[0]),
        pltpu.make_async_copy(grad_middle_hbm, grad_stream, load_sem.at[1]),
    ]
    for load in loads:
        load.start()
    for index, (grad, proj) in enumerate(
        (
            (grad_query_ref, query_proj_ref),
            (grad_key_ref, key_proj_ref),
            (grad_value_ref, value_proj_ref),
        )
    ):
        columns = slice(index * local, (index + 1) * local)
        grad_heads[:, columns] = grad[...]
        projections[:, columns] = proj[...]
    token_columns(boxes_ref, docs_ref, pads_ref, info_ref)
    copies = []
    for block in range(blocks):
        at = slice(block * ROWS, (block + 1) * ROWS)
        part[at, :] = dot_last(grad_heads[at, :], projections[...])
        if block == 0:
            for load in first_loads:
                load.wait()
            add_pairs(first, landed)
            pl.semaphore_wait(pltpu.get_barrier_semaphore(), 3)
            scatter.send_second(first, second_hbm)
            kept_stores = [
                pltpu.make_async_copy(first.at[0, :, scatter.y], kept_hbm.at[0], scatter_sem.at[0]),
                pltpu.make_async_copy(first.at[1, :, scatter.x], kept_hbm.at[1], scatter_sem.at[1]),
            ]
            for store in kept_stores:
                store.start()
        copy = partner_copy(
            part.at[pl.ds(block * ROWS, ROWS)],
            other.at[pl.ds(block * ROWS, ROWS)],
            send_sem.at[block],
            recv_sem.at[block],
        )
        copy.start()
        copies.append(copy)
    out_loads = [
        pltpu.make_async_copy(source, target, load_sem.at[2 + index])
        for index, (source, target) in enumerate(
            [(middle_hbm, middle), (part_out_hbm, part_out), (other_out_hbm, other_out)]
        )
    ]
    for load in out_loads:
        load.start()
    weight_grad[:, : 3 * local] = dot_rows(input_ref[...], grad_heads[...])
    weight_grad[:, 3 * local :] = grad_output_ref[...]
    weight_store = pltpu.make_async_copy(weight_grad, grad_heads_hbm, grad_sem)
    weight_store.start()
    for load in loads:
        load.wait()
    stores = []
    norm_total = jnp.zeros((8, width), jnp.float32)
    for block in range(blocks):
        at = slice(block * ROWS, (block + 1) * ROWS)
        values = stream[at, :]
        inverse = inverse_rms(values)
        hat = values * inverse
        copies[block].wait()
        grad_inner = part[at, :] + other[at, :]
        norm_total = norm_total + jnp.sum((grad_inner * hat).reshape(ROWS // 8, 8, width), axis=0)
        scaled = grad_inner * norm
        back = inverse * (scaled - hat * jnp.mean(scaled * hat, axis=1, keepdims=True))
        grad_values = grad_stream[at, :] + back
        grad_stream[at, :] = grad_values
        rows = pl.ds(block * ROWS, ROWS)
        store = pltpu.make_async_copy(
            grad_stream.at[rows], grad_stream_hbm.at[rows], store_sem.at[block]
        )
        store.start()
        stores.append(store)
        low = grad_values.astype(jnp.bfloat16)
        grad_low[at, :] = low
        area = (info_ref[at, 5:6] - info_ref[at, 1:2]) * (info_ref[at, 4:5] - info_ref[at, 0:1])
        grad_box[at, :] = split_two(dot_last(low, roi_ref[...]) / area.astype(jnp.float32))
    grad_norm_ref[...] = jnp.sum(norm_total, axis=0, keepdims=True)
    for load in out_loads:
        load.wait()
    for block in range(blocks):
        at = slice(block * ROWS, (block + 1) * ROWS)
        layer_low[at, :] = (middle[at, :] + (part_out[at, :] + other_out[at, :])).astype(
            jnp.bfloat16
        )
    layer_store = pltpu.make_async_copy(layer_low, layer_hbm, load_sem.at[2])
    layer_store.start()
    tile_rows = grad_map_ref.shape[0] // 128
    first_row = lax.axis_index("tensor") * tile_rows
    column = lax.broadcasted_iota(jnp.int32, (128, tokens), 0)
    inside = jnp.where(
        (column >= boxes_ref[0]) & (column < boxes_ref[2]), 1.0, 0.0
    ).astype(jnp.bfloat16)
    top = boxes_ref[1] - first_row
    bottom = boxes_ref[3] - first_row
    for row in range(tile_rows):
        chosen = jnp.where((top <= row) & (bottom > row), 1.0, 0.0).astype(jnp.bfloat16)
        sums = dot_plain(inside * chosen, grad_box[...])
        grad_map_ref[row * 128 : (row + 1) * 128, :] = sums[:, :128] + sums[:, 128:]
    grad_roi_ref[...] = dot_rows(grad_low[...], pooled_ref[...])
    layer_store.wait()
    for store in kept_stores:
        store.wait()
    scatter.await_second(second_hbm)
    scatter.sent_second(second_hbm)
    weight_store.wait()
    for store in stores:
        store.wait()


def end_layer(
    grad_heads,
    projections,
    attn_in,
    stream,
    grad_middle,
    attn_norm,
    roi_proj,
    pooled,
    places,
    grad_output,
    down,
    landed,
    outs,
    pixels,
):
    tokens, width = stream.shape
    local = grad_heads[0].shape[1]
    blocks = tokens // ROWS
    whole = pl.BlockSpec(memory_space=pltpu.VMEM)
    far = pl.BlockSpec(memory_space=pltpu.HBM)
    wide_sum = pltpu.VMEM((tokens, width), jnp.float32)
    _, depths, _, rows, half = landed.shape
    return pl.pallas_call(
        end_kernel,
        out_shape=(
            jax.ShapeDtypeStruct((tokens, width), jnp.float32),
            jax.ShapeDtypeStruct((width, 4 * local), jnp.float32),
            jax.ShapeDtypeStruct((2, depths, rows, half), jnp.float32),
            jax.ShapeDtypeStruct((2, depths, rows, half), jnp.float32),
            jax.ShapeDtypeStruct((tokens, width), jnp.bfloat16),
            jax.ShapeDtypeStruct((width, 128), jnp.float32),
            jax.ShapeDtypeStruct((pixels, 128), jnp.float32),
            jax.ShapeDtypeStruct((1, width), jnp.float32),
        ),
        in_specs=[whole] * 7 + [far, far] + [whole] * 7 + [far] * 5,
        out_specs=(far,) * 5 + (whole,) * 3,
        scratch_shapes=[
            pltpu.VMEM((tokens, 8), jnp.int32),
            pltpu.VMEM((tokens, 3 * local), jnp.bfloat16),
            pltpu.VMEM((width, 3 * local), jnp.bfloat16),
            wide_sum,
            wide_sum,
            wide_sum,
            wide_sum,
            pltpu.VMEM((width, 4 * local), jnp.float32),
            pltpu.VMEM((tokens, width), jnp.bfloat16),
            pltpu.VMEM((tokens, 256), jnp.bfloat16),
            pltpu.VMEM(landed.shape, jnp.float32),
            pltpu.VMEM(landed.shape, jnp.float32),
            wide_sum,
            wide_sum,
            wide_sum,
            pltpu.VMEM((tokens, width), jnp.bfloat16),
            pltpu.SemaphoreType.DMA((5,)),
            pltpu.SemaphoreType.DMA((blocks,)),
            pltpu.SemaphoreType.DMA,
            pltpu.SemaphoreType.DMA((blocks,)),
            pltpu.SemaphoreType.DMA((blocks,)),
            pltpu.SemaphoreType.DMA((3,)),
            *scatter_semaphores(4),
        ],
        compiler_params=pltpu.CompilerParams(
            collective_id=4, has_side_effects=True, vmem_limit_bytes=VMEM_LIMIT
        ),
        cost_estimate=pl.CostEstimate(
            flops=15 * 10**9, bytes_accessed=2 * 10**7, transcendentals=0
        ),
        name="end_layer",
    )(
        *grad_heads,
        *projections,
        attn_in,
        stream,
        grad_middle,
        attn_norm,
        roi_proj,
        pooled,
        *places,
        grad_output,
        down,
        landed,
        *outs,
    )


def unpack_kernel(
    places,
    sums_ref,
    own_ref,
    layer_in,
    stream_in,
    layer_out,
    stream_out,
    first_out,
    convs_out,
    gain_out,
    shift_out,
    roi_out,
    attn_norm_out,
    query_out,
    key_out,
    value_out,
    output_out,
    tables_out,
    ffn_norm_out,
    up_out,
    down_out,
    layer_kept,
    stream_kept,
    sem,
):
    loads = []
    copies = []
    count = sem.shape[1]
    for index, (source, kept, target) in enumerate(
        [(stream_in, stream_kept, stream_out), (layer_in, layer_kept, layer_out)]
    ):
        size = source.shape[0] // count
        for part in range(count):
            rows = pl.ds(part * size, size)
            loads.append(
                pltpu.make_async_copy(source.at[rows], kept.at[rows], sem.at[index, part])
            )
            copies.append(
                pltpu.make_async_copy(kept.at[rows], target.at[rows], sem.at[index, part])
            )
    for load in loads:
        load.start()
    for load, copy in zip(loads, copies):
        load.wait()
        copy.start()
    for target, begin in places:
        if target == "first":
            first_out[...] = sums_ref[begin : begin + first_out.shape[0], :]
        if target == "gain":
            gain_out[...] = sums_ref[begin : begin + LAYERS, :]
        if target == "shift":
            shift_out[...] = sums_ref[begin : begin + LAYERS, :]
        if target == "roi":
            roi_out[...] = sums_ref[begin : begin + roi_out.shape[0], :]
        if target == "small":
            attn_norm_out[...] = sums_ref[begin : begin + 1, : attn_norm_out.shape[1]]
            ffn_norm_out[...] = sums_ref[begin + 1 : begin + 2, : ffn_norm_out.shape[1]]
            for table in range(3):
                tables_out[table] = sums_ref[
                    begin + 2 : begin + 2 + tables_out.shape[1],
                    table * NBUCKET : (table + 1) * NBUCKET,
                ]
    for level in range(8):
        convs_out[level] = sums_ref[level * 128 : (level + 1) * 128, :]
    up_out[...] = own_ref[0]
    down_out[...] = own_ref[2]
    part = query_out.shape[1]
    for index, target in enumerate((query_out, key_out, value_out, output_out)):
        target[...] = own_ref[1, :, index * part : (index + 1) * part]
    for copy in copies:
        copy.wait()


def unpack(sums, own, layer_out, grad_stream, planes, heads):
    _, own_rows, columns = own.shape
    whole = pl.BlockSpec(memory_space=pltpu.VMEM)
    far = pl.BlockSpec(memory_space=pl.ANY)
    places = (("first", 1024), ("gain", 1032), ("shift", 1048), ("small", 1064), ("roi", 1072))

    def sized(*shape):
        return jax.ShapeDtypeStruct(shape, jnp.float32)

    return pl.pallas_call(
        functools.partial(unpack_kernel, places),
        out_shape=(
            jax.ShapeDtypeStruct(layer_out.shape, layer_out.dtype),
            jax.ShapeDtypeStruct(grad_stream.shape, grad_stream.dtype),
            sized(planes, 128),
            sized(8, 128, 128),
            sized(LAYERS, 128),
            sized(LAYERS, 128),
            sized(own_rows, 128),
            sized(1, own_rows),
            *[sized(own_rows, columns // 4)] * 4,
            sized(3, heads, NBUCKET),
            sized(1, own_rows),
            sized(own_rows, columns),
            sized(own_rows, columns),
        ),
        in_specs=[whole, whole, far, far],
        out_specs=(far, far) + (whole,) * 14,
        scratch_shapes=[
            pltpu.VMEM(layer_out.shape, layer_out.dtype),
            pltpu.VMEM(grad_stream.shape, grad_stream.dtype),
            pltpu.SemaphoreType.DMA((2, 4)),
        ],
        compiler_params=pltpu.CompilerParams(vmem_limit_bytes=VMEM_LIMIT),
        name="unpack",
    )(sums, own, layer_out, grad_stream)


def on_device(
    page_image,
    embeddings,
    cotangent,
    doc_ids,
    pad_mask,
    token_boxes,
    conv_first,
    conv_weights,
    group_gain,
    group_shift,
    roi_proj,
    attn_norm,
    query_proj,
    key_proj,
    value_proj,
    output_proj,
    bias_tables,
    ffn_norm,
    up_proj,
    down_proj,
):
    devices = lax.axis_size("dp") * lax.axis_size("tensor")
    feature_map, *records = stem_forward(
        page_image, conv_first, conv_weights, group_gain, group_shift, devices
    )
    places = (token_boxes, doc_ids, pad_mask)
    tables = bias_tables.swapaxes(1, 2)
    pooled, stream, attn_in, heads = box_forward(
        feature_map, places, embeddings, roi_proj, attn_norm, query_proj, key_proj, value_proj
    )
    context, exact, lse = attention_forward(tables, places, heads)
    middle, part_out, grad_middle, grad_context, grad_up, grad_down, grad_output, grad_ffn_norm = (
        middle_layer(context, stream, cotangent, output_proj, ffn_norm, up_proj, down_proj)
    )
    rows_count = lax.axis_size("dp")
    width = stream.shape[1]
    own_rows = width // rows_count

    def by_place(values):
        return values.reshape(rows_count // 4, 2, 2, own_rows, values.shape[1])

    down, up = by_place(grad_down), by_place(grad_up)
    *grad_heads, diagonals, landed, early, other_out = attention_backward(
        tables, places, heads, grad_context, exact, lse, down, up, part_out
    )
    grad_tables = bucket_grads(diagonals)
    grad_stream, grad_attn, kept, second, layer_out, grad_roi, grad_map, grad_attn_norm = end_layer(
        grad_heads,
        (query_proj, key_proj, value_proj),
        attn_in,
        stream,
        grad_middle,
        attn_norm,
        roi_proj,
        pooled,
        places,
        grad_output,
        down,
        landed,
        (middle, part_out, other_out),
        feature_map.shape[0],
    )
    local_heads = grad_tables.shape[0]
    split = grad_roi.reshape(rows_count, 2, own_rows // 2, grad_roi.shape[1])
    sums, own = stem_backward(
        grad_map,
        page_image,
        records,
        conv_weights,
        group_gain,
        group_shift,
        split,
        (grad_attn_norm, grad_ffn_norm),
        grad_tables,
        up,
        by_place(grad_attn),
        kept,
        second,
        early,
        devices,
    )
    outs = list(
        unpack(sums, own, layer_out, grad_stream, conv_first.shape[0], local_heads)
    )
    outs[6] = outs[6].T
    outs[7] = outs[7][0]
    outs[11] = outs[11].T
    outs[12] = outs[12].swapaxes(1, 2)
    outs[13] = outs[13][0]
    outs[15] = outs[15].T
    return tuple(outs)


def solution(mesh):
    placed = (
        P(None, ("dp", "tensor"), None),
        P("dp", None),
        P("dp", None),
        P("dp", None),
        P("dp", None),
        P(None, "dp", None),
        P(),
        P(),
        P(),
        P(),
        P(),
        P(),
        P(None, "tensor"),
        P(None, "tensor"),
        P(None, "tensor"),
        P("tensor", None),
        P(None, None, "tensor"),
        P(),
        P(None, "tensor"),
        P("tensor", None),
    )
    return jax.shard_map(
        on_device,
        mesh=mesh,
        in_specs=placed,
        out_specs=(
            P("dp", None),
            P("dp", None),
            P(),
            P(),
            P(),
            P(),
            P(None, "dp"),
            P("dp"),
            P("dp", "tensor"),
            P("dp", "tensor"),
            P("dp", "tensor"),
            P("tensor", "dp"),
            P(None, None, "tensor"),
            P("dp"),
            P("dp", "tensor"),
            P("tensor", "dp"),
        ),
        check_vma=False,
    )
```

```python
import functools

import jax
import jax.numpy as jnp
import numpy as np
from jax import lax
from jax.experimental import pallas as pl
from jax.experimental.pallas import tpu as pltpu
from jax.sharding import PartitionSpec as P

HDIM = 64
NBUCKET = 32
VMEM_LIMIT = 63 * 2**20
GROUPS = 32


bucket_edges = (12, 16, 23, 32, 46, 64, 91)
norm_eps = 1e-06
group_eps = 1e-05
masked_score = -1e30
highest = lax.Precision.HIGHEST


def bucket_of(relative):
    magnitude = jnp.abs(relative)
    coarse = jnp.full(relative.shape, 8, jnp.int32)
    for edge in bucket_edges:
        coarse = coarse + (magnitude >= edge).astype(jnp.int32)
    return jnp.where(magnitude < 8, magnitude, coarse) + jnp.where(relative > 0, 16, 0).astype(
        jnp.int32
    )


MESH = pl.DeviceIdType.MESH
LAYERS = 9
PIX_CHUNK = 256


def level_of(layer):
    return layer if layer <= 4 else 8 - layer


def stem_rows(pixels):
    return [pixels >> (2 * level_of(layer)) for layer in range(LAYERS)]


def row_starts(rows):
    starts = [0]
    for count in rows:
        starts.append(starts[-1] + count)
    return starts


def split_two(values):
    high = values.astype(jnp.bfloat16)
    low = (values - high.astype(jnp.float32)).astype(jnp.bfloat16)
    return jnp.concatenate([high, low], axis=1)


def group_sum(values):
    lane = lax.broadcasted_iota(jnp.int32, values.shape, 1)
    pairs = values + jnp.where(
        lane % 2 == 0, pltpu.roll(values, 127, 1), pltpu.roll(values, 1, 1)
    )
    return pairs + jnp.where(
        (lane // 2) % 2 == 0, pltpu.roll(pairs, 126, 1), pltpu.roll(pairs, 2, 1)
    )


def wide(row):
    return jnp.broadcast_to(row, (8, row.shape[1]))


def my_index():
    return lax.axis_index("dp") * 2 + lax.axis_index("tensor")


def greet_all(count):
    barrier = pltpu.get_barrier_semaphore()
    me = my_index()

    def greet(step, carry):
        other = lax.rem(me + step, count)
        pl.semaphore_signal(
            barrier, inc=1, device_id=(other // 2, lax.rem(other, 2)), device_id_type=MESH
        )
        return carry

    lax.fori_loop(1, count, greet, 0)


def greeted(count):
    pl.semaphore_wait(pltpu.get_barrier_semaphore(), count - 1)


def send_all(count, source, target, send_sem, recv_sem):
    me = my_index()

    def send(step, carry):
        other = lax.rem(me + step, count)
        pltpu.make_async_remote_copy(
            src_ref=source,
            dst_ref=target,
            send_sem=send_sem,
            recv_sem=recv_sem,
            device_id=(other // 2, lax.rem(other, 2)),
            device_id_type=MESH,
        ).start()
        return carry

    lax.fori_loop(1, count, send, 0, unroll=count <= 32)


def wait_all(count, slots, sem):
    part = slots.at[pl.ds(0, count - 1)]
    pltpu.make_async_copy(part, part, sem).wait()


def natural_places(tile_rows, columns):
    spacing = columns // 8
    places = []
    for row in range(tile_rows):
        for col in range(spacing):
            place = 0
            for bit in range(4):
                place = place * 4 + ((row >> bit) & 1) * 2 + ((col >> bit) & 1)
            places.append((row * columns + col, place * 8))
    return places


SCHEDULE = {
    'start': 'small split',
    8: 'u1b d3a v1a',
    7: 'v1b d3b e3a',
    6: 'u2',
    5: 'a1a e3b',
    4: 'v2',
    3: 'a1b u3a rows',
    2: 'b1a u3b v3a',
    1: 'b1b a2 v3b kept',
    0: 'a3a b2',
    'end': 'a3b',
    'last': 'b3a b3b',
}


def place_of(row):
    return row // 4, lax.rem(row // 2, 2), lax.rem(row, 2)


def start_remote(source, target, send_sem, recv_sem, row):
    pltpu.make_async_remote_copy(
        src_ref=source,
        dst_ref=target,
        send_sem=send_sem,
        recv_sem=recv_sem,
        device_id=(row, lax.axis_index("tensor")),
        device_id_type=MESH,
    ).start()


def await_bytes(buffer, sem):
    pltpu.make_async_copy(buffer, buffer, sem).wait()


def greet_rows(rows):
    for row in rows:
        pl.semaphore_signal(
            pltpu.get_barrier_semaphore(),
            inc=1,
            device_id=(row, lax.axis_index("tensor")),
            device_id_type=MESH,
        )


class Scatter:
    def __init__(self, width, left, send_sem, recv_sem):
        self.row = lax.axis_index("dp")
        self.z, self.y, self.x = place_of(self.row)
        self.across_x = self.row + 1 - 2 * self.x
        self.across_y = self.row + 2 - 4 * self.y
        self.width, self.left = width, left
        self.send_sem, self.recv_sem = send_sem, recv_sem

    def columns(self, source):
        half = source.shape[-1] // 2
        return pl.ds(self.left, self.width), pl.ds(half + self.left, self.width)

    def own_loads(self, source, own, sem):
        first, second = self.columns(source)
        return [
            pltpu.make_async_copy(source.at[:, :, self.x, :, first], own.at[0], sem.at[0]),
            pltpu.make_async_copy(source.at[:, self.y, :, :, second], own.at[1], sem.at[1]),
        ]

    def send_first(self, source, target, begin, size, shift=0):
        first, second = self.columns(source)
        depth = pl.ds(begin, size)
        landing = pl.ds(begin - shift, size)
        start_remote(
            source.at[depth, :, 1 - self.x, :, first],
            target.at[0, landing],
            self.send_sem.at[0],
            self.recv_sem.at[0],
            self.across_x,
        )
        start_remote(
            source.at[depth, 1 - self.y, :, :, second],
            target.at[1, landing],
            self.send_sem.at[1],
            self.recv_sem.at[1],
            self.across_y,
        )

    def await_first(self, landed):
        for side in range(2):
            await_bytes(landed.at[side], self.recv_sem.at[side])

    def sent_first(self, landed):
        for side in range(2):
            await_bytes(landed.at[side], self.send_sem.at[side])

    def send_second(self, source, target):
        start_remote(
            source.at[0, :, 1 - self.y],
            target.at[0],
            self.send_sem.at[2],
            self.recv_sem.at[2],
            self.across_y,
        )
        start_remote(
            source.at[1, :, 1 - self.x],
            target.at[1],
            self.send_sem.at[3],
            self.recv_sem.at[3],
            self.across_x,
        )

    def await_second(self, landed):
        for side in range(2):
            await_bytes(landed.at[side], self.recv_sem.at[2 + side])

    def sent_second(self, landed):
        for side in range(2):
            await_bytes(landed.at[side], self.send_sem.at[2 + side])

    def along_z(self, total, target, step):
        depths = total.shape[1]
        begins = [0]
        for index in range(step):
            begins.append(begins[-1] + (depths >> (index + 1)))
        bit = lax.rem(self.z // (1 << step), 2)
        if step == 0:
            return total, 0, begins[0], depths >> 1, bit
        return target, begins[step - 1], begins[step], depths >> (step + 1), bit

    def send_along(self, total, target, step):
        source, begin, landing, blocks, bit = self.along_z(total, target, step)
        other = self.row + (1 - 2 * bit) * (4 << step)
        for block in range(blocks):
            start_remote(
                source.at[:, begin + 2 * block + 1 - bit],
                target.at[:, landing + block],
                self.send_sem.at[4 + step],
                self.recv_sem.at[4 + step],
                other,
            )

    def add_along(self, total, target, step):
        source, begin, landing, blocks, bit = self.along_z(total, target, step)
        await_bytes(target.at[:, pl.ds(landing, blocks)], self.recv_sem.at[4 + step])
        for side in range(2):
            for block in range(blocks):
                target[side, landing + block] = (
                    target[side, landing + block] + source[side, begin + 2 * block + bit]
                )

    def finish(self, total, target, result, base, step):
        steps = z_steps(total.shape[1])
        for index in range(step, steps):
            if index > step:
                self.send_along(total, target, index)
            self.add_along(total, target, index)
        landing = self.along_z(total, target, steps - 1)[2]
        half = result.shape[-1] // 2
        for side in range(2):
            at = side * half + self.left
            result[base, :, at : at + self.width] = target[side, landing]

    def sent_along(self, total, target):
        for step in range(z_steps(total.shape[1])):
            _, _, landing, blocks, _ = self.along_z(total, target, step)
            await_bytes(target.at[:, pl.ds(landing, blocks)], self.send_sem.at[4 + step])


def z_steps(depths):
    return depths.bit_length() - 1


def add_pairs(left, right):
    for side in range(left.shape[0]):
        for depth in range(left.shape[1]):
            left[side, depth] = left[side, depth] + right[side, depth]


def scatter_semaphores(copies):
    return [pltpu.SemaphoreType.DMA((copies,)), pltpu.SemaphoreType.DMA((copies,))]


class ScatterHere(Scatter):
    refs = 8

    @staticmethod
    def scratch(depths, rows, width):
        pair = pltpu.VMEM((2, depths, 2, rows, width), jnp.float32)
        one = pltpu.VMEM((2, depths, rows, width), jnp.float32)
        return [pair, pair, one, one, one, pltpu.SemaphoreType.DMA((2,)), *scatter_semaphores(4 + z_steps(depths))]

    def __init__(self, source, left, refs):
        self.source = source
        self.own, self.first, self.second, self.total, self.third, load_sem, send, recv = refs
        super().__init__(self.own.shape[-1], left, send, recv)
        self.loads = self.own_loads(source, self.own, load_sem)
        for load in self.loads:
            load.start()

    def start_first(self, part):
        size = self.own.shape[1] // 2
        self.send_first(self.source, self.first, part * size, size)

    def start_second(self, landed=None):
        for load in self.loads:
            load.wait()
        self.await_first(self.first if landed is None else landed)
        add_pairs(self.own, self.first)
        self.send_second(self.own, self.second)

    def add_second(self):
        self.await_second(self.second)
        for side in range(2):
            kept = self.y if side == 0 else self.x
            for depth in range(self.total.shape[1]):
                self.total[side, depth] = self.own[side, depth, kept] + self.second[side, depth]

    def third_first(self):
        self.add_second()
        self.send_along(self.total, self.third, 0)

    def third_next(self):
        self.add_along(self.total, self.third, 0)
        self.send_along(self.total, self.third, 1)

    def end(self, result, base):
        self.finish(self.total, self.third, result, base, 1)

    def sent(self, landed=None):
        self.sent_first(self.first if landed is None else landed)
        self.sent_second(self.second)
        self.sent_along(self.total, self.third)


class ScatterRest(Scatter):
    refs = 6

    @staticmethod
    def scratch(depths, rows, width):
        one = pltpu.VMEM((2, depths, rows, width), jnp.float32)
        return [one, one, one, pltpu.SemaphoreType.DMA((2,)), *scatter_semaphores(4 + z_steps(depths))]

    def __init__(self, kept, arrived, left, refs):
        self.total, self.second, self.third, load_sem, send, recv = refs
        width = self.total.shape[-1]
        super().__init__(width, left, send, recv)
        columns = pl.ds(left, width)
        self.loads = [
            pltpu.make_async_copy(kept.at[:, :, :, columns], self.total, load_sem.at[0]),
            pltpu.make_async_copy(arrived.at[:, :, :, columns], self.second, load_sem.at[1]),
        ]
        for load in self.loads:
            load.start()

    def third_first(self):
        for load in self.loads:
            load.wait()
        add_pairs(self.total, self.second)
        self.send_along(self.total, self.third, 0)

    third_next = ScatterHere.third_next
    end = ScatterHere.end

    def sent(self):
        self.sent_along(self.total, self.third)


def stem_forward_kernel(
    count,
    places,
    image_ref,
    first_ref,
    weights_ref,
    gain_ref,
    shift_ref,
    feature_ref,
    norm_hbm,
    input_hbm,
    scale_ref,
    norm_ref,
    input_ref,
    natural,
    skip,
    current,
    source,
    slots,
    send_sem,
    recv_sem,
    store_sem,
):
    me = my_index()
    greet_all(count)
    pixels = feature_ref.shape[0]
    rows = stem_rows(pixels)
    norm_at = row_starts(rows)
    input_at = row_starts(rows[1:])
    skip_at = row_starts(rows[:4])
    spacing = 16
    for row in range(image_ref.shape[1]):
        natural[row * 128 : (row + 1) * 128, :] = lax.dot_general(
            image_ref[:, row, :],
            first_ref[...],
            (((0,), (0,)), ((), ())),
            preferred_element_type=jnp.float32,
        )
    for start, place in places:
        norm_ref[place : place + 8, :] = natural[pl.ds(start, 8, stride=spacing), :]
    stores = []
    for layer in range(LAYERS):
        height = rows[layer]
        chunk = min(height, PIX_CHUNK)
        base = norm_at[layer]
        total = jnp.zeros((8, 128), jnp.float32)
        if layer > 0:
            weights = weights_ref[layer - 1]
            stacked = jnp.concatenate([weights, weights], axis=0)

            def convolve(index, total):
                at = pl.multiple_of(index * chunk, chunk)
                values = jnp.dot(
                    split_two(input_ref[pl.ds(input_at[layer - 1] + at, chunk), :]),
                    stacked,
                    preferred_element_type=jnp.float32,
                )
                norm_ref[pl.ds(base + at, chunk), :] = values
                return total + jnp.sum(values.reshape(chunk // 8, 8, 128), axis=0)

        else:

            def convolve(index, total):
                at = pl.multiple_of(index * chunk, chunk)
                values = norm_ref[pl.ds(base + at, chunk), :]
                return total + jnp.sum(values.reshape(chunk // 8, 8, 128), axis=0)

        total = lax.fori_loop(0, height // chunk, convolve, total, unroll=True)
        mean = jnp.sum(total, axis=0, keepdims=True) * (1.0 / height)

        def deviate(index, total):
            at = pl.multiple_of(index * chunk, chunk)
            values = norm_ref[pl.ds(base + at, chunk), :] - mean
            return total + jnp.sum((values * values).reshape(chunk // 8, 8, 128), axis=0)

        square = lax.fori_loop(0, height // chunk, deviate, jnp.zeros((8, 128), jnp.float32), unroll=True)
        square = jnp.sum(square, axis=0, keepdims=True)
        stats = jnp.concatenate([mean, square], axis=0)
        source[layer] = stats
        slots[layer, me] = stats
        if layer == 0:
            greeted(count)
        send_all(
            count,
            source.at[layer],
            slots.at[layer, me],
            send_sem.at[layer],
            recv_sem.at[layer],
        )
        wait_all(count, slots.at[layer], recv_sem.at[layer])
        means = slots[layer, :, 0, :]
        centre = group_sum(wide(jnp.sum(means, axis=0, keepdims=True))) * (0.25 / count)
        apart = means - centre[0:1]
        spread = jnp.sum(slots[layer, :, 1, :], axis=0, keepdims=True) + height * jnp.sum(
            apart * apart, axis=0, keepdims=True
        )
        variance = group_sum(wide(spread)) * (1.0 / (4 * height * count))
        inverse = lax.rsqrt(variance + group_eps)[0:1]
        centre = centre[0:1]
        scale_ref[layer : layer + 1, :] = inverse
        gain = gain_ref[layer : layer + 1, :]
        shift = shift_ref[layer : layer + 1, :]

        def activate(start, size):
            normed = (norm_ref[pl.ds(base + start, size), :] - centre) * inverse
            norm_ref[pl.ds(base + start, size), :] = normed
            lifted = normed * gain + shift
            return lifted / (1.0 + jnp.exp(-lifted))

        if layer < 4:
            quarter = height // 4
            part = min(quarter, 64)

            def pool(index, carry):
                at = pl.multiple_of(index * part, part)
                mean_of = jnp.zeros((part, 128), jnp.float32)
                for corner in range(4):
                    value = activate(corner * quarter + at, part)
                    skip[pl.ds(skip_at[layer] + corner * quarter + at, part), :] = value
                    mean_of = mean_of + value
                input_ref[pl.ds(input_at[layer] + at, part), :] = mean_of * 0.25
                return carry

            lax.fori_loop(0, quarter // part, pool, 0, unroll=True)
        elif layer < 8:
            part = min(height, 64)
            skipped = skip_at[7 - layer]

            def grow(index, carry):
                at = pl.multiple_of(index * part, part)
                value = activate(at, part)
                for corner in range(4):
                    place = corner * height + at
                    input_ref[pl.ds(input_at[layer] + place, part), :] = (
                        value + skip[pl.ds(skipped + place, part), :]
                    )
                return carry

            lax.fori_loop(0, height // part, grow, 0, unroll=True)
        else:

            def finish(index, carry):
                at = pl.multiple_of(index * chunk, chunk)
                current[pl.ds(at, chunk), :] = activate(at, chunk)
                return carry

            lax.fori_loop(0, height // chunk, finish, 0, unroll=True)
        parts = [(norm_ref, norm_hbm, base, height)]
        if layer < 8:
            parts.append((input_ref, input_hbm, input_at[layer], rows[layer + 1]))
        for index, (source_ref, target, begin, size) in enumerate(parts):
            store = pltpu.make_async_copy(
                source_ref.at[pl.ds(begin, size)],
                target.at[pl.ds(begin, size)],
                store_sem.at[index, layer],
            )
            store.start()
            stores.append(store)
    for start, place in places:
        feature_ref[pl.ds(start, 8, stride=spacing), :] = current[place : place + 8, :]
    for layer in range(LAYERS):
        wait_all(count, slots.at[layer], send_sem.at[layer])
    for store in stores:
        store.wait()


def stem_backward_kernel(
    count,
    places,
    grad_ref,
    image_ref,
    norm_hbm,
    input_hbm,
    scale_ref,
    weights_ref,
    gain_ref,
    shift_ref,
    split_ref,
    attn_norm_ref,
    ffn_norm_ref,
    tables_ref,
    up_ref,
    attn_ref,
    kept_ref,
    second_ref,
    early_ref,
    small_out,
    large_out,
    norm_ref,
    input_ref,
    natural,
    ordered,
    active,
    grad_conv,
    skip,
    grads,
    product,
    source,
    slots,
    first_source,
    first_slots,
    parts,
    shared,
    send_sem,
    recv_sem,
    part_send,
    part_recv,
    share_send,
    share_recv,
    split_slots,
    split_half,
    small_ref,
    small_slots,
    row_send,
    row_recv,
    load_sem,
    *scatter_refs,
):
    me = my_index()
    row = lax.axis_index("dp")
    core = lax.axis_index("tensor")
    rows_count = count // 2
    greet_all(count)
    pixels = grad_ref.shape[0]
    rows = stem_rows(pixels)
    norm_at = row_starts(rows)
    input_at = row_starts(rows[1:])
    loads = []
    for index, (source_ref, target, begin, size) in enumerate(
        [
            (norm_hbm, norm_ref, norm_at[8], rows[8]),
            (input_hbm, input_ref, input_at[7], rows[8]),
            (norm_hbm, norm_ref, 0, norm_at[8]),
            (input_hbm, input_ref, 0, input_at[7]),
        ]
    ):
        loads.append(
            pltpu.make_async_copy(
                source_ref.at[pl.ds(begin, size)], target.at[pl.ds(begin, size)], load_sem.at[index]
            )
        )
        loads[-1].start()
    jobs = []
    for index, (source_ref, left) in enumerate(
        [(up_ref, 0), (up_ref, 1), (attn_ref, 0), (attn_ref, 1)]
    ):
        refs = scatter_refs[index * ScatterHere.refs : (index + 1) * ScatterHere.refs]
        jobs.append(ScatterHere(source_ref, left * refs[0].shape[-1], refs))
    rest = 4 * ScatterHere.refs
    for index in range(2):
        refs = scatter_refs[rest + index * ScatterRest.refs : rest + (index + 1) * ScatterRest.refs]
        jobs.append(ScatterRest(kept_ref, second_ref, index * refs[0].shape[-1], refs))
    up_left, up_right, attn_left, attn_right, down_left, down_right = jobs
    early = up_left.first.shape[1] // 2
    early_load = pltpu.make_async_copy(
        early_ref, up_left.first.at[:, pl.ds(0, early)], load_sem.at[4]
    )
    early_load.start()
    up_landed = up_left.first.at[:, pl.ds(early, early)]
    small_rows, split_rows = 1064, 1072
    own_rows = 2 * split_half.shape[1]
    small_ref[...] = jnp.zeros_like(small_ref)
    for device in range(rows_count):
        lanes = slice(device * own_rows, (device + 1) * own_rows)
        small_ref[device, 0:1, :own_rows] = attn_norm_ref[:, lanes]
        small_ref[device, 1:2, :own_rows] = ffn_norm_ref[:, lanes]
        small_ref[device, 2 : 2 + tables_ref.shape[0], : tables_ref.shape[1]] = tables_ref[...]
    skip_at = row_starts(rows[:4])
    spacing = 16
    owners = count // 8
    owned = parts.shape[1]
    for start, place in places:
        ordered[place : place + 8, :] = grad_ref[pl.ds(start, 8, stride=spacing), :]

    def send_rows(first, last, source_of, target, place):
        def send(step, carry):
            other = lax.rem(row + step, rows_count)
            pltpu.make_async_remote_copy(
                src_ref=source_of(other),
                dst_ref=target.at[row],
                send_sem=row_send.at[place],
                recv_sem=row_recv.at[place],
                device_id=(other, core),
                device_id_type=MESH,
            ).start()
            return carry

        lax.fori_loop(first, last, send, 0)

    def weight_grad(layer):
        height = rows[layer]
        chunk = min(height, 512)

        def add(index, total):
            at = pl.multiple_of(index * chunk, chunk)
            return total + lax.dot_general(
                input_ref[pl.ds(input_at[layer - 1] + at, chunk), :].astype(jnp.bfloat16),
                grad_conv[pl.ds(norm_at[layer] + at, chunk), :].astype(jnp.bfloat16),
                (((0,), (0,)), ((), ())),
                preferred_element_type=jnp.float32,
            )

        product[layer - 1] = lax.fori_loop(
            0, height // chunk, add, jnp.zeros((128, 128), jnp.float32), unroll=True
        ).reshape(owners, owned, 128)

        def send(index, carry):
            owner = layer - 1 + 8 * index

            @pl.when(owner != me)
            def _():
                pltpu.make_async_remote_copy(
                    src_ref=product.at[layer - 1, index],
                    dst_ref=parts.at[me],
                    send_sem=part_send,
                    recv_sem=part_recv,
                    device_id=(owner // 2, lax.rem(owner, 2)),
                    device_id_type=MESH,
                ).start()

            @pl.when(owner == me)
            def _():
                parts[me] = product[layer - 1, index]

            return carry

        lax.fori_loop(0, owners, send, 0)

    def send_small():
        small_slots[row] = small_ref[row]
        send_rows(1, rows_count, lambda other: small_ref.at[other], small_slots, 0)

    def send_split():
        split_slots[row] = split_ref[row, core]
        send_rows(1, rows_count, lambda other: split_ref.at[other, core], split_slots, 1)

    def add_rows():
        wait_all(rows_count, small_slots, row_recv.at[0])
        small_out[small_rows : small_rows + 8, :] = jnp.sum(small_slots[...], axis=0)
        wait_all(rows_count, split_slots, row_recv.at[1])
        split_half[core] = jnp.sum(split_slots[...], axis=0)
        swap.start()

    def keep_rows():
        swap.wait()
        size = split_half.shape[1]
        for part in range(2):
            begin = split_rows + part * size
            small_out[begin : begin + size, :] = split_half[part]

    swap = pltpu.make_async_remote_copy(
        src_ref=split_half.at[core],
        dst_ref=split_half.at[core],
        send_sem=row_send.at[2],
        recv_sem=row_recv.at[2],
        device_id=(row, 1 - core),
        device_id_type=MESH,
    )

    def second_of_up():
        early_load.wait()
        up_left.start_second(up_landed)

    steps = {
        "small": send_small,
        "split": send_split,
        "rows": add_rows,
        "kept": keep_rows,
        "u1b": lambda: up_left.start_first(1),
        "u2": second_of_up,
    }
    for mark, job in zip("uvabde", jobs):
        if mark in "vab":
            steps[mark + "1a"] = functools.partial(job.start_first, 0)
            steps[mark + "1b"] = functools.partial(job.start_first, 1)
            steps[mark + "2"] = job.start_second
        steps[mark + "3a"] = job.third_first
        steps[mark + "3b"] = job.third_next

    greeted(count)
    for name in SCHEDULE["start"].split():
        steps[name]()
    for layer in range(LAYERS - 1, -1, -1):
        height = rows[layer]
        chunk = min(height, PIX_CHUNK)
        base = norm_at[layer]
        gain = gain_ref[layer : layer + 1, :]
        shift = shift_ref[layer : layer + 1, :]
        inverse = scale_ref[layer : layer + 1, :]
        incoming = ordered if layer == 8 else grads
        if layer == 8:
            loads[0].wait()
        if layer == 7:
            loads[2].wait()
        if layer == 6:
            loads[3].wait()

        def activate(index, carry):
            first, second = carry
            at = pl.multiple_of(index * chunk, chunk)
            normed = norm_ref[pl.ds(base + at, chunk), :]
            lifted = normed * gain + shift
            sigma = 1.0 / (1.0 + jnp.exp(-lifted))
            value = incoming[pl.ds(at, chunk), :] * sigma * (1.0 + lifted * (1.0 - sigma))
            active[pl.ds(at, chunk), :] = value
            first = first + jnp.sum(value.reshape(chunk // 8, 8, 128), axis=0)
            second = second + jnp.sum((value * normed).reshape(chunk // 8, 8, 128), axis=0)
            return first, second

        zero = jnp.zeros((8, 128), jnp.float32)
        first, second = lax.fori_loop(0, height // chunk, activate, (zero, zero), unroll=True)
        sums = jnp.concatenate(
            [jnp.sum(first, axis=0, keepdims=True), jnp.sum(second, axis=0, keepdims=True)], axis=0
        )
        source[layer] = sums
        slots[layer, me] = sums
        send_all(
            count, source.at[layer], slots.at[layer, me], send_sem.at[layer], recv_sem.at[layer]
        )
        for name in SCHEDULE[layer].split():
            steps[name]()
        if layer == 7:
            loads[1].wait()
        if layer < 8:
            weight_grad(layer + 1)
        wait_all(count, slots.at[layer], recv_sem.at[layer])
        totals = jnp.sum(slots[layer], axis=0)
        small_out[1032 + layer : 1033 + layer, :] = totals[1:2]
        small_out[1048 + layer : 1049 + layer, :] = totals[0:1]
        share = 1.0 / (4 * height * count)
        first_mean = group_sum(wide(totals[0:1] * gain))[0:1] * share
        second_mean = group_sum(wide(totals[1:2] * gain))[0:1] * share

        def conv_grad(start, size):
            value = inverse * (
                active[pl.ds(start, size), :] * gain
                - first_mean
                - norm_ref[pl.ds(base + start, size), :] * second_mean
            )
            grad_conv[pl.ds(base + start, size), :] = value
            return value

        if layer > 0:
            weights = weights_ref[layer - 1]
            stacked = jnp.concatenate([weights, weights], axis=1)

            def input_grad(start, size):
                return lax.dot_general(
                    split_two(conv_grad(start, size)),
                    stacked,
                    (((1,), (1,)), ((), ())),
                    preferred_element_type=jnp.float32,
                )

        if layer > 4:
            quarter = height // 4
            part = min(quarter, 64)
            skipped = skip_at[8 - layer]

            def shrink(index, carry):
                at = pl.multiple_of(index * part, part)
                total = jnp.zeros((part, 128), jnp.float32)
                for corner in range(4):
                    place = corner * quarter + at
                    value = input_grad(place, part)
                    skip[pl.ds(skipped + place, part), :] = value
                    total = total + value
                grads[pl.ds(at, part), :] = total
                return carry

            lax.fori_loop(0, quarter // part, shrink, 0, unroll=True)
        elif layer > 0:
            part = min(height, 128)
            skipped = skip_at[layer - 1]

            def spread_out(index, carry):
                at = pl.multiple_of(index * part, part)
                value = input_grad(at, part) * 0.25
                for corner in range(4):
                    place = corner * height + at
                    grads[pl.ds(place, part), :] = value + skip[pl.ds(skipped + place, part), :]
                return carry

            lax.fori_loop(0, height // part, spread_out, 0, unroll=True)
        else:

            def finish(index, carry):
                at = pl.multiple_of(index * chunk, chunk)
                conv_grad(at, chunk)
                return carry

            lax.fori_loop(0, height // chunk, finish, 0, unroll=True)
    for start, place in places:
        natural[pl.ds(start, 8, stride=spacing), :] = grad_conv[place : place + 8, :]
    first_part = jnp.zeros(first_source.shape, jnp.float32)
    for line in range(image_ref.shape[1]):
        first_part = first_part + dot_plain(
            image_ref[:, line, :],
            natural[line * 128 : (line + 1) * 128, :].astype(jnp.bfloat16),
        )
    first_source[...] = first_part
    first_slots[me] = first_part
    send_all(count, first_source, first_slots.at[me], send_sem.at[LAYERS], recv_sem.at[LAYERS])
    for name in SCHEDULE["end"].split():
        steps[name]()
    wait_all(count, parts, part_recv)
    shared[row, core] = jnp.sum(parts[...], axis=0)
    own_share = shared.at[row, core]
    for step in range(1, rows_count):
        start_remote(
            own_share, own_share, share_send.at[0], share_recv.at[0], lax.rem(row + step, rows_count)
        )
    for job, base in ((down_left, 2), (down_right, 2), (up_left, 0), (up_right, 0)):
        job.end(large_out, base)
    for name in SCHEDULE["last"].split():
        steps[name]()
    wait_all(count, first_slots, recv_sem.at[LAYERS])
    small_out[1024 : 1024 + first_slots.shape[1], :] = jnp.sum(first_slots[...], axis=0)
    landed_shares = shared.at[pl.ds(0, rows_count - 1), core]
    await_bytes(landed_shares, share_recv.at[0])
    forward = partner_copy(
        shared.at[:, core], shared.at[:, core], share_send.at[1], share_recv.at[1]
    )
    forward.start()
    forward.wait()
    for device in range(count):
        begin = (device % 8) * 128 + (device // 8) * owned
        small_out[begin : begin + owned, :] = shared[device // 2, device % 2]
    attn_left.end(large_out, 1)
    for layer in range(LAYERS):
        wait_all(count, slots.at[layer], send_sem.at[layer])
    wait_all(count, first_slots, send_sem.at[LAYERS])
    wait_all(rows_count, small_slots, row_send.at[0])
    wait_all(rows_count, split_slots, row_send.at[1])
    wait_all(count, parts, part_send)
    await_bytes(landed_shares, share_send.at[0])
    up_left.sent(up_landed)
    for job in jobs[1:]:
        job.sent()
    attn_right.end(large_out, 1)


def stem_forward(page_image, conv_first, conv_weights, group_gain, group_shift, devices):
    planes, tile_rows, columns = page_image.shape
    pixels = tile_rows * columns
    rows = stem_rows(pixels)
    places = natural_places(tile_rows, columns)
    whole = pl.BlockSpec(memory_space=pltpu.VMEM)
    far = pl.BlockSpec(memory_space=pltpu.HBM)
    return pl.pallas_call(
        functools.partial(stem_forward_kernel, devices, places),
        out_shape=(
            jax.ShapeDtypeStruct((pixels, 128), jnp.float32),
            jax.ShapeDtypeStruct((sum(rows), 128), jnp.float32),
            jax.ShapeDtypeStruct((sum(rows[1:]), 128), jnp.float32),
            jax.ShapeDtypeStruct((LAYERS, 128), jnp.float32),
        ),
        in_specs=[whole] * 5,
        out_specs=(whole, far, far, whole),
        scratch_shapes=[
            pltpu.VMEM((sum(rows), 128), jnp.float32),
            pltpu.VMEM((sum(rows[1:]), 128), jnp.float32),
            pltpu.VMEM((pixels, 128), jnp.float32),
            pltpu.VMEM((sum(rows[:4]), 128), jnp.float32),
            pltpu.VMEM((pixels, 128), jnp.float32),
            pltpu.VMEM((LAYERS, 2, 128), jnp.float32),
            pltpu.VMEM((LAYERS, devices, 2, 128), jnp.float32),
            pltpu.SemaphoreType.DMA((LAYERS,)),
            pltpu.SemaphoreType.DMA((LAYERS,)),
            pltpu.SemaphoreType.DMA((2, LAYERS)),
        ],
        compiler_params=pltpu.CompilerParams(
            collective_id=0, has_side_effects=True, vmem_limit_bytes=VMEM_LIMIT
        ),
        cost_estimate=pl.CostEstimate(
            flops=54 * 10**9, bytes_accessed=2 * 10**7, transcendentals=0
        ),
        name="stem_forward",
    )(page_image, conv_first, conv_weights, group_gain, group_shift)


def stem_backward(
    grad_map,
    page_image,
    records,
    conv_weights,
    group_gain,
    group_shift,
    split,
    norm_grads,
    tables,
    up,
    attn,
    kept,
    second,
    early,
    devices,
):
    planes, tile_rows, columns = page_image.shape
    pixels = tile_rows * columns
    rows = stem_rows(pixels)
    norms, inputs, scales = records
    places = natural_places(tile_rows, columns)
    whole = pl.BlockSpec(memory_space=pltpu.VMEM)
    owned = 1024 // devices
    far = pl.BlockSpec(memory_space=pltpu.HBM)
    depths, _, _, own_rows, columns = up.shape
    return pl.pallas_call(
        functools.partial(stem_backward_kernel, devices, places),
        out_shape=(
            jax.ShapeDtypeStruct((1072 + 2 * split.shape[2], 128), jnp.float32),
            jax.ShapeDtypeStruct((3, own_rows, columns), jnp.float32),
        ),
        in_specs=[whole, whole, far, far] + [whole] * 8 + [far] * 5,
        out_specs=(whole,) * 2,
        scratch_shapes=[
            pltpu.VMEM((sum(rows), 128), jnp.float32),
            pltpu.VMEM((sum(rows[1:]), 128), jnp.float32),
            pltpu.VMEM((pixels, 128), jnp.float32),
            pltpu.VMEM((pixels, 128), jnp.float32),
            pltpu.VMEM((pixels, 128), jnp.float32),
            pltpu.VMEM((sum(rows), 128), jnp.float32),
            pltpu.VMEM((sum(rows[:4]), 128), jnp.float32),
            pltpu.VMEM((pixels, 128), jnp.float32),
            pltpu.VMEM((8, devices // 8, owned, 128), jnp.float32),
            pltpu.VMEM((LAYERS, 2, 128), jnp.float32),
            pltpu.VMEM((LAYERS, devices, 2, 128), jnp.float32),
            pltpu.VMEM((planes, 128), jnp.float32),
            pltpu.VMEM((devices, planes, 128), jnp.float32),
            pltpu.VMEM((devices, owned, 128), jnp.float32),
            pltpu.VMEM((devices // 2, 2, owned, 128), jnp.float32),
            pltpu.SemaphoreType.DMA((LAYERS + 1,)),
            pltpu.SemaphoreType.DMA((LAYERS + 1,)),
            pltpu.SemaphoreType.DMA,
            pltpu.SemaphoreType.DMA,
            pltpu.SemaphoreType.DMA((2,)),
            pltpu.SemaphoreType.DMA((2,)),
            pltpu.VMEM((devices // 2, *split.shape[2:]), jnp.float32),
            pltpu.VMEM(split.shape[1:], jnp.float32),
            pltpu.VMEM((devices // 2, 8, 128), jnp.float32),
            pltpu.VMEM((devices // 2, 8, 128), jnp.float32),
            pltpu.SemaphoreType.DMA((3,)),
            pltpu.SemaphoreType.DMA((3,)),
            pltpu.SemaphoreType.DMA((5,)),
            *(ScatterHere.scratch(depths, own_rows, columns // 4) * 4),
            *(ScatterRest.scratch(depths, own_rows, columns // 4) * 2),
        ],
        compiler_params=pltpu.CompilerParams(
            collective_id=1, has_side_effects=True, vmem_limit_bytes=VMEM_LIMIT
        ),
        cost_estimate=pl.CostEstimate(
            flops=65 * 10**9, bytes_accessed=2 * 10**7, transcendentals=0
        ),
        name="stem_backward",
    )(
        grad_map,
        page_image,
        norms,
        inputs,
        scales,
        conv_weights,
        group_gain,
        group_shift,
        split,
        *norm_grads,
        tables,
        up,
        attn,
        kept,
        second,
        early,
    )


TILE = 128
QROWS = 256
KIND_ROWS = 8
FAR_LANE = 32
LOW_LANE = 40
PAD_LANE = 48
DOC_LANE = 56


def dot_last(left, right):
    return lax.dot_general(
        left, right, (((1,), (1,)), ((), ())), preferred_element_type=jnp.float32
    )


def dot_plain(left, right):
    return jnp.dot(left, right, preferred_element_type=jnp.float32)


def bucket_vector(tables_ref, table, head, relative):
    buckets = bucket_of(relative)
    values = jnp.zeros(relative.shape, jnp.float32)
    for bucket in range(NBUCKET):
        values = jnp.where(buckets == bucket, tables_ref[table, head, bucket], values)
    return values


def signed_lanes(width):
    lane = lax.broadcasted_iota(jnp.int32, (8, width), 1)
    return jnp.where(lane < width // 2, lane, lane - width)


def rolled(row, height):
    return pltpu.roll(
        jnp.broadcast_to(row[0:1], (height, row.shape[1])), 0, 1, stride=1, stride_axis=0
    )


def token_columns(boxes_ref, docs_ref, pads_ref, info):
    rows = [boxes_ref[0], boxes_ref[1], docs_ref[...], pads_ref[...], boxes_ref[2], boxes_ref[3]]
    rows = rows + [jnp.zeros_like(rows[0])] * 2
    info[...] = jnp.concatenate(rows, axis=0).astype(jnp.float32).T.astype(jnp.int32)


def token_lanes(info_ref, one_hot_x, query_base, key_base, pad_tiles):
    tokens = info_ref.shape[0]
    lane = lax.broadcasted_iota(jnp.int32, (TILE, 128), 1)
    row = lax.broadcasted_iota(jnp.int32, (TILE, 128), 0)
    for tile in range(tokens // TILE):
        at = slice(tile * TILE, (tile + 1) * TILE)
        left = info_ref[at, 0:1]
        top = info_ref[at, 1:2]
        doc = info_ref[at, 2:3]
        hidden = jnp.where(info_ref[at, 3:4] > 0, 0.0, masked_score)
        one_hot_x[at, :] = (lane == left).astype(jnp.float32).astype(jnp.bfloat16)
        shared = jnp.where((lane == top) | (lane == DOC_LANE + doc), 1.0, 0.0)
        query_base[at, :] = jnp.where(lane == FAR_LANE + tile, 1.0, shared).astype(jnp.bfloat16)
        key = jnp.where((lane == FAR_LANE + tile) | (lane == LOW_LANE + tile), 1.0, shared)
        key = jnp.where(lane == PAD_LANE + tile, hidden, key)
        key_base[1, at, :] = key.astype(jnp.bfloat16)
        key_base[0, at, :] = pltpu.roll(key, 64, 1).astype(jnp.bfloat16)
        pad_tiles[at, :] = jnp.where(lane == row, 0.0, jnp.broadcast_to(hidden, (TILE, 128)))


def head_matrices(tables_ref, head, side):
    first = bucket_vector(tables_ref, 1, head, signed_lanes(256))
    across = rolled(first, 128)[:, :128].astype(jnp.bfloat16)
    second = rolled(bucket_vector(tables_ref, 2, head, signed_lanes(128)), 128)
    row = lax.broadcasted_iota(jnp.int32, (128, 128), 0)
    lane = lax.broadcasted_iota(jnp.int32, (128, 128), 1)
    mixed = jnp.where((row < FAR_LANE) & (lane < FAR_LANE), second, 0.0)
    gap = lane % 8 - (row - FAR_LANE)
    before = jnp.full((128, 128), tables_ref[0, head, NBUCKET // 2 - 1], jnp.float32)
    after = jnp.full((128, 128), tables_ref[0, head, NBUCKET - 1], jnp.float32)
    far = jnp.where(gap <= -2, before, jnp.where(gap >= 2, after, 0.0))
    high = far.astype(jnp.bfloat16).astype(jnp.float32)
    of_tile = (row >= FAR_LANE) & (row < LOW_LANE)
    mixed = jnp.where(of_tile & (lane >= FAR_LANE) & (lane < LOW_LANE), high, mixed)
    mixed = jnp.where(of_tile & (lane >= LOW_LANE) & (lane < PAD_LANE), far - high, mixed)
    mixed = jnp.where(
        of_tile & (lane >= PAD_LANE) & (lane < DOC_LANE) & (gap != 0), 1.0, mixed
    )
    docs = (row >= DOC_LANE) & (row < 64) & (lane >= DOC_LANE) & (lane < 64)
    mixed = jnp.where(docs & (row != lane), masked_score, mixed)
    if side == 0:
        mixed = pltpu.roll(mixed, 64, 1)
    near = rolled(bucket_vector(tables_ref, 0, head, -signed_lanes(512)), 128)
    tiles = {0: near[:, :128], 1: near[:, 384:], -1: near[:, 128:256]}
    return across, mixed.astype(jnp.bfloat16), tiles


def own_half(side, own, other):
    lane = lax.broadcasted_iota(jnp.int32, own.shape, 1)
    return jnp.where((lane < 64) if side == 0 else (lane >= 64), own, other)


def widen_operands(
    side, head, tables_ref, query_ref, key_ref, one_hot_x, query_base, key_base, query_wide, key_wide, near
):
    across, mixed, tiles = head_matrices(tables_ref, head, side)
    for gap in (-1, 0, 1):
        near[side, gap + 1] = tiles[gap]
    scaled = (query_ref[...].astype(jnp.float32) * HDIM ** (-0.5)).astype(jnp.bfloat16)
    query_wide[side, :, :128] = own_half(
        side, scaled, dot_plain(query_base[...], mixed).astype(jnp.bfloat16)
    )
    query_wide[side, :, 128:] = dot_plain(one_hot_x[...], across).astype(jnp.bfloat16)
    key_wide[side, :, :128] = own_half(side, key_ref[...], key_base[side])
    key_wide[side, :, 128:] = one_hot_x[...]


def near_scores(scores, side, block, tile, near, pad_tiles):
    halves = []
    for half in range(QROWS // TILE):
        part = scores[:, half * TILE : (half + 1) * TILE]
        gap = tile - (block * (QROWS // TILE) + half)
        if abs(gap) <= 1:
            part = part + near[side, gap + 1]
        if gap == 0:
            part = part + pad_tiles[tile * TILE : (tile + 1) * TILE, :]
        halves.append(part)
    return jnp.concatenate(halves, axis=1)


def attention_forward_kernel(
    tables_ref,
    boxes_ref,
    docs_ref,
    pads_ref,
    query_ref,
    key_ref,
    value_ref,
    context_ref,
    exact_ref,
    lse_ref,
    info_ref,
    one_hot_x,
    query_base,
    key_base,
    pad_tiles,
    query_wide,
    key_wide,
    near,
    scores,
    weights,
):
    pair = pl.program_id(0)
    tokens = query_ref.shape[0]

    @pl.when(pair == 0)
    def _():
        token_columns(boxes_ref, docs_ref, pads_ref, info_ref)
        token_lanes(info_ref, one_hot_x, query_base, key_base, pad_tiles)

    def widen(side):
        widen_operands(
            side, pair * 2 + side, tables_ref, query_ref, key_ref, one_hot_x, query_base, key_base,
            query_wide, key_wide, near,
        )

    widen(0)
    values = value_ref[...].T
    steps = [(block, side) for block in range(tokens // QROWS) for side in range(2)]

    def products(step):
        block, side = step
        scores[side] = dot_last(
            key_wide[side], query_wide[side, block * QROWS : (block + 1) * QROWS, :]
        )

    def collect():
        block, side, total = waiting.pop(0)
        columns = slice(block * QROWS, (block + 1) * QROWS)
        context = dot_plain(values[side * 64 : (side + 1) * 64, :], weights[side])
        contexts.append(context * (1.0 / total))
        if side == 1:
            context = jnp.concatenate(contexts, axis=0)
            contexts.clear()
            exact_ref[:, columns] = context
            context_ref[columns, :] = context.T.astype(jnp.bfloat16)

    products(steps[0])
    widen(1)
    contexts = []
    waiting = []
    for index, (block, side) in enumerate(steps):
        columns = slice(block * QROWS, (block + 1) * QROWS)
        if index + 1 < len(steps):
            products(steps[index + 1])
        if waiting:
            collect()
        top = jnp.full((8, QROWS), masked_score, jnp.float32)
        for tile in range(tokens // TILE):
            at = slice(tile * TILE, (tile + 1) * TILE)
            part = scores[side, at, :]
            if any(abs(tile - 2 * block - half) <= 1 for half in range(2)):
                part = near_scores(part, side, block, tile, near, pad_tiles)
                scores[side, at, :] = part
            top = jnp.maximum(top, jnp.max(part.reshape(TILE // 8, 8, QROWS), axis=0))
        top = jnp.max(top, axis=0, keepdims=True)
        total = jnp.zeros((8, QROWS), jnp.float32)
        for tile in range(tokens // TILE):
            at = slice(tile * TILE, (tile + 1) * TILE)
            part = jnp.exp(scores[side, at, :] - top)
            total = total + jnp.sum(part.reshape(TILE // 8, 8, QROWS), axis=0)
            weights[side, at, :] = part.astype(jnp.bfloat16)
        total = jnp.sum(total, axis=0, keepdims=True)
        lse_ref[0, side : side + 1, columns] = top + jnp.log(total)
        waiting.append((block, side, total))
        if index + 1 == len(steps):
            collect()


def attention_backward_kernel(
    early,
    tables_ref,
    boxes_ref,
    docs_ref,
    pads_ref,
    query_ref,
    key_ref,
    value_ref,
    grad_ref,
    exact_ref,
    lse_ref,
    down_ref,
    up_ref,
    part_out,
    grad_query_ref,
    grad_key_ref,
    grad_value_ref,
    diagonal_ref,
    down_landed,
    up_landed,
    other_out,
    info_ref,
    one_hot_x,
    query_base,
    key_base,
    pad_tiles,
    reverse,
    query_wide,
    key_wide,
    near,
    scores,
    grad_probs,
    probs_low,
    grad_low,
    key_turned,
    grad_near,
    grad_blocks,
    grad_key,
    grad_value,
    down_send,
    down_recv,
    up_send,
    up_recv,
    out_send,
    out_recv,
):
    pair = pl.program_id(0)
    tokens = query_ref.shape[0]
    down = Scatter(down_landed.shape[-1], 0, down_send, down_recv)
    up = Scatter(up_landed.shape[-1], 0, up_send, up_recv)

    @pl.when(pair == 0)
    def _():
        greet_partner()
        greet_rows((down.across_x, down.across_y))
        pl.semaphore_wait(pltpu.get_barrier_semaphore(), 3)
        down.send_first(down_ref, down_landed, early, down_landed.shape[1] - early)
        up.send_first(up_ref, up_landed, 0, up_landed.shape[1])
        partner_copy(part_out, other_out, out_send, out_recv).start()
        token_columns(boxes_ref, docs_ref, pads_ref, info_ref)
        token_lanes(info_ref, one_hot_x, query_base, key_base, pad_tiles)
        lane = lax.broadcasted_iota(jnp.int32, (TILE, 128), 1)
        for tile in range(tokens // TILE):
            at = slice(tile * TILE, (tile + 1) * TILE)
            left = info_ref[at, 0:1]
            top = info_ref[at, 1:2]
            reverse[at, :128] = jnp.where(lane == 127 - left, 1.0, 0.0).astype(jnp.bfloat16)
            reverse[at, 128:] = jnp.where(
                (lane == 31 - top) | (lane == FAR_LANE + tile), 1.0, 0.0
            ).astype(jnp.bfloat16)

    for side in range(2):
        widen_operands(
            side, pair * 2 + side, tables_ref, query_ref, key_ref, one_hot_x, query_base, key_base,
            query_wide, key_wide, near,
        )
        key_turned[side] = key_wide[side].T
    grad_near[...] = jnp.zeros_like(grad_near)
    grad_blocks[...] = jnp.zeros_like(grad_blocks)
    values = [
        own_half(side, value_ref[...], jnp.zeros(value_ref.shape, jnp.bfloat16)) for side in range(2)
    ]
    for block in range(tokens // QROWS):
        columns = slice(block * QROWS, (block + 1) * QROWS)
        grad_block = grad_ref[columns, :]
        product = grad_block.astype(jnp.float32).T * exact_ref[:, columns]
        scaled = (query_ref[columns, :].astype(jnp.float32) * HDIM ** (-0.5)).astype(jnp.bfloat16)
        turned = []
        key_terms = []
        value_terms = []
        for side in range(2):
            delta = jnp.sum(product[side * 64 : (side + 1) * 64, :], axis=0, keepdims=True)
            lse = lse_ref[0, side : side + 1, columns]
            scores[side] = dot_last(key_wide[side], query_wide[side, columns, :])
            grad_probs[side] = dot_last(values[side], grad_block)
            for tile in range(tokens // TILE):
                at = slice(tile * TILE, (tile + 1) * TILE)
                part = near_scores(scores[side, at, :], side, block, tile, near, pad_tiles)
                probs = jnp.exp(part - lse)
                grad_part = probs * (grad_probs[side, at, :] - delta)
                probs_low[side, at, :] = probs.astype(jnp.bfloat16)
                grad_low[side, at, :] = grad_part.astype(jnp.bfloat16)
                for half in range(QROWS // TILE):
                    gap = tile - (block * (QROWS // TILE) + half)
                    if abs(gap) <= 1:
                        grad_near[side, gap + 1] += grad_part[:, half * TILE : (half + 1) * TILE]
            value_terms.append(dot_plain(probs_low[side], grad_block))
            key_terms.append(dot_plain(grad_low[side], scaled))
            sums = dot_plain(key_turned[side], grad_low[side])
            turned.append(sums[side * 64 : (side + 1) * 64, :])
            grad_blocks[side] += dot_plain(sums.astype(jnp.bfloat16), reverse[columns, :])
        grad_query_ref[columns, :] = (
            (jnp.concatenate(turned, axis=0) * HDIM ** (-0.5)).T.astype(jnp.bfloat16)
        )
        key_term = own_half(0, key_terms[0], key_terms[1])
        value_term = own_half(0, value_terms[0], value_terms[1])
        if block == 0:
            grad_key[...] = key_term
            grad_value[...] = value_term
        else:
            grad_key[...] += key_term
            grad_value[...] += value_term
    grad_key_ref[...] = grad_key[...].astype(jnp.bfloat16)
    grad_value_ref[...] = grad_value[...].astype(jnp.bfloat16)
    row = lax.broadcasted_iota(jnp.int32, (128, 128), 0)
    lane = lax.broadcasted_iota(jnp.int32, (128, 128), 1)
    flip = jnp.where(row + lane == 127, 1.0, 0.0).astype(jnp.bfloat16)
    blank = jnp.zeros((128, 128), jnp.float32)

    def diagonal_sums(values):
        spread = jnp.concatenate([values, blank], axis=1)
        return jnp.sum(
            pltpu.roll(spread, 0, 1, stride=1, stride_axis=0), axis=0, keepdims=True
        )

    for side in range(2):
        misc = 64 * (1 - side)
        sums = [diagonal_sums(grad_blocks[side, 128:, :128])]
        below = grad_blocks[side, misc : misc + 64, 128:]
        small_row = lax.broadcasted_iota(jnp.int32, (64, 128), 0)
        small_lane = lax.broadcasted_iota(jnp.int32, (64, 128), 1)
        upright = jnp.where((small_row < FAR_LANE) & (small_lane < FAR_LANE), below, 0.0)
        sums.append(diagonal_sums(jnp.concatenate([upright, jnp.zeros((64, 128), jnp.float32)], axis=0)))
        for gap in range(3):
            tile = grad_near[side, gap]
            high = tile.astype(jnp.bfloat16)
            rest = (tile - high.astype(jnp.float32)).astype(jnp.bfloat16)
            sums.append(diagonal_sums(dot_plain(high, flip) + dot_plain(rest, flip)))
        gap = (small_row - FAR_LANE) - (small_lane - FAR_LANE)
        inside = (
            (small_row >= FAR_LANE)
            & (small_row < LOW_LANE)
            & (small_lane >= FAR_LANE)
            & (small_lane < LOW_LANE)
        )
        for chosen in (gap <= -2, gap >= 2):
            far = jnp.sum(jnp.where(inside & chosen, below, 0.0), axis=0, keepdims=True)
            sums.append(jnp.concatenate([far, blank[0:1]], axis=1))
        sums.append(jnp.zeros((1, 256), jnp.float32))
        diagonal_ref[side] = jnp.concatenate(sums, axis=0)

    @pl.when(pair == pl.num_programs(0) - 1)
    def _():
        late = down_landed.at[:, pl.ds(early, down_landed.shape[1] - early)]
        for scatter, landed in ((down, late), (up, up_landed)):
            scatter.await_first(landed)
            scatter.sent_first(landed)
        await_bytes(other_out, out_recv)
        await_bytes(other_out, out_send)


def attention_scratch(tokens):
    return [
        pltpu.VMEM((tokens, 8), jnp.int32),
        pltpu.VMEM((tokens, 128), jnp.bfloat16),
        pltpu.VMEM((tokens, 128), jnp.bfloat16),
        pltpu.VMEM((2, tokens, 128), jnp.bfloat16),
        pltpu.VMEM((tokens, 128), jnp.float32),
    ], [
        pltpu.VMEM((2, tokens, 256), jnp.bfloat16),
        pltpu.VMEM((2, tokens, 256), jnp.bfloat16),
        pltpu.VMEM((2, 3, TILE, TILE), jnp.float32),
        pltpu.VMEM((2, tokens, QROWS), jnp.float32),
    ]


def attention_forward(tables, places, heads):
    tokens, width = heads.shape[0], heads.shape[1] // 3
    pairs = width // 128
    own = pl.BlockSpec((tokens, 128), lambda pair: (0, pair))
    fixed, moving = attention_scratch(tokens)
    return pl.pallas_call(
        attention_forward_kernel,
        grid=(pairs,),
        out_shape=(
            jax.ShapeDtypeStruct((tokens, width), jnp.bfloat16),
            jax.ShapeDtypeStruct((width, tokens), jnp.float32),
            jax.ShapeDtypeStruct((pairs, 2, tokens), jnp.float32),
        ),
        in_specs=[
            pl.BlockSpec(memory_space=pltpu.SMEM),
            *[pl.BlockSpec(memory_space=pltpu.VMEM)] * 3,
            own,
            pl.BlockSpec((tokens, 128), lambda pair: (0, pairs + pair)),
            pl.BlockSpec((tokens, 128), lambda pair: (0, 2 * pairs + pair)),
        ],
        out_specs=(
            own,
            pl.BlockSpec((128, tokens), lambda pair: (pair, 0)),
            pl.BlockSpec((1, 2, tokens), lambda pair: (pair, 0, 0)),
        ),
        scratch_shapes=fixed
        + moving
        + [
            pltpu.VMEM((2, tokens, QROWS), jnp.bfloat16),
        ],
        compiler_params=pltpu.CompilerParams(
            dimension_semantics=("arbitrary",), vmem_limit_bytes=VMEM_LIMIT
        ),
        cost_estimate=pl.CostEstimate(
            flops=23 * 10**9, bytes_accessed=2 * 10**7, transcendentals=0
        ),
        name="attention_forward",
    )(tables, *places, heads, heads, heads)


def attention_backward(tables, places, heads, grad_context, exact, lse, down, up, part_out, early):
    tokens, width = grad_context.shape
    pairs = width // 128
    own = pl.BlockSpec((tokens, 128), lambda pair: (0, pair))
    fixed, moving = attention_scratch(tokens)
    low = jax.ShapeDtypeStruct((tokens, width), jnp.bfloat16)
    depths, _, _, rows, columns = down.shape
    return pl.pallas_call(
        functools.partial(attention_backward_kernel, early),
        grid=(pairs,),
        out_shape=(
            low,
            low,
            low,
            jax.ShapeDtypeStruct((2 * pairs, 8, 256), jnp.float32),
            jax.ShapeDtypeStruct((2, depths, 2, rows, columns // 2), jnp.float32),
            jax.ShapeDtypeStruct((2, depths // 2, 2, rows, columns // 4), jnp.float32),
            jax.ShapeDtypeStruct(part_out.shape, jnp.float32),
        ),
        in_specs=[
            pl.BlockSpec(memory_space=pltpu.SMEM),
            *[pl.BlockSpec(memory_space=pltpu.VMEM)] * 3,
            own,
            pl.BlockSpec((tokens, 128), lambda pair: (0, pairs + pair)),
            pl.BlockSpec((tokens, 128), lambda pair: (0, 2 * pairs + pair)),
            own,
            pl.BlockSpec((128, tokens), lambda pair: (pair, 0)),
            pl.BlockSpec((1, 2, tokens), lambda pair: (pair, 0, 0)),
            *[pl.BlockSpec(memory_space=pltpu.HBM)] * 3,
        ],
        out_specs=(
            own,
            own,
            own,
            pl.BlockSpec((2, 8, 256), lambda pair: (pair, 0, 0)),
            *[pl.BlockSpec(memory_space=pltpu.HBM)] * 3,
        ),
        scratch_shapes=fixed
        + [pltpu.VMEM((tokens, 256), jnp.bfloat16)]
        + moving
        + [
            pltpu.VMEM((2, tokens, QROWS), jnp.float32),
            pltpu.VMEM((2, tokens, QROWS), jnp.bfloat16),
            pltpu.VMEM((2, tokens, QROWS), jnp.bfloat16),
            pltpu.VMEM((2, 256, tokens), jnp.bfloat16),
            pltpu.VMEM((2, 3, TILE, TILE), jnp.float32),
            pltpu.VMEM((2, 256, 256), jnp.float32),
            pltpu.VMEM((tokens, 128), jnp.float32),
            pltpu.VMEM((tokens, 128), jnp.float32),
            *scatter_semaphores(2),
            *scatter_semaphores(2),
            pltpu.SemaphoreType.DMA,
            pltpu.SemaphoreType.DMA,
        ],
        compiler_params=pltpu.CompilerParams(
            dimension_semantics=("arbitrary",),
            collective_id=5,
            has_side_effects=True,
            vmem_limit_bytes=VMEM_LIMIT,
        ),
        cost_estimate=pl.CostEstimate(
            flops=30 * 10**9, bytes_accessed=2 * 10**7, transcendentals=0
        ),
        name="attention_backward",
    )(tables, *places, heads, heads, heads, grad_context, exact, lse, down, up, part_out)


def known_bucket(relative):
    magnitude = np.abs(relative)
    coarse = 8 + sum((magnitude >= edge).astype(int) for edge in bucket_edges)
    return np.where(magnitude < 8, magnitude, coarse) + np.where(relative > 0, 16, 0)


def bucket_grads(diagonals):
    lane = np.arange(256)
    far = np.zeros(256, int)
    wide_buckets = [
        known_bucket(lane - 127),
        known_bucket(lane - 31),
        known_bucket(lane - 127 - TILE),
        known_bucket(lane - 127),
        known_bucket(lane - 127 + TILE),
        far + NBUCKET // 2 - 1,
        far + NBUCKET - 1,
    ]
    table_of = (1, 2, 0, 0, 0, 0, 0)
    slots = np.stack([bucket + NBUCKET * table for bucket, table in zip(wide_buckets, table_of)])
    slots = jnp.asarray(slots, jnp.int32)
    chosen = (slots[..., None] == jnp.arange(3 * NBUCKET, dtype=jnp.int32)).astype(jnp.float32)
    return jnp.einsum("hrc,rcb->hb", diagonals[:, :7], chosen, precision=highest)


ROWS = 256
MIDDLE_ROWS = 256


def greet_partner():
    pl.semaphore_signal(
        pltpu.get_barrier_semaphore(),
        inc=1,
        device_id=(lax.axis_index("dp"), 1 - lax.axis_index("tensor")),
        device_id_type=MESH,
    )


def partner_copy(source, target, send_sem, recv_sem):
    return pltpu.make_async_remote_copy(
        src_ref=source,
        dst_ref=target,
        send_sem=send_sem,
        recv_sem=recv_sem,
        device_id=(lax.axis_index("dp"), 1 - lax.axis_index("tensor")),
        device_id_type=MESH,
    )


def dot_rows(left, right):
    return lax.dot_general(
        left, right, (((0,), (0,)), ((), ())), preferred_element_type=jnp.float32
    )


def inverse_rms(values):
    return lax.rsqrt(jnp.mean(values * values, axis=1, keepdims=True) + norm_eps)


def box_kernel(
    feature_ref,
    boxes_ref,
    docs_ref,
    pads_ref,
    embedded_ref,
    roi_ref,
    norm_ref,
    query_proj_ref,
    key_proj_ref,
    value_proj_ref,
    pooled_ref,
    stream_hbm,
    input_hbm,
    heads_hbm,
    stream_ref,
    input_ref,
    heads_ref,
    info_ref,
    features,
    mask,
    part,
    received,
    projections,
    send_sem,
    recv_sem,
    store_sem,
):
    greet_partner()
    token_columns(boxes_ref, docs_ref, pads_ref, info_ref)
    tokens = info_ref.shape[0]
    pixels = feature_ref.shape[0]
    tile_rows = pixels // 128
    first_row = lax.axis_index("tensor") * tile_rows
    features[...] = split_two(feature_ref[...])
    lane = lax.broadcasted_iota(jnp.int32, (ROWS, 128), 1)
    copies = []
    for block in range(tokens // ROWS):
        at = slice(block * ROWS, (block + 1) * ROWS)
        column = (lane >= info_ref[at, 0:1]) & (lane < info_ref[at, 4:5])
        column = jnp.where(column, 1.0, 0.0)
        top = jnp.broadcast_to(info_ref[at, 1:2], (ROWS, 128)) - first_row
        bottom = jnp.broadcast_to(info_ref[at, 5:6], (ROWS, 128)) - first_row
        for row in range(tile_rows):
            inside = jnp.where((top <= row) & (bottom > row), column, 0.0)
            mask[block % 2, :, row * 128 : (row + 1) * 128] = inside.astype(jnp.bfloat16)
        sums = dot_plain(mask[block % 2], features[...])
        part[at, :] = sums[:, :128] + sums[:, 128:]
        if block == 0:
            pl.semaphore_wait(pltpu.get_barrier_semaphore(), 1)
        copy = partner_copy(
            part.at[pl.ds(block * ROWS, ROWS)],
            received.at[pl.ds(block * ROWS, ROWS)],
            send_sem.at[block],
            recv_sem.at[block],
        )
        copy.start()
        copies.append(copy)
    stores = []
    width = query_proj_ref.shape[1]
    for index, ref in enumerate((query_proj_ref, key_proj_ref, value_proj_ref)):
        projections[:, index * width : (index + 1) * width] = ref[...]
    for block in range(tokens // ROWS):
        at = slice(block * ROWS, (block + 1) * ROWS)
        copies[block].wait_recv()
        area = (info_ref[at, 5:6] - info_ref[at, 1:2]) * (info_ref[at, 4:5] - info_ref[at, 0:1])
        pooled = ((part[at, :] + received[at, :]) / area.astype(jnp.float32)).astype(jnp.bfloat16)
        pooled_ref[at, :] = pooled
        stream = embedded_ref[at, :].astype(jnp.float32) + dot_plain(pooled, roi_ref[...])
        stream_ref[at, :] = stream
        attn_in = (stream * inverse_rms(stream) * norm_ref[...].reshape(1, -1)).astype(jnp.bfloat16)
        input_ref[at, :] = attn_in
        heads_ref[at, :] = dot_plain(attn_in, projections[...]).astype(jnp.bfloat16)
        rows = pl.ds(block * ROWS, ROWS)
        for index, (source, target) in enumerate(
            [(stream_ref, stream_hbm), (input_ref, input_hbm), (heads_ref, heads_hbm)]
        ):
            store = pltpu.make_async_copy(
                source.at[rows], target.at[rows], store_sem.at[index, block]
            )
            store.start()
            stores.append(store)
    for copy in copies:
        copy.wait_send()
    for store in stores:
        store.wait()


def box_forward(
    feature_map, places, embeddings, roi_proj, attn_norm, query_proj, key_proj, value_proj
):
    tokens, width = embeddings.shape
    local = query_proj.shape[1]
    blocks = tokens // ROWS
    whole = pl.BlockSpec(memory_space=pltpu.VMEM)
    far = pl.BlockSpec(memory_space=pltpu.HBM)
    return pl.pallas_call(
        box_kernel,
        out_shape=(
            jax.ShapeDtypeStruct((tokens, 128), jnp.bfloat16),
            jax.ShapeDtypeStruct((tokens, width), jnp.float32),
            jax.ShapeDtypeStruct((tokens, width), jnp.bfloat16),
            jax.ShapeDtypeStruct((tokens, 3 * local), jnp.bfloat16),
        ),
        in_specs=[whole] * 10,
        out_specs=(whole, far, far, far),
        scratch_shapes=[
            pltpu.VMEM((tokens, width), jnp.float32),
            pltpu.VMEM((tokens, width), jnp.bfloat16),
            pltpu.VMEM((tokens, 3 * local), jnp.bfloat16),
            pltpu.VMEM((tokens, 8), jnp.int32),
            pltpu.VMEM((feature_map.shape[0], 256), jnp.bfloat16),
            pltpu.VMEM((2, ROWS, feature_map.shape[0]), jnp.bfloat16),
            pltpu.VMEM((tokens, 128), jnp.float32),
            pltpu.VMEM((tokens, 128), jnp.float32),
            pltpu.VMEM((width, 3 * local), jnp.bfloat16),
            pltpu.SemaphoreType.DMA((blocks,)),
            pltpu.SemaphoreType.DMA((blocks,)),
            pltpu.SemaphoreType.DMA((3, blocks)),
        ],
        compiler_params=pltpu.CompilerParams(
            collective_id=2, has_side_effects=True, vmem_limit_bytes=VMEM_LIMIT
        ),
        cost_estimate=pl.CostEstimate(
            flops=12 * 10**9, bytes_accessed=2 * 10**7, transcendentals=0
        ),
        name="box_forward",
    )(
        feature_map,
        *places,
        embeddings,
        roi_proj,
        attn_norm,
        query_proj,
        key_proj,
        value_proj,
    )


def middle_kernel(
    early,
    context_ref,
    stream_hbm,
    cotangent_hbm,
    output_ref,
    norm_ref,
    up_hbm,
    down_hbm,
    middle_hbm,
    part_out_hbm,
    grad_middle_hbm,
    grad_context_hbm,
    grad_up_hbm,
    grad_down_hbm,
    early_hbm,
    grad_output_ref,
    grad_norm_ref,
    middle,
    cotangent,
    up,
    down,
    part,
    other,
    part_out,
    other_grad,
    ffn_in,
    hidden,
    grad_pre,
    staged,
    grad_low,
    grad_context,
    load_sem,
    store_sem,
    grad_sem,
    send_sem,
    recv_sem,
    early_send,
    early_recv,
):
    scatter = Scatter(early_hbm.shape[-1], 0, early_send, early_recv)
    greet_partner()
    greet_rows((scatter.across_x, scatter.across_y))
    norm = norm_ref[...].reshape(1, -1)
    tokens, width = stream_hbm.shape
    units = up_hbm.shape[1]
    blocks = tokens // MIDDLE_ROWS
    loads = [
        pltpu.make_async_copy(source, target, load_sem.at[index])
        for index, (source, target) in enumerate(
            [(cotangent_hbm, cotangent), (down_hbm, down), (stream_hbm, middle), (up_hbm, up)]
        )
    ]
    for load in loads:
        load.start()
    attn_copies = []
    for block in range(blocks):
        at = slice(block * MIDDLE_ROWS, (block + 1) * MIDDLE_ROWS)
        part[at, :] = dot_plain(context_ref[at, :], output_ref[...])
        if block == 0:
            pl.semaphore_wait(pltpu.get_barrier_semaphore(), 3)
        copy = partner_copy(
            part.at[pl.ds(block * MIDDLE_ROWS, MIDDLE_ROWS)],
            other.at[pl.ds(block * MIDDLE_ROWS, MIDDLE_ROWS)],
            send_sem.at[0, block],
            recv_sem.at[0, block],
        )
        copy.start()
        attn_copies.append(copy)
    for load in loads:
        load.wait()
    out_stores = []
    grad_copies = []
    for block in range(blocks):
        at = slice(block * MIDDLE_ROWS, (block + 1) * MIDDLE_ROWS)
        grad_hidden = dot_last(cotangent[at, :], down[...])
        attn_copies[block].wait()
        values = middle[at, :] + (part[at, :] + other[at, :])
        middle[at, :] = values
        inner = (values * inverse_rms(values) * norm).astype(jnp.bfloat16)
        ffn_in[at, :] = inner
        pre_act = dot_plain(inner, up[...])
        below = 0.5 * (1.0 + lax.erf(pre_act * (0.5**0.5)))
        density = jnp.exp(-0.5 * (pre_act * pre_act)) * 0.3989422804014327
        hidden[at, :] = (pre_act * below).astype(jnp.bfloat16)
        grad_pre[at, :] = (grad_hidden * (below + pre_act * density)).astype(jnp.bfloat16)
        part[at, :] = dot_last(grad_pre[at, :], up[...])
        copy = partner_copy(
            part.at[pl.ds(block * MIDDLE_ROWS, MIDDLE_ROWS)],
            other_grad.at[pl.ds(block * MIDDLE_ROWS, MIDDLE_ROWS)],
            send_sem.at[1, block],
            recv_sem.at[1, block],
        )
        copy.start()
        grad_copies.append(copy)
        part_out[at, :] = dot_plain(hidden[at, :], down[...])
        for index, (source, target) in enumerate([(middle, middle_hbm), (part_out, part_out_hbm)]):
            rows = pl.ds(block * MIDDLE_ROWS, MIDDLE_ROWS)
            store = pltpu.make_async_copy(
                source.at[rows], target.at[rows], store_sem.at[2 + index, block]
            )
            store.start()
            out_stores.append(store)
    half = width // 2
    stores = []
    for index, slot in enumerate((0, 1, 2, 1)):
        rows = slice((index % 2) * half, (index % 2 + 1) * half)
        if index == 3:
            stores[1].wait()
        if index < 2:
            staged[slot] = dot_rows(cotangent[:, rows], hidden[...])
            target = grad_down_hbm
        else:
            staged[slot] = dot_rows(ffn_in[:, rows], grad_pre[...])
            target = grad_up_hbm
        store = pltpu.make_async_copy(
            staged.at[slot], target.at[pl.ds((index % 2) * half, half)], grad_sem.at[index]
        )
        store.start()
        stores.append(store)
        if index == 0:
            size = early_hbm.shape[3]
            columns = scatter.columns(grad_down_hbm)
            for depth in range(early):
                for other_place in range(2):
                    for side, begin, partner in (
                        (0, 2 * other_place + 1 - scatter.x, scatter.across_x),
                        (1, 2 * (1 - scatter.y) + other_place, scatter.across_y),
                    ):
                        begin = pl.multiple_of((depth * 4 + begin) * size, 8)
                        start_remote(
                            staged.at[0, pl.ds(begin, size), columns[side]],
                            early_hbm.at[side, depth, other_place],
                            early_send.at[side],
                            early_recv.at[side],
                            partner,
                        )
    norm_total = jnp.zeros((8, width), jnp.float32)
    for block in range(blocks):
        at = slice(block * MIDDLE_ROWS, (block + 1) * MIDDLE_ROWS)
        values = middle[at, :]
        inverse = inverse_rms(values)
        hat = values * inverse
        grad_copies[block].wait()
        grad_inner = part[at, :] + other_grad[at, :]
        norm_total = norm_total + jnp.sum((grad_inner * hat).reshape(MIDDLE_ROWS // 8, 8, width), axis=0)
        scaled = grad_inner * norm
        back = inverse * (scaled - hat * jnp.mean(scaled * hat, axis=1, keepdims=True))
        grad_values = cotangent[at, :].astype(jnp.float32) + back
        out_stores[2 * block].wait()
        middle[at, :] = grad_values
        low = grad_values.astype(jnp.bfloat16)
        grad_low[at, :] = low
        grad_context[at, :] = dot_last(low, output_ref[...]).astype(jnp.bfloat16)
        for index, (source, target) in enumerate(
            [
                (middle, grad_middle_hbm),
                (grad_context, grad_context_hbm),
            ]
        ):
            rows = pl.ds(block * MIDDLE_ROWS, MIDDLE_ROWS)
            store = pltpu.make_async_copy(
                source.at[rows], target.at[rows], store_sem.at[index, block]
            )
            store.start()
            stores.append(store)
    grad_norm_ref[...] = jnp.sum(norm_total, axis=0, keepdims=True)
    grad_output_ref[...] = dot_rows(grad_low[...], context_ref[...])
    del stores[1]
    for store in stores + out_stores[1::2]:
        store.wait()
    if early:
        scatter.await_first(early_hbm)
        scatter.sent_first(early_hbm)


def middle_layer(
    context, stream, cotangent, output_proj, ffn_norm, up_proj, down_proj, depths, own_rows, early
):
    tokens, width = stream.shape
    units = up_proj.shape[1]
    local = context.shape[1]
    blocks = tokens // MIDDLE_ROWS
    whole = pl.BlockSpec(memory_space=pltpu.VMEM)
    far = pl.BlockSpec(memory_space=pl.ANY)
    wide_sum = pltpu.VMEM((tokens, width), jnp.float32)
    wide_low = pltpu.VMEM((tokens, width), jnp.bfloat16)
    unit_low = pltpu.VMEM((tokens, units), jnp.bfloat16)
    return pl.pallas_call(
        functools.partial(middle_kernel, early),
        out_shape=(
            jax.ShapeDtypeStruct((tokens, width), jnp.float32),
            jax.ShapeDtypeStruct((tokens, width), jnp.float32),
            jax.ShapeDtypeStruct((tokens, width), jnp.float32),
            jax.ShapeDtypeStruct((tokens, local), jnp.bfloat16),
            jax.ShapeDtypeStruct((width, units), jnp.float32),
            jax.ShapeDtypeStruct((width, units), jnp.float32),
            jax.ShapeDtypeStruct((2, max(early, 1), 2, own_rows, units // 2), jnp.float32),
            jax.ShapeDtypeStruct((width, local), jnp.float32),
            jax.ShapeDtypeStruct((1, width), jnp.float32),
        ),
        in_specs=[whole, far, far, whole, whole, far, far],
        out_specs=(far,) * 7 + (whole, whole),
        scratch_shapes=[
            wide_sum,
            wide_low,
            pltpu.VMEM((width, units), jnp.bfloat16),
            pltpu.VMEM((units, width), jnp.bfloat16),
            wide_sum,
            wide_sum,
            wide_sum,
            wide_sum,
            wide_low,
            unit_low,
            unit_low,
            pltpu.VMEM((3, width // 2, units), jnp.float32),
            wide_low,
            pltpu.VMEM((tokens, local), jnp.bfloat16),
            pltpu.SemaphoreType.DMA((4,)),
            pltpu.SemaphoreType.DMA((4, blocks)),
            pltpu.SemaphoreType.DMA((4,)),
            pltpu.SemaphoreType.DMA((2, blocks)),
            pltpu.SemaphoreType.DMA((2, blocks)),
            *scatter_semaphores(2),
        ],
        compiler_params=pltpu.CompilerParams(
            collective_id=3, has_side_effects=True, vmem_limit_bytes=VMEM_LIMIT
        ),
        cost_estimate=pl.CostEstimate(
            flops=32 * 10**9, bytes_accessed=2 * 10**7, transcendentals=0
        ),
        name="middle_layer",
    )(context, stream, cotangent, output_proj, ffn_norm, up_proj, down_proj)


def end_kernel(
    early,
    grad_query_ref,
    grad_key_ref,
    grad_value_ref,
    query_proj_ref,
    key_proj_ref,
    value_proj_ref,
    input_ref,
    stream_hbm,
    grad_middle_hbm,
    norm_ref,
    roi_ref,
    pooled_ref,
    boxes_ref,
    docs_ref,
    pads_ref,
    grad_output_ref,
    down_hbm,
    early_hbm,
    landed_hbm,
    middle_hbm,
    part_out_hbm,
    other_out_hbm,
    grad_stream_hbm,
    grad_heads_hbm,
    kept_hbm,
    second_hbm,
    layer_hbm,
    grad_roi_ref,
    grad_map_ref,
    grad_norm_ref,
    info_ref,
    grad_heads,
    projections,
    stream,
    grad_stream,
    part,
    other,
    weight_grad,
    grad_low,
    grad_box,
    first,
    landed,
    middle,
    part_out,
    other_out,
    layer_low,
    attn_in,
    operand_sem,
    load_sem,
    store_sem,
    grad_sem,
    send_sem,
    recv_sem,
    scatter_sem,
    scatter_send,
    scatter_recv,
):
    tokens, width = stream_hbm.shape
    local = grad_query_ref.shape[1]
    blocks = tokens // ROWS
    scatter = Scatter(first.shape[-1], 0, scatter_send, scatter_recv)
    greet_partner()
    norm = norm_ref[...].reshape(1, -1)
    greet_rows((scatter.across_x, scatter.across_y))
    operand_loads = []
    for index, (grad, proj) in enumerate(
        (
            (grad_query_ref, query_proj_ref),
            (grad_key_ref, key_proj_ref),
            (grad_value_ref, value_proj_ref),
        )
    ):
        columns = pl.ds(index * local, local)
        operand_loads.append(
            pltpu.make_async_copy(grad, grad_heads.at[:, columns], operand_sem.at[2 * index])
        )
        operand_loads.append(
            pltpu.make_async_copy(proj, projections.at[:, columns], operand_sem.at[2 * index + 1])
        )
    operand_loads.append(pltpu.make_async_copy(input_ref, attn_in, operand_sem.at[6]))
    first_loads = scatter.own_loads(down_hbm, first, scatter_sem)
    late = pl.ds(early, landed.shape[1] - early)
    first_loads.append(
        pltpu.make_async_copy(landed_hbm.at[:, late], landed.at[:, late], scatter_sem.at[2])
    )
    if early:
        first_loads.append(
            pltpu.make_async_copy(early_hbm, landed.at[:, pl.ds(0, early)], scatter_sem.at[3])
        )
    for load in first_loads + operand_loads:
        load.start()
    loads = [
        pltpu.make_async_copy(stream_hbm, stream, load_sem.at[0]),
        pltpu.make_async_copy(grad_middle_hbm, grad_stream, load_sem.at[1]),
    ]
    for load in loads:
        load.start()
    for load in first_loads:
        load.wait()
    add_pairs(first, landed)
    pl.semaphore_wait(pltpu.get_barrier_semaphore(), 3)
    scatter.send_second(first, second_hbm)
    kept_stores = [
        pltpu.make_async_copy(first.at[0, :, scatter.y], kept_hbm.at[0], scatter_sem.at[0]),
        pltpu.make_async_copy(first.at[1, :, scatter.x], kept_hbm.at[1], scatter_sem.at[1]),
    ]
    for store in kept_stores:
        store.start()
    token_columns(boxes_ref, docs_ref, pads_ref, info_ref)
    for load in operand_loads:
        load.wait()
    copies = []
    for block in range(blocks):
        at = slice(block * ROWS, (block + 1) * ROWS)
        part[at, :] = dot_last(grad_heads[at, :], projections[...])
        copy = partner_copy(
            part.at[pl.ds(block * ROWS, ROWS)],
            other.at[pl.ds(block * ROWS, ROWS)],
            send_sem.at[block],
            recv_sem.at[block],
        )
        copy.start()
        copies.append(copy)
    out_loads = [
        pltpu.make_async_copy(source, target, load_sem.at[2 + index])
        for index, (source, target) in enumerate(
            [(middle_hbm, middle), (part_out_hbm, part_out), (other_out_hbm, other_out)]
        )
    ]
    for load in out_loads:
        load.start()

    def add_weights(index):
        columns = slice(index * local, (index + 1) * local)
        weight_grad[:, columns] = dot_rows(attn_in[...], grad_heads[:, columns])

    add_weights(0)
    weight_grad[:, 3 * local :] = grad_output_ref[...]
    weight_store = pltpu.make_async_copy(weight_grad, grad_heads_hbm, grad_sem)
    for load in loads:
        load.wait()
    stores = []
    norm_total = jnp.zeros((8, width), jnp.float32)
    for block in range(blocks):
        at = slice(block * ROWS, (block + 1) * ROWS)
        values = stream[at, :]
        inverse = inverse_rms(values)
        hat = values * inverse
        if block in (1, 2):
            add_weights(block)
        if block == 2:
            weight_store.start()
        copies[block].wait()
        grad_inner = part[at, :] + other[at, :]
        norm_total = norm_total + jnp.sum((grad_inner * hat).reshape(ROWS // 8, 8, width), axis=0)
        scaled = grad_inner * norm
        back = inverse * (scaled - hat * jnp.mean(scaled * hat, axis=1, keepdims=True))
        grad_values = grad_stream[at, :] + back
        grad_stream[at, :] = grad_values
        rows = pl.ds(block * ROWS, ROWS)
        store = pltpu.make_async_copy(
            grad_stream.at[rows], grad_stream_hbm.at[rows], store_sem.at[block]
        )
        store.start()
        stores.append(store)
        low = grad_values.astype(jnp.bfloat16)
        grad_low[at, :] = low
        area = (info_ref[at, 5:6] - info_ref[at, 1:2]) * (info_ref[at, 4:5] - info_ref[at, 0:1])
        grad_box[at, :] = split_two(dot_last(low, roi_ref[...]) / area.astype(jnp.float32))
    grad_norm_ref[...] = jnp.sum(norm_total, axis=0, keepdims=True)
    for load in out_loads:
        load.wait()
    layer_store = pltpu.make_async_copy(layer_low, layer_hbm, load_sem.at[2])
    tile_rows = grad_map_ref.shape[0] // 128
    first_row = lax.axis_index("tensor") * tile_rows
    column = lax.broadcasted_iota(jnp.int32, (128, tokens), 0)
    inside = jnp.where(
        (column >= boxes_ref[0]) & (column < boxes_ref[2]), 1.0, 0.0
    ).astype(jnp.bfloat16)
    top = boxes_ref[1] - first_row
    bottom = boxes_ref[3] - first_row
    for row in range(tile_rows):
        if row < 2 * blocks:
            at = slice(row * ROWS // 2, (row + 1) * ROWS // 2)
            layer_low[at, :] = (middle[at, :] + (part_out[at, :] + other_out[at, :])).astype(
                jnp.bfloat16
            )
        if row == 2 * blocks:
            layer_store.start()
        chosen = jnp.where((top <= row) & (bottom > row), 1.0, 0.0).astype(jnp.bfloat16)
        sums = dot_plain(inside * chosen, grad_box[...])
        grad_map_ref[row * 128 : (row + 1) * 128, :] = sums[:, :128] + sums[:, 128:]
    grad_roi_ref[...] = dot_rows(grad_low[...], pooled_ref[...])
    layer_store.wait()
    for store in kept_stores:
        store.wait()
    scatter.await_second(second_hbm)
    scatter.sent_second(second_hbm)
    weight_store.wait()
    for store in stores:
        store.wait()


def end_layer(
    grad_heads,
    projections,
    attn_in,
    stream,
    grad_middle,
    attn_norm,
    roi_proj,
    pooled,
    places,
    grad_output,
    down,
    landed,
    early_landed,
    outs,
    pixels,
    early,
):
    tokens, width = stream.shape
    local = grad_heads[0].shape[1]
    blocks = tokens // ROWS
    whole = pl.BlockSpec(memory_space=pltpu.VMEM)
    far = pl.BlockSpec(memory_space=pltpu.HBM)
    wide_sum = pltpu.VMEM((tokens, width), jnp.float32)
    _, depths, _, rows, half = landed.shape
    return pl.pallas_call(
        functools.partial(end_kernel, early),
        out_shape=(
            jax.ShapeDtypeStruct((tokens, width), jnp.float32),
            jax.ShapeDtypeStruct((width, 4 * local), jnp.float32),
            jax.ShapeDtypeStruct((2, depths, rows, half), jnp.float32),
            jax.ShapeDtypeStruct((2, depths, rows, half), jnp.float32),
            jax.ShapeDtypeStruct((tokens, width), jnp.bfloat16),
            jax.ShapeDtypeStruct((width, 128), jnp.float32),
            jax.ShapeDtypeStruct((pixels, 128), jnp.float32),
            jax.ShapeDtypeStruct((1, width), jnp.float32),
        ),
        in_specs=[far] * 9 + [whole] * 7 + [far] * 6,
        out_specs=(far,) * 5 + (whole,) * 3,
        scratch_shapes=[
            pltpu.VMEM((tokens, 8), jnp.int32),
            pltpu.VMEM((tokens, 3 * local), jnp.bfloat16),
            pltpu.VMEM((width, 3 * local), jnp.bfloat16),
            wide_sum,
            wide_sum,
            wide_sum,
            wide_sum,
            pltpu.VMEM((width, 4 * local), jnp.float32),
            pltpu.VMEM((tokens, width), jnp.bfloat16),
            pltpu.VMEM((tokens, 256), jnp.bfloat16),
            pltpu.VMEM(landed.shape, jnp.float32),
            pltpu.VMEM(landed.shape, jnp.float32),
            wide_sum,
            wide_sum,
            wide_sum,
            pltpu.VMEM((tokens, width), jnp.bfloat16),
            pltpu.VMEM((tokens, width), jnp.bfloat16),
            pltpu.SemaphoreType.DMA((7,)),
            pltpu.SemaphoreType.DMA((5,)),
            pltpu.SemaphoreType.DMA((blocks,)),
            pltpu.SemaphoreType.DMA,
            pltpu.SemaphoreType.DMA((blocks,)),
            pltpu.SemaphoreType.DMA((blocks,)),
            pltpu.SemaphoreType.DMA((4,)),
            *scatter_semaphores(4),
        ],
        compiler_params=pltpu.CompilerParams(
            collective_id=4, has_side_effects=True, vmem_limit_bytes=VMEM_LIMIT
        ),
        cost_estimate=pl.CostEstimate(
            flops=15 * 10**9, bytes_accessed=2 * 10**7, transcendentals=0
        ),
        name="end_layer",
    )(
        *grad_heads,
        *projections,
        attn_in,
        stream,
        grad_middle,
        attn_norm,
        roi_proj,
        pooled,
        *places,
        grad_output,
        down,
        early_landed,
        landed,
        *outs,
    )


def unpack_kernel(
    places,
    sums_ref,
    own_ref,
    layer_in,
    stream_in,
    layer_out,
    stream_out,
    first_out,
    convs_out,
    gain_out,
    shift_out,
    roi_out,
    attn_norm_out,
    query_out,
    key_out,
    value_out,
    output_out,
    tables_out,
    ffn_norm_out,
    up_out,
    down_out,
    layer_kept,
    stream_kept,
    sem,
):
    loads = []
    copies = []
    count = sem.shape[1]
    for index, (source, kept, target) in enumerate(
        [(stream_in, stream_kept, stream_out), (layer_in, layer_kept, layer_out)]
    ):
        size = source.shape[0] // count
        for part in range(count):
            rows = pl.ds(part * size, size)
            loads.append(
                pltpu.make_async_copy(source.at[rows], kept.at[rows], sem.at[index, part])
            )
            copies.append(
                pltpu.make_async_copy(kept.at[rows], target.at[rows], sem.at[index, part])
            )
    for load in loads:
        load.start()
    for load, copy in zip(loads, copies):
        load.wait()
        copy.start()
    for target, begin in places:
        if target == "first":
            first_out[...] = sums_ref[begin : begin + first_out.shape[0], :]
        if target == "gain":
            gain_out[...] = sums_ref[begin : begin + LAYERS, :]
        if target == "shift":
            shift_out[...] = sums_ref[begin : begin + LAYERS, :]
        if target == "roi":
            roi_out[...] = sums_ref[begin : begin + roi_out.shape[0], :]
        if target == "small":
            attn_norm_out[...] = sums_ref[begin : begin + 1, : attn_norm_out.shape[1]]
            ffn_norm_out[...] = sums_ref[begin + 1 : begin + 2, : ffn_norm_out.shape[1]]
            for table in range(3):
                tables_out[table] = sums_ref[
                    begin + 2 : begin + 2 + tables_out.shape[1],
                    table * NBUCKET : (table + 1) * NBUCKET,
                ]
    for level in range(8):
        convs_out[level] = sums_ref[level * 128 : (level + 1) * 128, :]
    up_out[...] = own_ref[0]
    down_out[...] = own_ref[2]
    part = query_out.shape[1]
    for index, target in enumerate((query_out, key_out, value_out, output_out)):
        target[...] = own_ref[1, :, index * part : (index + 1) * part]
    for copy in copies:
        copy.wait()


def unpack(sums, own, layer_out, grad_stream, planes, heads):
    _, own_rows, columns = own.shape
    whole = pl.BlockSpec(memory_space=pltpu.VMEM)
    far = pl.BlockSpec(memory_space=pl.ANY)
    places = (("first", 1024), ("gain", 1032), ("shift", 1048), ("small", 1064), ("roi", 1072))

    def sized(*shape):
        return jax.ShapeDtypeStruct(shape, jnp.float32)

    return pl.pallas_call(
        functools.partial(unpack_kernel, places),
        out_shape=(
            jax.ShapeDtypeStruct(layer_out.shape, layer_out.dtype),
            jax.ShapeDtypeStruct(grad_stream.shape, grad_stream.dtype),
            sized(planes, 128),
            sized(8, 128, 128),
            sized(LAYERS, 128),
            sized(LAYERS, 128),
            sized(own_rows, 128),
            sized(1, own_rows),
            *[sized(own_rows, columns // 4)] * 4,
            sized(3, heads, NBUCKET),
            sized(1, own_rows),
            sized(own_rows, columns),
            sized(own_rows, columns),
        ),
        in_specs=[whole, whole, far, far],
        out_specs=(far, far) + (whole,) * 14,
        scratch_shapes=[
            pltpu.VMEM(layer_out.shape, layer_out.dtype),
            pltpu.VMEM(grad_stream.shape, grad_stream.dtype),
            pltpu.SemaphoreType.DMA((2, 4)),
        ],
        compiler_params=pltpu.CompilerParams(vmem_limit_bytes=VMEM_LIMIT),
        name="unpack",
    )(sums, own, layer_out, grad_stream)


def on_device(
    page_image,
    embeddings,
    cotangent,
    doc_ids,
    pad_mask,
    token_boxes,
    conv_first,
    conv_weights,
    group_gain,
    group_shift,
    roi_proj,
    attn_norm,
    query_proj,
    key_proj,
    value_proj,
    output_proj,
    bias_tables,
    ffn_norm,
    up_proj,
    down_proj,
):
    devices = lax.axis_size("dp") * lax.axis_size("tensor")
    feature_map, *records = stem_forward(
        page_image, conv_first, conv_weights, group_gain, group_shift, devices
    )
    places = (token_boxes, doc_ids, pad_mask)
    tables = bias_tables.swapaxes(1, 2)
    pooled, stream, attn_in, heads = box_forward(
        feature_map, places, embeddings, roi_proj, attn_norm, query_proj, key_proj, value_proj
    )
    context, exact, lse = attention_forward(tables, places, heads)
    rows_count = lax.axis_size("dp")
    width = stream.shape[1]
    own_rows = width // rows_count
    depths = rows_count // 4
    early = depths // 4 if own_rows % 8 == 0 else 0
    (
        middle,
        part_out,
        grad_middle,
        grad_context,
        grad_up,
        grad_down,
        early_landed,
        grad_output,
        grad_ffn_norm,
    ) = middle_layer(
        context,
        stream,
        cotangent,
        output_proj,
        ffn_norm,
        up_proj,
        down_proj,
        depths,
        own_rows,
        early,
    )

    def by_place(values):
        return values.reshape(depths, 2, 2, own_rows, values.shape[1])

    down, up = by_place(grad_down), by_place(grad_up)
    *grad_heads, diagonals, landed, up_landed, other_out = attention_backward(
        tables, places, heads, grad_context, exact, lse, down, up, part_out, early
    )
    grad_tables = bucket_grads(diagonals)
    grad_stream, grad_attn, kept, second, layer_out, grad_roi, grad_map, grad_attn_norm = end_layer(
        grad_heads,
        (query_proj, key_proj, value_proj),
        attn_in,
        stream,
        grad_middle,
        attn_norm,
        roi_proj,
        pooled,
        places,
        grad_output,
        down,
        landed,
        early_landed,
        (middle, part_out, other_out),
        feature_map.shape[0],
        early,
    )
    local_heads = grad_tables.shape[0]
    split = grad_roi.reshape(rows_count, 2, own_rows // 2, grad_roi.shape[1])
    sums, own = stem_backward(
        grad_map,
        page_image,
        records,
        conv_weights,
        group_gain,
        group_shift,
        split,
        (grad_attn_norm, grad_ffn_norm),
        grad_tables,
        up,
        by_place(grad_attn),
        kept,
        second,
        up_landed,
        devices,
    )
    outs = list(
        unpack(sums, own, layer_out, grad_stream, conv_first.shape[0], local_heads)
    )
    outs[6] = outs[6].T
    outs[7] = outs[7][0]
    outs[11] = outs[11].T
    outs[12] = outs[12].swapaxes(1, 2)
    outs[13] = outs[13][0]
    outs[15] = outs[15].T
    return tuple(outs)


def solution(mesh):
    placed = (
        P(None, ("dp", "tensor"), None),
        P("dp", None),
        P("dp", None),
        P("dp", None),
        P("dp", None),
        P(None, "dp", None),
        P(),
        P(),
        P(),
        P(),
        P(),
        P(),
        P(None, "tensor"),
        P(None, "tensor"),
        P(None, "tensor"),
        P("tensor", None),
        P(None, None, "tensor"),
        P(),
        P(None, "tensor"),
        P("tensor", None),
    )
    return jax.shard_map(
        on_device,
        mesh=mesh,
        in_specs=placed,
        out_specs=(
            P("dp", None),
            P("dp", None),
            P(),
            P(),
            P(),
            P(),
            P(None, "dp"),
            P("dp"),
            P("dp", "tensor"),
            P("dp", "tensor"),
            P("dp", "tensor"),
            P("tensor", "dp"),
            P(None, None, "tensor"),
            P("dp"),
            P("dp", "tensor"),
            P("tensor", "dp"),
        ),
        check_vma=False,
    )
```

```python
import functools

import jax
import jax.numpy as jnp
import numpy as np
from jax import lax
from jax.experimental import pallas as pl
from jax.experimental.pallas import tpu as pltpu
from jax.sharding import PartitionSpec as P

HDIM = 64
NBUCKET = 32
VMEM_LIMIT = 63 * 2**20
GROUPS = 32


bucket_edges = (12, 16, 23, 32, 46, 64, 91)
norm_eps = 1e-06
group_eps = 1e-05
masked_score = -1e30
highest = lax.Precision.HIGHEST


def bucket_of(relative):
    magnitude = jnp.abs(relative)
    coarse = jnp.full(relative.shape, 8, jnp.int32)
    for edge in bucket_edges:
        coarse = coarse + (magnitude >= edge).astype(jnp.int32)
    return jnp.where(magnitude < 8, magnitude, coarse) + jnp.where(relative > 0, 16, 0).astype(
        jnp.int32
    )


MESH = pl.DeviceIdType.MESH
LAYERS = 9
PIX_CHUNK = 256


def level_of(layer):
    return layer if layer <= 4 else 8 - layer


def stem_rows(pixels):
    return [pixels >> (2 * level_of(layer)) for layer in range(LAYERS)]


def row_starts(rows):
    starts = [0]
    for count in rows:
        starts.append(starts[-1] + count)
    return starts


def split_two(values):
    high = values.astype(jnp.bfloat16)
    low = (values - high.astype(jnp.float32)).astype(jnp.bfloat16)
    return jnp.concatenate([high, low], axis=1)


def group_sum(values):
    lane = lax.broadcasted_iota(jnp.int32, values.shape, 1)
    pairs = values + jnp.where(
        lane % 2 == 0, pltpu.roll(values, 127, 1), pltpu.roll(values, 1, 1)
    )
    return pairs + jnp.where(
        (lane // 2) % 2 == 0, pltpu.roll(pairs, 126, 1), pltpu.roll(pairs, 2, 1)
    )


def wide(row):
    return jnp.broadcast_to(row, (8, row.shape[1]))


def my_index():
    return lax.axis_index("dp") * 2 + lax.axis_index("tensor")


def greet_all(count):
    barrier = pltpu.get_barrier_semaphore()
    me = my_index()

    def greet(step, carry):
        other = lax.rem(me + step, count)
        pl.semaphore_signal(
            barrier, inc=1, device_id=(other // 2, lax.rem(other, 2)), device_id_type=MESH
        )
        return carry

    lax.fori_loop(1, count, greet, 0)


def greeted(count):
    pl.semaphore_wait(pltpu.get_barrier_semaphore(), count - 1)


def send_all(count, source, target, send_sem, recv_sem):
    me = my_index()

    def send(step, carry):
        other = lax.rem(me + step, count)
        pltpu.make_async_remote_copy(
            src_ref=source,
            dst_ref=target,
            send_sem=send_sem,
            recv_sem=recv_sem,
            device_id=(other // 2, lax.rem(other, 2)),
            device_id_type=MESH,
        ).start()
        return carry

    lax.fori_loop(1, count, send, 0, unroll=count <= 32)


def wait_all(count, slots, sem):
    part = slots.at[pl.ds(0, count - 1)]
    pltpu.make_async_copy(part, part, sem).wait()


def natural_places(tile_rows, columns):
    spacing = columns // 8
    places = []
    for row in range(tile_rows):
        for col in range(spacing):
            place = 0
            for bit in range(4):
                place = place * 4 + ((row >> bit) & 1) * 2 + ((col >> bit) & 1)
            places.append((row * columns + col, place * 8))
    return places


SCHEDULE = {
    'start': 'small split',
    8: 'u1b d3a v1a',
    7: 'v1b d3b e3a',
    6: 'u2',
    5: 'a1a e3b',
    4: 'v2',
    3: 'a1b u3a rows',
    2: 'b1a u3b v3a',
    1: 'b1b a2 v3b kept',
    0: 'a3a b2',
    'end': 'a3b',
    'last': 'b3a b3b',
}


def place_of(row):
    return row // 4, lax.rem(row // 2, 2), lax.rem(row, 2)


def start_remote(source, target, send_sem, recv_sem, row):
    pltpu.make_async_remote_copy(
        src_ref=source,
        dst_ref=target,
        send_sem=send_sem,
        recv_sem=recv_sem,
        device_id=(row, lax.axis_index("tensor")),
        device_id_type=MESH,
    ).start()


def await_bytes(buffer, sem):
    pltpu.make_async_copy(buffer, buffer, sem).wait()


def greet_rows(rows):
    for row in rows:
        pl.semaphore_signal(
            pltpu.get_barrier_semaphore(),
            inc=1,
            device_id=(row, lax.axis_index("tensor")),
            device_id_type=MESH,
        )


class Scatter:
    def __init__(self, width, left, send_sem, recv_sem):
        self.row = lax.axis_index("dp")
        self.z, self.y, self.x = place_of(self.row)
        self.across_x = self.row + 1 - 2 * self.x
        self.across_y = self.row + 2 - 4 * self.y
        self.width, self.left = width, left
        self.send_sem, self.recv_sem = send_sem, recv_sem

    def columns(self, source):
        half = source.shape[-1] // 2
        return pl.ds(self.left, self.width), pl.ds(half + self.left, self.width)

    def own_loads(self, source, own, sem):
        first, second = self.columns(source)
        return [
            pltpu.make_async_copy(source.at[:, :, self.x, :, first], own.at[0], sem.at[0]),
            pltpu.make_async_copy(source.at[:, self.y, :, :, second], own.at[1], sem.at[1]),
        ]

    def send_first(self, source, target, begin, size, shift=0):
        first, second = self.columns(source)
        depth = pl.ds(begin, size)
        landing = pl.ds(begin - shift, size)
        start_remote(
            source.at[depth, :, 1 - self.x, :, first],
            target.at[0, landing],
            self.send_sem.at[0],
            self.recv_sem.at[0],
            self.across_x,
        )
        start_remote(
            source.at[depth, 1 - self.y, :, :, second],
            target.at[1, landing],
            self.send_sem.at[1],
            self.recv_sem.at[1],
            self.across_y,
        )

    def await_first(self, landed):
        for side in range(2):
            await_bytes(landed.at[side], self.recv_sem.at[side])

    def sent_first(self, landed):
        for side in range(2):
            await_bytes(landed.at[side], self.send_sem.at[side])

    def send_second(self, source, target):
        start_remote(
            source.at[0, :, 1 - self.y],
            target.at[0],
            self.send_sem.at[2],
            self.recv_sem.at[2],
            self.across_y,
        )
        start_remote(
            source.at[1, :, 1 - self.x],
            target.at[1],
            self.send_sem.at[3],
            self.recv_sem.at[3],
            self.across_x,
        )

    def await_second(self, landed):
        for side in range(2):
            await_bytes(landed.at[side], self.recv_sem.at[2 + side])

    def sent_second(self, landed):
        for side in range(2):
            await_bytes(landed.at[side], self.send_sem.at[2 + side])

    def along_z(self, total, target, step):
        depths = total.shape[1]
        begins = [0]
        for index in range(step):
            begins.append(begins[-1] + (depths >> (index + 1)))
        bit = lax.rem(self.z // (1 << step), 2)
        if step == 0:
            return total, 0, begins[0], depths >> 1, bit
        return target, begins[step - 1], begins[step], depths >> (step + 1), bit

    def send_along(self, total, target, step):
        source, begin, landing, blocks, bit = self.along_z(total, target, step)
        other = self.row + (1 - 2 * bit) * (4 << step)
        for block in range(blocks):
            start_remote(
                source.at[:, begin + 2 * block + 1 - bit],
                target.at[:, landing + block],
                self.send_sem.at[4 + step],
                self.recv_sem.at[4 + step],
                other,
            )

    def add_along(self, total, target, step):
        source, begin, landing, blocks, bit = self.along_z(total, target, step)
        await_bytes(target.at[:, pl.ds(landing, blocks)], self.recv_sem.at[4 + step])
        for side in range(2):
            for block in range(blocks):
                target[side, landing + block] = (
                    target[side, landing + block] + source[side, begin + 2 * block + bit]
                )

    def finish(self, total, target, result, base, step):
        steps = z_steps(total.shape[1])
        for index in range(step, steps):
            if index > step:
                self.send_along(total, target, index)
            self.add_along(total, target, index)
        landing = self.along_z(total, target, steps - 1)[2]
        half = result.shape[-1] // 2
        for side in range(2):
            at = side * half + self.left
            result[base, :, at : at + self.width] = target[side, landing]

    def sent_along(self, total, target):
        for step in range(z_steps(total.shape[1])):
            _, _, landing, blocks, _ = self.along_z(total, target, step)
            await_bytes(target.at[:, pl.ds(landing, blocks)], self.send_sem.at[4 + step])


def z_steps(depths):
    return depths.bit_length() - 1


def add_pairs(left, right):
    for side in range(left.shape[0]):
        for depth in range(left.shape[1]):
            left[side, depth] = left[side, depth] + right[side, depth]


def scatter_semaphores(copies):
    return [pltpu.SemaphoreType.DMA((copies,)), pltpu.SemaphoreType.DMA((copies,))]


class ScatterHere(Scatter):
    refs = 8

    @staticmethod
    def scratch(depths, rows, width):
        pair = pltpu.VMEM((2, depths, 2, rows, width), jnp.float32)
        one = pltpu.VMEM((2, depths, rows, width), jnp.float32)
        return [pair, pair, one, one, one, pltpu.SemaphoreType.DMA((2,)), *scatter_semaphores(4 + z_steps(depths))]

    def __init__(self, source, left, refs):
        self.source = source
        self.own, self.first, self.second, self.total, self.third, load_sem, send, recv = refs
        super().__init__(self.own.shape[-1], left, send, recv)
        self.loads = self.own_loads(source, self.own, load_sem)
        for load in self.loads:
            load.start()

    def start_first(self, part):
        size = self.own.shape[1] // 2
        self.send_first(self.source, self.first, part * size, size)

    def start_second(self, landed=None):
        for load in self.loads:
            load.wait()
        self.await_first(self.first if landed is None else landed)
        add_pairs(self.own, self.first)
        self.send_second(self.own, self.second)

    def add_second(self):
        self.await_second(self.second)
        for side in range(2):
            kept = self.y if side == 0 else self.x
            for depth in range(self.total.shape[1]):
                self.total[side, depth] = self.own[side, depth, kept] + self.second[side, depth]

    def third_first(self):
        self.add_second()
        self.send_along(self.total, self.third, 0)

    def third_next(self):
        self.add_along(self.total, self.third, 0)
        self.send_along(self.total, self.third, 1)

    def end(self, result, base):
        self.finish(self.total, self.third, result, base, 1)

    def sent(self, landed=None):
        self.sent_first(self.first if landed is None else landed)
        self.sent_second(self.second)
        self.sent_along(self.total, self.third)


class ScatterRest(Scatter):
    refs = 6

    @staticmethod
    def scratch(depths, rows, width):
        one = pltpu.VMEM((2, depths, rows, width), jnp.float32)
        return [one, one, one, pltpu.SemaphoreType.DMA((2,)), *scatter_semaphores(4 + z_steps(depths))]

    def __init__(self, kept, arrived, left, refs):
        self.total, self.second, self.third, load_sem, send, recv = refs
        width = self.total.shape[-1]
        super().__init__(width, left, send, recv)
        columns = pl.ds(left, width)
        self.loads = [
            pltpu.make_async_copy(kept.at[:, :, :, columns], self.total, load_sem.at[0]),
            pltpu.make_async_copy(arrived.at[:, :, :, columns], self.second, load_sem.at[1]),
        ]
        for load in self.loads:
            load.start()

    def third_first(self):
        for load in self.loads:
            load.wait()
        add_pairs(self.total, self.second)
        self.send_along(self.total, self.third, 0)

    third_next = ScatterHere.third_next
    end = ScatterHere.end

    def sent(self):
        self.sent_along(self.total, self.third)


def stem_forward_kernel(
    count,
    places,
    image_ref,
    first_ref,
    weights_ref,
    gain_ref,
    shift_ref,
    feature_ref,
    norm_hbm,
    input_hbm,
    scale_ref,
    norm_ref,
    input_ref,
    natural,
    skip,
    current,
    source,
    slots,
    send_sem,
    recv_sem,
    store_sem,
):
    me = my_index()
    greet_all(count)
    pixels = feature_ref.shape[0]
    rows = stem_rows(pixels)
    norm_at = row_starts(rows)
    input_at = row_starts(rows[1:])
    skip_at = row_starts(rows[:4])
    spacing = 16
    for row in range(image_ref.shape[1]):
        natural[row * 128 : (row + 1) * 128, :] = lax.dot_general(
            image_ref[:, row, :],
            first_ref[...],
            (((0,), (0,)), ((), ())),
            preferred_element_type=jnp.float32,
        )
    for start, place in places:
        norm_ref[place : place + 8, :] = natural[pl.ds(start, 8, stride=spacing), :]
    stores = []
    for layer in range(LAYERS):
        height = rows[layer]
        chunk = min(height, PIX_CHUNK)
        base = norm_at[layer]
        total = jnp.zeros((8, 128), jnp.float32)
        if layer > 0:
            weights = weights_ref[layer - 1]
            stacked = jnp.concatenate([weights, weights], axis=0)

            def convolve(index, total):
                at = pl.multiple_of(index * chunk, chunk)
                values = jnp.dot(
                    split_two(input_ref[pl.ds(input_at[layer - 1] + at, chunk), :]),
                    stacked,
                    preferred_element_type=jnp.float32,
                )
                norm_ref[pl.ds(base + at, chunk), :] = values
                return total + jnp.sum(values.reshape(chunk // 8, 8, 128), axis=0)

        else:

            def convolve(index, total):
                at = pl.multiple_of(index * chunk, chunk)
                values = norm_ref[pl.ds(base + at, chunk), :]
                return total + jnp.sum(values.reshape(chunk // 8, 8, 128), axis=0)

        total = lax.fori_loop(0, height // chunk, convolve, total, unroll=True)
        mean = jnp.sum(total, axis=0, keepdims=True) * (1.0 / height)

        def deviate(index, total):
            at = pl.multiple_of(index * chunk, chunk)
            values = norm_ref[pl.ds(base + at, chunk), :] - mean
            return total + jnp.sum((values * values).reshape(chunk // 8, 8, 128), axis=0)

        square = lax.fori_loop(0, height // chunk, deviate, jnp.zeros((8, 128), jnp.float32), unroll=True)
        square = jnp.sum(square, axis=0, keepdims=True)
        stats = jnp.concatenate([mean, square], axis=0)
        source[layer] = stats
        slots[layer, me] = stats
        if layer == 0:
            greeted(count)
        send_all(
            count,
            source.at[layer],
            slots.at[layer, me],
            send_sem.at[layer],
            recv_sem.at[layer],
        )
        wait_all(count, slots.at[layer], recv_sem.at[layer])
        means = slots[layer, :, 0, :]
        centre = group_sum(wide(jnp.sum(means, axis=0, keepdims=True))) * (0.25 / count)
        apart = means - centre[0:1]
        spread = jnp.sum(slots[layer, :, 1, :], axis=0, keepdims=True) + height * jnp.sum(
            apart * apart, axis=0, keepdims=True
        )
        variance = group_sum(wide(spread)) * (1.0 / (4 * height * count))
        inverse = lax.rsqrt(variance + group_eps)[0:1]
        centre = centre[0:1]
        scale_ref[layer : layer + 1, :] = inverse
        gain = gain_ref[layer : layer + 1, :]
        shift = shift_ref[layer : layer + 1, :]

        def activate(start, size):
            normed = (norm_ref[pl.ds(base + start, size), :] - centre) * inverse
            norm_ref[pl.ds(base + start, size), :] = normed
            lifted = normed * gain + shift
            return lifted / (1.0 + jnp.exp(-lifted))

        if layer < 4:
            quarter = height // 4
            part = min(quarter, 64)

            def pool(index, carry):
                at = pl.multiple_of(index * part, part)
                mean_of = jnp.zeros((part, 128), jnp.float32)
                for corner in range(4):
                    value = activate(corner * quarter + at, part)
                    skip[pl.ds(skip_at[layer] + corner * quarter + at, part), :] = value
                    mean_of = mean_of + value
                input_ref[pl.ds(input_at[layer] + at, part), :] = mean_of * 0.25
                return carry

            lax.fori_loop(0, quarter // part, pool, 0, unroll=True)
        elif layer < 8:
            part = min(height, 64)
            skipped = skip_at[7 - layer]

            def grow(index, carry):
                at = pl.multiple_of(index * part, part)
                value = activate(at, part)
                for corner in range(4):
                    place = corner * height + at
                    input_ref[pl.ds(input_at[layer] + place, part), :] = (
                        value + skip[pl.ds(skipped + place, part), :]
                    )
                return carry

            lax.fori_loop(0, height // part, grow, 0, unroll=True)
        else:

            def finish(index, carry):
                at = pl.multiple_of(index * chunk, chunk)
                current[pl.ds(at, chunk), :] = activate(at, chunk)
                return carry

            lax.fori_loop(0, height // chunk, finish, 0, unroll=True)
        parts = [(norm_ref, norm_hbm, base, height)]
        if layer < 8:
            parts.append((input_ref, input_hbm, input_at[layer], rows[layer + 1]))
        for index, (source_ref, target, begin, size) in enumerate(parts):
            store = pltpu.make_async_copy(
                source_ref.at[pl.ds(begin, size)],
                target.at[pl.ds(begin, size)],
                store_sem.at[index, layer],
            )
            store.start()
            stores.append(store)
    for start, place in places:
        natural[pl.ds(start, 8, stride=spacing), :] = current[place : place + 8, :]
    feature_ref[...] = natural[:pixels, :]
    for layer in range(LAYERS):
        wait_all(count, slots.at[layer], send_sem.at[layer])
    for store in stores:
        store.wait()


def stem_backward_kernel(
    count,
    places,
    grad_ref,
    image_ref,
    norm_hbm,
    input_hbm,
    scale_ref,
    weights_ref,
    gain_ref,
    shift_ref,
    split_ref,
    attn_norm_ref,
    ffn_norm_ref,
    tables_ref,
    up_ref,
    attn_ref,
    kept_ref,
    second_ref,
    early_ref,
    small_out,
    large_out,
    norm_ref,
    input_ref,
    natural,
    ordered,
    active,
    grad_conv,
    skip,
    grads,
    product,
    source,
    slots,
    first_source,
    first_slots,
    parts,
    shared,
    send_sem,
    recv_sem,
    part_send,
    part_recv,
    share_send,
    share_recv,
    split_slots,
    split_half,
    small_ref,
    small_slots,
    row_send,
    row_recv,
    load_sem,
    *scatter_refs,
):
    me = my_index()
    row = lax.axis_index("dp")
    core = lax.axis_index("tensor")
    rows_count = count // 2
    greet_all(count)
    pixels = grad_ref.shape[0]
    rows = stem_rows(pixels)
    norm_at = row_starts(rows)
    input_at = row_starts(rows[1:])
    loads = []
    for index, (source_ref, target, begin, size) in enumerate(
        [
            (norm_hbm, norm_ref, norm_at[8], rows[8]),
            (input_hbm, input_ref, input_at[7], rows[8]),
            (norm_hbm, norm_ref, 0, norm_at[8]),
            (input_hbm, input_ref, 0, input_at[7]),
        ]
    ):
        loads.append(
            pltpu.make_async_copy(
                source_ref.at[pl.ds(begin, size)], target.at[pl.ds(begin, size)], load_sem.at[index]
            )
        )
        loads[-1].start()
    jobs = []
    for index, (source_ref, left) in enumerate(
        [(up_ref, 0), (up_ref, 1), (attn_ref, 0), (attn_ref, 1)]
    ):
        refs = scatter_refs[index * ScatterHere.refs : (index + 1) * ScatterHere.refs]
        jobs.append(ScatterHere(source_ref, left * refs[0].shape[-1], refs))
    rest = 4 * ScatterHere.refs
    for index in range(2):
        refs = scatter_refs[rest + index * ScatterRest.refs : rest + (index + 1) * ScatterRest.refs]
        jobs.append(ScatterRest(kept_ref, second_ref, index * refs[0].shape[-1], refs))
    up_left, up_right, attn_left, attn_right, down_left, down_right = jobs
    early = up_left.first.shape[1] // 2
    early_load = pltpu.make_async_copy(
        early_ref, up_left.first.at[:, pl.ds(0, early)], load_sem.at[4]
    )
    early_load.start()
    up_landed = up_left.first.at[:, pl.ds(early, early)]
    small_rows, split_rows = 1064, 1072
    own_rows = 2 * split_half.shape[1]
    small_ref[...] = jnp.zeros_like(small_ref)
    for device in range(rows_count):
        lanes = slice(device * own_rows, (device + 1) * own_rows)
        small_ref[device, 0:1, :own_rows] = attn_norm_ref[:, lanes]
        small_ref[device, 1:2, :own_rows] = ffn_norm_ref[:, lanes]
        small_ref[device, 2 : 2 + tables_ref.shape[0], : tables_ref.shape[1]] = tables_ref[...]
    skip_at = row_starts(rows[:4])
    spacing = 16
    owners = count // 8
    owned = parts.shape[1]
    natural[:pixels, :] = grad_ref[...]
    for start, place in places:
        ordered[place : place + 8, :] = natural[pl.ds(start, 8, stride=spacing), :]

    def send_rows(first, last, source_of, target, place):
        def send(step, carry):
            other = lax.rem(row + step, rows_count)
            pltpu.make_async_remote_copy(
                src_ref=source_of(other),
                dst_ref=target.at[row],
                send_sem=row_send.at[place],
                recv_sem=row_recv.at[place],
                device_id=(other, core),
                device_id_type=MESH,
            ).start()
            return carry

        lax.fori_loop(first, last, send, 0)

    def weight_grad(layer):
        height = rows[layer]
        chunk = min(height, 512)

        def add(index, total):
            at = pl.multiple_of(index * chunk, chunk)
            return total + lax.dot_general(
                input_ref[pl.ds(input_at[layer - 1] + at, chunk), :].astype(jnp.bfloat16),
                grad_conv[pl.ds(norm_at[layer] + at, chunk), :].astype(jnp.bfloat16),
                (((0,), (0,)), ((), ())),
                preferred_element_type=jnp.float32,
            )

        product[layer - 1] = lax.fori_loop(
            0, height // chunk, add, jnp.zeros((128, 128), jnp.float32), unroll=True
        ).reshape(owners, owned, 128)

        def send(index, carry):
            owner = layer - 1 + 8 * index

            @pl.when(owner != me)
            def _():
                pltpu.make_async_remote_copy(
                    src_ref=product.at[layer - 1, index],
                    dst_ref=parts.at[me],
                    send_sem=part_send,
                    recv_sem=part_recv,
                    device_id=(owner // 2, lax.rem(owner, 2)),
                    device_id_type=MESH,
                ).start()

            @pl.when(owner == me)
            def _():
                parts[me] = product[layer - 1, index]

            return carry

        lax.fori_loop(0, owners, send, 0)

    def send_small():
        small_slots[row] = small_ref[row]
        send_rows(1, rows_count, lambda other: small_ref.at[other], small_slots, 0)

    def send_split():
        split_slots[row] = split_ref[row, core]
        send_rows(1, rows_count, lambda other: split_ref.at[other, core], split_slots, 1)

    def add_rows():
        wait_all(rows_count, small_slots, row_recv.at[0])
        small_out[small_rows : small_rows + 8, :] = jnp.sum(small_slots[...], axis=0)
        wait_all(rows_count, split_slots, row_recv.at[1])
        split_half[core] = jnp.sum(split_slots[...], axis=0)
        swap.start()

    def keep_rows():
        swap.wait()
        size = split_half.shape[1]
        for part in range(2):
            begin = split_rows + part * size
            small_out[begin : begin + size, :] = split_half[part]

    swap = pltpu.make_async_remote_copy(
        src_ref=split_half.at[core],
        dst_ref=split_half.at[core],
        send_sem=row_send.at[2],
        recv_sem=row_recv.at[2],
        device_id=(row, 1 - core),
        device_id_type=MESH,
    )

    def second_of_up():
        early_load.wait()
        up_left.start_second(up_landed)

    steps = {
        "small": send_small,
        "split": send_split,
        "rows": add_rows,
        "kept": keep_rows,
        "u1b": lambda: up_left.start_first(1),
        "u2": second_of_up,
    }
    for mark, job in zip("uvabde", jobs):
        if mark in "vab":
            steps[mark + "1a"] = functools.partial(job.start_first, 0)
            steps[mark + "1b"] = functools.partial(job.start_first, 1)
            steps[mark + "2"] = job.start_second
        steps[mark + "3a"] = job.third_first
        steps[mark + "3b"] = job.third_next

    greeted(count)
    for name in SCHEDULE["start"].split():
        steps[name]()
    for layer in range(LAYERS - 1, -1, -1):
        height = rows[layer]
        chunk = min(height, PIX_CHUNK)
        base = norm_at[layer]
        gain = gain_ref[layer : layer + 1, :]
        shift = shift_ref[layer : layer + 1, :]
        inverse = scale_ref[layer : layer + 1, :]
        incoming = ordered if layer == 8 else grads
        if layer == 8:
            loads[0].wait()
        if layer == 7:
            loads[2].wait()
        if layer == 6:
            loads[3].wait()

        def activate(index, carry):
            first, second = carry
            at = pl.multiple_of(index * chunk, chunk)
            normed = norm_ref[pl.ds(base + at, chunk), :]
            lifted = normed * gain + shift
            sigma = 1.0 / (1.0 + jnp.exp(-lifted))
            value = incoming[pl.ds(at, chunk), :] * sigma * (1.0 + lifted * (1.0 - sigma))
            active[pl.ds(at, chunk), :] = value
            first = first + jnp.sum(value.reshape(chunk // 8, 8, 128), axis=0)
            second = second + jnp.sum((value * normed).reshape(chunk // 8, 8, 128), axis=0)
            return first, second

        zero = jnp.zeros((8, 128), jnp.float32)
        first, second = lax.fori_loop(0, height // chunk, activate, (zero, zero), unroll=True)
        sums = jnp.concatenate(
            [jnp.sum(first, axis=0, keepdims=True), jnp.sum(second, axis=0, keepdims=True)], axis=0
        )
        source[layer] = sums
        slots[layer, me] = sums
        send_all(
            count, source.at[layer], slots.at[layer, me], send_sem.at[layer], recv_sem.at[layer]
        )
        for name in SCHEDULE[layer].split():
            steps[name]()
        if layer == 7:
            loads[1].wait()
        if layer < 8:
            weight_grad(layer + 1)
        wait_all(count, slots.at[layer], recv_sem.at[layer])
        totals = jnp.sum(slots[layer], axis=0)
        small_out[1032 + layer : 1033 + layer, :] = totals[1:2]
        small_out[1048 + layer : 1049 + layer, :] = totals[0:1]
        share = 1.0 / (4 * height * count)
        first_mean = group_sum(wide(totals[0:1] * gain))[0:1] * share
        second_mean = group_sum(wide(totals[1:2] * gain))[0:1] * share

        def conv_grad(start, size):
            value = inverse * (
                active[pl.ds(start, size), :] * gain
                - first_mean
                - norm_ref[pl.ds(base + start, size), :] * second_mean
            )
            grad_conv[pl.ds(base + start, size), :] = value
            return value

        if layer > 0:
            weights = weights_ref[layer - 1]
            stacked = jnp.concatenate([weights, weights], axis=1)

            def input_grad(start, size):
                return lax.dot_general(
                    split_two(conv_grad(start, size)),
                    stacked,
                    (((1,), (1,)), ((), ())),
                    preferred_element_type=jnp.float32,
                )

        if layer > 4:
            quarter = height // 4
            part = min(quarter, 64)
            skipped = skip_at[8 - layer]

            def shrink(index, carry):
                at = pl.multiple_of(index * part, part)
                total = jnp.zeros((part, 128), jnp.float32)
                for corner in range(4):
                    place = corner * quarter + at
                    value = input_grad(place, part)
                    skip[pl.ds(skipped + place, part), :] = value
                    total = total + value
                grads[pl.ds(at, part), :] = total
                return carry

            lax.fori_loop(0, quarter // part, shrink, 0, unroll=True)
        elif layer > 0:
            part = min(height, 128)
            skipped = skip_at[layer - 1]

            def spread_out(index, carry):
                at = pl.multiple_of(index * part, part)
                value = input_grad(at, part) * 0.25
                for corner in range(4):
                    place = corner * height + at
                    grads[pl.ds(place, part), :] = value + skip[pl.ds(skipped + place, part), :]
                return carry

            lax.fori_loop(0, height // part, spread_out, 0, unroll=True)
        else:

            def finish(index, carry):
                at = pl.multiple_of(index * chunk, chunk)
                conv_grad(at, chunk)
                return carry

            lax.fori_loop(0, height // chunk, finish, 0, unroll=True)
    for start, place in places:
        natural[pl.ds(start, 8, stride=spacing), :] = grad_conv[place : place + 8, :]
    first_part = jnp.zeros(first_source.shape, jnp.float32)
    for line in range(image_ref.shape[1]):
        first_part = first_part + dot_plain(
            image_ref[:, line, :],
            natural[line * 128 : (line + 1) * 128, :].astype(jnp.bfloat16),
        )
    first_source[...] = first_part
    first_slots[me] = first_part
    send_all(count, first_source, first_slots.at[me], send_sem.at[LAYERS], recv_sem.at[LAYERS])
    for name in SCHEDULE["end"].split():
        steps[name]()
    wait_all(count, parts, part_recv)
    shared[row, core] = jnp.sum(parts[...], axis=0)
    own_share = shared.at[row, core]
    for step in range(1, rows_count):
        start_remote(
            own_share, own_share, share_send.at[0], share_recv.at[0], lax.rem(row + step, rows_count)
        )
    for job, base in ((down_left, 2), (down_right, 2), (up_left, 0), (up_right, 0)):
        job.end(large_out, base)
    for name in SCHEDULE["last"].split():
        steps[name]()
    wait_all(count, first_slots, recv_sem.at[LAYERS])
    small_out[1024 : 1024 + first_slots.shape[1], :] = jnp.sum(first_slots[...], axis=0)
    landed_shares = shared.at[pl.ds(0, rows_count - 1), core]
    await_bytes(landed_shares, share_recv.at[0])
    forward = partner_copy(
        shared.at[:, core], shared.at[:, core], share_send.at[1], share_recv.at[1]
    )
    forward.start()
    forward.wait()
    for device in range(count):
        begin = (device % 8) * 128 + (device // 8) * owned
        small_out[begin : begin + owned, :] = shared[device // 2, device % 2]
    attn_left.end(large_out, 1)
    for layer in range(LAYERS):
        wait_all(count, slots.at[layer], send_sem.at[layer])
    wait_all(count, first_slots, send_sem.at[LAYERS])
    wait_all(rows_count, small_slots, row_send.at[0])
    wait_all(rows_count, split_slots, row_send.at[1])
    wait_all(count, parts, part_send)
    await_bytes(landed_shares, share_send.at[0])
    up_left.sent(up_landed)
    for job in jobs[1:]:
        job.sent()
    attn_right.end(large_out, 1)


def stem_forward(page_image, conv_first, conv_weights, group_gain, group_shift, devices):
    planes, tile_rows, columns = page_image.shape
    pixels = tile_rows * columns
    rows = stem_rows(pixels)
    places = natural_places(tile_rows, columns)
    whole = pl.BlockSpec(memory_space=pltpu.VMEM)
    far = pl.BlockSpec(memory_space=pltpu.HBM)
    return pl.pallas_call(
        functools.partial(stem_forward_kernel, devices, places),
        out_shape=(
            jax.ShapeDtypeStruct((pixels, 128), jnp.float32),
            jax.ShapeDtypeStruct((sum(rows), 128), jnp.float32),
            jax.ShapeDtypeStruct((sum(rows[1:]), 128), jnp.float32),
            jax.ShapeDtypeStruct((16, 128), jnp.float32),
        ),
        in_specs=[whole] * 5,
        out_specs=(whole, far, far, whole),
        scratch_shapes=[
            pltpu.VMEM((sum(rows), 128), jnp.float32),
            pltpu.VMEM((sum(rows[1:]), 128), jnp.float32),
            pltpu.VMEM((pixels + 128, 128), jnp.float32),
            pltpu.VMEM((sum(rows[:4]), 128), jnp.float32),
            pltpu.VMEM((pixels, 128), jnp.float32),
            pltpu.VMEM((LAYERS, 2, 128), jnp.float32),
            pltpu.VMEM((LAYERS, devices, 2, 128), jnp.float32),
            pltpu.SemaphoreType.DMA((LAYERS,)),
            pltpu.SemaphoreType.DMA((LAYERS,)),
            pltpu.SemaphoreType.DMA((2, LAYERS)),
        ],
        compiler_params=pltpu.CompilerParams(
            collective_id=0, has_side_effects=True, vmem_limit_bytes=VMEM_LIMIT
        ),
        cost_estimate=pl.CostEstimate(
            flops=54 * 10**9, bytes_accessed=2 * 10**7, transcendentals=0
        ),
        name="stem_forward",
    )(page_image, conv_first, conv_weights, group_gain, group_shift)


def stem_backward(
    grad_map,
    page_image,
    records,
    conv_weights,
    group_gain,
    group_shift,
    split,
    norm_grads,
    tables,
    up,
    attn,
    kept,
    second,
    early,
    devices,
):
    planes, tile_rows, columns = page_image.shape
    pixels = tile_rows * columns
    rows = stem_rows(pixels)
    norms, inputs, scales = records
    places = natural_places(tile_rows, columns)
    whole = pl.BlockSpec(memory_space=pltpu.VMEM)
    owned = 1024 // devices
    far = pl.BlockSpec(memory_space=pltpu.HBM)
    depths, _, _, own_rows, columns = up.shape
    return pl.pallas_call(
        functools.partial(stem_backward_kernel, devices, places),
        out_shape=(
            jax.ShapeDtypeStruct((1072 + 2 * split.shape[2], 128), jnp.float32),
            jax.ShapeDtypeStruct((3, own_rows, columns), jnp.float32),
        ),
        in_specs=[whole, whole, far, far] + [whole] * 8 + [far] * 5,
        out_specs=(whole,) * 2,
        scratch_shapes=[
            pltpu.VMEM((sum(rows), 128), jnp.float32),
            pltpu.VMEM((sum(rows[1:]), 128), jnp.float32),
            pltpu.VMEM((pixels + 128, 128), jnp.float32),
            pltpu.VMEM((pixels, 128), jnp.float32),
            pltpu.VMEM((pixels, 128), jnp.float32),
            pltpu.VMEM((sum(rows), 128), jnp.float32),
            pltpu.VMEM((sum(rows[:4]), 128), jnp.float32),
            pltpu.VMEM((pixels, 128), jnp.float32),
            pltpu.VMEM((8, devices // 8, owned, 128), jnp.float32),
            pltpu.VMEM((LAYERS, 2, 128), jnp.float32),
            pltpu.VMEM((LAYERS, devices, 2, 128), jnp.float32),
            pltpu.VMEM((planes, 128), jnp.float32),
            pltpu.VMEM((devices, planes, 128), jnp.float32),
            pltpu.VMEM((devices, owned, 128), jnp.float32),
            pltpu.VMEM((devices // 2, 2, owned, 128), jnp.float32),
            pltpu.SemaphoreType.DMA((LAYERS + 1,)),
            pltpu.SemaphoreType.DMA((LAYERS + 1,)),
            pltpu.SemaphoreType.DMA,
            pltpu.SemaphoreType.DMA,
            pltpu.SemaphoreType.DMA((2,)),
            pltpu.SemaphoreType.DMA((2,)),
            pltpu.VMEM((devices // 2, *split.shape[2:]), jnp.float32),
            pltpu.VMEM(split.shape[1:], jnp.float32),
            pltpu.VMEM((devices // 2 + 1, 8, 128), jnp.float32),
            pltpu.VMEM((devices // 2, 8, 128), jnp.float32),
            pltpu.SemaphoreType.DMA((3,)),
            pltpu.SemaphoreType.DMA((3,)),
            pltpu.SemaphoreType.DMA((5,)),
            *(ScatterHere.scratch(depths, own_rows, columns // 4) * 4),
            *(ScatterRest.scratch(depths, own_rows, columns // 4) * 2),
        ],
        compiler_params=pltpu.CompilerParams(
            collective_id=1, has_side_effects=True, vmem_limit_bytes=VMEM_LIMIT
        ),
        cost_estimate=pl.CostEstimate(
            flops=65 * 10**9, bytes_accessed=2 * 10**7, transcendentals=0
        ),
        name="stem_backward",
    )(
        grad_map,
        page_image,
        norms,
        inputs,
        scales,
        conv_weights,
        group_gain,
        group_shift,
        split,
        *norm_grads,
        tables,
        up,
        attn,
        kept,
        second,
        early,
    )


TILE = 128
QROWS = 256
KIND_ROWS = 8
FAR_LANE = 32
LOW_LANE = 40
PAD_LANE = 48
DOC_LANE = 56


def dot_last(left, right):
    return lax.dot_general(
        left, right, (((1,), (1,)), ((), ())), preferred_element_type=jnp.float32
    )


def dot_plain(left, right):
    return jnp.dot(left, right, preferred_element_type=jnp.float32)


def bucket_vector(tables_ref, table, head, relative):
    buckets = bucket_of(relative)
    values = jnp.zeros(relative.shape, jnp.float32)
    for bucket in range(NBUCKET):
        values = jnp.where(buckets == bucket, tables_ref[table, head, bucket], values)
    return values


def signed_lanes(width):
    lane = lax.broadcasted_iota(jnp.int32, (8, width), 1)
    return jnp.where(lane < width // 2, lane, lane - width)


def rolled(row, height):
    return pltpu.roll(
        jnp.broadcast_to(row[0:1], (height, row.shape[1])), 0, 1, stride=1, stride_axis=0
    )


def token_columns(boxes_ref, docs_ref, pads_ref, info):
    rows = [boxes_ref[0], boxes_ref[1], docs_ref[...], pads_ref[...], boxes_ref[2], boxes_ref[3]]
    rows = rows + [jnp.zeros_like(rows[0])] * 2
    info[...] = jnp.concatenate(rows, axis=0).astype(jnp.float32).T.astype(jnp.int32)


def token_lanes(info_ref, one_hot_x, query_base, key_base, pad_tiles):
    tokens = info_ref.shape[0]
    lane = lax.broadcasted_iota(jnp.int32, (TILE, 128), 1)
    row = lax.broadcasted_iota(jnp.int32, (TILE, 128), 0)
    for tile in range(tokens // TILE):
        at = slice(tile * TILE, (tile + 1) * TILE)
        left = info_ref[at, 0:1]
        top = info_ref[at, 1:2]
        doc = info_ref[at, 2:3]
        hidden = jnp.where(info_ref[at, 3:4] > 0, 0.0, masked_score)
        one_hot_x[at, :] = (lane == left).astype(jnp.float32).astype(jnp.bfloat16)
        shared = jnp.where((lane == top) | (lane == DOC_LANE + doc), 1.0, 0.0)
        query_base[at, :] = jnp.where(lane == FAR_LANE + tile, 1.0, shared).astype(jnp.bfloat16)
        key = jnp.where((lane == FAR_LANE + tile) | (lane == LOW_LANE + tile), 1.0, shared)
        key = jnp.where(lane == PAD_LANE + tile, hidden, key)
        key_base[1, at, :] = key.astype(jnp.bfloat16)
        key_base[0, at, :] = pltpu.roll(key, 64, 1).astype(jnp.bfloat16)
        pad_tiles[at, :] = jnp.where(lane == row, 0.0, jnp.broadcast_to(hidden, (TILE, 128)))


def head_matrices(tables_ref, head, side):
    first = bucket_vector(tables_ref, 1, head, signed_lanes(256))
    across = rolled(first, 128)[:, :128].astype(jnp.bfloat16)
    second = rolled(bucket_vector(tables_ref, 2, head, signed_lanes(128)), 128)
    row = lax.broadcasted_iota(jnp.int32, (128, 128), 0)
    lane = lax.broadcasted_iota(jnp.int32, (128, 128), 1)
    mixed = jnp.where((row < FAR_LANE) & (lane < FAR_LANE), second, 0.0)
    gap = lane % 8 - (row - FAR_LANE)
    before = jnp.full((128, 128), tables_ref[0, head, NBUCKET // 2 - 1], jnp.float32)
    after = jnp.full((128, 128), tables_ref[0, head, NBUCKET - 1], jnp.float32)
    far = jnp.where(gap <= -2, before, jnp.where(gap >= 2, after, 0.0))
    high = far.astype(jnp.bfloat16).astype(jnp.float32)
    of_tile = (row >= FAR_LANE) & (row < LOW_LANE)
    mixed = jnp.where(of_tile & (lane >= FAR_LANE) & (lane < LOW_LANE), high, mixed)
    mixed = jnp.where(of_tile & (lane >= LOW_LANE) & (lane < PAD_LANE), far - high, mixed)
    mixed = jnp.where(
        of_tile & (lane >= PAD_LANE) & (lane < DOC_LANE) & (gap != 0), 1.0, mixed
    )
    docs = (row >= DOC_LANE) & (row < 64) & (lane >= DOC_LANE) & (lane < 64)
    mixed = jnp.where(docs & (row != lane), masked_score, mixed)
    if side == 0:
        mixed = pltpu.roll(mixed, 64, 1)
    near = rolled(bucket_vector(tables_ref, 0, head, -signed_lanes(512)), 128)
    tiles = {0: near[:, :128], 1: near[:, 384:], -1: near[:, 128:256]}
    return across, mixed.astype(jnp.bfloat16), tiles


def own_half(side, own, other):
    lane = lax.broadcasted_iota(jnp.int32, own.shape, 1)
    return jnp.where((lane < 64) if side == 0 else (lane >= 64), own, other)


def widen_operands(
    side, head, tables_ref, query_ref, key_ref, one_hot_x, query_base, key_base, query_wide, key_wide, near
):
    across, mixed, tiles = head_matrices(tables_ref, head, side)
    for gap in (-1, 0, 1):
        near[side, gap + 1] = tiles[gap]
    scaled = (query_ref[...].astype(jnp.float32) * HDIM ** (-0.5)).astype(jnp.bfloat16)
    query_wide[side, :, :128] = own_half(
        side, scaled, dot_plain(query_base[...], mixed).astype(jnp.bfloat16)
    )
    query_wide[side, :, 128:] = dot_plain(one_hot_x[...], across).astype(jnp.bfloat16)
    key_wide[side, :, :128] = own_half(side, key_ref[...], key_base[side])
    key_wide[side, :, 128:] = one_hot_x[...]


def near_scores(scores, side, block, tile, near, pad_tiles):
    halves = []
    for half in range(QROWS // TILE):
        part = scores[:, half * TILE : (half + 1) * TILE]
        gap = tile - (block * (QROWS // TILE) + half)
        if abs(gap) <= 1:
            part = part + near[side, gap + 1]
        if gap == 0:
            part = part + pad_tiles[tile * TILE : (tile + 1) * TILE, :]
        halves.append(part)
    return jnp.concatenate(halves, axis=1)


def attention_forward_kernel(
    tables_ref,
    boxes_ref,
    docs_ref,
    pads_ref,
    query_ref,
    key_ref,
    value_ref,
    context_ref,
    exact_ref,
    lse_ref,
    info_ref,
    one_hot_x,
    query_base,
    key_base,
    pad_tiles,
    query_wide,
    key_wide,
    near,
    scores,
    weights,
):
    pair = pl.program_id(0)
    tokens = query_ref.shape[0]

    @pl.when(pair == 0)
    def _():
        token_columns(boxes_ref, docs_ref, pads_ref, info_ref)
        token_lanes(info_ref, one_hot_x, query_base, key_base, pad_tiles)

    def widen(side):
        widen_operands(
            side, pair * 2 + side, tables_ref, query_ref, key_ref, one_hot_x, query_base, key_base,
            query_wide, key_wide, near,
        )

    widen(0)
    values = value_ref[...].T
    steps = [(block, side) for block in range(tokens // QROWS) for side in range(2)]

    def products(step):
        block, side = step
        scores[side] = dot_last(
            key_wide[side], query_wide[side, block * QROWS : (block + 1) * QROWS, :]
        )

    def collect():
        block, side, total = waiting.pop(0)
        columns = slice(block * QROWS, (block + 1) * QROWS)
        context = dot_plain(values[side * 64 : (side + 1) * 64, :], weights[side])
        contexts.append(context * (1.0 / total))
        if side == 1:
            context = jnp.concatenate(contexts, axis=0)
            contexts.clear()
            exact_ref[:, columns] = context
            context_ref[columns, :] = context.T.astype(jnp.bfloat16)

    products(steps[0])
    widen(1)
    contexts = []
    waiting = []
    log_sums = []
    for index, (block, side) in enumerate(steps):
        columns = slice(block * QROWS, (block + 1) * QROWS)
        if index + 1 < len(steps):
            products(steps[index + 1])
        if waiting:
            collect()
        top = jnp.full((8, QROWS), masked_score, jnp.float32)
        for tile in range(tokens // TILE):
            at = slice(tile * TILE, (tile + 1) * TILE)
            part = scores[side, at, :]
            if any(abs(tile - 2 * block - half) <= 1 for half in range(2)):
                part = near_scores(part, side, block, tile, near, pad_tiles)
                scores[side, at, :] = part
            top = jnp.maximum(top, jnp.max(part.reshape(TILE // 8, 8, QROWS), axis=0))
        top = jnp.max(top, axis=0, keepdims=True)
        total = jnp.zeros((8, QROWS), jnp.float32)
        for tile in range(tokens // TILE):
            at = slice(tile * TILE, (tile + 1) * TILE)
            part = jnp.exp(scores[side, at, :] - top)
            total = total + jnp.sum(part.reshape(TILE // 8, 8, QROWS), axis=0)
            weights[side, at, :] = part.astype(jnp.bfloat16)
        total = jnp.sum(total, axis=0, keepdims=True)
        log_sums.append(top + jnp.log(total))
        if side == 1:
            lse_ref[0, :, columns] = jnp.concatenate(log_sums, axis=0)
            log_sums.clear()
        waiting.append((block, side, total))
        if index + 1 == len(steps):
            collect()


def attention_backward_kernel(
    early,
    tables_ref,
    boxes_ref,
    docs_ref,
    pads_ref,
    query_ref,
    key_ref,
    value_ref,
    grad_ref,
    exact_ref,
    lse_ref,
    down_ref,
    up_ref,
    part_out,
    grad_query_ref,
    grad_key_ref,
    grad_value_ref,
    diagonal_ref,
    down_landed,
    up_landed,
    other_out,
    info_ref,
    one_hot_x,
    query_base,
    key_base,
    pad_tiles,
    reverse,
    query_wide,
    key_wide,
    near,
    scores,
    grad_probs,
    probs_low,
    grad_low,
    key_turned,
    grad_near,
    grad_blocks,
    grad_key,
    grad_value,
    down_send,
    down_recv,
    up_send,
    up_recv,
    out_send,
    out_recv,
):
    pair = pl.program_id(0)
    tokens = query_ref.shape[0]
    down = Scatter(down_landed.shape[-1], 0, down_send, down_recv)
    up = Scatter(up_landed.shape[-1], 0, up_send, up_recv)

    @pl.when(pair == 0)
    def _():
        greet_partner()
        greet_rows((down.across_x, down.across_y))
        pl.semaphore_wait(pltpu.get_barrier_semaphore(), 3)
        down.send_first(down_ref, down_landed, early, down_landed.shape[1] - early)
        up.send_first(up_ref, up_landed, 0, up_landed.shape[1])
        partner_copy(part_out, other_out, out_send, out_recv).start()
        token_columns(boxes_ref, docs_ref, pads_ref, info_ref)
        token_lanes(info_ref, one_hot_x, query_base, key_base, pad_tiles)
        lane = lax.broadcasted_iota(jnp.int32, (TILE, 128), 1)
        for tile in range(tokens // TILE):
            at = slice(tile * TILE, (tile + 1) * TILE)
            left = info_ref[at, 0:1]
            top = info_ref[at, 1:2]
            reverse[at, :128] = jnp.where(lane == 127 - left, 1.0, 0.0).astype(jnp.bfloat16)
            reverse[at, 128:] = jnp.where(
                (lane == 31 - top) | (lane == FAR_LANE + tile), 1.0, 0.0
            ).astype(jnp.bfloat16)

    for side in range(2):
        widen_operands(
            side, pair * 2 + side, tables_ref, query_ref, key_ref, one_hot_x, query_base, key_base,
            query_wide, key_wide, near,
        )
        key_turned[side] = key_wide[side].T
    grad_near[...] = jnp.zeros_like(grad_near)
    grad_blocks[...] = jnp.zeros_like(grad_blocks)
    values = [
        own_half(side, value_ref[...], jnp.zeros(value_ref.shape, jnp.bfloat16)) for side in range(2)
    ]
    for block in range(tokens // QROWS):
        columns = slice(block * QROWS, (block + 1) * QROWS)
        grad_block = grad_ref[columns, :]
        product = grad_block.astype(jnp.float32).T * exact_ref[:, columns]
        scaled = (query_ref[columns, :].astype(jnp.float32) * HDIM ** (-0.5)).astype(jnp.bfloat16)
        turned = []
        key_terms = []
        value_terms = []
        for side in range(2):
            delta = jnp.sum(product[side * 64 : (side + 1) * 64, :], axis=0, keepdims=True)
            lse = lse_ref[0, side : side + 1, columns]
            scores[side] = dot_last(key_wide[side], query_wide[side, columns, :])
            grad_probs[side] = dot_last(values[side], grad_block)
            for tile in range(tokens // TILE):
                at = slice(tile * TILE, (tile + 1) * TILE)
                part = near_scores(scores[side, at, :], side, block, tile, near, pad_tiles)
                probs = jnp.exp(part - lse)
                grad_part = probs * (grad_probs[side, at, :] - delta)
                probs_low[side, at, :] = probs.astype(jnp.bfloat16)
                grad_low[side, at, :] = grad_part.astype(jnp.bfloat16)
                for half in range(QROWS // TILE):
                    gap = tile - (block * (QROWS // TILE) + half)
                    if abs(gap) <= 1:
                        grad_near[side, gap + 1] += grad_part[:, half * TILE : (half + 1) * TILE]
            value_terms.append(dot_plain(probs_low[side], grad_block))
            key_terms.append(dot_plain(grad_low[side], scaled))
            sums = dot_plain(key_turned[side], grad_low[side])
            turned.append(sums[side * 64 : (side + 1) * 64, :])
            grad_blocks[side] += dot_plain(sums.astype(jnp.bfloat16), reverse[columns, :])
        grad_query_ref[columns, :] = (
            (jnp.concatenate(turned, axis=0) * HDIM ** (-0.5)).T.astype(jnp.bfloat16)
        )
        key_term = own_half(0, key_terms[0], key_terms[1])
        value_term = own_half(0, value_terms[0], value_terms[1])
        if block == 0:
            grad_key[...] = key_term
            grad_value[...] = value_term
        else:
            grad_key[...] += key_term
            grad_value[...] += value_term
    grad_key_ref[...] = grad_key[...].astype(jnp.bfloat16)
    grad_value_ref[...] = grad_value[...].astype(jnp.bfloat16)
    row = lax.broadcasted_iota(jnp.int32, (128, 128), 0)
    lane = lax.broadcasted_iota(jnp.int32, (128, 128), 1)
    flip = jnp.where(row + lane == 127, 1.0, 0.0).astype(jnp.bfloat16)
    blank = jnp.zeros((128, 128), jnp.float32)

    def diagonal_sums(values):
        spread = jnp.concatenate([values, blank], axis=1)
        return jnp.sum(
            pltpu.roll(spread, 0, 1, stride=1, stride_axis=0), axis=0, keepdims=True
        )

    for side in range(2):
        misc = 64 * (1 - side)
        sums = [diagonal_sums(grad_blocks[side, 128:, :128])]
        below = grad_blocks[side, misc : misc + 64, 128:]
        small_row = lax.broadcasted_iota(jnp.int32, (64, 128), 0)
        small_lane = lax.broadcasted_iota(jnp.int32, (64, 128), 1)
        upright = jnp.where((small_row < FAR_LANE) & (small_lane < FAR_LANE), below, 0.0)
        sums.append(diagonal_sums(jnp.concatenate([upright, jnp.zeros((64, 128), jnp.float32)], axis=0)))
        for gap in range(3):
            tile = grad_near[side, gap]
            high = tile.astype(jnp.bfloat16)
            rest = (tile - high.astype(jnp.float32)).astype(jnp.bfloat16)
            sums.append(diagonal_sums(dot_plain(high, flip) + dot_plain(rest, flip)))
        gap = (small_row - FAR_LANE) - (small_lane - FAR_LANE)
        inside = (
            (small_row >= FAR_LANE)
            & (small_row < LOW_LANE)
            & (small_lane >= FAR_LANE)
            & (small_lane < LOW_LANE)
        )
        for chosen in (gap <= -2, gap >= 2):
            far = jnp.sum(jnp.where(inside & chosen, below, 0.0), axis=0, keepdims=True)
            sums.append(jnp.concatenate([far, blank[0:1]], axis=1))
        sums.append(jnp.zeros((1, 256), jnp.float32))
        diagonal_ref[side] = jnp.concatenate(sums, axis=0)

    @pl.when(pair == pl.num_programs(0) - 1)
    def _():
        late = down_landed.at[:, pl.ds(early, down_landed.shape[1] - early)]
        for scatter, landed in ((down, late), (up, up_landed)):
            scatter.await_first(landed)
            scatter.sent_first(landed)
        await_bytes(other_out, out_recv)
        await_bytes(other_out, out_send)


def attention_scratch(tokens):
    return [
        pltpu.VMEM((tokens, 8), jnp.int32),
        pltpu.VMEM((tokens, 128), jnp.bfloat16),
        pltpu.VMEM((tokens, 128), jnp.bfloat16),
        pltpu.VMEM((2, tokens, 128), jnp.bfloat16),
        pltpu.VMEM((tokens, 128), jnp.float32),
    ], [
        pltpu.VMEM((2, tokens, 256), jnp.bfloat16),
        pltpu.VMEM((2, tokens, 256), jnp.bfloat16),
        pltpu.VMEM((2, 3, TILE, TILE), jnp.float32),
        pltpu.VMEM((2, tokens, QROWS), jnp.float32),
    ]


def attention_forward(tables, places, heads):
    tokens, width = heads.shape[0], heads.shape[1] // 3
    pairs = width // 128
    own = pl.BlockSpec((tokens, 128), lambda pair: (0, pair))
    fixed, moving = attention_scratch(tokens)
    return pl.pallas_call(
        attention_forward_kernel,
        grid=(pairs,),
        out_shape=(
            jax.ShapeDtypeStruct((tokens, width), jnp.bfloat16),
            jax.ShapeDtypeStruct((width, tokens), jnp.float32),
            jax.ShapeDtypeStruct((pairs, 2, tokens), jnp.float32),
        ),
        in_specs=[
            pl.BlockSpec(memory_space=pltpu.SMEM),
            *[pl.BlockSpec(memory_space=pltpu.VMEM)] * 3,
            own,
            pl.BlockSpec((tokens, 128), lambda pair: (0, pairs + pair)),
            pl.BlockSpec((tokens, 128), lambda pair: (0, 2 * pairs + pair)),
        ],
        out_specs=(
            own,
            pl.BlockSpec((128, tokens), lambda pair: (pair, 0)),
            pl.BlockSpec((1, 2, tokens), lambda pair: (pair, 0, 0)),
        ),
        scratch_shapes=fixed
        + moving
        + [
            pltpu.VMEM((2, tokens, QROWS), jnp.bfloat16),
        ],
        compiler_params=pltpu.CompilerParams(
            dimension_semantics=("arbitrary",), vmem_limit_bytes=VMEM_LIMIT
        ),
        cost_estimate=pl.CostEstimate(
            flops=23 * 10**9, bytes_accessed=2 * 10**7, transcendentals=0
        ),
        name="attention_forward",
    )(tables, *places, heads, heads, heads)


def attention_backward(tables, places, heads, grad_context, exact, lse, down, up, part_out, early):
    tokens, width = grad_context.shape
    pairs = width // 128
    own = pl.BlockSpec((tokens, 128), lambda pair: (0, pair))
    fixed, moving = attention_scratch(tokens)
    low = jax.ShapeDtypeStruct((tokens, width), jnp.bfloat16)
    depths, _, _, rows, columns = down.shape
    return pl.pallas_call(
        functools.partial(attention_backward_kernel, early),
        grid=(pairs,),
        out_shape=(
            low,
            low,
            low,
            jax.ShapeDtypeStruct((2 * pairs, 8, 256), jnp.float32),
            jax.ShapeDtypeStruct((2, depths, 2, rows, columns // 2), jnp.float32),
            jax.ShapeDtypeStruct((2, depths // 2, 2, rows, columns // 4), jnp.float32),
            jax.ShapeDtypeStruct(part_out.shape, jnp.float32),
        ),
        in_specs=[
            pl.BlockSpec(memory_space=pltpu.SMEM),
            *[pl.BlockSpec(memory_space=pltpu.VMEM)] * 3,
            own,
            pl.BlockSpec((tokens, 128), lambda pair: (0, pairs + pair)),
            pl.BlockSpec((tokens, 128), lambda pair: (0, 2 * pairs + pair)),
            own,
            pl.BlockSpec((128, tokens), lambda pair: (pair, 0)),
            pl.BlockSpec((1, 2, tokens), lambda pair: (pair, 0, 0)),
            *[pl.BlockSpec(memory_space=pltpu.HBM)] * 3,
        ],
        out_specs=(
            own,
            own,
            own,
            pl.BlockSpec((2, 8, 256), lambda pair: (pair, 0, 0)),
            *[pl.BlockSpec(memory_space=pltpu.HBM)] * 3,
        ),
        scratch_shapes=fixed
        + [pltpu.VMEM((tokens, 256), jnp.bfloat16)]
        + moving
        + [
            pltpu.VMEM((2, tokens, QROWS), jnp.float32),
            pltpu.VMEM((2, tokens, QROWS), jnp.bfloat16),
            pltpu.VMEM((2, tokens, QROWS), jnp.bfloat16),
            pltpu.VMEM((2, 256, tokens), jnp.bfloat16),
            pltpu.VMEM((2, 3, TILE, TILE), jnp.float32),
            pltpu.VMEM((2, 256, 256), jnp.float32),
            pltpu.VMEM((tokens, 128), jnp.float32),
            pltpu.VMEM((tokens, 128), jnp.float32),
            *scatter_semaphores(2),
            *scatter_semaphores(2),
            pltpu.SemaphoreType.DMA,
            pltpu.SemaphoreType.DMA,
        ],
        compiler_params=pltpu.CompilerParams(
            dimension_semantics=("arbitrary",),
            collective_id=5,
            has_side_effects=True,
            vmem_limit_bytes=VMEM_LIMIT,
        ),
        cost_estimate=pl.CostEstimate(
            flops=30 * 10**9, bytes_accessed=2 * 10**7, transcendentals=0
        ),
        name="attention_backward",
    )(tables, *places, heads, heads, heads, grad_context, exact, lse, down, up, part_out)


def known_bucket(relative):
    magnitude = np.abs(relative)
    coarse = 8 + sum((magnitude >= edge).astype(int) for edge in bucket_edges)
    return np.where(magnitude < 8, magnitude, coarse) + np.where(relative > 0, 16, 0)


def bucket_grads(diagonals):
    lane = np.arange(256)
    far = np.zeros(256, int)
    wide_buckets = [
        known_bucket(lane - 127),
        known_bucket(lane - 31),
        known_bucket(lane - 127 - TILE),
        known_bucket(lane - 127),
        known_bucket(lane - 127 + TILE),
        far + NBUCKET // 2 - 1,
        far + NBUCKET - 1,
    ]
    table_of = (1, 2, 0, 0, 0, 0, 0)
    slots = np.stack([bucket + NBUCKET * table for bucket, table in zip(wide_buckets, table_of)])
    slots = jnp.asarray(slots, jnp.int32)
    chosen = (slots[..., None] == jnp.arange(3 * NBUCKET, dtype=jnp.int32)).astype(jnp.float32)
    return jnp.einsum("hrc,rcb->hb", diagonals[:, :7], chosen, precision=highest)


ROWS = 256
MIDDLE_ROWS = 256


def greet_partner():
    pl.semaphore_signal(
        pltpu.get_barrier_semaphore(),
        inc=1,
        device_id=(lax.axis_index("dp"), 1 - lax.axis_index("tensor")),
        device_id_type=MESH,
    )


def partner_copy(source, target, send_sem, recv_sem):
    return pltpu.make_async_remote_copy(
        src_ref=source,
        dst_ref=target,
        send_sem=send_sem,
        recv_sem=recv_sem,
        device_id=(lax.axis_index("dp"), 1 - lax.axis_index("tensor")),
        device_id_type=MESH,
    )


def dot_rows(left, right):
    return lax.dot_general(
        left, right, (((0,), (0,)), ((), ())), preferred_element_type=jnp.float32
    )


def inverse_rms(values):
    return lax.rsqrt(jnp.mean(values * values, axis=1, keepdims=True) + norm_eps)


def box_kernel(
    feature_ref,
    boxes_ref,
    docs_ref,
    pads_ref,
    embedded_ref,
    roi_ref,
    norm_ref,
    query_proj_ref,
    key_proj_ref,
    value_proj_ref,
    pooled_ref,
    stream_hbm,
    input_hbm,
    heads_hbm,
    stream_ref,
    input_ref,
    heads_ref,
    info_ref,
    features,
    mask,
    part,
    received,
    projections,
    send_sem,
    recv_sem,
    store_sem,
):
    greet_partner()
    token_columns(boxes_ref, docs_ref, pads_ref, info_ref)
    tokens = info_ref.shape[0]
    pixels = feature_ref.shape[0]
    tile_rows = pixels // 128
    first_row = lax.axis_index("tensor") * tile_rows
    features[...] = split_two(feature_ref[...])
    lane = lax.broadcasted_iota(jnp.int32, (ROWS, 128), 1)
    copies = []
    for block in range(tokens // ROWS):
        at = slice(block * ROWS, (block + 1) * ROWS)
        column = (lane >= info_ref[at, 0:1]) & (lane < info_ref[at, 4:5])
        column = jnp.where(column, 1.0, 0.0)
        top = jnp.broadcast_to(info_ref[at, 1:2], (ROWS, 128)) - first_row
        bottom = jnp.broadcast_to(info_ref[at, 5:6], (ROWS, 128)) - first_row
        for row in range(tile_rows):
            inside = jnp.where((top <= row) & (bottom > row), column, 0.0)
            mask[block % 2, :, row * 128 : (row + 1) * 128] = inside.astype(jnp.bfloat16)
        sums = dot_plain(mask[block % 2], features[...])
        part[at, :] = sums[:, :128] + sums[:, 128:]
        if block == 0:
            pl.semaphore_wait(pltpu.get_barrier_semaphore(), 1)
        copy = partner_copy(
            part.at[pl.ds(block * ROWS, ROWS)],
            received.at[pl.ds(block * ROWS, ROWS)],
            send_sem.at[block],
            recv_sem.at[block],
        )
        copy.start()
        copies.append(copy)
    stores = []
    width = query_proj_ref.shape[1]
    for index, ref in enumerate((query_proj_ref, key_proj_ref, value_proj_ref)):
        projections[:, index * width : (index + 1) * width] = ref[...]
    for block in range(tokens // ROWS):
        at = slice(block * ROWS, (block + 1) * ROWS)
        copies[block].wait_recv()
        area = (info_ref[at, 5:6] - info_ref[at, 1:2]) * (info_ref[at, 4:5] - info_ref[at, 0:1])
        pooled = ((part[at, :] + received[at, :]) / area.astype(jnp.float32)).astype(jnp.bfloat16)
        pooled_ref[at, :] = pooled
        stream = embedded_ref[at, :].astype(jnp.float32) + dot_plain(pooled, roi_ref[...])
        stream_ref[at, :] = stream
        attn_in = (stream * inverse_rms(stream) * norm_ref[...].reshape(1, -1)).astype(jnp.bfloat16)
        input_ref[at, :] = attn_in
        heads_ref[at, :] = dot_plain(attn_in, projections[...]).astype(jnp.bfloat16)
        rows = pl.ds(block * ROWS, ROWS)
        for index, (source, target) in enumerate(
            [(stream_ref, stream_hbm), (input_ref, input_hbm), (heads_ref, heads_hbm)]
        ):
            store = pltpu.make_async_copy(
                source.at[rows], target.at[rows], store_sem.at[index, block]
            )
            store.start()
            stores.append(store)
    for copy in copies:
        copy.wait_send()
    for store in stores:
        store.wait()


def box_forward(
    feature_map, places, embeddings, roi_proj, attn_norm, query_proj, key_proj, value_proj
):
    tokens, width = embeddings.shape
    local = query_proj.shape[1]
    blocks = tokens // ROWS
    whole = pl.BlockSpec(memory_space=pltpu.VMEM)
    far = pl.BlockSpec(memory_space=pltpu.HBM)
    return pl.pallas_call(
        box_kernel,
        out_shape=(
            jax.ShapeDtypeStruct((tokens, 128), jnp.bfloat16),
            jax.ShapeDtypeStruct((tokens, width), jnp.float32),
            jax.ShapeDtypeStruct((tokens, width), jnp.bfloat16),
            jax.ShapeDtypeStruct((tokens, 3 * local), jnp.bfloat16),
        ),
        in_specs=[whole] * 10,
        out_specs=(whole, far, far, far),
        scratch_shapes=[
            pltpu.VMEM((tokens, width), jnp.float32),
            pltpu.VMEM((tokens, width), jnp.bfloat16),
            pltpu.VMEM((tokens, 3 * local), jnp.bfloat16),
            pltpu.VMEM((tokens, 8), jnp.int32),
            pltpu.VMEM((feature_map.shape[0], 256), jnp.bfloat16),
            pltpu.VMEM((2, ROWS, feature_map.shape[0]), jnp.bfloat16),
            pltpu.VMEM((tokens, 128), jnp.float32),
            pltpu.VMEM((tokens, 128), jnp.float32),
            pltpu.VMEM((width, 3 * local), jnp.bfloat16),
            pltpu.SemaphoreType.DMA((blocks,)),
            pltpu.SemaphoreType.DMA((blocks,)),
            pltpu.SemaphoreType.DMA((3, blocks)),
        ],
        compiler_params=pltpu.CompilerParams(
            collective_id=2, has_side_effects=True, vmem_limit_bytes=VMEM_LIMIT
        ),
        cost_estimate=pl.CostEstimate(
            flops=12 * 10**9, bytes_accessed=2 * 10**7, transcendentals=0
        ),
        name="box_forward",
    )(
        feature_map,
        *places,
        embeddings,
        roi_proj,
        attn_norm,
        query_proj,
        key_proj,
        value_proj,
    )


def middle_kernel(
    early,
    context_ref,
    stream_hbm,
    cotangent_hbm,
    output_ref,
    norm_ref,
    up_hbm,
    down_hbm,
    middle_hbm,
    part_out_hbm,
    grad_middle_hbm,
    grad_context_hbm,
    grad_up_hbm,
    grad_down_hbm,
    early_hbm,
    grad_output_ref,
    grad_norm_ref,
    middle,
    cotangent,
    up,
    down,
    part,
    other,
    part_out,
    other_grad,
    ffn_in,
    hidden,
    grad_pre,
    staged,
    grad_low,
    grad_context,
    load_sem,
    store_sem,
    grad_sem,
    send_sem,
    recv_sem,
    early_send,
    early_recv,
):
    scatter = Scatter(early_hbm.shape[-1], 0, early_send, early_recv)
    greet_partner()
    greet_rows((scatter.across_x, scatter.across_y))
    norm = norm_ref[...].reshape(1, -1)
    tokens, width = stream_hbm.shape
    units = up_hbm.shape[1]
    blocks = tokens // MIDDLE_ROWS
    loads = [
        pltpu.make_async_copy(source, target, load_sem.at[index])
        for index, (source, target) in enumerate(
            [(cotangent_hbm, cotangent), (down_hbm, down), (stream_hbm, middle), (up_hbm, up)]
        )
    ]
    for load in loads:
        load.start()
    attn_copies = []
    for block in range(blocks):
        at = slice(block * MIDDLE_ROWS, (block + 1) * MIDDLE_ROWS)
        part[at, :] = dot_plain(context_ref[at, :], output_ref[...])
        if block == 0:
            pl.semaphore_wait(pltpu.get_barrier_semaphore(), 3)
        copy = partner_copy(
            part.at[pl.ds(block * MIDDLE_ROWS, MIDDLE_ROWS)],
            other.at[pl.ds(block * MIDDLE_ROWS, MIDDLE_ROWS)],
            send_sem.at[0, block],
            recv_sem.at[0, block],
        )
        copy.start()
        attn_copies.append(copy)
    for load in loads:
        load.wait()
    out_stores = []
    grad_copies = []
    for block in range(blocks):
        at = slice(block * MIDDLE_ROWS, (block + 1) * MIDDLE_ROWS)
        grad_hidden = dot_last(cotangent[at, :], down[...])
        attn_copies[block].wait()
        values = middle[at, :] + (part[at, :] + other[at, :])
        middle[at, :] = values
        inner = (values * inverse_rms(values) * norm).astype(jnp.bfloat16)
        ffn_in[at, :] = inner
        pre_act = dot_plain(inner, up[...])
        below = 0.5 * (1.0 + lax.erf(pre_act * (0.5**0.5)))
        density = jnp.exp(-0.5 * (pre_act * pre_act)) * 0.3989422804014327
        hidden[at, :] = (pre_act * below).astype(jnp.bfloat16)
        grad_pre[at, :] = (grad_hidden * (below + pre_act * density)).astype(jnp.bfloat16)
        part[at, :] = dot_last(grad_pre[at, :], up[...])
        copy = partner_copy(
            part.at[pl.ds(block * MIDDLE_ROWS, MIDDLE_ROWS)],
            other_grad.at[pl.ds(block * MIDDLE_ROWS, MIDDLE_ROWS)],
            send_sem.at[1, block],
            recv_sem.at[1, block],
        )
        copy.start()
        grad_copies.append(copy)
        part_out[at, :] = dot_plain(hidden[at, :], down[...])
        for index, (source, target) in enumerate([(middle, middle_hbm), (part_out, part_out_hbm)]):
            rows = pl.ds(block * MIDDLE_ROWS, MIDDLE_ROWS)
            store = pltpu.make_async_copy(
                source.at[rows], target.at[rows], store_sem.at[2 + index, block]
            )
            store.start()
            out_stores.append(store)
    half = width // 2
    stores = []
    for index, slot in enumerate((0, 1, 2, 1)):
        rows = slice((index % 2) * half, (index % 2 + 1) * half)
        if index == 3:
            stores[1].wait()
        if index < 2:
            staged[slot] = dot_rows(cotangent[:, rows], hidden[...])
            target = grad_down_hbm
        else:
            staged[slot] = dot_rows(ffn_in[:, rows], grad_pre[...])
            target = grad_up_hbm
        store = pltpu.make_async_copy(
            staged.at[slot], target.at[pl.ds((index % 2) * half, half)], grad_sem.at[index]
        )
        store.start()
        stores.append(store)
        if index == 0:
            size = early_hbm.shape[3]
            columns = scatter.columns(grad_down_hbm)
            for depth in range(early):
                for other_place in range(2):
                    for side, begin, partner in (
                        (0, 2 * other_place + 1 - scatter.x, scatter.across_x),
                        (1, 2 * (1 - scatter.y) + other_place, scatter.across_y),
                    ):
                        begin = pl.multiple_of((depth * 4 + begin) * size, 8)
                        start_remote(
                            staged.at[0, pl.ds(begin, size), columns[side]],
                            early_hbm.at[side, depth, other_place],
                            early_send.at[side],
                            early_recv.at[side],
                            partner,
                        )
    norm_total = jnp.zeros((8, width), jnp.float32)
    for block in range(blocks):
        at = slice(block * MIDDLE_ROWS, (block + 1) * MIDDLE_ROWS)
        values = middle[at, :]
        inverse = inverse_rms(values)
        hat = values * inverse
        grad_copies[block].wait()
        grad_inner = part[at, :] + other_grad[at, :]
        norm_total = norm_total + jnp.sum((grad_inner * hat).reshape(MIDDLE_ROWS // 8, 8, width), axis=0)
        scaled = grad_inner * norm
        back = inverse * (scaled - hat * jnp.mean(scaled * hat, axis=1, keepdims=True))
        grad_values = cotangent[at, :].astype(jnp.float32) + back
        out_stores[2 * block].wait()
        middle[at, :] = grad_values
        low = grad_values.astype(jnp.bfloat16)
        grad_low[at, :] = low
        grad_context[at, :] = dot_last(low, output_ref[...]).astype(jnp.bfloat16)
        for index, (source, target) in enumerate(
            [
                (middle, grad_middle_hbm),
                (grad_context, grad_context_hbm),
            ]
        ):
            rows = pl.ds(block * MIDDLE_ROWS, MIDDLE_ROWS)
            store = pltpu.make_async_copy(
                source.at[rows], target.at[rows], store_sem.at[index, block]
            )
            store.start()
            stores.append(store)
    grad_norm_ref[...] = jnp.sum(norm_total, axis=0, keepdims=True)
    grad_output_ref[...] = dot_rows(grad_low[...], context_ref[...])
    del stores[1]
    for store in stores + out_stores[1::2]:
        store.wait()
    if early:
        scatter.await_first(early_hbm)
        scatter.sent_first(early_hbm)


def middle_layer(
    context, stream, cotangent, output_proj, ffn_norm, up_proj, down_proj, depths, own_rows, early
):
    tokens, width = stream.shape
    units = up_proj.shape[1]
    local = context.shape[1]
    blocks = tokens // MIDDLE_ROWS
    whole = pl.BlockSpec(memory_space=pltpu.VMEM)
    far = pl.BlockSpec(memory_space=pl.ANY)
    wide_sum = pltpu.VMEM((tokens, width), jnp.float32)
    wide_low = pltpu.VMEM((tokens, width), jnp.bfloat16)
    unit_low = pltpu.VMEM((tokens, units), jnp.bfloat16)
    return pl.pallas_call(
        functools.partial(middle_kernel, early),
        out_shape=(
            jax.ShapeDtypeStruct((tokens, width), jnp.float32),
            jax.ShapeDtypeStruct((tokens, width), jnp.float32),
            jax.ShapeDtypeStruct((tokens, width), jnp.float32),
            jax.ShapeDtypeStruct((tokens, local), jnp.bfloat16),
            jax.ShapeDtypeStruct((width, units), jnp.float32),
            jax.ShapeDtypeStruct((width, units), jnp.float32),
            jax.ShapeDtypeStruct((2, max(early, 1), 2, own_rows, units // 2), jnp.float32),
            jax.ShapeDtypeStruct((width, local), jnp.float32),
            jax.ShapeDtypeStruct((1, width), jnp.float32),
        ),
        in_specs=[whole, far, far, whole, whole, far, far],
        out_specs=(far,) * 7 + (whole, whole),
        scratch_shapes=[
            wide_sum,
            wide_low,
            pltpu.VMEM((width, units), jnp.bfloat16),
            pltpu.VMEM((units, width), jnp.bfloat16),
            wide_sum,
            wide_sum,
            wide_sum,
            wide_sum,
            wide_low,
            unit_low,
            unit_low,
            pltpu.VMEM((3, width // 2, units), jnp.float32),
            wide_low,
            pltpu.VMEM((tokens, local), jnp.bfloat16),
            pltpu.SemaphoreType.DMA((4,)),
            pltpu.SemaphoreType.DMA((4, blocks)),
            pltpu.SemaphoreType.DMA((4,)),
            pltpu.SemaphoreType.DMA((2, blocks)),
            pltpu.SemaphoreType.DMA((2, blocks)),
            *scatter_semaphores(2),
        ],
        compiler_params=pltpu.CompilerParams(
            collective_id=3, has_side_effects=True, vmem_limit_bytes=VMEM_LIMIT
        ),
        cost_estimate=pl.CostEstimate(
            flops=32 * 10**9, bytes_accessed=2 * 10**7, transcendentals=0
        ),
        name="middle_layer",
    )(context, stream, cotangent, output_proj, ffn_norm, up_proj, down_proj)


def end_kernel(
    early,
    grad_query_ref,
    grad_key_ref,
    grad_value_ref,
    query_proj_ref,
    key_proj_ref,
    value_proj_ref,
    input_ref,
    stream_hbm,
    grad_middle_hbm,
    norm_ref,
    roi_ref,
    pooled_ref,
    boxes_ref,
    docs_ref,
    pads_ref,
    grad_output_ref,
    down_hbm,
    early_hbm,
    landed_hbm,
    middle_hbm,
    part_out_hbm,
    other_out_hbm,
    grad_stream_hbm,
    grad_heads_hbm,
    kept_hbm,
    second_hbm,
    layer_hbm,
    grad_roi_ref,
    grad_map_ref,
    grad_norm_ref,
    info_ref,
    grad_heads,
    projections,
    stream,
    grad_stream,
    part,
    other,
    weight_grad,
    grad_low,
    grad_box,
    first,
    landed,
    middle,
    part_out,
    other_out,
    layer_low,
    attn_in,
    operand_sem,
    load_sem,
    store_sem,
    grad_sem,
    send_sem,
    recv_sem,
    scatter_sem,
    scatter_send,
    scatter_recv,
):
    tokens, width = stream_hbm.shape
    local = grad_query_ref.shape[1]
    blocks = tokens // ROWS
    scatter = Scatter(first.shape[-1], 0, scatter_send, scatter_recv)
    greet_partner()
    norm = norm_ref[...].reshape(1, -1)
    greet_rows((scatter.across_x, scatter.across_y))
    operand_loads = []
    for index, (grad, proj) in enumerate(
        (
            (grad_query_ref, query_proj_ref),
            (grad_key_ref, key_proj_ref),
            (grad_value_ref, value_proj_ref),
        )
    ):
        columns = pl.ds(index * local, local)
        operand_loads.append(
            pltpu.make_async_copy(grad, grad_heads.at[:, columns], operand_sem.at[2 * index])
        )
        operand_loads.append(
            pltpu.make_async_copy(proj, projections.at[:, columns], operand_sem.at[2 * index + 1])
        )
    operand_loads.append(pltpu.make_async_copy(input_ref, attn_in, operand_sem.at[6]))
    first_loads = scatter.own_loads(down_hbm, first, scatter_sem)
    late = pl.ds(early, landed.shape[1] - early)
    first_loads.append(
        pltpu.make_async_copy(landed_hbm.at[:, late], landed.at[:, late], scatter_sem.at[2])
    )
    if early:
        first_loads.append(
            pltpu.make_async_copy(early_hbm, landed.at[:, pl.ds(0, early)], scatter_sem.at[3])
        )
    for load in first_loads + operand_loads:
        load.start()
    loads = [
        pltpu.make_async_copy(stream_hbm, stream, load_sem.at[0]),
        pltpu.make_async_copy(grad_middle_hbm, grad_stream, load_sem.at[1]),
    ]
    for load in loads:
        load.start()
    for load in first_loads:
        load.wait()
    add_pairs(first, landed)
    pl.semaphore_wait(pltpu.get_barrier_semaphore(), 3)
    scatter.send_second(first, second_hbm)
    kept_stores = [
        pltpu.make_async_copy(first.at[0, :, scatter.y], kept_hbm.at[0], scatter_sem.at[0]),
        pltpu.make_async_copy(first.at[1, :, scatter.x], kept_hbm.at[1], scatter_sem.at[1]),
    ]
    for store in kept_stores:
        store.start()
    token_columns(boxes_ref, docs_ref, pads_ref, info_ref)
    for load in operand_loads:
        load.wait()
    copies = []
    for block in range(blocks):
        at = slice(block * ROWS, (block + 1) * ROWS)
        part[at, :] = dot_last(grad_heads[at, :], projections[...])
        copy = partner_copy(
            part.at[pl.ds(block * ROWS, ROWS)],
            other.at[pl.ds(block * ROWS, ROWS)],
            send_sem.at[block],
            recv_sem.at[block],
        )
        copy.start()
        copies.append(copy)
    out_loads = [
        pltpu.make_async_copy(source, target, load_sem.at[2 + index])
        for index, (source, target) in enumerate(
            [(middle_hbm, middle), (part_out_hbm, part_out), (other_out_hbm, other_out)]
        )
    ]
    for load in out_loads:
        load.start()

    def add_weights(index):
        columns = slice(index * local, (index + 1) * local)
        weight_grad[:, columns] = dot_rows(attn_in[...], grad_heads[:, columns])

    add_weights(0)
    weight_grad[:, 3 * local :] = grad_output_ref[...]
    weight_store = pltpu.make_async_copy(weight_grad, grad_heads_hbm, grad_sem)
    for load in loads:
        load.wait()
    stores = []
    norm_total = jnp.zeros((8, width), jnp.float32)
    for block in range(blocks):
        at = slice(block * ROWS, (block + 1) * ROWS)
        values = stream[at, :]
        inverse = inverse_rms(values)
        hat = values * inverse
        if block in (1, 2):
            add_weights(block)
        if block == 2:
            weight_store.start()
        copies[block].wait()
        grad_inner = part[at, :] + other[at, :]
        norm_total = norm_total + jnp.sum((grad_inner * hat).reshape(ROWS // 8, 8, width), axis=0)
        scaled = grad_inner * norm
        back = inverse * (scaled - hat * jnp.mean(scaled * hat, axis=1, keepdims=True))
        grad_values = grad_stream[at, :] + back
        grad_stream[at, :] = grad_values
        rows = pl.ds(block * ROWS, ROWS)
        store = pltpu.make_async_copy(
            grad_stream.at[rows], grad_stream_hbm.at[rows], store_sem.at[block]
        )
        store.start()
        stores.append(store)
        low = grad_values.astype(jnp.bfloat16)
        grad_low[at, :] = low
        area = (info_ref[at, 5:6] - info_ref[at, 1:2]) * (info_ref[at, 4:5] - info_ref[at, 0:1])
        grad_box[at, :] = split_two(dot_last(low, roi_ref[...]) / area.astype(jnp.float32))
    grad_norm_ref[...] = jnp.sum(norm_total, axis=0, keepdims=True)
    for load in out_loads:
        load.wait()
    layer_store = pltpu.make_async_copy(layer_low, layer_hbm, load_sem.at[2])
    tile_rows = grad_map_ref.shape[0] // 128
    first_row = lax.axis_index("tensor") * tile_rows
    column = lax.broadcasted_iota(jnp.int32, (128, tokens), 0)
    inside = jnp.where(
        (column >= boxes_ref[0]) & (column < boxes_ref[2]), 1.0, 0.0
    ).astype(jnp.bfloat16)
    top = boxes_ref[1] - first_row
    bottom = boxes_ref[3] - first_row
    for row in range(tile_rows):
        if row < 2 * blocks:
            at = slice(row * ROWS // 2, (row + 1) * ROWS // 2)
            layer_low[at, :] = (middle[at, :] + (part_out[at, :] + other_out[at, :])).astype(
                jnp.bfloat16
            )
        if row == 2 * blocks:
            layer_store.start()
        chosen = jnp.where((top <= row) & (bottom > row), 1.0, 0.0).astype(jnp.bfloat16)
        sums = dot_plain(inside * chosen, grad_box[...])
        grad_map_ref[row * 128 : (row + 1) * 128, :] = sums[:, :128] + sums[:, 128:]
    grad_roi_ref[...] = dot_rows(grad_low[...], pooled_ref[...])
    layer_store.wait()
    for store in kept_stores:
        store.wait()
    scatter.await_second(second_hbm)
    scatter.sent_second(second_hbm)
    weight_store.wait()
    for store in stores:
        store.wait()


def end_layer(
    grad_heads,
    projections,
    attn_in,
    stream,
    grad_middle,
    attn_norm,
    roi_proj,
    pooled,
    places,
    grad_output,
    down,
    landed,
    early_landed,
    outs,
    pixels,
    early,
):
    tokens, width = stream.shape
    local = grad_heads[0].shape[1]
    blocks = tokens // ROWS
    whole = pl.BlockSpec(memory_space=pltpu.VMEM)
    far = pl.BlockSpec(memory_space=pltpu.HBM)
    wide_sum = pltpu.VMEM((tokens, width), jnp.float32)
    _, depths, _, rows, half = landed.shape
    return pl.pallas_call(
        functools.partial(end_kernel, early),
        out_shape=(
            jax.ShapeDtypeStruct((tokens, width), jnp.float32),
            jax.ShapeDtypeStruct((width, 4 * local), jnp.float32),
            jax.ShapeDtypeStruct((2, depths, rows, half), jnp.float32),
            jax.ShapeDtypeStruct((2, depths, rows, half), jnp.float32),
            jax.ShapeDtypeStruct((tokens, width), jnp.bfloat16),
            jax.ShapeDtypeStruct((width, 128), jnp.float32),
            jax.ShapeDtypeStruct((pixels, 128), jnp.float32),
            jax.ShapeDtypeStruct((1, width), jnp.float32),
        ),
        in_specs=[far] * 9 + [whole] * 7 + [far] * 6,
        out_specs=(far,) * 5 + (whole,) * 3,
        scratch_shapes=[
            pltpu.VMEM((tokens, 8), jnp.int32),
            pltpu.VMEM((tokens, 3 * local), jnp.bfloat16),
            pltpu.VMEM((width, 3 * local), jnp.bfloat16),
            wide_sum,
            wide_sum,
            wide_sum,
            wide_sum,
            pltpu.VMEM((width, 4 * local), jnp.float32),
            pltpu.VMEM((tokens, width), jnp.bfloat16),
            pltpu.VMEM((tokens, 256), jnp.bfloat16),
            pltpu.VMEM(landed.shape, jnp.float32),
            pltpu.VMEM(landed.shape, jnp.float32),
            wide_sum,
            wide_sum,
            wide_sum,
            pltpu.VMEM((tokens, width), jnp.bfloat16),
            pltpu.VMEM((tokens, width), jnp.bfloat16),
            pltpu.SemaphoreType.DMA((7,)),
            pltpu.SemaphoreType.DMA((5,)),
            pltpu.SemaphoreType.DMA((blocks,)),
            pltpu.SemaphoreType.DMA,
            pltpu.SemaphoreType.DMA((blocks,)),
            pltpu.SemaphoreType.DMA((blocks,)),
            pltpu.SemaphoreType.DMA((4,)),
            *scatter_semaphores(4),
        ],
        compiler_params=pltpu.CompilerParams(
            collective_id=4, has_side_effects=True, vmem_limit_bytes=VMEM_LIMIT
        ),
        cost_estimate=pl.CostEstimate(
            flops=15 * 10**9, bytes_accessed=2 * 10**7, transcendentals=0
        ),
        name="end_layer",
    )(
        *grad_heads,
        *projections,
        attn_in,
        stream,
        grad_middle,
        attn_norm,
        roi_proj,
        pooled,
        *places,
        grad_output,
        down,
        early_landed,
        landed,
        *outs,
    )


def unpack_kernel(
    places,
    sums_ref,
    own_ref,
    layer_in,
    stream_in,
    layer_out,
    stream_out,
    first_out,
    convs_out,
    gain_out,
    shift_out,
    roi_out,
    attn_norm_out,
    query_out,
    key_out,
    value_out,
    output_out,
    tables_out,
    ffn_norm_out,
    up_out,
    down_out,
    layer_kept,
    stream_kept,
    sem,
):
    loads = []
    copies = []
    count = sem.shape[1]
    for index, (source, kept, target) in enumerate(
        [(stream_in, stream_kept, stream_out), (layer_in, layer_kept, layer_out)]
    ):
        size = source.shape[0] // count
        for part in range(count):
            rows = pl.ds(part * size, size)
            loads.append(
                pltpu.make_async_copy(source.at[rows], kept.at[rows], sem.at[index, part])
            )
            copies.append(
                pltpu.make_async_copy(kept.at[rows], target.at[rows], sem.at[index, part])
            )
    for load in loads:
        load.start()
    for load, copy in zip(loads, copies):
        load.wait()
        copy.start()
    for target, begin in places:
        if target == "first":
            first_out[...] = sums_ref[begin : begin + first_out.shape[0], :]
        if target == "gain":
            gain_out[...] = sums_ref[begin : begin + LAYERS, :]
        if target == "shift":
            shift_out[...] = sums_ref[begin : begin + LAYERS, :]
        if target == "roi":
            roi_out[...] = sums_ref[begin : begin + roi_out.shape[0], :]
        if target == "small":
            attn_norm_out[...] = sums_ref[begin : begin + 1, : attn_norm_out.shape[1]]
            ffn_norm_out[...] = sums_ref[begin + 1 : begin + 2, : ffn_norm_out.shape[1]]
            for table in range(3):
                tables_out[table] = sums_ref[
                    begin + 2 : begin + 2 + tables_out.shape[1],
                    table * NBUCKET : (table + 1) * NBUCKET,
                ]
    for level in range(8):
        convs_out[level] = sums_ref[level * 128 : (level + 1) * 128, :]
    up_out[...] = own_ref[0]
    down_out[...] = own_ref[2]
    part = query_out.shape[1]
    for index, target in enumerate((query_out, key_out, value_out, output_out)):
        target[...] = own_ref[1, :, index * part : (index + 1) * part]
    for copy in copies:
        copy.wait()


def unpack(sums, own, layer_out, grad_stream, planes, heads):
    _, own_rows, columns = own.shape
    whole = pl.BlockSpec(memory_space=pltpu.VMEM)
    far = pl.BlockSpec(memory_space=pl.ANY)
    places = (("first", 1024), ("gain", 1032), ("shift", 1048), ("small", 1064), ("roi", 1072))

    def sized(*shape):
        return jax.ShapeDtypeStruct(shape, jnp.float32)

    return pl.pallas_call(
        functools.partial(unpack_kernel, places),
        out_shape=(
            jax.ShapeDtypeStruct(layer_out.shape, layer_out.dtype),
            jax.ShapeDtypeStruct(grad_stream.shape, grad_stream.dtype),
            sized(planes, 128),
            sized(8, 128, 128),
            sized(LAYERS, 128),
            sized(LAYERS, 128),
            sized(own_rows, 128),
            sized(1, own_rows),
            *[sized(own_rows, columns // 4)] * 4,
            sized(3, heads, NBUCKET),
            sized(1, own_rows),
            sized(own_rows, columns),
            sized(own_rows, columns),
        ),
        in_specs=[whole, whole, far, far],
        out_specs=(far, far) + (whole,) * 14,
        scratch_shapes=[
            pltpu.VMEM(layer_out.shape, layer_out.dtype),
            pltpu.VMEM(grad_stream.shape, grad_stream.dtype),
            pltpu.SemaphoreType.DMA((2, 4)),
        ],
        compiler_params=pltpu.CompilerParams(vmem_limit_bytes=VMEM_LIMIT),
        name="unpack",
    )(sums, own, layer_out, grad_stream)


def on_device(
    page_image,
    embeddings,
    cotangent,
    doc_ids,
    pad_mask,
    token_boxes,
    conv_first,
    conv_weights,
    group_gain,
    group_shift,
    roi_proj,
    attn_norm,
    query_proj,
    key_proj,
    value_proj,
    output_proj,
    bias_tables,
    ffn_norm,
    up_proj,
    down_proj,
):
    devices = lax.axis_size("dp") * lax.axis_size("tensor")
    feature_map, *records = stem_forward(
        page_image, conv_first, conv_weights, group_gain, group_shift, devices
    )
    places = (token_boxes, doc_ids, pad_mask)
    tables = bias_tables.swapaxes(1, 2)
    pooled, stream, attn_in, heads = box_forward(
        feature_map, places, embeddings, roi_proj, attn_norm, query_proj, key_proj, value_proj
    )
    context, exact, lse = attention_forward(tables, places, heads)
    rows_count = lax.axis_size("dp")
    width = stream.shape[1]
    own_rows = width // rows_count
    depths = rows_count // 4
    early = depths // 4 if own_rows % 8 == 0 else 0
    (
        middle,
        part_out,
        grad_middle,
        grad_context,
        grad_up,
        grad_down,
        early_landed,
        grad_output,
        grad_ffn_norm,
    ) = middle_layer(
        context,
        stream,
        cotangent,
        output_proj,
        ffn_norm,
        up_proj,
        down_proj,
        depths,
        own_rows,
        early,
    )

    def by_place(values):
        return values.reshape(depths, 2, 2, own_rows, values.shape[1])

    down, up = by_place(grad_down), by_place(grad_up)
    *grad_heads, diagonals, landed, up_landed, other_out = attention_backward(
        tables, places, heads, grad_context, exact, lse, down, up, part_out, early
    )
    grad_tables = bucket_grads(diagonals)
    grad_stream, grad_attn, kept, second, layer_out, grad_roi, grad_map, grad_attn_norm = end_layer(
        grad_heads,
        (query_proj, key_proj, value_proj),
        attn_in,
        stream,
        grad_middle,
        attn_norm,
        roi_proj,
        pooled,
        places,
        grad_output,
        down,
        landed,
        early_landed,
        (middle, part_out, other_out),
        feature_map.shape[0],
        early,
    )
    local_heads = grad_tables.shape[0]
    split = grad_roi.reshape(rows_count, 2, own_rows // 2, grad_roi.shape[1])
    sums, own = stem_backward(
        grad_map,
        page_image,
        records,
        conv_weights,
        group_gain,
        group_shift,
        split,
        (grad_attn_norm, grad_ffn_norm),
        grad_tables,
        up,
        by_place(grad_attn),
        kept,
        second,
        up_landed,
        devices,
    )
    outs = list(
        unpack(sums, own, layer_out, grad_stream, conv_first.shape[0], local_heads)
    )
    outs[6] = outs[6].T
    outs[7] = outs[7][0]
    outs[11] = outs[11].T
    outs[12] = outs[12].swapaxes(1, 2)
    outs[13] = outs[13][0]
    outs[15] = outs[15].T
    return tuple(outs)


def solution(mesh):
    placed = (
        P(None, ("dp", "tensor"), None),
        P("dp", None),
        P("dp", None),
        P("dp", None),
        P("dp", None),
        P(None, "dp", None),
        P(),
        P(),
        P(),
        P(),
        P(),
        P(),
        P(None, "tensor"),
        P(None, "tensor"),
        P(None, "tensor"),
        P("tensor", None),
        P(None, None, "tensor"),
        P(),
        P(None, "tensor"),
        P("tensor", None),
    )
    return jax.shard_map(
        on_device,
        mesh=mesh,
        in_specs=placed,
        out_specs=(
            P("dp", None),
            P("dp", None),
            P(),
            P(),
            P(),
            P(),
            P(None, "dp"),
            P("dp"),
            P("dp", "tensor"),
            P("dp", "tensor"),
            P("dp", "tensor"),
            P("tensor", "dp"),
            P(None, None, "tensor"),
            P("dp"),
            P("dp", "tensor"),
            P("tensor", "dp"),
        ),
        check_vma=False,
    )
```
